32 devices in a mesh: dp: 8 (over z, y), blk: 2 (over core), tensor: 2 (over x).
Axes of the slice: x: 2, y: 2, z: 4, core: 2. Of those that a mesh axis runs over, the one named last changes fastest.
Arguments:
- block_in: bfloat16 [16, 512, 768], P('dp', 'blk'), may hold values from -6 to 6
- crop_shape: int32 [16], P('dp'), may hold values from 0 to 2, as said below
- norm_gains: float32 [2, 768], replicated, may hold values from 0.5 to 1.5
- shifts: float32 [4, 768], replicated, may hold values from -1.75 to 1.75
- qkv_weight: bfloat16 [3, 768, 768], P(None, None, 'tensor'), may hold values from -0.21875 to 0.21875
- qv_bias: float32 [2, 768], P(None, 'tensor'), may hold values from -1.75 to 1.75
- out_weight: bfloat16 [768, 768], P('tensor'), may hold values from -0.875 to 0.875
- up_weight: bfloat16 [768, 3072], P(None, 'tensor'), may hold values from -0.21875 to 0.21875
- up_bias: float32 [3072], P('tensor'), may hold values from -1.75 to 1.75
- down_weight: bfloat16 [3072, 768], P('tensor'), may hold values from -0.109375 to 0.109375
- tconv_weight: bfloat16 [768, 1024], replicated, may hold values from -0.21875 to 0.21875
- kernels: bfloat16 [2, 3456, 128], replicated, may hold values from -0.109375 to 0.109375
- grad_out: bfloat16 [16, 512, 768], P('dp', 'blk'), may hold values from -6 to 6
- grad_decoded: bfloat16 [16, 16, 16, 16, 128], P(('dp', 'tensor'), 'blk'), may hold values from -6 to 6
Outputs:
- block_out: bfloat16 [16, 512, 768], P('dp', 'blk')
- decoded: bfloat16 [16, 16, 16, 16, 128], P(('dp', 'tensor'), 'blk')
- grad_input: bfloat16 [16, 512, 768], P('dp', 'blk')
- grad_gains: float32 [2, 768], replicated
- grad_shifts: float32 [4, 768], replicated
- grad_qkv: float32 [3, 768, 768], P(None, None, 'tensor')
- grad_qv_bias: float32 [2, 768], P(None, 'tensor')
- grad_out_weight: float32 [768, 768], P('tensor')
- grad_up: float32 [768, 3072], P(None, 'tensor')
- grad_up_bias: float32 [3072], P('tensor')
- grad_down: float32 [3072, 768], P('tensor')
- grad_tconv: float32 [768, 1024], P(None, 'tensor')
- grad_kernels: float32 [2, 3456, 128], P(None, None, 'tensor')
The draws below stay inside these ranges and needn't reach their ends.
Inputs may be any that keep to these rules, and one draw needn't show every extreme that they name: `crop_shape`: among the 2 items held by one index of dp, at least one has id 2.
All inputs are finite; a program needn't handle non-finite values.
Results may differ from the reference program's by a relative error of at most 0.025.
Values may be sent and summed in bfloat16 or wider, within the bound.
A program may use at most 256 MiB of HBM per device.

```python
import jax
import jax.numpy as jnp
from jax import lax

D = 768
FF = 3072
CH = 128
GRID = 8
ITEMS_DEV = 2
HD = 64
PATCHES = 512
VOX = 16
ITEMS = 16
N_TENSOR = 2


def draw_crop_shape(key, part):
    key = jax.random.fold_in(key, 11)
    shapes = jax.random.randint(jax.random.fold_in(key, 1), (ITEMS // ITEMS_DEV, ITEMS_DEV), 0, 3, dtype=jnp.int32)
    chosen = jax.random.randint(jax.random.fold_in(key, 2), (ITEMS // ITEMS_DEV, 1), 0, ITEMS_DEV, dtype=jnp.int32)
    places = jnp.arange(ITEMS_DEV, dtype=jnp.int32)[None, :]
    return jnp.where(places == chosen, 2, shapes).reshape(ITEMS).astype(jnp.int32)


def level_of(rng, shape, shards, smallest, top_value):
    def one(dim, blocks):
        steps = jax.random.uniform(jax.random.fold_in(jax.random.fold_in(rng, 6), dim), (blocks,), jnp.float32, smallest / len(shards), top_value / len(shards))
        return jnp.repeat(jnp.exp(steps), shape[dim] // blocks).reshape((-1,) + (1,) * (len(shape) - dim - 1))

    level = one(*shards[0])
    for cut in shards[1:]:
        level = level * one(*cut)
    return level


def scatter_about(key, shape, deviation, bound, cuts=(), held_as=jnp.bfloat16):
    drawn = jax.random.normal(key, shape, jnp.float32) * deviation
    if len(cuts) > 0:
        drawn = level_of(key, shape, cuts, -0.22, 0.18) * drawn
    return jnp.clip(drawn, min=-bound, max=bound).astype(held_as)


def setup_inputs(seed: int = 0) -> dict:
    seeds = jax.random.split(jax.random.key(seed), 15)
    block_in = scatter_about(seeds[0], (ITEMS, PATCHES, D), 1.0, 6.0, ((0, 8), (1, 2)))
    crop_shape = draw_crop_shape(jax.random.fold_in(seeds[14], 71), 0)
    norm_gains = jnp.clip(1.0 + 0.1 * jax.random.normal(seeds[2], (2, D), jnp.float32), 0.5, 1.5)
    shifts = scatter_about(seeds[3], (4, D), 0.3, 1.75, (), jnp.float32)
    qkv_weight = scatter_about(seeds[4], (3, D, D), D ** -0.5, 0.21875, ((2, 2),))
    qv_bias = scatter_about(seeds[5], (2, D), 0.3, 1.75, ((1, 2),), jnp.float32)
    out_weight = scatter_about(seeds[6], (D, D), (D // 16) ** -0.5, 0.875, ((0, 2),))
    up_weight = scatter_about(seeds[7], (D, FF), D ** -0.5, 0.21875, ((1, 2),))
    up_bias = scatter_about(seeds[8], (FF,), 0.3, 1.75, ((0, 2),), jnp.float32)
    down_weight = scatter_about(seeds[9], (FF, D), FF ** -0.5, 0.109375, ((0, 2),))
    tconv_weight = scatter_about(seeds[10], (D, 8 * CH), D ** -0.5, 0.21875)
    kernels = scatter_about(seeds[11], (2, 27 * CH, CH), (27 * CH) ** -0.5, 0.109375)
    grad_out = scatter_about(seeds[12], (ITEMS, PATCHES, D), 1.0, 6.0, ((0, 8), (1, 2)))
    grad_decoded = scatter_about(seeds[13], (ITEMS, VOX, VOX, VOX, CH), 1.0, 6.0, ((0, 16), (1, 2)))
    return {"block_in": block_in, "crop_shape": crop_shape, "norm_gains": norm_gains, "shifts": shifts, "qkv_weight": qkv_weight, "qv_bias": qv_bias, "out_weight": out_weight, "up_weight": up_weight, "up_bias": up_bias, "down_weight": down_weight, "tconv_weight": tconv_weight, "kernels": kernels, "grad_out": grad_out, "grad_decoded": grad_decoded}


HIGH = lax.Precision.HIGHEST

@jax.custom_vjp
def low(v):
    return lax.optimization_barrier(v.astype(jnp.bfloat16)).astype(jnp.float32)

@jax.custom_vjp
def low_back(v):
    return v

def low_keep(v):
    return (low(v), None)

def low_pass(kept, grad):
    return (grad,)

def back_keep(v):
    return (v, None)

def back_low(kept, grad):
    return (low(grad),)
low.defvjp(low_keep, low_pass)
low_back.defvjp(back_keep, back_low)

def layer_norm(value, gain, shift):
    centre = value - lax.optimization_barrier(jnp.mean(value, axis=-1, keepdims=True))
    spread = lax.optimization_barrier(jnp.mean(centre * centre, axis=-1, keepdims=True))
    return centre * lax.rsqrt(spread + 1e-06) * gain + shift

def patch_valid(crop_ids):
    extent_depth = jnp.where(crop_ids == 0, GRID * 3 // 4, jnp.where(crop_ids == 1, GRID // 2, GRID))
    extent_side = jnp.where(crop_ids == 0, GRID * 3 // 4, GRID)
    places = jnp.arange(GRID * GRID * GRID, dtype=jnp.int32)
    depth = places // (GRID * GRID)
    across = places // GRID % GRID
    along = places % GRID
    inside = (depth[None, :] < extent_depth[:, None]) & (across[None, :] < extent_side[:, None]) & (along[None, :] < extent_side[:, None])
    return inside.astype(jnp.float32)

def voxel_mask(valid):
    grid = valid.reshape(valid.shape[0], -1, GRID, GRID)
    for axis_at in (1, 2, 3):
        grid = jnp.repeat(grid, 2, axis=axis_at)
    return grid[..., None]

def to_voxels(lifted):
    count, rows, columns = lifted.shape
    depth = rows // (GRID * GRID)
    channels = columns // 8
    shaped = lifted.reshape(count, depth, GRID, GRID, 2, 2, 2, channels)
    return shaped.transpose(0, 1, 4, 2, 5, 3, 6, 7).reshape(count, 2 * depth, 2 * GRID, 2 * GRID, channels)

def conv_three(field, kernel):
    channels = kernel.shape[1]
    shaped = kernel.reshape(3, 3, 3, channels, channels)
    return lax.conv_general_dilated(field, shaped, (1, 1, 1), 'SAME', dimension_numbers=('NDHWC', 'DHWIO', 'NDHWC'), precision=HIGH)

def instance_norm(level, voxel_valid):
    count = lax.optimization_barrier(jnp.sum(voxel_valid, axis=(1, 2, 3), keepdims=True))
    mean = lax.optimization_barrier(jnp.sum(voxel_valid * level, axis=(1, 2, 3), keepdims=True)) / count
    second = lax.optimization_barrier(jnp.sum(voxel_valid * level * level, axis=(1, 2, 3), keepdims=True)) / count
    return (level - mean) * lax.rsqrt(second - mean * mean + 1e-05)

def forward(params, block_in, valid):
    norm_gains, shifts, qkv_weight, qv_bias, out_weight, up_weight, up_bias, down_weight, tconv_weight, kernels = params
    count, length, width = block_in.shape
    head_count = width // HD
    normed = low(layer_norm(block_in, norm_gains[0], shifts[0]))
    project = jnp.einsum('gpd,cde->cgpe', normed, qkv_weight, precision=HIGH)
    query = low(low_back(project[0] + qv_bias[0])).reshape(count, length, head_count, HD)
    keys = low(low_back(project[1])).reshape(count, length, head_count, HD)
    values = low(low_back(project[2] + qv_bias[1])).reshape(count, length, head_count, HD)
    scores = low_back(jnp.einsum('gqhe,gkhe->ghqk', query, keys, precision=HIGH) * HD ** (-0.5))
    scores = jnp.where(valid[:, None, None, :] > 0.5, scores, -1000000000.0)
    probs = low(low_back(jax.nn.softmax(scores, axis=-1)))
    mixed = jnp.einsum('ghqk,gkhe->gqhe', probs, values, precision=HIGH).reshape(count, length, width)
    mixed = low(low_back(mixed))
    share = width // N_TENSOR
    partial_value = jnp.einsum('gpte,ted->tgpd', mixed.reshape(count, length, N_TENSOR, share), out_weight.reshape(N_TENSOR, share, width), precision=HIGH)
    middle = block_in + low_back(lax.optimization_barrier(jnp.sum(low(partial_value), axis=0)) + shifts[2])
    normed_two = low(layer_norm(middle, norm_gains[1], shifts[1]))
    hidden = low_back(jnp.einsum('gpd,df->gpf', normed_two, up_weight, precision=HIGH) + up_bias)
    active = low(jax.nn.gelu(hidden))
    share = FF // N_TENSOR
    partial_value = jnp.einsum('gptf,tfd->tgpd', active.reshape(count, length, N_TENSOR, share), down_weight.reshape(N_TENSOR, share, width), precision=HIGH)
    block_out = middle + low_back(lax.optimization_barrier(jnp.sum(low(partial_value), axis=0)) + shifts[3])
    tapped = low(block_out)
    lifted = low_back(jnp.einsum('gpd,dk->gpk', tapped, tconv_weight, precision=HIGH))
    voxel_valid = voxel_mask(valid)
    field = low(to_voxels(lifted) * voxel_valid)
    level = low_back(conv_three(field, kernels[0]))
    field = low(jax.nn.silu(instance_norm(level, voxel_valid)) * voxel_valid)
    level = low_back(conv_three(field, kernels[1]))
    decoded = jax.nn.silu(instance_norm(level, voxel_valid)) * voxel_valid
    return (block_out, decoded)

def reference(block_in, crop_shape, norm_gains, shifts, qkv_weight, qv_bias, out_weight, up_weight, up_bias, down_weight, tconv_weight, kernels, grad_out, grad_decoded):
    params = tuple((weight_arg.astype(jnp.float32) for weight_arg in (norm_gains, shifts, qkv_weight, qv_bias, out_weight, up_weight, up_bias, down_weight, tconv_weight, kernels)))
    groups = ITEMS // ITEMS_DEV

    def regroup(array):
        return array.reshape((groups, ITEMS_DEV) + array.shape[1:])

    def one_group(totals, pieces):
        block_piece, crop_piece, out_piece, dec_piece = pieces
        valid = patch_valid(crop_piece)

        def run(weights, inputs):
            return forward(weights, inputs, valid)
        outputs, backward = jax.vjp(run, params, block_piece.astype(jnp.float32))
        grads, grad_in = backward((out_piece.astype(jnp.float32), dec_piece.astype(jnp.float32)))
        totals = jax.tree.map(jnp.add, totals, grads)
        return (totals, (outputs[0].astype(jnp.bfloat16), outputs[1].astype(jnp.bfloat16), grad_in.astype(jnp.bfloat16)))
    starts = jax.tree.map(jnp.zeros_like, params)
    totals, results = lax.scan(one_group, starts, (regroup(block_in), regroup(crop_shape), regroup(grad_out), regroup(grad_decoded)))
    block_out = results[0].reshape(block_in.shape)
    decoded = results[1].reshape(grad_decoded.shape)
    grad_input = results[2].reshape(block_in.shape)
    return (block_out, decoded, grad_input, totals[0], totals[1], totals[2], totals[3], totals[4], totals[5], totals[6], totals[7], totals[8], totals[9])
```

```python
import functools

import jax
import jax.numpy as jnp
from jax import lax
from jax.experimental import pallas as pl
from jax.experimental.pallas import tpu as pltpu
from jax.sharding import PartitionSpec as P

GRID = 8
HD = 64

MESH = pl.DeviceIdType.MESH
GROUP = 8
FAR = 4


def place():
    dp = lax.axis_index("dp")
    blk = lax.axis_index("blk")
    tensor = lax.axis_index("tensor")
    near = lax.rem(dp, 2)
    far = lax.rem(dp // 2, FAR)
    first = dp // GROUP * GROUP
    return (dp, blk, tensor, near, far, first)


def peers():
    dp, blk, tensor, near, far, first = place()
    core = (dp, 1 - blk, tensor)
    cross = (dp, blk, 1 - tensor)
    beside = (first + 2 * far + 1 - near, blk, tensor)
    along = [(first + 2 * lax.rem(far + step, FAR) + near, blk, tensor) for step in range(1, FAR)]
    return (core, cross, beside, along)


def greet(devices):
    barrier = pltpu.get_barrier_semaphore()
    for device in devices:
        pl.semaphore_signal(barrier, inc=1, device_id=device, device_id_type=MESH)
    pl.semaphore_wait(barrier, len(devices))


def remote(src, dst, send, recv, device):
    return pltpu.make_async_remote_copy(
        src_ref=src, dst_ref=dst, send_sem=send, recv_sem=recv, device_id=device,
        device_id_type=MESH,
    )


def rows_at(start, size):
    return pl.ds(pl.multiple_of(start, 16), size)


def add_into(target, target_at, parts, rows, tile):
    @pl.loop(0, rows // tile)
    def _(step):
        at = step * tile
        total = None
        for ref, offset in parts:
            piece = ref[rows_at(offset + at, tile), :].astype(jnp.float32)
            total = piece if total is None else total + piece
        target[rows_at(target_at + at, tile), :] = total.astype(jnp.bfloat16)


class Sum:
    def __init__(self, own, from_core, from_near, from_far, total, send, recv):
        self.own, self.from_core, self.from_near = own, from_core, from_near
        self.from_far, self.total = from_far, total
        self.send, self.recv = send, recv
        self.rows = own.shape[0]
        self.half, self.quarter, self.piece = self.rows // 2, self.rows // 4, self.rows // 16
        dp, self.blk, tensor, self.near, self.far, first = place()
        self.core, cross, self.beside, self.along = peers()
        self.tile = 48 if self.piece % 48 == 0 else 32
        self.waiting = []

    def start(self, index, src, dst, device):
        copy = remote(src, dst, self.send.at[index], self.recv.at[index], device)
        copy.start()
        self.waiting.append(copy)
        return copy

    def step0(self):
        self.c0 = self.start(
            0, self.own.at[rows_at((1 - self.blk) * self.half, self.half)], self.from_core,
            self.core,
        )

    def step1(self):
        self.c0.wait_recv()
        add_into(
            self.from_core, 0, [(self.from_core, 0), (self.own, self.blk * self.half)],
            self.half, self.tile,
        )
        self.c1 = self.start(
            1, self.from_core.at[rows_at((1 - self.near) * self.quarter, self.quarter)],
            self.from_near, self.beside,
        )

    def step2(self):
        self.c1.wait_recv()
        add_into(
            self.from_near, 0,
            [(self.from_near, 0), (self.from_core, self.near * self.quarter)],
            self.quarter, self.tile,
        )
        self.c2 = []
        for step in range(1, FAR):
            whose = lax.rem(self.far + step, FAR)
            self.c2.append(
                self.start(
                    1 + step, self.from_near.at[rows_at(whose * self.piece, self.piece)],
                    self.from_far.at[step - 1], self.along[step - 1],
                )
            )

    def step3(self):
        for copy in self.c2:
            copy.wait_recv()
        self.base = self.blk * self.half + self.near * self.quarter
        at = self.base + self.far * self.piece
        add_into(
            self.total, at,
            [(self.from_near, self.far * self.piece)]
            + [(self.from_far.at[step], 0) for step in range(FAR - 1)],
            self.piece, self.tile,
        )
        self.c3 = []
        for step in range(1, FAR):
            where = self.total.at[rows_at(at, self.piece)]
            self.c3.append(self.start(1 + FAR - 1 + step, where, where, self.along[step - 1]))

    def step4(self):
        for copy in self.c3:
            copy.wait_recv()
        where = self.total.at[rows_at(self.base, self.quarter)]
        self.c4 = self.start(2 * FAR, where, where, self.beside)

    def step5(self):
        self.c4.wait_recv()
        where = self.total.at[rows_at(self.blk * self.half, self.half)]
        self.c5 = self.start(2 * FAR + 1, where, where, self.core)

    def step6(self):
        self.c5.wait_recv()
        for copy in self.waiting:
            copy.wait_send()


COPIES = 2 * FAR + 2


def sum_scratch(rows, columns):
    return [
        pltpu.VMEM((rows // 2, columns), jnp.bfloat16),
        pltpu.VMEM((rows // 4, columns), jnp.bfloat16),
        pltpu.VMEM((FAR - 1, rows // 16, columns), jnp.bfloat16),
    ]


def total_kernel(count, *refs):
    owns, totals = refs[:count], refs[count : 2 * count]
    scratch = refs[2 * count :]
    send, recv = scratch[3 * count :]
    core, cross, beside, along = peers()
    greet([core, beside] + along)
    sums = [
        Sum(owns[i], *scratch[3 * i : 3 * i + 3], totals[i], send.at[i], recv.at[i])
        for i in range(count)
    ]
    for wave in range(count + 6):
        for i in range(count):
            if 0 <= wave - i <= 6:
                getattr(sums[i], "step" + str(wave - i))()


def total_over_group(arrays):
    count = len(arrays)
    scratch = []
    for array in arrays:
        scratch += sum_scratch(*array.shape)
    return pl.pallas_call(
        functools.partial(total_kernel, count),
        out_shape=[jax.ShapeDtypeStruct(array.shape, jnp.bfloat16) for array in arrays],
        in_specs=[pl.BlockSpec(memory_space=pltpu.VMEM)] * count,
        out_specs=[pl.BlockSpec(memory_space=pltpu.VMEM)] * count,
        scratch_shapes=scratch
        + [pltpu.SemaphoreType.DMA((count, COPIES)), pltpu.SemaphoreType.DMA((count, COPIES))],
        name="weight_sums",
        compiler_params=pltpu.CompilerParams(
            collective_id=0, has_side_effects=True, vmem_limit_bytes=60 * 2**20
        ),
    )(*arrays)


def swap(value, axis):
    return lax.ppermute(value, axis, [(0, 1), (1, 0)])


def pair_sum(value):
    return value.astype(jnp.float32) + swap(value, "tensor").astype(jnp.float32)


def extended(block, sides, width):
    for axis, dim in sides:
        count = lax.axis_size(axis)
        forward = [(i, i + 1) for i in range(count - 1)]
        backward = [(target, source) for source, target in forward]
        low = lax.ppermute(
            lax.slice_in_dim(block, block.shape[dim] - width, None, axis=dim), axis, forward
        )
        high = lax.ppermute(lax.slice_in_dim(block, 0, width, axis=dim), axis, backward)
        block = jnp.concatenate([low, block, high], axis=dim)
    return block


def layer_norm(value, gain, shift):
    centre = value - jnp.mean(value, axis=-1, keepdims=True)
    spread = jnp.mean(centre * centre, axis=-1, keepdims=True)
    return centre * lax.rsqrt(spread + 1e-06) * gain + shift


def patch_valid(crop_ids):
    extent_depth = jnp.where(
        crop_ids == 0, GRID * 3 // 4, jnp.where(crop_ids == 1, GRID // 2, GRID)
    )
    extent_side = jnp.where(crop_ids == 0, GRID * 3 // 4, GRID)
    places = jnp.arange(GRID * GRID * GRID, dtype=jnp.int32)
    depth = places // (GRID * GRID)
    across = places // GRID % GRID
    along = places % GRID
    inside = (
        (depth[None, :] < extent_depth[:, None])
        & (across[None, :] < extent_side[:, None])
        & (along[None, :] < extent_side[:, None])
    )
    return inside.astype(jnp.float32)


def voxel_mask(valid):
    grid = valid.reshape(valid.shape[0], -1, GRID, GRID)
    for axis_at in (1, 2, 3):
        grid = jnp.repeat(grid, 2, axis=axis_at)
    return grid[..., None]


def to_voxels(lifted):
    count, rows, columns = lifted.shape
    depth = rows // (GRID * GRID)
    channels = columns // 8
    shaped = lifted.reshape(count, depth, GRID, GRID, 2, 2, 2, channels)
    return shaped.transpose(0, 1, 4, 2, 5, 3, 6, 7).reshape(
        count, 2 * depth, 2 * GRID, 2 * GRID, channels
    )


def from_voxels(field):
    count, depth, height, breadth, channels = field.shape
    shaped = field.reshape(count, depth // 2, 2, GRID, 2, GRID, 2, channels)
    return shaped.transpose(0, 1, 3, 5, 2, 4, 6, 7).reshape(
        count, depth // 2 * GRID * GRID, 8 * channels
    )


def columns_of(padded):
    count, depth, height, breadth, channels = padded.shape
    depth, height, breadth = (depth - 2, height - 2, breadth - 2)
    pieces = [
        padded[
            :, deep_at : deep_at + depth, high_at : high_at + height, wide_at : wide_at + breadth, :
        ]
        for deep_at in range(3)
        for high_at in range(3)
        for wide_at in range(3)
    ]
    return jnp.concatenate(pieces, axis=-1).reshape(count * depth * height * breadth, 27 * channels)


def with_rims(field):
    deeper = extended(field, (("blk", 1),), 1)
    return jnp.pad(deeper, ((0, 0), (0, 0), (1, 1), (1, 1), (0, 0)))


def channel_sums(first_term, second_term):
    sums = jnp.stack([jnp.sum(first_term, axis=(1, 2, 3)), jnp.sum(second_term, axis=(1, 2, 3))])
    return sums + swap(sums, "blk")


def norm_forward(level, voxel_valid, voxel_count):
    sums = channel_sums(voxel_valid * level, voxel_valid * level * level)
    mean = (sums[0] / voxel_count)[:, None, None, None, :]
    second = (sums[1] / voxel_count)[:, None, None, None, :]
    scale = lax.rsqrt(second - mean * mean + 1e-05)
    return ((level - mean) * scale, scale)


def norm_backward(dnormed, normed, scale, voxel_valid, voxel_count):
    sums = channel_sums(dnormed, dnormed * normed)
    mean_grad = (sums[0] / voxel_count)[:, None, None, None, :]
    mean_cross = (sums[1] / voxel_count)[:, None, None, None, :]
    return scale * (dnormed - voxel_valid * (mean_grad + normed * mean_cross))


def conv_forward(field, kernel):
    padded = with_rims(field)
    level = jnp.dot(columns_of(padded), kernel, preferred_element_type=jnp.float32)
    return (padded, level.reshape(field.shape[:4] + (kernel.shape[1],)))


def conv_input_grad(dlevel, kernel):
    channels = kernel.shape[1]
    flipped = (
        kernel.reshape(27, channels, channels)[::-1]
        .transpose(0, 2, 1)
        .reshape(27 * channels, channels)
    )
    result = jnp.dot(columns_of(with_rims(dlevel)), flipped, preferred_element_type=jnp.float32)
    return result.reshape(dlevel.shape[:4] + (channels,))


def body(
    block_in,
    crop_shape,
    norm_gains,
    shifts,
    qkv_weight,
    qv_bias,
    out_weight,
    up_weight,
    up_bias,
    down_weight,
    tconv_weight,
    kernels,
    grad_out,
    grad_decoded,
):
    item_count, slab_rows, width_all = block_in.shape
    local_width = qkv_weight.shape[2]
    local_heads = local_width // HD
    scale_factor = HD ** (-0.5)
    valid_full = patch_valid(crop_shape)
    patch_total = valid_full.shape[1]
    valid_local = lax.dynamic_slice_in_dim(
        valid_full, lax.axis_index("blk") * slab_rows, slab_rows, 1
    )
    key_valid = valid_full[:, None, None, :] > 0.5
    inputs = block_in.astype(jnp.float32)
    normed_one = layer_norm(inputs, norm_gains[0], shifts[0]).astype(jnp.bfloat16)
    project = jnp.einsum(
        "isd,cde->cise", normed_one, qkv_weight, preferred_element_type=jnp.float32
    )
    query = (project[0] + qv_bias[0]).astype(jnp.bfloat16)
    keys = project[1].astype(jnp.bfloat16)
    values = (project[2] + qv_bias[1]).astype(jnp.bfloat16)
    key_value = lax.all_gather(jnp.stack([keys, values]), "blk", axis=2, tiled=True)
    query_heads = query.reshape(item_count, slab_rows, local_heads, HD)
    key_heads = key_value[0].reshape(item_count, patch_total, local_heads, HD)
    value_heads = key_value[1].reshape(item_count, patch_total, local_heads, HD)

    def score_block():
        raw = (
            jnp.einsum(
                "iqhe,ikhe->ihqk", query_heads, key_heads, preferred_element_type=jnp.float32
            )
            * scale_factor
        )
        return jnp.where(key_valid, raw, -1000000000.0)

    scores = score_block()
    top_score = jnp.max(scores, axis=-1, keepdims=True)
    weights = jnp.exp(scores - top_score)
    weight_sum = jnp.sum(weights, axis=-1, keepdims=True)
    probs = weights / weight_sum
    log_total = top_score + jnp.log(weight_sum)
    mixed = jnp.einsum(
        "ihqk,ikhe->iqhe",
        probs.astype(jnp.bfloat16),
        value_heads,
        preferred_element_type=jnp.float32,
    )
    mixed_low = mixed.reshape(item_count, slab_rows, local_width).astype(jnp.bfloat16)
    partial_value = jnp.einsum(
        "ise,ed->isd", mixed_low, out_weight, preferred_element_type=jnp.float32
    )
    partial_value = lax.optimization_barrier(partial_value.astype(jnp.bfloat16)).astype(jnp.float32)
    middle = inputs + (
        pair_sum(partial_value.astype(jnp.bfloat16)) + shifts[2]
    )
    normed_two = layer_norm(middle, norm_gains[1], shifts[1]).astype(jnp.bfloat16)
    hidden = (
        jnp.einsum("isd,df->isf", normed_two, up_weight, preferred_element_type=jnp.float32)
        + up_bias
    )
    active_low = jax.nn.gelu(hidden).astype(jnp.bfloat16)
    partial_value = jnp.einsum(
        "isf,fd->isd", active_low, down_weight, preferred_element_type=jnp.float32
    )
    partial_value = lax.optimization_barrier(partial_value.astype(jnp.bfloat16)).astype(jnp.float32)
    block_out = middle + (
        pair_sum(partial_value.astype(jnp.bfloat16)) + shifts[3]
    )
    out_low = block_out.astype(jnp.bfloat16)
    per_device = item_count // lax.axis_size("tensor")
    first_item = lax.axis_index("tensor") * per_device
    tapped = lax.dynamic_slice_in_dim(out_low, first_item, per_device, 0)
    my_valid = lax.dynamic_slice_in_dim(valid_local, first_item, per_device, 0)
    voxel_count = 8.0 * jnp.sum(
        lax.dynamic_slice_in_dim(valid_full, first_item, per_device, 0), axis=1, keepdims=True
    )
    voxel_valid = voxel_mask(my_valid)
    lifted = jnp.einsum("isd,dk->isk", tapped, tconv_weight, preferred_element_type=jnp.float32)
    field_one = (to_voxels(lifted) * voxel_valid).astype(jnp.bfloat16)
    padded_one, level = conv_forward(field_one, kernels[0])
    normed_dec_one, scale_one = norm_forward(level, voxel_valid, voxel_count)
    field_two = (jax.nn.silu(normed_dec_one) * voxel_valid).astype(jnp.bfloat16)
    padded_two, level = conv_forward(field_two, kernels[1])
    normed_dec_two, scale_two = norm_forward(level, voxel_valid, voxel_count)
    decoded = (jax.nn.silu(normed_dec_two) * voxel_valid).astype(jnp.bfloat16)
    channels = kernels.shape[2]
    silu_two, silu_back_two = jax.vjp(jax.nn.silu, normed_dec_two)
    dnormed = silu_back_two(grad_decoded.astype(jnp.float32) * voxel_valid)[0]
    dlevel = norm_backward(dnormed, normed_dec_two, scale_two, voxel_valid, voxel_count).astype(
        jnp.bfloat16
    )
    grad_kernel_two = jnp.einsum(
        "rk,rc->kc",
        columns_of(padded_two),
        dlevel.reshape(-1, channels),
        preferred_element_type=jnp.float32,
    )
    dfield_two = conv_input_grad(dlevel, kernels[1])
    silu_one, silu_back_one = jax.vjp(jax.nn.silu, normed_dec_one)
    dnormed = silu_back_one(dfield_two * voxel_valid)[0]
    dlevel = norm_backward(dnormed, normed_dec_one, scale_one, voxel_valid, voxel_count).astype(
        jnp.bfloat16
    )
    grad_kernel_one = jnp.einsum(
        "rk,rc->kc",
        columns_of(padded_one),
        dlevel.reshape(-1, channels),
        preferred_element_type=jnp.float32,
    )
    dfield_one = conv_input_grad(dlevel, kernels[0])
    dlifted = from_voxels(dfield_one * voxel_valid).astype(jnp.bfloat16)
    grad_tconv = jnp.einsum("isd,isk->dk", tapped, dlifted, preferred_element_type=jnp.float32)
    dtapped = jnp.einsum("isk,dk->isd", dlifted, tconv_weight, preferred_element_type=jnp.float32)
    grad_kernel_pair = jnp.stack([grad_kernel_one, grad_kernel_two])
    low = jnp.bfloat16
    mine = lax.axis_index("tensor")
    tconv_halves = grad_tconv.astype(low).reshape(768, 2, 512)
    kernel_halves = (
        grad_kernel_pair.astype(low).reshape(2, 3456, 2, 64).transpose(2, 1, 0, 3)
        .reshape(2, 3456, 128)
    )
    keep = lax.dynamic_index_in_dim(tconv_halves, mine, 1, False)
    give = lax.dynamic_index_in_dim(tconv_halves, 1 - mine, 1, False)
    tconv_part = (keep + swap(give, "tensor")).astype(low)
    keep = lax.dynamic_index_in_dim(kernel_halves, mine, 0, False)
    give = lax.dynamic_index_in_dim(kernel_halves, 1 - mine, 0, False)
    kernel_part = jnp.pad((keep + swap(give, "tensor")).astype(low), ((0, 128), (0, 0)))
    dtap_all = lax.all_gather(dtapped.astype(jnp.bfloat16), "tensor", axis=0, tiled=True).astype(
        dtapped.dtype
    )
    dout = grad_out.astype(jnp.float32) + dtap_all
    ddown = dout.astype(jnp.bfloat16)
    grad_shift_three = jnp.sum(ddown.astype(jnp.float32), axis=(0, 1))
    grad_down = jnp.einsum("isf,isd->fd", active_low, ddown, preferred_element_type=jnp.float32)
    dactive = jnp.einsum("isd,fd->isf", ddown, down_weight, preferred_element_type=jnp.float32)
    gelu_value, gelu_back = jax.vjp(jax.nn.gelu, hidden)
    dhidden = gelu_back(dactive)[0].astype(jnp.bfloat16)
    grad_up_bias = jnp.sum(dhidden.astype(jnp.float32), axis=(0, 1))
    grad_up = jnp.einsum("isd,isf->df", normed_two, dhidden, preferred_element_type=jnp.float32)
    dnormed_two = pair_sum(
        jnp.einsum("isf,df->isd", dhidden, up_weight, preferred_element_type=jnp.float32).astype(
            jnp.bfloat16
        )
    )
    norm_value, norm_back_two = jax.vjp(layer_norm, middle, norm_gains[1], shifts[1])
    dmid_norm, grad_gain_one, grad_shift_one = norm_back_two(dnormed_two)
    dmiddle = dout + dmid_norm
    dattn = dmiddle.astype(jnp.bfloat16)
    grad_shift_two = jnp.sum(dattn.astype(jnp.float32), axis=(0, 1))
    grad_out_weight = jnp.einsum(
        "ise,isd->ed", mixed_low, dattn, preferred_element_type=jnp.float32
    )
    dmixed = jnp.einsum(
        "isd,ed->ise", dattn, out_weight, preferred_element_type=jnp.float32
    ).astype(jnp.bfloat16)
    dmixed_heads = dmixed.reshape(item_count, slab_rows, local_heads, HD)
    probs_again = jnp.exp(score_block() - log_total)
    dprobs = jnp.einsum(
        "iqhe,ikhe->ihqk", dmixed_heads, value_heads, preferred_element_type=jnp.float32
    )
    dprobs = lax.optimization_barrier(dprobs.astype(jnp.bfloat16)).astype(jnp.float32)
    dscores = (
        probs_again * (dprobs - jnp.sum(probs_again * dprobs, axis=-1, keepdims=True))
    ).astype(jnp.bfloat16)
    dquery = (
        jnp.einsum("ihqk,ikhe->iqhe", dscores, key_heads, preferred_element_type=jnp.float32)
        * scale_factor
    ).astype(jnp.bfloat16)
    dkey_part = (
        jnp.einsum("ihqk,iqhe->ikhe", dscores, query_heads, preferred_element_type=jnp.float32)
        * scale_factor
    )
    dvalue_part = jnp.einsum(
        "ihqk,iqhe->ikhe",
        probs_again.astype(jnp.bfloat16),
        dmixed_heads,
        preferred_element_type=jnp.float32,
    )
    kv_parts = jnp.stack(
        [
            dkey_part.reshape(item_count, patch_total, local_width),
            dvalue_part.reshape(item_count, patch_total, local_width),
        ]
    )
    kv_grads = lax.psum_scatter(
        kv_parts.astype(jnp.bfloat16), "blk", scatter_dimension=2, tiled=True
    )
    dproject = jnp.stack(
        [dquery.reshape(item_count, slab_rows, local_width), kv_grads[0], kv_grads[1]]
    )
    grad_qv_bias = jnp.stack(
        [
            jnp.sum(dproject[0].astype(jnp.float32), axis=(0, 1)),
            jnp.sum(dproject[2].astype(jnp.float32), axis=(0, 1)),
        ]
    )
    grad_qkv = jnp.einsum("isd,cise->cde", normed_one, dproject, preferred_element_type=jnp.float32)
    dnormed_one = pair_sum(
        jnp.einsum(
            "cise,cde->isd", dproject, qkv_weight, preferred_element_type=jnp.float32
        ).astype(jnp.bfloat16)
    )
    norm_first, norm_back_one = jax.vjp(layer_norm, inputs, norm_gains[0], shifts[0])
    din_norm, grad_gain_zero, grad_shift_zero = norm_back_one(dnormed_one)
    grad_input = (dmiddle + din_norm).astype(jnp.bfloat16)
    grad_gains = jnp.stack([grad_gain_zero, grad_gain_one])
    grad_shifts = jnp.stack([grad_shift_zero, grad_shift_one, grad_shift_two, grad_shift_three])
    small = lax.psum((grad_gains, grad_shifts, grad_qv_bias, grad_up_bias), ("dp", "blk"))
    big = total_over_group(
        [
            kernel_part,
            tconv_part,
            grad_down.astype(low),
            grad_up.astype(low),
            jnp.concatenate([grad_out_weight[:, :384], grad_out_weight[:, 384:]]).astype(low),
            grad_qkv.astype(low).reshape(2304, 384),
        ]
    )
    big = [array.astype(jnp.float32) for array in big]
    groups = lax.axis_size("dp") // GROUP
    if groups > 1:
        same = [[part * GROUP + i for part in range(groups)] for i in range(GROUP)]
        big = [lax.psum(array, "dp", axis_index_groups=same) for array in big]
    sum_kernel, sum_tconv, sum_down, sum_up, sum_out, sum_qkv = big
    sum_kernel = sum_kernel[:3456].reshape(3456, 2, 64).transpose(1, 0, 2)
    return (
        out_low,
        decoded,
        grad_input,
        small[0],
        small[1],
        sum_qkv.reshape(3, 768, 384),
        small[2],
        jnp.concatenate([sum_out[:384], sum_out[384:]], axis=1),
        sum_up,
        small[3],
        sum_down,
        sum_tconv,
        sum_kernel,
    )


def solution(mesh):
    return jax.shard_map(
        body,
        mesh=mesh,
        in_specs=(
            P("dp", "blk", None),
            P("dp"),
            P(),
            P(),
            P(None, None, "tensor"),
            P(None, "tensor"),
            P("tensor", None),
            P(None, "tensor"),
            P("tensor"),
            P("tensor", None),
            P(),
            P(),
            P("dp", "blk", None),
            P(("dp", "tensor"), "blk", None, None, None),
        ),
        out_specs=(
            P("dp", "blk", None),
            P(("dp", "tensor"), "blk", None, None, None),
            P("dp", "blk", None),
            P(),
            P(),
            P(None, None, "tensor"),
            P(None, "tensor"),
            P("tensor", None),
            P(None, "tensor"),
            P("tensor"),
            P("tensor", None),
            P(None, "tensor"),
            P(None, None, "tensor"),
        ),
        check_vma=False,
    )
```

```python
import functools

import jax
import jax.numpy as jnp
from jax import lax
from jax.experimental import pallas as pl
from jax.experimental.pallas import tpu as pltpu
from jax.sharding import PartitionSpec as P

GRID = 8
HD = 64

MESH = pl.DeviceIdType.MESH
GROUP = 8
FAR = 4


def place():
    dp = lax.axis_index("dp")
    blk = lax.axis_index("blk")
    tensor = lax.axis_index("tensor")
    near = lax.rem(dp, 2)
    far = lax.rem(dp // 2, FAR)
    first = dp // GROUP * GROUP
    return (dp, blk, tensor, near, far, first)


def peers():
    dp, blk, tensor, near, far, first = place()
    core = (dp, 1 - blk, tensor)
    cross = (dp, blk, 1 - tensor)
    beside = (first + 2 * far + 1 - near, blk, tensor)
    along = [(first + 2 * lax.rem(far + step, FAR) + near, blk, tensor) for step in range(1, FAR)]
    return (core, cross, beside, along)


def greet(devices):
    barrier = pltpu.get_barrier_semaphore()
    for device in devices:
        pl.semaphore_signal(barrier, inc=1, device_id=device, device_id_type=MESH)
    pl.semaphore_wait(barrier, len(devices))


def remote(src, dst, send, recv, device):
    return pltpu.make_async_remote_copy(
        src_ref=src, dst_ref=dst, send_sem=send, recv_sem=recv, device_id=device,
        device_id_type=MESH,
    )


def rows_at(start, size):
    return pl.ds(pl.multiple_of(start, 16), size)


def add_into(target, target_at, parts, rows, tile):
    @pl.loop(0, rows // tile)
    def _(step):
        at = step * tile
        total = None
        for ref, offset in parts:
            piece = ref[rows_at(offset + at, tile), :].astype(jnp.float32)
            total = piece if total is None else total + piece
        target[rows_at(target_at + at, tile), :] = total.astype(jnp.bfloat16)


class Sum:
    def __init__(self, own, from_core, from_near, from_far, total, send, recv):
        self.own, self.from_core, self.from_near = own, from_core, from_near
        self.from_far, self.total = from_far, total
        self.send, self.recv = send, recv
        self.rows = own.shape[0]
        self.half, self.quarter, self.piece = self.rows // 2, self.rows // 4, self.rows // 16
        dp, self.blk, tensor, self.near, self.far, first = place()
        self.core, cross, self.beside, self.along = peers()
        self.tile = 48 if self.piece % 48 == 0 else 32
        self.waiting = []

    def start(self, index, src, dst, device):
        copy = remote(src, dst, self.send.at[index], self.recv.at[index], device)
        copy.start()
        self.waiting.append(copy)
        return copy

    def step0(self):
        self.c0 = self.start(
            0, self.own.at[rows_at((1 - self.blk) * self.half, self.half)], self.from_core,
            self.core,
        )

    def step1(self):
        self.c0.wait_recv()
        add_into(
            self.from_core, 0, [(self.from_core, 0), (self.own, self.blk * self.half)],
            self.half, self.tile,
        )
        self.c1 = self.start(
            1, self.from_core.at[rows_at((1 - self.near) * self.quarter, self.quarter)],
            self.from_near, self.beside,
        )

    def step2(self):
        self.c1.wait_recv()
        add_into(
            self.from_near, 0,
            [(self.from_near, 0), (self.from_core, self.near * self.quarter)],
            self.quarter, self.tile,
        )
        self.c2 = []
        for step in range(1, FAR):
            whose = lax.rem(self.far + step, FAR)
            self.c2.append(
                self.start(
                    1 + step, self.from_near.at[rows_at(whose * self.piece, self.piece)],
                    self.from_far.at[step - 1], self.along[step - 1],
                )
            )

    def step3(self):
        for copy in self.c2:
            copy.wait_recv()
        self.base = self.blk * self.half + self.near * self.quarter
        at = self.base + self.far * self.piece
        add_into(
            self.total, at,
            [(self.from_near, self.far * self.piece)]
            + [(self.from_far.at[step], 0) for step in range(FAR - 1)],
            self.piece, self.tile,
        )
        self.c3 = []
        for step in range(1, FAR):
            where = self.total.at[rows_at(at, self.piece)]
            self.c3.append(self.start(1 + FAR - 1 + step, where, where, self.along[step - 1]))

    def step4(self):
        for copy in self.c3:
            copy.wait_recv()
        where = self.total.at[rows_at(self.base, self.quarter)]
        self.c4 = self.start(2 * FAR, where, where, self.beside)

    def step5(self):
        self.c4.wait_recv()
        where = self.total.at[rows_at(self.blk * self.half, self.half)]
        self.c5 = self.start(2 * FAR + 1, where, where, self.core)

    def step6(self):
        self.c5.wait_recv()
        for copy in self.waiting:
            copy.wait_send()


COPIES = 2 * FAR + 2


def sum_scratch(rows, columns):
    return [
        pltpu.VMEM((rows // 2, columns), jnp.bfloat16),
        pltpu.VMEM((rows // 4, columns), jnp.bfloat16),
        pltpu.VMEM((FAR - 1, rows // 16, columns), jnp.bfloat16),
    ]


def total_kernel(count, *refs):
    owns, totals = refs[:count], refs[count : 2 * count]
    scratch = refs[2 * count :]
    send, recv = scratch[3 * count :]
    core, cross, beside, along = peers()
    greet([core, beside] + along)
    sums = [
        Sum(owns[i], *scratch[3 * i : 3 * i + 3], totals[i], send.at[i], recv.at[i])
        for i in range(count)
    ]
    for wave in range(count + 6):
        for i in range(count):
            if 0 <= wave - i <= 6:
                getattr(sums[i], "step" + str(wave - i))()


def total_over_group(arrays):
    count = len(arrays)
    scratch = []
    for array in arrays:
        scratch += sum_scratch(*array.shape)
    return pl.pallas_call(
        functools.partial(total_kernel, count),
        out_shape=[jax.ShapeDtypeStruct(array.shape, jnp.bfloat16) for array in arrays],
        in_specs=[pl.BlockSpec(memory_space=pltpu.VMEM)] * count,
        out_specs=[pl.BlockSpec(memory_space=pltpu.VMEM)] * count,
        scratch_shapes=scratch
        + [pltpu.SemaphoreType.DMA((count, COPIES)), pltpu.SemaphoreType.DMA((count, COPIES))],
        name="weight_sums",
        compiler_params=pltpu.CompilerParams(
            collective_id=0, has_side_effects=True, vmem_limit_bytes=60 * 2**20
        ),
    )(*arrays)


DEPTH = 8
SIDE = 8
WIDE = 16
CH = 128
PAIR = 2 * CH
ROWS = DEPTH * SIDE * WIDE
TAPS = [(deep, wide) for deep in range(3) for wide in range(3)]
PADDED_TAPS = 28


def nt_dot(left, right):
    return lax.dot_general(
        left, right, (((1,), (1,)), ((), ())), preferred_element_type=jnp.float32
    )


def tn_dot(left, right):
    return lax.dot_general(
        left, right, (((0,), (0,)), ((), ())), preferred_element_type=jnp.float32
    )


def dot(left, right):
    return jnp.dot(left, right, preferred_element_type=jnp.float32)


def half_sums(row):
    return row[:, :CH] + row[:, CH:]


def twice(row):
    return jnp.concatenate([row, row], axis=1)


def row_and_column(size):
    return (
        lax.broadcasted_iota(jnp.int32, (size, size), 0),
        lax.broadcasted_iota(jnp.int32, (size, size), 1),
    )


def shift_matrix(step):
    row, column = row_and_column(PAIR)
    same = (row // WIDE) == (column // WIDE)
    return jnp.where(same & (row + step == column), 1.0, 0.0).astype(jnp.bfloat16)


def weave_matrix():
    row, column = row_and_column(PAIR)
    source = lax.rem(row, 2) * CH + row // WIDE * SIDE + lax.rem(row, WIDE) // 2
    return jnp.where(source == column, 1.0, 0.0).astype(jnp.bfloat16)


def unweave_matrix():
    row, column = row_and_column(PAIR)
    source = lax.rem(column, 2) * CH + column // WIDE * SIDE + lax.rem(column, WIDE) // 2
    return jnp.where(source == row, 1.0, 0.0).astype(jnp.bfloat16)


def lay_kernel(kernels_ref, index, weights):
    zero = jnp.zeros((CH, CH), jnp.bfloat16)
    for at, (deep, wide) in enumerate(TAPS):
        weights[at, 3 * CH :, :CH] = zero
        weights[at, :CH, CH:] = zero
        for high in range(3):
            offset = ((deep * 3 + high) * 3 + wide) * CH
            block = kernels_ref[index, offset : offset + CH, :]
            weights[at, high * CH : (high + 1) * CH, :CH] = block
            weights[at, (high + 1) * CH : (high + 2) * CH, CH:] = block


def lay_flipped(kernels_ref, index, weights):
    zero = jnp.zeros((CH, CH), jnp.bfloat16)
    for at, (deep, wide) in enumerate(TAPS):
        weights[at, :CH, 3 * CH :] = zero
        weights[at, CH:, :CH] = zero
        for high in range(3):
            offset = (((2 - deep) * 3 + 2 - high) * 3 + 2 - wide) * CH
            block = kernels_ref[index, offset : offset + CH, :]
            weights[at, :CH, high * CH : (high + 1) * CH] = block
            weights[at, CH:, (high + 1) * CH : (high + 2) * CH] = block


def four_heights(field, wide, start, count):
    depths = pl.ds(start, count)
    low = field[wide, depths, 0:SIDE, :, CH:]
    middle = field[wide, depths, 1 : SIDE + 1, :, :]
    high = field[wide, depths, 2 : SIDE + 2, :, :CH]
    joined = jnp.concatenate([low, middle, high], axis=-1)
    return joined.reshape(count * SIDE * WIDE, 4 * CH)


def conv_tile(field, weights, multiply, level, start):
    total = None
    for at, (deep, wide) in enumerate(TAPS):
        product = multiply(four_heights(field, wide, start + deep, 2), weights[at])
        total = product if total is None else total + product
    level[pl.ds(pl.multiple_of(start * CH, 2 * CH), 2 * CH), :] = total


def conv(field, weights, multiply, level, arrive):
    @pl.loop(0, 2)
    def _(step):
        conv_tile(field, weights, multiply, level, 2 + 2 * step)

    arrive()

    @pl.loop(0, 2)
    def _(step):
        conv_tile(field, weights, multiply, level, 6 * step)


def clear_rims(field, blk):
    for wide in range(3):
        field[wide, :, 0] = jnp.zeros((DEPTH + 2, WIDE, PAIR), jnp.bfloat16)
        field[wide, :, SIDE + 1] = jnp.zeros((DEPTH + 2, WIDE, PAIR), jnp.bfloat16)
        field[wide, 9 * blk] = jnp.zeros((SIDE + 2, WIDE, PAIR), jnp.bfloat16)


def place_rows(field, before, after, step, value):
    shape = (2, SIDE, WIDE, PAIR)
    depths = pl.ds(1 + 2 * step, 2)
    field[1, depths, 1 : SIDE + 1] = value.reshape(shape)
    field[0, depths, 1 : SIDE + 1] = dot(before, value).astype(jnp.bfloat16).reshape(shape)
    field[2, depths, 1 : SIDE + 1] = dot(after, value).astype(jnp.bfloat16).reshape(shape)


def kernel_grad(field, dlevel_turned, index, out, tensor_half):
    for at, (deep, wide) in enumerate(TAPS):
        joined = four_heights(field, wide, deep, DEPTH)
        block = dot(dlevel_turned[...], joined)
        for high in range(3):
            part = (
                block[:CH, high * CH : (high + 1) * CH]
                + block[CH:, (high + 1) * CH : (high + 2) * CH]
            )
            offset = ((deep * 3 + high) * 3 + wide) * CH
            turned = part.T.astype(jnp.bfloat16)
            for half in range(2):
                out[half, offset : offset + CH, index * 64 : (index + 1) * 64] = turned[
                    :, half * 64 : (half + 1) * 64
                ]


def decoder_kernel(
    tapped,
    tconv,
    kernels,
    grad_decoded,
    mask,
    inverse,
    decoded,
    block_all,
    dtap_all,
    grad_tconv,
    grad_kernels,
    field_one,
    field_two,
    dlevel_two,
    dlevel_one,
    weights_one,
    weights_two,
    flipped_two,
    flipped_one,
    level_one,
    level_two,
    dfield,
    turned_two,
    turned_one,
    dlifted,
    tapped_from,
    dtap_mine,
    dtap_from,
    sums_mine,
    sums_from,
    send,
    recv,
):
    dp, blk, tensor, near, far, first = place()
    core, cross, beside, along = peers()
    greet([core, cross])
    low = jnp.bfloat16
    row_tiles = ROWS // PAIR

    copies = []

    def start(index, src, dst, device):
        copy = remote(src, dst, send.at[index], recv.at[index], device)
        copy.start()
        copies.append(copy)
        return copy

    give_tapped = start(0, tapped, tapped_from, cross)

    before, after = shift_matrix(-1), shift_matrix(1)

    def send_edge(index, field):
        return start(
            index,
            field.at[:, DEPTH - 7 * blk, 1 : SIDE + 1],
            field.at[:, 9 * blk, 1 : SIDE + 1],
            core,
        )

    def rows_of(step):
        return pl.ds(pl.multiple_of(step * PAIR, PAIR), PAIR)

    def mask_rows(step):
        return twice(mask[rows_of(step), :])

    def totals(slot, pair):
        sums_mine[slot, 0:1, :] = half_sums(pair[0])
        sums_mine[slot, 1:2, :] = half_sums(pair[1])
        return start(5 + slot, sums_mine.at[slot], sums_from.at[slot], core)

    def means(slot, copy):
        copy.wait_recv()
        both = (sums_mine[slot] + sums_from[slot]) * inverse[...]
        return both[0:1, :], both[1:2, :]

    zero_pair = (jnp.zeros((1, PAIR), jnp.float32), jnp.zeros((1, PAIR), jnp.float32))

    for field in (field_one, field_two, dlevel_two, dlevel_one):
        clear_rims(field, blk)
    weave = weave_matrix()
    for piece in range(2):
        tokens = slice(piece * CH, (piece + 1) * CH)
        for a in range(2):
            lifted = dot(tapped[tokens, :], tconv[:, a * 512 : (a + 1) * 512])
            side = [
                jnp.concatenate([lifted[:, c * CH : (c + 1) * CH],
                                 lifted[:, (2 + c) * CH : (3 + c) * CH]], axis=1)
                for c in range(2)
            ]
            woven = dot(weave, jnp.concatenate(side, axis=0).astype(low))
            for depth in range(2):
                at = 2 * (2 * piece + depth) + a
                rows = slice(depth * CH, (depth + 1) * CH)
                value = woven[rows, :] * twice(mask[at * CH : (at + 1) * CH, :])
                level_one[at * CH : (at + 1) * CH, :] = value

    @pl.loop(0, row_tiles)
    def _(step):
        place_rows(field_one, before, after, step, level_one[rows_of(step), :].astype(low))

    edge = send_edge(1, field_one)
    lay_kernel(kernels, 0, weights_one)
    conv(field_one, weights_one, dot, level_one, edge.wait_recv)

    def forward_sums(level):
        def add(step, pair):
            value = level[rows_of(step), :]
            kept = value * mask_rows(step)
            return (
                pair[0] + jnp.sum(kept, axis=0, keepdims=True),
                pair[1] + jnp.sum(kept * value, axis=0, keepdims=True),
            )

        return lax.fori_loop(0, row_tiles, add, zero_pair)

    def mean_and_scale(slot, copy):
        mean, second = means(slot, copy)
        return twice(mean), twice(lax.rsqrt(second - mean * mean + 1e-05))

    def sigmoid(value):
        return 0.5 * jnp.tanh(0.5 * value) + 0.5

    copy = totals(0, forward_sums(level_one))
    lay_kernel(kernels, 1, weights_two)
    mean_one, scale_one = mean_and_scale(0, copy)

    @pl.loop(0, row_tiles)
    def _(step):
        normed = (level_one[rows_of(step), :] - mean_one) * scale_one
        level_one[rows_of(step), :] = normed
        value = normed * sigmoid(normed) * mask_rows(step)
        place_rows(field_two, before, after, step, value.astype(low))

    edge = send_edge(2, field_two)
    lay_flipped(kernels, 1, flipped_two)
    conv(field_two, weights_two, dot, level_two, edge.wait_recv)
    copy = totals(1, forward_sums(level_two))
    lay_flipped(kernels, 0, flipped_one)
    mean_two, scale_two = mean_and_scale(1, copy)

    def two_depths(ref, step, b):
        return ref[pl.ds(2 * step, 2), :, b].reshape(PAIR, CH)

    def decode(step, pair):
        normed = (level_two[rows_of(step), :] - mean_two) * scale_two
        level_two[rows_of(step), :] = normed
        kept = mask_rows(step)
        gate = sigmoid(normed)
        value = (normed * gate * kept).astype(low)
        for b in range(2):
            decoded[pl.ds(2 * step, 2), :, b] = value[:, b * CH : (b + 1) * CH].reshape(
                2, SIDE, WIDE, CH
            )
        grad = jnp.concatenate(
            [two_depths(grad_decoded, step, 0), two_depths(grad_decoded, step, 1)], axis=1
        ).astype(jnp.float32)
        dnormed = gate * (1.0 + normed * (1.0 - gate)) * kept * grad
        dfield[rows_of(step), :] = dnormed
        return (
            pair[0] + jnp.sum(dnormed, axis=0, keepdims=True),
            pair[1] + jnp.sum(dnormed * normed, axis=0, keepdims=True),
        )

    copy = totals(2, lax.fori_loop(0, row_tiles, decode, zero_pair))

    def level_grad(slot, copy, level, scale, field, turned):
        mean_grad, mean_cross = means(slot, copy)
        mean_grad, mean_cross = twice(mean_grad), twice(mean_cross)

        @pl.loop(0, row_tiles)
        def _(step):
            centred = mean_grad + level[rows_of(step), :] * mean_cross
            value = scale * (dfield[rows_of(step), :] - mask_rows(step) * centred)
            place_rows(field, before, after, step, value.astype(low))
            turned[:, rows_of(step)] = value.T.astype(low)

    level_grad(2, copy, level_two, scale_two, dlevel_two, turned_two)
    edge = send_edge(3, dlevel_two)
    conv(dlevel_two, flipped_two, nt_dot, dfield, edge.wait_recv)

    def back_one(step, pair):
        normed = level_one[rows_of(step), :]
        gate = sigmoid(normed)
        dnormed = gate * (1.0 + normed * (1.0 - gate)) * mask_rows(step) * dfield[rows_of(step), :]
        dfield[rows_of(step), :] = dnormed
        return (
            pair[0] + jnp.sum(dnormed, axis=0, keepdims=True),
            pair[1] + jnp.sum(dnormed * normed, axis=0, keepdims=True),
        )

    copy = totals(3, lax.fori_loop(0, row_tiles, back_one, zero_pair))
    level_grad(3, copy, level_one, scale_one, dlevel_one, turned_one)
    edge = send_edge(4, dlevel_one)
    conv(dlevel_one, flipped_one, nt_dot, dfield, edge.wait_recv)

    unweave = unweave_matrix()
    for piece in range(2):
        tokens = slice(piece * CH, (piece + 1) * CH)
        for a in range(2):
            parts = []
            for depth in range(2):
                at = 2 * (2 * piece + depth) + a
                rows = slice(at * CH, (at + 1) * CH)
                parts.append(dfield[rows, :] * twice(mask[rows, :]))
            apart = dot(unweave, jnp.concatenate(parts, axis=0).astype(low)).astype(low)
            for c in range(2):
                for b in range(2):
                    column = ((a * 2 + b) * 2 + c) * CH
                    dlifted[tokens, column : column + CH] = apart[
                        c * CH : (c + 1) * CH, b * CH : (b + 1) * CH
                    ]
    dtap_mine[...] = nt_dot(dlifted[...], tconv[...]).astype(low)
    give_dtap = start(9, dtap_mine, dtap_from, cross)
    grad_tconv[...] = tn_dot(tapped[...], dlifted[...]).astype(low)
    for half in range(2):
        grad_kernels[half, 27 * CH :, :] = jnp.zeros((CH, CH), low)
    kernel_grad(field_two, turned_two, 1, grad_kernels, tensor)
    kernel_grad(field_one, turned_one, 0, grad_kernels, tensor)
    give_tapped.wait_recv()
    block_all[tensor] = tapped[...]
    block_all[1 - tensor] = tapped_from[...]
    give_dtap.wait_recv()
    dtap_all[tensor] = dtap_mine[...]
    dtap_all[1 - tensor] = dtap_from[...]
    for copy in copies:
        copy.wait_send()


def decoder_section(tapped, tconv_weight, kernels, grad_decoded, mask, inverse):
    low = jnp.bfloat16
    vmem = pl.BlockSpec(memory_space=pltpu.VMEM)
    field = pltpu.VMEM((3, DEPTH + 2, SIDE + 2, WIDE, PAIR), low)
    plane = pltpu.VMEM((ROWS, PAIR), jnp.float32)
    return pl.pallas_call(
        decoder_kernel,
        out_shape=[
            jax.ShapeDtypeStruct((DEPTH, SIDE, 2, WIDE, CH), low),
            jax.ShapeDtypeStruct((2,) + tapped.shape, low),
            jax.ShapeDtypeStruct((2,) + tapped.shape, low),
            jax.ShapeDtypeStruct(tconv_weight.shape, low),
            jax.ShapeDtypeStruct((2, PADDED_TAPS * CH, CH), low),
        ],
        in_specs=[vmem] * 6,
        out_specs=[vmem] * 5,
        scratch_shapes=[field] * 4
        + [pltpu.VMEM((9, 4 * CH, PAIR), low)] * 2
        + [pltpu.VMEM((9, PAIR, 4 * CH), low)] * 2
        + [plane] * 3
        + [pltpu.VMEM((PAIR, ROWS), low)] * 2
        + [
            pltpu.VMEM((tapped.shape[0], tconv_weight.shape[1]), low),
            pltpu.VMEM(tapped.shape, low),
            pltpu.VMEM(tapped.shape, low),
            pltpu.VMEM(tapped.shape, low),
            pltpu.VMEM((4, 8, CH), jnp.float32),
            pltpu.VMEM((4, 8, CH), jnp.float32),
            pltpu.SemaphoreType.DMA((10,)),
            pltpu.SemaphoreType.DMA((10,)),
        ],
        name="decoder_section",
        compiler_params=pltpu.CompilerParams(
            collective_id=1, has_side_effects=True, vmem_limit_bytes=60 * 2**20
        ),
    )(tapped, tconv_weight, kernels, grad_decoded, mask, inverse)


def swap(value, axis):
    return lax.ppermute(value, axis, [(0, 1), (1, 0)])


def pair_sum(value):
    return value.astype(jnp.float32) + swap(value, "tensor").astype(jnp.float32)


def extended(block, sides, width):
    for axis, dim in sides:
        count = lax.axis_size(axis)
        forward = [(i, i + 1) for i in range(count - 1)]
        backward = [(target, source) for source, target in forward]
        low = lax.ppermute(
            lax.slice_in_dim(block, block.shape[dim] - width, None, axis=dim), axis, forward
        )
        high = lax.ppermute(lax.slice_in_dim(block, 0, width, axis=dim), axis, backward)
        block = jnp.concatenate([low, block, high], axis=dim)
    return block


def layer_norm(value, gain, shift):
    centre = value - jnp.mean(value, axis=-1, keepdims=True)
    spread = jnp.mean(centre * centre, axis=-1, keepdims=True)
    return centre * lax.rsqrt(spread + 1e-06) * gain + shift


def patch_valid(crop_ids):
    extent_depth = jnp.where(
        crop_ids == 0, GRID * 3 // 4, jnp.where(crop_ids == 1, GRID // 2, GRID)
    )
    extent_side = jnp.where(crop_ids == 0, GRID * 3 // 4, GRID)
    places = jnp.arange(GRID * GRID * GRID, dtype=jnp.int32)
    depth = places // (GRID * GRID)
    across = places // GRID % GRID
    along = places % GRID
    inside = (
        (depth[None, :] < extent_depth[:, None])
        & (across[None, :] < extent_side[:, None])
        & (along[None, :] < extent_side[:, None])
    )
    return inside.astype(jnp.float32)


def voxel_mask(valid):
    grid = valid.reshape(valid.shape[0], -1, GRID, GRID)
    for axis_at in (1, 2, 3):
        grid = jnp.repeat(grid, 2, axis=axis_at)
    return grid[..., None]


def to_voxels(lifted):
    count, rows, columns = lifted.shape
    depth = rows // (GRID * GRID)
    channels = columns // 8
    shaped = lifted.reshape(count, depth, GRID, GRID, 2, 2, 2, channels)
    return shaped.transpose(0, 1, 4, 2, 5, 3, 6, 7).reshape(
        count, 2 * depth, 2 * GRID, 2 * GRID, channels
    )


def from_voxels(field):
    count, depth, height, breadth, channels = field.shape
    shaped = field.reshape(count, depth // 2, 2, GRID, 2, GRID, 2, channels)
    return shaped.transpose(0, 1, 3, 5, 2, 4, 6, 7).reshape(
        count, depth // 2 * GRID * GRID, 8 * channels
    )


def columns_of(padded):
    count, depth, height, breadth, channels = padded.shape
    depth, height, breadth = (depth - 2, height - 2, breadth - 2)
    pieces = [
        padded[
            :, deep_at : deep_at + depth, high_at : high_at + height, wide_at : wide_at + breadth, :
        ]
        for deep_at in range(3)
        for high_at in range(3)
        for wide_at in range(3)
    ]
    return jnp.concatenate(pieces, axis=-1).reshape(count * depth * height * breadth, 27 * channels)


def with_rims(field):
    deeper = extended(field, (("blk", 1),), 1)
    return jnp.pad(deeper, ((0, 0), (0, 0), (1, 1), (1, 1), (0, 0)))


def channel_sums(first_term, second_term):
    sums = jnp.stack([jnp.sum(first_term, axis=(1, 2, 3)), jnp.sum(second_term, axis=(1, 2, 3))])
    return sums + swap(sums, "blk")


def norm_forward(level, voxel_valid, voxel_count):
    sums = channel_sums(voxel_valid * level, voxel_valid * level * level)
    mean = (sums[0] / voxel_count)[:, None, None, None, :]
    second = (sums[1] / voxel_count)[:, None, None, None, :]
    scale = lax.rsqrt(second - mean * mean + 1e-05)
    return ((level - mean) * scale, scale)


def norm_backward(dnormed, normed, scale, voxel_valid, voxel_count):
    sums = channel_sums(dnormed, dnormed * normed)
    mean_grad = (sums[0] / voxel_count)[:, None, None, None, :]
    mean_cross = (sums[1] / voxel_count)[:, None, None, None, :]
    return scale * (dnormed - voxel_valid * (mean_grad + normed * mean_cross))


def conv_forward(field, kernel):
    padded = with_rims(field)
    level = jnp.dot(columns_of(padded), kernel, preferred_element_type=jnp.float32)
    return (padded, level.reshape(field.shape[:4] + (kernel.shape[1],)))


def conv_input_grad(dlevel, kernel):
    channels = kernel.shape[1]
    flipped = (
        kernel.reshape(27, channels, channels)[::-1]
        .transpose(0, 2, 1)
        .reshape(27 * channels, channels)
    )
    result = jnp.dot(columns_of(with_rims(dlevel)), flipped, preferred_element_type=jnp.float32)
    return result.reshape(dlevel.shape[:4] + (channels,))


def body(
    block_in,
    crop_shape,
    norm_gains,
    shifts,
    qkv_weight,
    qv_bias,
    out_weight,
    up_weight,
    up_bias,
    down_weight,
    tconv_weight,
    kernels,
    grad_out,
    grad_decoded,
):
    item_count, slab_rows, width_all = block_in.shape
    local_width = qkv_weight.shape[2]
    local_heads = local_width // HD
    scale_factor = HD ** (-0.5)
    valid_full = patch_valid(crop_shape)
    patch_total = valid_full.shape[1]
    valid_local = lax.dynamic_slice_in_dim(
        valid_full, lax.axis_index("blk") * slab_rows, slab_rows, 1
    )
    key_valid = valid_full[:, None, None, :] > 0.5
    inputs = block_in.astype(jnp.float32)
    normed_one = layer_norm(inputs, norm_gains[0], shifts[0]).astype(jnp.bfloat16)
    project = jnp.einsum(
        "isd,cde->cise", normed_one, qkv_weight, preferred_element_type=jnp.float32
    )
    query = (project[0] + qv_bias[0]).astype(jnp.bfloat16)
    keys = project[1].astype(jnp.bfloat16)
    values = (project[2] + qv_bias[1]).astype(jnp.bfloat16)
    key_value = lax.all_gather(jnp.stack([keys, values]), "blk", axis=2, tiled=True)
    query_heads = query.reshape(item_count, slab_rows, local_heads, HD)
    key_heads = key_value[0].reshape(item_count, patch_total, local_heads, HD)
    value_heads = key_value[1].reshape(item_count, patch_total, local_heads, HD)

    def score_block():
        raw = (
            jnp.einsum(
                "iqhe,ikhe->ihqk", query_heads, key_heads, preferred_element_type=jnp.float32
            )
            * scale_factor
        )
        return jnp.where(key_valid, raw, -1000000000.0)

    scores = score_block()
    top_score = jnp.max(scores, axis=-1, keepdims=True)
    weights = jnp.exp(scores - top_score)
    weight_sum = jnp.sum(weights, axis=-1, keepdims=True)
    probs = weights / weight_sum
    log_total = top_score + jnp.log(weight_sum)
    mixed = jnp.einsum(
        "ihqk,ikhe->iqhe",
        probs.astype(jnp.bfloat16),
        value_heads,
        preferred_element_type=jnp.float32,
    )
    mixed_low = mixed.reshape(item_count, slab_rows, local_width).astype(jnp.bfloat16)
    partial_value = jnp.einsum(
        "ise,ed->isd", mixed_low, out_weight, preferred_element_type=jnp.float32
    )
    partial_value = lax.optimization_barrier(partial_value.astype(jnp.bfloat16)).astype(jnp.float32)
    middle = inputs + (
        pair_sum(partial_value.astype(jnp.bfloat16)) + shifts[2]
    )
    normed_two = layer_norm(middle, norm_gains[1], shifts[1]).astype(jnp.bfloat16)
    hidden = (
        jnp.einsum("isd,df->isf", normed_two, up_weight, preferred_element_type=jnp.float32)
        + up_bias
    )
    active_low = jax.nn.gelu(hidden).astype(jnp.bfloat16)
    partial_value = jnp.einsum(
        "isf,fd->isd", active_low, down_weight, preferred_element_type=jnp.float32
    )
    partial_value = lax.optimization_barrier(partial_value.astype(jnp.bfloat16)).astype(jnp.float32)
    block_out = middle + (
        pair_sum(partial_value.astype(jnp.bfloat16)) + shifts[3]
    )
    out_low = block_out.astype(jnp.bfloat16)
    per_device = item_count // lax.axis_size("tensor")
    first_item = lax.axis_index("tensor") * per_device
    tapped = lax.dynamic_slice_in_dim(out_low, first_item, per_device, 0)
    my_valid = lax.dynamic_slice_in_dim(valid_local, first_item, per_device, 0)
    voxel_count = 8.0 * jnp.sum(
        lax.dynamic_slice_in_dim(valid_full, first_item, per_device, 0), axis=1, keepdims=True
    )
    voxel_valid = voxel_mask(my_valid)
    mask = jnp.broadcast_to(
        voxel_valid[0, :, ::2].reshape(ROWS, 1), (ROWS, CH)
    )
    inverse = jnp.broadcast_to(1.0 / voxel_count, (8, CH))
    decoded, block_all, dtap_all, grad_tconv, kernel_halves = decoder_section(
        tapped[0],
        tconv_weight,
        kernels,
        grad_decoded.reshape(DEPTH, SIDE, 2, WIDE, CH),
        mask,
        inverse,
    )
    decoded = decoded.reshape(grad_decoded.shape)
    low = jnp.bfloat16
    mine = lax.axis_index("tensor")
    tconv_halves = grad_tconv.astype(low).reshape(768, 2, 512)
    keep = lax.dynamic_index_in_dim(tconv_halves, mine, 1, False)
    give = lax.dynamic_index_in_dim(tconv_halves, 1 - mine, 1, False)
    tconv_part = (keep + swap(give, "tensor")).astype(low)
    keep = lax.dynamic_index_in_dim(kernel_halves, mine, 0, False)
    give = lax.dynamic_index_in_dim(kernel_halves, 1 - mine, 0, False)
    kernel_part = (keep + swap(give, "tensor")).astype(low)
    dout = grad_out.astype(jnp.float32) + dtap_all
    ddown = dout.astype(jnp.bfloat16)
    grad_shift_three = jnp.sum(ddown.astype(jnp.float32), axis=(0, 1))
    grad_down = jnp.einsum("isf,isd->fd", active_low, ddown, preferred_element_type=jnp.float32)
    dactive = jnp.einsum("isd,fd->isf", ddown, down_weight, preferred_element_type=jnp.float32)
    gelu_value, gelu_back = jax.vjp(jax.nn.gelu, hidden)
    dhidden = gelu_back(dactive)[0].astype(jnp.bfloat16)
    grad_up_bias = jnp.sum(dhidden.astype(jnp.float32), axis=(0, 1))
    grad_up = jnp.einsum("isd,isf->df", normed_two, dhidden, preferred_element_type=jnp.float32)
    dnormed_two = pair_sum(
        jnp.einsum("isf,df->isd", dhidden, up_weight, preferred_element_type=jnp.float32).astype(
            jnp.bfloat16
        )
    )
    norm_value, norm_back_two = jax.vjp(layer_norm, middle, norm_gains[1], shifts[1])
    dmid_norm, grad_gain_one, grad_shift_one = norm_back_two(dnormed_two)
    dmiddle = dout + dmid_norm
    dattn = dmiddle.astype(jnp.bfloat16)
    grad_shift_two = jnp.sum(dattn.astype(jnp.float32), axis=(0, 1))
    grad_out_weight = jnp.einsum(
        "ise,isd->ed", mixed_low, dattn, preferred_element_type=jnp.float32
    )
    dmixed = jnp.einsum(
        "isd,ed->ise", dattn, out_weight, preferred_element_type=jnp.float32
    ).astype(jnp.bfloat16)
    dmixed_heads = dmixed.reshape(item_count, slab_rows, local_heads, HD)
    probs_again = jnp.exp(score_block() - log_total)
    dprobs = jnp.einsum(
        "iqhe,ikhe->ihqk", dmixed_heads, value_heads, preferred_element_type=jnp.float32
    )
    dprobs = lax.optimization_barrier(dprobs.astype(jnp.bfloat16)).astype(jnp.float32)
    dscores = (
        probs_again * (dprobs - jnp.sum(probs_again * dprobs, axis=-1, keepdims=True))
    ).astype(jnp.bfloat16)
    dquery = (
        jnp.einsum("ihqk,ikhe->iqhe", dscores, key_heads, preferred_element_type=jnp.float32)
        * scale_factor
    ).astype(jnp.bfloat16)
    dkey_part = (
        jnp.einsum("ihqk,iqhe->ikhe", dscores, query_heads, preferred_element_type=jnp.float32)
        * scale_factor
    )
    dvalue_part = jnp.einsum(
        "ihqk,iqhe->ikhe",
        probs_again.astype(jnp.bfloat16),
        dmixed_heads,
        preferred_element_type=jnp.float32,
    )
    kv_parts = jnp.stack(
        [
            dkey_part.reshape(item_count, patch_total, local_width),
            dvalue_part.reshape(item_count, patch_total, local_width),
        ]
    )
    kv_grads = lax.psum_scatter(
        kv_parts.astype(jnp.bfloat16), "blk", scatter_dimension=2, tiled=True
    )
    dproject = jnp.stack(
        [dquery.reshape(item_count, slab_rows, local_width), kv_grads[0], kv_grads[1]]
    )
    grad_qv_bias = jnp.stack(
        [
            jnp.sum(dproject[0].astype(jnp.float32), axis=(0, 1)),
            jnp.sum(dproject[2].astype(jnp.float32), axis=(0, 1)),
        ]
    )
    grad_qkv = jnp.einsum("isd,cise->cde", normed_one, dproject, preferred_element_type=jnp.float32)
    dnormed_one = pair_sum(
        jnp.einsum(
            "cise,cde->isd", dproject, qkv_weight, preferred_element_type=jnp.float32
        ).astype(jnp.bfloat16)
    )
    norm_first, norm_back_one = jax.vjp(layer_norm, inputs, norm_gains[0], shifts[0])
    din_norm, grad_gain_zero, grad_shift_zero = norm_back_one(dnormed_one)
    grad_input = (dmiddle + din_norm).astype(jnp.bfloat16)
    grad_gains = jnp.stack([grad_gain_zero, grad_gain_one])
    grad_shifts = jnp.stack([grad_shift_zero, grad_shift_one, grad_shift_two, grad_shift_three])
    small = lax.psum((grad_gains, grad_shifts, grad_qv_bias, grad_up_bias), ("dp", "blk"))
    big = total_over_group(
        [
            kernel_part,
            tconv_part,
            grad_down.astype(low),
            grad_up.astype(low),
            jnp.concatenate([grad_out_weight[:, :384], grad_out_weight[:, 384:]]).astype(low),
            grad_qkv.astype(low).reshape(2304, 384),
        ]
    )
    big = [array.astype(jnp.float32) for array in big]
    groups = lax.axis_size("dp") // GROUP
    if groups > 1:
        same = [[part * GROUP + i for part in range(groups)] for i in range(GROUP)]
        big = [lax.psum(array, "dp", axis_index_groups=same) for array in big]
    sum_kernel, sum_tconv, sum_down, sum_up, sum_out, sum_qkv = big
    sum_kernel = sum_kernel[:3456].reshape(3456, 2, 64).transpose(1, 0, 2)
    return (
        out_low,
        decoded,
        grad_input,
        small[0],
        small[1],
        sum_qkv.reshape(3, 768, 384),
        small[2],
        jnp.concatenate([sum_out[:384], sum_out[384:]], axis=1),
        sum_up,
        small[3],
        sum_down,
        sum_tconv,
        sum_kernel,
    )


def solution(mesh):
    return jax.shard_map(
        body,
        mesh=mesh,
        in_specs=(
            P("dp", "blk", None),
            P("dp"),
            P(),
            P(),
            P(None, None, "tensor"),
            P(None, "tensor"),
            P("tensor", None),
            P(None, "tensor"),
            P("tensor"),
            P("tensor", None),
            P(),
            P(),
            P("dp", "blk", None),
            P(("dp", "tensor"), "blk", None, None, None),
        ),
        out_specs=(
            P("dp", "blk", None),
            P(("dp", "tensor"), "blk", None, None, None),
            P("dp", "blk", None),
            P(),
            P(),
            P(None, None, "tensor"),
            P(None, "tensor"),
            P("tensor", None),
            P(None, "tensor"),
            P("tensor"),
            P("tensor", None),
            P(None, "tensor"),
            P(None, None, "tensor"),
        ),
        check_vma=False,
    )
```

```python
import functools

import jax
import jax.numpy as jnp
from jax import lax
from jax.experimental import pallas as pl
from jax.experimental.pallas import tpu as pltpu
from jax.sharding import PartitionSpec as P

GRID = 8
HD = 64

MESH = pl.DeviceIdType.MESH
GROUP = 8
FAR = 4


def place():
    dp = lax.axis_index("dp")
    blk = lax.axis_index("blk")
    tensor = lax.axis_index("tensor")
    near = lax.rem(dp, 2)
    far = lax.rem(dp // 2, FAR)
    first = dp // GROUP * GROUP
    return (dp, blk, tensor, near, far, first)


def peers():
    dp, blk, tensor, near, far, first = place()
    core = (dp, 1 - blk, tensor)
    cross = (dp, blk, 1 - tensor)
    beside = (first + 2 * far + 1 - near, blk, tensor)
    along = [(first + 2 * lax.rem(far + step, FAR) + near, blk, tensor) for step in range(1, FAR)]
    return (core, cross, beside, along)


def greet(devices):
    barrier = pltpu.get_barrier_semaphore()
    for device in devices:
        pl.semaphore_signal(barrier, inc=1, device_id=device, device_id_type=MESH)
    pl.semaphore_wait(barrier, len(devices))


def remote(src, dst, send, recv, device):
    return pltpu.make_async_remote_copy(
        src_ref=src, dst_ref=dst, send_sem=send, recv_sem=recv, device_id=device,
        device_id_type=MESH,
    )


def rows_at(start, size):
    return pl.ds(pl.multiple_of(start, 16), size)


def add_into(target, target_at, parts, rows, tile):
    @pl.loop(0, rows // tile)
    def _(step):
        at = step * tile
        total = None
        for ref, offset in parts:
            piece = ref[rows_at(offset + at, tile), :].astype(jnp.float32)
            total = piece if total is None else total + piece
        target[rows_at(target_at + at, tile), :] = total.astype(jnp.bfloat16)


class Sum:
    def __init__(self, own, from_core, from_near, from_far, total, send, recv):
        self.own, self.from_core, self.from_near = own, from_core, from_near
        self.from_far, self.total = from_far, total
        self.send, self.recv = send, recv
        self.rows = own.shape[0]
        self.half, self.quarter, self.piece = self.rows // 2, self.rows // 4, self.rows // 16
        dp, self.blk, tensor, self.near, self.far, first = place()
        self.core, cross, self.beside, self.along = peers()
        self.tile = 48 if self.piece % 48 == 0 else 32
        self.waiting = []

    def start(self, index, src, dst, device):
        copy = remote(src, dst, self.send.at[index], self.recv.at[index], device)
        copy.start()
        self.waiting.append(copy)
        return copy

    def step0(self):
        self.c0 = self.start(
            0, self.own.at[rows_at((1 - self.blk) * self.half, self.half)], self.from_core,
            self.core,
        )

    def step1(self):
        self.c0.wait_recv()
        add_into(
            self.from_core, 0, [(self.from_core, 0), (self.own, self.blk * self.half)],
            self.half, self.tile,
        )
        self.c1 = self.start(
            1, self.from_core.at[rows_at((1 - self.near) * self.quarter, self.quarter)],
            self.from_near, self.beside,
        )

    def step2(self):
        self.c1.wait_recv()
        add_into(
            self.from_near, 0,
            [(self.from_near, 0), (self.from_core, self.near * self.quarter)],
            self.quarter, self.tile,
        )
        self.c2 = []
        for step in range(1, FAR):
            whose = lax.rem(self.far + step, FAR)
            self.c2.append(
                self.start(
                    1 + step, self.from_near.at[rows_at(whose * self.piece, self.piece)],
                    self.from_far.at[step - 1], self.along[step - 1],
                )
            )

    def step3(self):
        for copy in self.c2:
            copy.wait_recv()
        self.base = self.blk * self.half + self.near * self.quarter
        at = self.base + self.far * self.piece
        add_into(
            self.total, at,
            [(self.from_near, self.far * self.piece)]
            + [(self.from_far.at[step], 0) for step in range(FAR - 1)],
            self.piece, self.tile,
        )
        self.c3 = []
        for step in range(1, FAR):
            where = self.total.at[rows_at(at, self.piece)]
            self.c3.append(self.start(1 + FAR - 1 + step, where, where, self.along[step - 1]))

    def step4(self):
        for copy in self.c3:
            copy.wait_recv()
        where = self.total.at[rows_at(self.base, self.quarter)]
        self.c4 = self.start(2 * FAR, where, where, self.beside)

    def step5(self):
        self.c4.wait_recv()
        where = self.total.at[rows_at(self.blk * self.half, self.half)]
        self.c5 = self.start(2 * FAR + 1, where, where, self.core)

    def step6(self):
        self.c5.wait_recv()
        for copy in self.waiting:
            copy.wait_send()


COPIES = 2 * FAR + 2


def sum_scratch(rows, columns):
    return [
        pltpu.VMEM((rows // 2, columns), jnp.bfloat16),
        pltpu.VMEM((rows // 4, columns), jnp.bfloat16),
        pltpu.VMEM((FAR - 1, rows // 16, columns), jnp.bfloat16),
    ]


def total_kernel(count, *refs):
    owns, totals = refs[:count], refs[count : 2 * count]
    scratch = refs[2 * count :]
    send, recv = scratch[3 * count :]
    core, cross, beside, along = peers()
    greet([core, beside] + along)
    sums = [
        Sum(owns[i], *scratch[3 * i : 3 * i + 3], totals[i], send.at[i], recv.at[i])
        for i in range(count)
    ]
    for wave in range(count + 6):
        for i in range(count):
            if 0 <= wave - i <= 6:
                getattr(sums[i], "step" + str(wave - i))()


def total_over_group(arrays):
    count = len(arrays)
    scratch = []
    for array in arrays:
        scratch += sum_scratch(*array.shape)
    return pl.pallas_call(
        functools.partial(total_kernel, count),
        out_shape=[jax.ShapeDtypeStruct(array.shape, jnp.bfloat16) for array in arrays],
        in_specs=[pl.BlockSpec(memory_space=pltpu.VMEM)] * count,
        out_specs=[pl.BlockSpec(memory_space=pltpu.VMEM)] * count,
        scratch_shapes=scratch
        + [pltpu.SemaphoreType.DMA((count, COPIES)), pltpu.SemaphoreType.DMA((count, COPIES))],
        name="weight_sums",
        compiler_params=pltpu.CompilerParams(
            collective_id=0, has_side_effects=True, vmem_limit_bytes=60 * 2**20
        ),
    )(*arrays)


DEPTH = 8
SIDE = 8
WIDE = 16
CH = 128
PAIR = 2 * CH
ROWS = DEPTH * SIDE * WIDE
TAPS = [(deep, wide) for deep in range(3) for wide in range(3)]
PADDED_TAPS = 28


def nt_dot(left, right):
    return lax.dot_general(
        left, right, (((1,), (1,)), ((), ())), preferred_element_type=jnp.float32
    )


def tn_dot(left, right):
    return lax.dot_general(
        left, right, (((0,), (0,)), ((), ())), preferred_element_type=jnp.float32
    )


def dot(left, right):
    return jnp.dot(left, right, preferred_element_type=jnp.float32)


def half_sums(row):
    return row[:, :CH] + row[:, CH:]


def twice(row):
    return jnp.concatenate([row, row], axis=1)


def row_and_column(size):
    return (
        lax.broadcasted_iota(jnp.int32, (size, size), 0),
        lax.broadcasted_iota(jnp.int32, (size, size), 1),
    )


def shift_matrix(step):
    row, column = row_and_column(PAIR)
    same = (row // WIDE) == (column // WIDE)
    return jnp.where(same & (row + step == column), 1.0, 0.0).astype(jnp.bfloat16)


def weave_matrix():
    row, column = row_and_column(PAIR)
    source = lax.rem(row, 2) * CH + row // WIDE * SIDE + lax.rem(row, WIDE) // 2
    return jnp.where(source == column, 1.0, 0.0).astype(jnp.bfloat16)


def unweave_matrix():
    row, column = row_and_column(PAIR)
    source = lax.rem(column, 2) * CH + column // WIDE * SIDE + lax.rem(column, WIDE) // 2
    return jnp.where(source == row, 1.0, 0.0).astype(jnp.bfloat16)


def lay_kernel(kernels_ref, index, weights):
    zero = jnp.zeros((CH, CH), jnp.bfloat16)
    for at, (deep, wide) in enumerate(TAPS):
        weights[at, 3 * CH :, :CH] = zero
        weights[at, :CH, CH:] = zero
        for high in range(3):
            offset = ((deep * 3 + high) * 3 + wide) * CH
            block = kernels_ref[index, offset : offset + CH, :]
            weights[at, high * CH : (high + 1) * CH, :CH] = block
            weights[at, (high + 1) * CH : (high + 2) * CH, CH:] = block


def lay_flipped(kernels_ref, index, weights):
    zero = jnp.zeros((CH, CH), jnp.bfloat16)
    for at, (deep, wide) in enumerate(TAPS):
        weights[at, :CH, 3 * CH :] = zero
        weights[at, CH:, :CH] = zero
        for high in range(3):
            offset = (((2 - deep) * 3 + 2 - high) * 3 + 2 - wide) * CH
            block = kernels_ref[index, offset : offset + CH, :]
            weights[at, :CH, high * CH : (high + 1) * CH] = block
            weights[at, CH:, (high + 1) * CH : (high + 2) * CH] = block


def four_heights(field, wide, start, count):
    depths = pl.ds(start, count)
    low = field[wide, depths, 0:SIDE, :, CH:]
    middle = field[wide, depths, 1 : SIDE + 1, :, :]
    high = field[wide, depths, 2 : SIDE + 2, :, :CH]
    joined = jnp.concatenate([low, middle, high], axis=-1)
    return joined.reshape(count * SIDE * WIDE, 4 * CH)


def conv_tile(field, weights, multiply, level, start):
    total = None
    for at, (deep, wide) in enumerate(TAPS):
        product = multiply(four_heights(field, wide, start + deep, 2), weights[at])
        total = product if total is None else total + product
    level[pl.ds(pl.multiple_of(start * CH, 2 * CH), 2 * CH), :] = total


def conv(field, weights, multiply, level, arrive):
    @pl.loop(0, 2)
    def _(step):
        conv_tile(field, weights, multiply, level, 2 + 2 * step)

    arrive()

    @pl.loop(0, 2)
    def _(step):
        conv_tile(field, weights, multiply, level, 6 * step)


def clear_rims(field, blk):
    for wide in range(3):
        field[wide, :, 0] = jnp.zeros((DEPTH + 2, WIDE, PAIR), jnp.bfloat16)
        field[wide, :, SIDE + 1] = jnp.zeros((DEPTH + 2, WIDE, PAIR), jnp.bfloat16)
        field[wide, 9 * blk] = jnp.zeros((SIDE + 2, WIDE, PAIR), jnp.bfloat16)


def place_rows(field, before, after, step, value):
    shape = (2, SIDE, WIDE, PAIR)
    depths = pl.ds(1 + 2 * step, 2)
    field[1, depths, 1 : SIDE + 1] = value.reshape(shape)
    field[0, depths, 1 : SIDE + 1] = dot(before, value).astype(jnp.bfloat16).reshape(shape)
    field[2, depths, 1 : SIDE + 1] = dot(after, value).astype(jnp.bfloat16).reshape(shape)


def kernel_grad(field, dlevel_turned, index, out, tensor_half):
    for at, (deep, wide) in enumerate(TAPS):
        joined = four_heights(field, wide, deep, DEPTH)
        block = dot(dlevel_turned[...], joined)
        for high in range(3):
            part = (
                block[:CH, high * CH : (high + 1) * CH]
                + block[CH:, (high + 1) * CH : (high + 2) * CH]
            )
            offset = ((deep * 3 + high) * 3 + wide) * CH
            turned = part.T.astype(jnp.bfloat16)
            for half in range(2):
                out[half, offset : offset + CH, index * 64 : (index + 1) * 64] = turned[
                    :, half * 64 : (half + 1) * 64
                ]


def decoder_kernel(
    tapped,
    tconv,
    kernels,
    grad_decoded,
    mask,
    inverse,
    decoded,
    block_all,
    dtap_all,
    grad_tconv,
    grad_kernels,
    field_one,
    field_two,
    dlevel_two,
    dlevel_one,
    weights_one,
    weights_two,
    flipped_two,
    flipped_one,
    level_one,
    level_two,
    dfield,
    turned_two,
    turned_one,
    dlifted,
    tapped_from,
    dtap_mine,
    dtap_from,
    sums_mine,
    sums_from,
    send,
    recv,
):
    dp, blk, tensor, near, far, first = place()
    core, cross, beside, along = peers()
    greet([core, cross])
    low = jnp.bfloat16
    row_tiles = ROWS // PAIR

    copies = []

    def start(index, src, dst, device):
        copy = remote(src, dst, send.at[index], recv.at[index], device)
        copy.start()
        copies.append(copy)
        return copy

    give_tapped = start(0, tapped, tapped_from, cross)

    before, after = shift_matrix(-1), shift_matrix(1)

    def send_edge(index, field):
        return start(
            index,
            field.at[:, DEPTH - 7 * blk, 1 : SIDE + 1],
            field.at[:, 9 * blk, 1 : SIDE + 1],
            core,
        )

    def rows_of(step):
        return pl.ds(pl.multiple_of(step * PAIR, PAIR), PAIR)

    def mask_rows(step):
        return twice(mask[rows_of(step), :])

    def totals(slot, pair):
        sums_mine[slot, 0:1, :] = half_sums(pair[0])
        sums_mine[slot, 1:2, :] = half_sums(pair[1])
        return start(5 + slot, sums_mine.at[slot], sums_from.at[slot], core)

    def means(slot, copy):
        copy.wait_recv()
        both = (sums_mine[slot] + sums_from[slot]) * inverse[...]
        return both[0:1, :], both[1:2, :]

    zero_pair = (jnp.zeros((1, PAIR), jnp.float32), jnp.zeros((1, PAIR), jnp.float32))

    for field in (field_one, field_two, dlevel_two, dlevel_one):
        clear_rims(field, blk)
    weave = weave_matrix()
    for piece in range(2):
        tokens = slice(piece * CH, (piece + 1) * CH)
        for a in range(2):
            lifted = dot(tapped[tokens, :], tconv[:, a * 512 : (a + 1) * 512])
            side = [
                jnp.concatenate([lifted[:, c * CH : (c + 1) * CH],
                                 lifted[:, (2 + c) * CH : (3 + c) * CH]], axis=1)
                for c in range(2)
            ]
            woven = dot(weave, jnp.concatenate(side, axis=0).astype(low))
            for depth in range(2):
                at = 2 * (2 * piece + depth) + a
                rows = slice(depth * CH, (depth + 1) * CH)
                value = woven[rows, :] * twice(mask[at * CH : (at + 1) * CH, :])
                level_one[at * CH : (at + 1) * CH, :] = value

    @pl.loop(0, row_tiles)
    def _(step):
        place_rows(field_one, before, after, step, level_one[rows_of(step), :].astype(low))

    edge = send_edge(1, field_one)
    lay_kernel(kernels, 0, weights_one)
    conv(field_one, weights_one, dot, level_one, edge.wait_recv)

    def forward_sums(level):
        def add(step, pair):
            value = level[rows_of(step), :]
            kept = value * mask_rows(step)
            return (
                pair[0] + jnp.sum(kept, axis=0, keepdims=True),
                pair[1] + jnp.sum(kept * value, axis=0, keepdims=True),
            )

        return lax.fori_loop(0, row_tiles, add, zero_pair)

    def mean_and_scale(slot, copy):
        mean, second = means(slot, copy)
        return twice(mean), twice(lax.rsqrt(second - mean * mean + 1e-05))

    def sigmoid(value):
        return 0.5 * jnp.tanh(0.5 * value) + 0.5

    copy = totals(0, forward_sums(level_one))
    lay_kernel(kernels, 1, weights_two)
    mean_one, scale_one = mean_and_scale(0, copy)

    @pl.loop(0, row_tiles)
    def _(step):
        normed = (level_one[rows_of(step), :] - mean_one) * scale_one
        level_one[rows_of(step), :] = normed
        value = normed * sigmoid(normed) * mask_rows(step)
        place_rows(field_two, before, after, step, value.astype(low))

    edge = send_edge(2, field_two)
    lay_flipped(kernels, 1, flipped_two)
    conv(field_two, weights_two, dot, level_two, edge.wait_recv)
    copy = totals(1, forward_sums(level_two))
    lay_flipped(kernels, 0, flipped_one)
    mean_two, scale_two = mean_and_scale(1, copy)

    def two_depths(ref, step, b):
        return ref[pl.ds(2 * step, 2), :, b].reshape(PAIR, CH)

    def decode(step, pair):
        normed = (level_two[rows_of(step), :] - mean_two) * scale_two
        level_two[rows_of(step), :] = normed
        kept = mask_rows(step)
        gate = sigmoid(normed)
        value = (normed * gate * kept).astype(low)
        for b in range(2):
            decoded[pl.ds(2 * step, 2), :, b] = value[:, b * CH : (b + 1) * CH].reshape(
                2, SIDE, WIDE, CH
            )
        grad = jnp.concatenate(
            [two_depths(grad_decoded, step, 0), two_depths(grad_decoded, step, 1)], axis=1
        ).astype(jnp.float32)
        dnormed = gate * (1.0 + normed * (1.0 - gate)) * kept * grad
        dfield[rows_of(step), :] = dnormed
        return (
            pair[0] + jnp.sum(dnormed, axis=0, keepdims=True),
            pair[1] + jnp.sum(dnormed * normed, axis=0, keepdims=True),
        )

    copy = totals(2, lax.fori_loop(0, row_tiles, decode, zero_pair))

    def level_grad(slot, copy, level, scale, field, turned):
        mean_grad, mean_cross = means(slot, copy)
        mean_grad, mean_cross = twice(mean_grad), twice(mean_cross)

        @pl.loop(0, row_tiles)
        def _(step):
            centred = mean_grad + level[rows_of(step), :] * mean_cross
            value = scale * (dfield[rows_of(step), :] - mask_rows(step) * centred)
            place_rows(field, before, after, step, value.astype(low))
            turned[:, rows_of(step)] = value.T.astype(low)

    level_grad(2, copy, level_two, scale_two, dlevel_two, turned_two)
    edge = send_edge(3, dlevel_two)
    conv(dlevel_two, flipped_two, nt_dot, dfield, edge.wait_recv)

    def back_one(step, pair):
        normed = level_one[rows_of(step), :]
        gate = sigmoid(normed)
        dnormed = gate * (1.0 + normed * (1.0 - gate)) * mask_rows(step) * dfield[rows_of(step), :]
        dfield[rows_of(step), :] = dnormed
        return (
            pair[0] + jnp.sum(dnormed, axis=0, keepdims=True),
            pair[1] + jnp.sum(dnormed * normed, axis=0, keepdims=True),
        )

    copy = totals(3, lax.fori_loop(0, row_tiles, back_one, zero_pair))
    level_grad(3, copy, level_one, scale_one, dlevel_one, turned_one)
    edge = send_edge(4, dlevel_one)
    conv(dlevel_one, flipped_one, nt_dot, dfield, edge.wait_recv)

    unweave = unweave_matrix()
    for piece in range(2):
        tokens = slice(piece * CH, (piece + 1) * CH)
        for a in range(2):
            parts = []
            for depth in range(2):
                at = 2 * (2 * piece + depth) + a
                rows = slice(at * CH, (at + 1) * CH)
                parts.append(dfield[rows, :] * twice(mask[rows, :]))
            apart = dot(unweave, jnp.concatenate(parts, axis=0).astype(low)).astype(low)
            for c in range(2):
                for b in range(2):
                    column = ((a * 2 + b) * 2 + c) * CH
                    dlifted[tokens, column : column + CH] = apart[
                        c * CH : (c + 1) * CH, b * CH : (b + 1) * CH
                    ]
    dtap_mine[...] = nt_dot(dlifted[...], tconv[...]).astype(low)
    give_dtap = start(9, dtap_mine, dtap_from, cross)
    grad_tconv[...] = tn_dot(tapped[...], dlifted[...]).astype(low)
    for half in range(2):
        grad_kernels[half, 27 * CH :, :] = jnp.zeros((CH, CH), low)
    kernel_grad(field_two, turned_two, 1, grad_kernels, tensor)
    kernel_grad(field_one, turned_one, 0, grad_kernels, tensor)
    give_tapped.wait_recv()
    block_all[tensor] = tapped[...]
    block_all[1 - tensor] = tapped_from[...]
    give_dtap.wait_recv()
    dtap_all[tensor] = dtap_mine[...]
    dtap_all[1 - tensor] = dtap_from[...]
    for copy in copies:
        copy.wait_send()


def decoder_section(tapped, tconv_weight, kernels, grad_decoded, mask, inverse):
    low = jnp.bfloat16
    vmem = pl.BlockSpec(memory_space=pltpu.VMEM)
    field = pltpu.VMEM((3, DEPTH + 2, SIDE + 2, WIDE, PAIR), low)
    plane = pltpu.VMEM((ROWS, PAIR), jnp.float32)
    return pl.pallas_call(
        decoder_kernel,
        out_shape=[
            jax.ShapeDtypeStruct((DEPTH, SIDE, 2, WIDE, CH), low),
            jax.ShapeDtypeStruct((2,) + tapped.shape, low),
            jax.ShapeDtypeStruct((2,) + tapped.shape, low),
            jax.ShapeDtypeStruct(tconv_weight.shape, low),
            jax.ShapeDtypeStruct((2, PADDED_TAPS * CH, CH), low),
        ],
        in_specs=[vmem] * 6,
        out_specs=[vmem] * 5,
        scratch_shapes=[field] * 4
        + [pltpu.VMEM((9, 4 * CH, PAIR), low)] * 2
        + [pltpu.VMEM((9, PAIR, 4 * CH), low)] * 2
        + [plane] * 3
        + [pltpu.VMEM((PAIR, ROWS), low)] * 2
        + [
            pltpu.VMEM((tapped.shape[0], tconv_weight.shape[1]), low),
            pltpu.VMEM(tapped.shape, low),
            pltpu.VMEM(tapped.shape, low),
            pltpu.VMEM(tapped.shape, low),
            pltpu.VMEM((4, 8, CH), jnp.float32),
            pltpu.VMEM((4, 8, CH), jnp.float32),
            pltpu.SemaphoreType.DMA((10,)),
            pltpu.SemaphoreType.DMA((10,)),
        ],
        name="decoder_section",
        compiler_params=pltpu.CompilerParams(
            collective_id=1, has_side_effects=True, vmem_limit_bytes=60 * 2**20
        ),
    )(tapped, tconv_weight, kernels, grad_decoded, mask, inverse)


GELU_RATE = 0.7978845608028654
GELU_CUBE = 0.044715


def rows_sum(value):
    return jnp.sum(value, axis=0, keepdims=True)


def lane_mean(value):
    return jnp.mean(value, axis=-1, keepdims=True)


def centred(value):
    centre = value - lane_mean(value)
    return centre, lax.rsqrt(lane_mean(centre * centre) + 1e-06)


def head_only(pair, head):
    lane = lax.broadcasted_iota(jnp.int32, pair.shape, 1)
    return jnp.where((lane // HD) == head, pair, jnp.zeros_like(pair))


def forward_kernel(
    block_in,
    gains,
    shifts,
    qkv_hbm,
    qv_bias,
    out_hbm,
    up_hbm,
    up_bias,
    down_hbm,
    key_mask,
    normed_one_hbm,
    query_hbm,
    key_value_hbm,
    probs_hbm,
    mixed_hbm,
    middle_hbm,
    normed_two_hbm,
    active_hbm,
    slope_hbm,
    tapped,
    qkv,
    out_weight,
    up,
    down,
    normed_one,
    query,
    key_value,
    probs,
    mixed,
    middle,
    normed_two,
    active,
    slope,
    values_turned,
    part_mine,
    part_from,
    feed_mine,
    feed_from,
    load_sem,
    store_sem,
    send,
    recv,
):
    dp, blk, tensor, near, far, first = place()
    core, cross, beside, along = peers()
    low = jnp.bfloat16
    items, slab, width = block_in.shape
    local = query.shape[1]
    units = active.shape[1]

    loads = []
    for index, (src, dst) in enumerate(
        [(qkv_hbm, qkv), (out_hbm, out_weight), (up_hbm, up), (down_hbm, down)]
    ):
        copy = pltpu.make_async_copy(src, dst, load_sem.at[index])
        copy.start()
        loads.append(copy)
    greet([core, cross])
    copies = []
    stores = []

    def start(index, src, dst, device):
        copy = remote(src, dst, send.at[index], recv.at[index], device)
        copy.start()
        copies.append(copy)
        return copy

    def store(src, dst):
        copy = pltpu.make_async_copy(src, dst, store_sem.at[len(stores)])
        copy.start()
        stores.append(copy)

    tile = 64

    for item in range(items):

        @pl.loop(0, slab // tile)
        def _(step):
            value = block_in[item, rows_at(step * tile, tile), :].astype(jnp.float32)
            centre, scale = centred(value)
            normed = centre * scale * gains[0:1, :] + shifts[0:1, :]
            normed_one[rows_at(item * slab + step * tile, tile), :] = normed.astype(low)

    store(normed_one, normed_one_hbm)
    loads[0].wait()
    kv_copies = []
    for item in range(items):
        rows = slice(item * slab, (item + 1) * slab)
        for c in range(2):
            project = dot(normed_one[rows, :], qkv[1 + c])
            if c == 1:
                project = project + qv_bias[1:2, :]
            key_value[item, c, :slab, :] = project.astype(low)
        kv_copies.append(
            start(
                item,
                key_value.at[item, :, pl.ds(0, slab), :],
                key_value.at[item, :, pl.ds(slab, slab), :],
                core,
            )
        )
    for item in range(items):
        rows = slice(item * slab, (item + 1) * slab)
        query[rows, :] = (dot(normed_one[rows, :], qkv[0]) + qv_bias[0:1, :]).astype(low)
    store(query, query_hbm)

    part_copies = []
    for item in range(items):
        rows = slice(item * slab, (item + 1) * slab)
        kv_copies[item].wait_recv()
        values_turned[...] = key_value[item, 1].astype(jnp.float32).T.astype(low)
        keep = key_mask[item] > 0.5
        keep = jnp.concatenate([keep] * (slab // 128), axis=1)
        for pair in range(local // 128):
            lanes = slice(pair * 128, (pair + 1) * 128)
            keys = key_value[item, 0, :, lanes]
            asked = query[rows, lanes] * jnp.asarray(HD ** (-0.5), low)
            turned = []
            for head in range(2):
                scores = nt_dot(keys, head_only(asked, head))
                scores = jnp.where(keep, scores, -1000000000.0)
                weights = jnp.exp(scores - jnp.max(scores, axis=0, keepdims=True))
                prob = (weights * (1.0 / rows_sum(weights))).astype(low)
                probs[item, 2 * pair + head] = prob
                at = pair * 128 + head * HD
                turned.append(dot(values_turned[at : at + HD, :], prob))
            mixed[rows, lanes] = jnp.concatenate(turned, axis=0).T.astype(low)
        store(probs.at[item], probs_hbm.at[item])
        if item == 0:
            loads[1].wait()
        part_mine[item] = dot(mixed[rows, :], out_weight[...]).astype(low)
        part_copies.append(start(2 + item, part_mine.at[item], part_from.at[item], cross))
    store(key_value, key_value_hbm)
    store(mixed, mixed_hbm)

    for item in range(items):
        if item == 0:
            loads[2].wait()
        part_copies[item].wait_recv()

        @pl.loop(0, slab // tile)
        def _(step):
            at = rows_at(step * tile, tile)
            attended = part_mine[item, at, :].astype(jnp.float32) + part_from[item, at, :].astype(
                jnp.float32
            )
            value = block_in[item, at, :].astype(jnp.float32) + (attended + shifts[2:3, :])
            middle[item, at, :] = value
            centre, scale = centred(value)
            normed = centre * scale * gains[1:2, :] + shifts[1:2, :]
            normed_two[rows_at(item * slab + step * tile, tile), :] = normed.astype(low)

        rows = slice(item * slab, (item + 1) * slab)

        @pl.loop(0, units // 256)
        def _(step):
            lanes = pl.ds(pl.multiple_of(step * 256, 256), 256)
            value = dot(normed_two[rows, :], up[:, lanes]) + up_bias[:, lanes]
            square = value * value
            bent = jnp.tanh(GELU_RATE * value * (1.0 + GELU_CUBE * square))
            half = 0.5 * (1.0 + bent)
            active[rows, lanes] = (value * half).astype(low)
            inner = GELU_RATE * (1.0 + 3.0 * GELU_CUBE * square)
            slope[rows, lanes] = (half + 0.5 * value * (1.0 - bent * bent) * inner).astype(low)

        if item == 0:
            loads[3].wait()

        @pl.loop(0, width // 256)
        def _(step):
            lanes = pl.ds(pl.multiple_of(step * 256, 256), 256)
            feed_mine[item, :, lanes] = dot(active[rows, :], down[:, lanes]).astype(low)

    store(middle, middle_hbm)
    store(normed_two, normed_two_hbm)
    store(active, active_hbm)
    store(slope, slope_hbm)
    feed = start(4, feed_mine.at[1 - tensor], feed_from, cross)
    feed.wait_recv()

    @pl.loop(0, slab // tile)
    def _(step):
        at = rows_at(step * tile, tile)
        fed = feed_mine[tensor, at, :].astype(jnp.float32) + feed_from[at, :].astype(jnp.float32)
        tapped[at, :] = (middle[tensor, at, :] + (fed + shifts[3:4, :])).astype(low)

    for copy in copies:
        copy.wait_send()
    for copy in stores:
        copy.wait()


def forward_section(
    block_in, gains, shifts, qkv, qv_bias, out_weight, up, up_bias, down, key_mask
):
    low = jnp.bfloat16
    items, slab, width = block_in.shape
    tokens = items * slab
    local = qkv.shape[2]
    units = up.shape[1]
    heads = local // HD
    patches = key_mask.shape[1]
    vmem = pl.BlockSpec(memory_space=pltpu.VMEM)
    hbm = pl.BlockSpec(memory_space=pl.ANY)
    kept = [
        ((tokens, width), low),
        ((tokens, local), low),
        ((items, 2, patches, local), low),
        ((items, heads, patches, slab), low),
        ((tokens, local), low),
        ((items, slab, width), jnp.float32),
        ((tokens, width), low),
        ((tokens, units), low),
        ((tokens, units), low),
    ]
    return pl.pallas_call(
        forward_kernel,
        out_shape=[jax.ShapeDtypeStruct(*one) for one in kept]
        + [jax.ShapeDtypeStruct((slab, width), low)],
        in_specs=[vmem, vmem, vmem, hbm, vmem, hbm, hbm, vmem, hbm, vmem],
        out_specs=[hbm] * 9 + [vmem],
        scratch_shapes=[pltpu.VMEM(one.shape, low) for one in (qkv, out_weight, up, down)]
        + [pltpu.VMEM(*one) for one in kept]
        + [
            pltpu.VMEM((local, patches), low),
            pltpu.VMEM(block_in.shape, low),
            pltpu.VMEM(block_in.shape, low),
            pltpu.VMEM(block_in.shape, low),
            pltpu.VMEM((slab, width), low),
            pltpu.SemaphoreType.DMA((4,)),
            pltpu.SemaphoreType.DMA((16,)),
            pltpu.SemaphoreType.DMA((5,)),
            pltpu.SemaphoreType.DMA((5,)),
        ],
        name="forward_section",
        compiler_params=pltpu.CompilerParams(
            collective_id=2, has_side_effects=True, vmem_limit_bytes=60 * 2**20
        ),
    )(block_in, gains, shifts, qkv, qv_bias, out_weight, up, up_bias, down, key_mask)


def swap(value, axis):
    return lax.ppermute(value, axis, [(0, 1), (1, 0)])


def pair_sum(value):
    return value.astype(jnp.float32) + swap(value, "tensor").astype(jnp.float32)


def extended(block, sides, width):
    for axis, dim in sides:
        count = lax.axis_size(axis)
        forward = [(i, i + 1) for i in range(count - 1)]
        backward = [(target, source) for source, target in forward]
        low = lax.ppermute(
            lax.slice_in_dim(block, block.shape[dim] - width, None, axis=dim), axis, forward
        )
        high = lax.ppermute(lax.slice_in_dim(block, 0, width, axis=dim), axis, backward)
        block = jnp.concatenate([low, block, high], axis=dim)
    return block


def layer_norm(value, gain, shift):
    centre = value - jnp.mean(value, axis=-1, keepdims=True)
    spread = jnp.mean(centre * centre, axis=-1, keepdims=True)
    return centre * lax.rsqrt(spread + 1e-06) * gain + shift


def patch_valid(crop_ids):
    extent_depth = jnp.where(
        crop_ids == 0, GRID * 3 // 4, jnp.where(crop_ids == 1, GRID // 2, GRID)
    )
    extent_side = jnp.where(crop_ids == 0, GRID * 3 // 4, GRID)
    places = jnp.arange(GRID * GRID * GRID, dtype=jnp.int32)
    depth = places // (GRID * GRID)
    across = places // GRID % GRID
    along = places % GRID
    inside = (
        (depth[None, :] < extent_depth[:, None])
        & (across[None, :] < extent_side[:, None])
        & (along[None, :] < extent_side[:, None])
    )
    return inside.astype(jnp.float32)


def voxel_mask(valid):
    grid = valid.reshape(valid.shape[0], -1, GRID, GRID)
    for axis_at in (1, 2, 3):
        grid = jnp.repeat(grid, 2, axis=axis_at)
    return grid[..., None]


def to_voxels(lifted):
    count, rows, columns = lifted.shape
    depth = rows // (GRID * GRID)
    channels = columns // 8
    shaped = lifted.reshape(count, depth, GRID, GRID, 2, 2, 2, channels)
    return shaped.transpose(0, 1, 4, 2, 5, 3, 6, 7).reshape(
        count, 2 * depth, 2 * GRID, 2 * GRID, channels
    )


def from_voxels(field):
    count, depth, height, breadth, channels = field.shape
    shaped = field.reshape(count, depth // 2, 2, GRID, 2, GRID, 2, channels)
    return shaped.transpose(0, 1, 3, 5, 2, 4, 6, 7).reshape(
        count, depth // 2 * GRID * GRID, 8 * channels
    )


def columns_of(padded):
    count, depth, height, breadth, channels = padded.shape
    depth, height, breadth = (depth - 2, height - 2, breadth - 2)
    pieces = [
        padded[
            :, deep_at : deep_at + depth, high_at : high_at + height, wide_at : wide_at + breadth, :
        ]
        for deep_at in range(3)
        for high_at in range(3)
        for wide_at in range(3)
    ]
    return jnp.concatenate(pieces, axis=-1).reshape(count * depth * height * breadth, 27 * channels)


def with_rims(field):
    deeper = extended(field, (("blk", 1),), 1)
    return jnp.pad(deeper, ((0, 0), (0, 0), (1, 1), (1, 1), (0, 0)))


def channel_sums(first_term, second_term):
    sums = jnp.stack([jnp.sum(first_term, axis=(1, 2, 3)), jnp.sum(second_term, axis=(1, 2, 3))])
    return sums + swap(sums, "blk")


def norm_forward(level, voxel_valid, voxel_count):
    sums = channel_sums(voxel_valid * level, voxel_valid * level * level)
    mean = (sums[0] / voxel_count)[:, None, None, None, :]
    second = (sums[1] / voxel_count)[:, None, None, None, :]
    scale = lax.rsqrt(second - mean * mean + 1e-05)
    return ((level - mean) * scale, scale)


def norm_backward(dnormed, normed, scale, voxel_valid, voxel_count):
    sums = channel_sums(dnormed, dnormed * normed)
    mean_grad = (sums[0] / voxel_count)[:, None, None, None, :]
    mean_cross = (sums[1] / voxel_count)[:, None, None, None, :]
    return scale * (dnormed - voxel_valid * (mean_grad + normed * mean_cross))


def conv_forward(field, kernel):
    padded = with_rims(field)
    level = jnp.dot(columns_of(padded), kernel, preferred_element_type=jnp.float32)
    return (padded, level.reshape(field.shape[:4] + (kernel.shape[1],)))


def conv_input_grad(dlevel, kernel):
    channels = kernel.shape[1]
    flipped = (
        kernel.reshape(27, channels, channels)[::-1]
        .transpose(0, 2, 1)
        .reshape(27 * channels, channels)
    )
    result = jnp.dot(columns_of(with_rims(dlevel)), flipped, preferred_element_type=jnp.float32)
    return result.reshape(dlevel.shape[:4] + (channels,))


def body(
    block_in,
    crop_shape,
    norm_gains,
    shifts,
    qkv_weight,
    qv_bias,
    out_weight,
    up_weight,
    up_bias,
    down_weight,
    tconv_weight,
    kernels,
    grad_out,
    grad_decoded,
):
    item_count, slab_rows, width_all = block_in.shape
    local_width = qkv_weight.shape[2]
    local_heads = local_width // HD
    scale_factor = HD ** (-0.5)
    valid_full = patch_valid(crop_shape)
    patch_total = valid_full.shape[1]
    valid_local = lax.dynamic_slice_in_dim(
        valid_full, lax.axis_index("blk") * slab_rows, slab_rows, 1
    )
    valid_other = lax.dynamic_slice_in_dim(
        valid_full, (1 - lax.axis_index("blk")) * slab_rows, slab_rows, 1
    )
    key_order = jnp.concatenate([valid_local, valid_other], axis=1)
    key_mask = jnp.broadcast_to(key_order[:, :, None], key_order.shape + (128,))
    (
        normed_one,
        query,
        key_value,
        probs_turned,
        mixed_low,
        middle,
        normed_two,
        active_low,
        slope,
        tapped,
    ) = forward_section(
        block_in,
        norm_gains,
        shifts,
        qkv_weight,
        qv_bias,
        out_weight,
        up_weight,
        up_bias[None, :],
        down_weight,
        key_mask,
    )
    per_device = item_count // lax.axis_size("tensor")
    first_item = lax.axis_index("tensor") * per_device
    my_valid = lax.dynamic_slice_in_dim(valid_local, first_item, per_device, 0)
    voxel_count = 8.0 * jnp.sum(
        lax.dynamic_slice_in_dim(valid_full, first_item, per_device, 0), axis=1, keepdims=True
    )
    voxel_valid = voxel_mask(my_valid)
    mask = jnp.broadcast_to(
        voxel_valid[0, :, ::2].reshape(ROWS, 1), (ROWS, CH)
    )
    inverse = jnp.broadcast_to(1.0 / voxel_count, (8, CH))
    decoded, block_all, dtap_all, grad_tconv, kernel_halves = decoder_section(
        tapped,
        tconv_weight,
        kernels,
        grad_decoded.reshape(DEPTH, SIDE, 2, WIDE, CH),
        mask,
        inverse,
    )
    decoded = decoded.reshape(grad_decoded.shape)
    low = jnp.bfloat16
    mine = lax.axis_index("tensor")
    tconv_halves = grad_tconv.astype(low).reshape(768, 2, 512)
    keep = lax.dynamic_index_in_dim(tconv_halves, mine, 1, False)
    give = lax.dynamic_index_in_dim(tconv_halves, 1 - mine, 1, False)
    tconv_part = (keep + swap(give, "tensor")).astype(low)
    keep = lax.dynamic_index_in_dim(kernel_halves, mine, 0, False)
    give = lax.dynamic_index_in_dim(kernel_halves, 1 - mine, 0, False)
    kernel_part = (keep + swap(give, "tensor")).astype(low)
    out_low = block_all
    scale_factor = HD ** (-0.5)
    local_heads = local_width // HD
    inputs = block_in.astype(jnp.float32)
    normed_one = normed_one.reshape(block_in.shape)
    normed_two = normed_two.reshape(block_in.shape)
    mixed_low = mixed_low.reshape(item_count, slab_rows, local_width)
    active_low = active_low.reshape(item_count, slab_rows, -1)
    slope = slope.reshape(item_count, slab_rows, -1)
    query_heads = query.reshape(item_count, slab_rows, local_heads, HD)
    key_heads = key_value[:, 0].reshape(item_count, patch_total, local_heads, HD)
    value_heads = key_value[:, 1].reshape(item_count, patch_total, local_heads, HD)
    probs_again = probs_turned.transpose(0, 1, 3, 2).astype(jnp.float32)
    dout = grad_out.astype(jnp.float32) + dtap_all
    ddown = dout.astype(jnp.bfloat16)
    grad_shift_three = jnp.sum(ddown.astype(jnp.float32), axis=(0, 1))
    grad_down = jnp.einsum("isf,isd->fd", active_low, ddown, preferred_element_type=jnp.float32)
    dactive = jnp.einsum("isd,fd->isf", ddown, down_weight, preferred_element_type=jnp.float32)
    dhidden = (dactive * slope).astype(jnp.bfloat16)
    grad_up_bias = jnp.sum(dhidden.astype(jnp.float32), axis=(0, 1))
    grad_up = jnp.einsum("isd,isf->df", normed_two, dhidden, preferred_element_type=jnp.float32)
    dnormed_two = pair_sum(
        jnp.einsum("isf,df->isd", dhidden, up_weight, preferred_element_type=jnp.float32).astype(
            jnp.bfloat16
        )
    )
    norm_value, norm_back_two = jax.vjp(layer_norm, middle, norm_gains[1], shifts[1])
    dmid_norm, grad_gain_one, grad_shift_one = norm_back_two(dnormed_two)
    dmiddle = dout + dmid_norm
    dattn = dmiddle.astype(jnp.bfloat16)
    grad_shift_two = jnp.sum(dattn.astype(jnp.float32), axis=(0, 1))
    grad_out_weight = jnp.einsum(
        "ise,isd->ed", mixed_low, dattn, preferred_element_type=jnp.float32
    )
    dmixed = jnp.einsum(
        "isd,ed->ise", dattn, out_weight, preferred_element_type=jnp.float32
    ).astype(jnp.bfloat16)
    dmixed_heads = dmixed.reshape(item_count, slab_rows, local_heads, HD)
    dprobs = jnp.einsum(
        "iqhe,ikhe->ihqk", dmixed_heads, value_heads, preferred_element_type=jnp.float32
    )
    dprobs = lax.optimization_barrier(dprobs.astype(jnp.bfloat16)).astype(jnp.float32)
    dscores = (
        probs_again * (dprobs - jnp.sum(probs_again * dprobs, axis=-1, keepdims=True))
    ).astype(jnp.bfloat16)
    dquery = (
        jnp.einsum("ihqk,ikhe->iqhe", dscores, key_heads, preferred_element_type=jnp.float32)
        * scale_factor
    ).astype(jnp.bfloat16)
    dkey_part = (
        jnp.einsum("ihqk,iqhe->ikhe", dscores, query_heads, preferred_element_type=jnp.float32)
        * scale_factor
    )
    dvalue_part = jnp.einsum(
        "ihqk,iqhe->ikhe",
        probs_again.astype(jnp.bfloat16),
        dmixed_heads,
        preferred_element_type=jnp.float32,
    )
    kv_parts = jnp.stack(
        [
            dkey_part.reshape(item_count, patch_total, local_width),
            dvalue_part.reshape(item_count, patch_total, local_width),
        ]
    )
    kv_parts = kv_parts.astype(jnp.bfloat16)
    kv_grads = kv_parts[:, :, :slab_rows] + swap(kv_parts[:, :, slab_rows:], "blk")
    dproject = jnp.stack(
        [dquery.reshape(item_count, slab_rows, local_width), kv_grads[0], kv_grads[1]]
    )
    grad_qv_bias = jnp.stack(
        [
            jnp.sum(dproject[0].astype(jnp.float32), axis=(0, 1)),
            jnp.sum(dproject[2].astype(jnp.float32), axis=(0, 1)),
        ]
    )
    grad_qkv = jnp.einsum("isd,cise->cde", normed_one, dproject, preferred_element_type=jnp.float32)
    dnormed_one = pair_sum(
        jnp.einsum(
            "cise,cde->isd", dproject, qkv_weight, preferred_element_type=jnp.float32
        ).astype(jnp.bfloat16)
    )
    norm_first, norm_back_one = jax.vjp(layer_norm, inputs, norm_gains[0], shifts[0])
    din_norm, grad_gain_zero, grad_shift_zero = norm_back_one(dnormed_one)
    grad_input = (dmiddle + din_norm).astype(jnp.bfloat16)
    grad_gains = jnp.stack([grad_gain_zero, grad_gain_one])
    grad_shifts = jnp.stack([grad_shift_zero, grad_shift_one, grad_shift_two, grad_shift_three])
    small = lax.psum((grad_gains, grad_shifts, grad_qv_bias, grad_up_bias), ("dp", "blk"))
    big = total_over_group(
        [
            kernel_part,
            tconv_part,
            grad_down.astype(low),
            grad_up.astype(low),
            jnp.concatenate([grad_out_weight[:, :384], grad_out_weight[:, 384:]]).astype(low),
            grad_qkv.astype(low).reshape(2304, 384),
        ]
    )
    big = [array.astype(jnp.float32) for array in big]
    groups = lax.axis_size("dp") // GROUP
    if groups > 1:
        same = [[part * GROUP + i for part in range(groups)] for i in range(GROUP)]
        big = [lax.psum(array, "dp", axis_index_groups=same) for array in big]
    sum_kernel, sum_tconv, sum_down, sum_up, sum_out, sum_qkv = big
    sum_kernel = sum_kernel[:3456].reshape(3456, 2, 64).transpose(1, 0, 2)
    return (
        out_low,
        decoded,
        grad_input,
        small[0],
        small[1],
        sum_qkv.reshape(3, 768, 384),
        small[2],
        jnp.concatenate([sum_out[:384], sum_out[384:]], axis=1),
        sum_up,
        small[3],
        sum_down,
        sum_tconv,
        sum_kernel,
    )


def solution(mesh):
    return jax.shard_map(
        body,
        mesh=mesh,
        in_specs=(
            P("dp", "blk", None),
            P("dp"),
            P(),
            P(),
            P(None, None, "tensor"),
            P(None, "tensor"),
            P("tensor", None),
            P(None, "tensor"),
            P("tensor"),
            P("tensor", None),
            P(),
            P(),
            P("dp", "blk", None),
            P(("dp", "tensor"), "blk", None, None, None),
        ),
        out_specs=(
            P("dp", "blk", None),
            P(("dp", "tensor"), "blk", None, None, None),
            P("dp", "blk", None),
            P(),
            P(),
            P(None, None, "tensor"),
            P(None, "tensor"),
            P("tensor", None),
            P(None, "tensor"),
            P("tensor"),
            P("tensor", None),
            P(None, "tensor"),
            P(None, None, "tensor"),
        ),
        check_vma=False,
    )
```

```python
import functools
import types

import jax
import jax.numpy as jnp
from jax import lax
from jax.experimental import pallas as pl
from jax.experimental.pallas import tpu as pltpu
from jax.sharding import PartitionSpec as P

GRID = 8
HD = 64

MESH = pl.DeviceIdType.MESH
GROUP = 8
FAR = 4


def place():
    dp = lax.axis_index("dp")
    blk = lax.axis_index("blk")
    tensor = lax.axis_index("tensor")
    near = lax.rem(dp, 2)
    far = lax.rem(dp // 2, FAR)
    first = dp // GROUP * GROUP
    return (dp, blk, tensor, near, far, first)


def peers():
    dp, blk, tensor, near, far, first = place()
    core = (dp, 1 - blk, tensor)
    cross = (dp, blk, 1 - tensor)
    beside = (first + 2 * far + 1 - near, blk, tensor)
    along = [(first + 2 * lax.rem(far + step, FAR) + near, blk, tensor) for step in range(1, FAR)]
    return (core, cross, beside, along)


def greet(devices):
    barrier = pltpu.get_barrier_semaphore()
    for device in devices:
        pl.semaphore_signal(barrier, inc=1, device_id=device, device_id_type=MESH)
    pl.semaphore_wait(barrier, len(devices))


def remote(src, dst, send, recv, device):
    return pltpu.make_async_remote_copy(
        src_ref=src, dst_ref=dst, send_sem=send, recv_sem=recv, device_id=device,
        device_id_type=MESH,
    )


def rows_at(start, size):
    return pl.ds(pl.multiple_of(start, 16), size)


DEPTH = 8
SIDE = 8
WIDE = 16
CH = 128
PAIR = 2 * CH
ROWS = DEPTH * SIDE * WIDE
TAPS = [(deep, wide) for deep in range(3) for wide in range(3)]
PADDED_TAPS = 28


def nt_dot(left, right):
    return lax.dot_general(
        left, right, (((1,), (1,)), ((), ())), preferred_element_type=jnp.float32
    )


def tn_dot(left, right):
    return lax.dot_general(
        left, right, (((0,), (0,)), ((), ())), preferred_element_type=jnp.float32
    )


def dot(left, right):
    return jnp.dot(left, right, preferred_element_type=jnp.float32)


def half_sums(row):
    return row[:, :CH] + row[:, CH:]


def twice(row):
    return jnp.concatenate([row, row], axis=1)


def row_and_column(size):
    return (
        lax.broadcasted_iota(jnp.int32, (size, size), 0),
        lax.broadcasted_iota(jnp.int32, (size, size), 1),
    )


def shift_matrix(step):
    row, column = row_and_column(PAIR)
    same = (row // WIDE) == (column // WIDE)
    return jnp.where(same & (row + step == column), 1.0, 0.0).astype(jnp.bfloat16)


def weave_matrix():
    row, column = row_and_column(PAIR)
    source = lax.rem(row, 2) * CH + row // WIDE * SIDE + lax.rem(row, WIDE) // 2
    return jnp.where(source == column, 1.0, 0.0).astype(jnp.bfloat16)


def unweave_matrix():
    row, column = row_and_column(PAIR)
    source = lax.rem(column, 2) * CH + column // WIDE * SIDE + lax.rem(column, WIDE) // 2
    return jnp.where(source == row, 1.0, 0.0).astype(jnp.bfloat16)


def lay_kernel(kernels_ref, index, weights):
    zero = jnp.zeros((CH, CH), jnp.bfloat16)
    for at, (deep, wide) in enumerate(TAPS):
        weights[at, 3 * CH :, :CH] = zero
        weights[at, :CH, CH:] = zero
        for high in range(3):
            offset = ((deep * 3 + high) * 3 + wide) * CH
            block = kernels_ref[index, offset : offset + CH, :]
            weights[at, high * CH : (high + 1) * CH, :CH] = block
            weights[at, (high + 1) * CH : (high + 2) * CH, CH:] = block


def lay_flipped(kernels_ref, index, weights):
    zero = jnp.zeros((CH, CH), jnp.bfloat16)
    for at, (deep, wide) in enumerate(TAPS):
        weights[at, :CH, 3 * CH :] = zero
        weights[at, CH:, :CH] = zero
        for high in range(3):
            offset = (((2 - deep) * 3 + 2 - high) * 3 + 2 - wide) * CH
            block = kernels_ref[index, offset : offset + CH, :]
            weights[at, :CH, high * CH : (high + 1) * CH] = block
            weights[at, CH:, (high + 1) * CH : (high + 2) * CH] = block


def four_heights(field, wide, start, count):
    depths = pl.ds(start, count)
    low = field[wide, depths, 0:SIDE, :, CH:]
    middle = field[wide, depths, 1 : SIDE + 1, :, :]
    high = field[wide, depths, 2 : SIDE + 2, :, :CH]
    joined = jnp.concatenate([low, middle, high], axis=-1)
    return joined.reshape(count * SIDE * WIDE, 4 * CH)


def conv_tile(field, weights, multiply, level, start):
    total = None
    for at, (deep, wide) in enumerate(TAPS):
        product = multiply(four_heights(field, wide, start + deep, 2), weights[at])
        total = product if total is None else total + product
    level[pl.ds(pl.multiple_of(start * CH, 2 * CH), 2 * CH), :] = total


def conv(field, weights, multiply, level, arrive):
    @pl.loop(0, 2)
    def _(step):
        conv_tile(field, weights, multiply, level, 2 + 2 * step)

    arrive()

    @pl.loop(0, 2)
    def _(step):
        conv_tile(field, weights, multiply, level, 6 * step)


def clear_rims(field, blk):
    for wide in range(3):
        field[wide, :, 0] = jnp.zeros((DEPTH + 2, WIDE, PAIR), jnp.bfloat16)
        field[wide, :, SIDE + 1] = jnp.zeros((DEPTH + 2, WIDE, PAIR), jnp.bfloat16)
        field[wide, 9 * blk] = jnp.zeros((SIDE + 2, WIDE, PAIR), jnp.bfloat16)


def place_rows(field, before, after, step, value):
    shape = (2, SIDE, WIDE, PAIR)
    depths = pl.ds(1 + 2 * step, 2)
    field[1, depths, 1 : SIDE + 1] = value.reshape(shape)
    field[0, depths, 1 : SIDE + 1] = dot(before, value).astype(jnp.bfloat16).reshape(shape)
    field[2, depths, 1 : SIDE + 1] = dot(after, value).astype(jnp.bfloat16).reshape(shape)


def kernel_grad(field, dlevel_turned, index, out, tensor_half):
    for at, (deep, wide) in enumerate(TAPS):
        joined = four_heights(field, wide, deep, DEPTH)
        block = dot(dlevel_turned[...], joined)
        for high in range(3):
            part = (
                block[:CH, high * CH : (high + 1) * CH]
                + block[CH:, (high + 1) * CH : (high + 2) * CH]
            )
            offset = ((deep * 3 + high) * 3 + wide) * CH
            turned = part.T.astype(jnp.bfloat16)
            for half in range(2):
                out[half, offset : offset + CH, index * 64 : (index + 1) * 64] = turned[
                    :, half * 64 : (half + 1) * 64
                ]


def decoder_kernel(
    tapped,
    tconv,
    kernels,
    grad_decoded,
    mask,
    inverse,
    decoded,
    block_all,
    dtap_all,
    grad_tconv,
    grad_kernels,
    field_one,
    field_two,
    dlevel_two,
    dlevel_one,
    weights_one,
    weights_two,
    flipped_two,
    flipped_one,
    level_one,
    level_two,
    dfield,
    turned_two,
    turned_one,
    dlifted,
    tapped_from,
    dtap_mine,
    dtap_from,
    sums_mine,
    sums_from,
    send,
    recv,
):
    dp, blk, tensor, near, far, first = place()
    core, cross, beside, along = peers()
    greet([core, cross])
    low = jnp.bfloat16
    row_tiles = ROWS // PAIR

    copies = []

    def start(index, src, dst, device):
        copy = remote(src, dst, send.at[index], recv.at[index], device)
        copy.start()
        copies.append(copy)
        return copy

    give_tapped = start(0, tapped, tapped_from, cross)

    before, after = shift_matrix(-1), shift_matrix(1)

    def send_edge(index, field):
        return start(
            index,
            field.at[:, DEPTH - 7 * blk, 1 : SIDE + 1],
            field.at[:, 9 * blk, 1 : SIDE + 1],
            core,
        )

    def rows_of(step):
        return pl.ds(pl.multiple_of(step * PAIR, PAIR), PAIR)

    def mask_rows(step):
        return twice(mask[rows_of(step), :])

    def totals(slot, pair):
        sums_mine[slot, 0:1, :] = half_sums(pair[0])
        sums_mine[slot, 1:2, :] = half_sums(pair[1])
        return start(5 + slot, sums_mine.at[slot], sums_from.at[slot], core)

    def means(slot, copy):
        copy.wait_recv()
        both = (sums_mine[slot] + sums_from[slot]) * inverse[...]
        return both[0:1, :], both[1:2, :]

    zero_pair = (jnp.zeros((1, PAIR), jnp.float32), jnp.zeros((1, PAIR), jnp.float32))

    for field in (field_one, field_two, dlevel_two, dlevel_one):
        clear_rims(field, blk)
    weave = weave_matrix()
    for piece in range(2):
        tokens = slice(piece * CH, (piece + 1) * CH)
        for a in range(2):
            lifted = dot(tapped[tokens, :], tconv[:, a * 512 : (a + 1) * 512])
            side = [
                jnp.concatenate([lifted[:, c * CH : (c + 1) * CH],
                                 lifted[:, (2 + c) * CH : (3 + c) * CH]], axis=1)
                for c in range(2)
            ]
            woven = dot(weave, jnp.concatenate(side, axis=0).astype(low))
            for depth in range(2):
                at = 2 * (2 * piece + depth) + a
                rows = slice(depth * CH, (depth + 1) * CH)
                value = woven[rows, :] * twice(mask[at * CH : (at + 1) * CH, :])
                level_one[at * CH : (at + 1) * CH, :] = value

    @pl.loop(0, row_tiles)
    def _(step):
        place_rows(field_one, before, after, step, level_one[rows_of(step), :].astype(low))

    edge = send_edge(1, field_one)
    lay_kernel(kernels, 0, weights_one)
    conv(field_one, weights_one, dot, level_one, edge.wait_recv)

    def forward_sums(level):
        def add(step, pair):
            value = level[rows_of(step), :]
            kept = value * mask_rows(step)
            return (
                pair[0] + jnp.sum(kept, axis=0, keepdims=True),
                pair[1] + jnp.sum(kept * value, axis=0, keepdims=True),
            )

        return lax.fori_loop(0, row_tiles, add, zero_pair)

    def mean_and_scale(slot, copy):
        mean, second = means(slot, copy)
        return twice(mean), twice(lax.rsqrt(second - mean * mean + 1e-05))

    def sigmoid(value):
        return 0.5 * jnp.tanh(0.5 * value) + 0.5

    copy = totals(0, forward_sums(level_one))
    lay_kernel(kernels, 1, weights_two)
    mean_one, scale_one = mean_and_scale(0, copy)

    @pl.loop(0, row_tiles)
    def _(step):
        normed = (level_one[rows_of(step), :] - mean_one) * scale_one
        level_one[rows_of(step), :] = normed
        value = normed * sigmoid(normed) * mask_rows(step)
        place_rows(field_two, before, after, step, value.astype(low))

    edge = send_edge(2, field_two)
    lay_flipped(kernels, 1, flipped_two)
    conv(field_two, weights_two, dot, level_two, edge.wait_recv)
    copy = totals(1, forward_sums(level_two))
    lay_flipped(kernels, 0, flipped_one)
    mean_two, scale_two = mean_and_scale(1, copy)

    def two_depths(ref, step, b):
        return ref[pl.ds(2 * step, 2), :, b].reshape(PAIR, CH)

    def decode(step, pair):
        normed = (level_two[rows_of(step), :] - mean_two) * scale_two
        level_two[rows_of(step), :] = normed
        kept = mask_rows(step)
        gate = sigmoid(normed)
        value = (normed * gate * kept).astype(low)
        for b in range(2):
            decoded[pl.ds(2 * step, 2), :, b] = value[:, b * CH : (b + 1) * CH].reshape(
                2, SIDE, WIDE, CH
            )
        grad = jnp.concatenate(
            [two_depths(grad_decoded, step, 0), two_depths(grad_decoded, step, 1)], axis=1
        ).astype(jnp.float32)
        dnormed = gate * (1.0 + normed * (1.0 - gate)) * kept * grad
        dfield[rows_of(step), :] = dnormed
        return (
            pair[0] + jnp.sum(dnormed, axis=0, keepdims=True),
            pair[1] + jnp.sum(dnormed * normed, axis=0, keepdims=True),
        )

    copy = totals(2, lax.fori_loop(0, row_tiles, decode, zero_pair))

    def level_grad(slot, copy, level, scale, field, turned):
        mean_grad, mean_cross = means(slot, copy)
        mean_grad, mean_cross = twice(mean_grad), twice(mean_cross)

        @pl.loop(0, row_tiles)
        def _(step):
            centred = mean_grad + level[rows_of(step), :] * mean_cross
            value = scale * (dfield[rows_of(step), :] - mask_rows(step) * centred)
            place_rows(field, before, after, step, value.astype(low))
            turned[:, rows_of(step)] = value.T.astype(low)

    level_grad(2, copy, level_two, scale_two, dlevel_two, turned_two)
    edge = send_edge(3, dlevel_two)
    conv(dlevel_two, flipped_two, nt_dot, dfield, edge.wait_recv)

    def back_one(step, pair):
        normed = level_one[rows_of(step), :]
        gate = sigmoid(normed)
        dnormed = gate * (1.0 + normed * (1.0 - gate)) * mask_rows(step) * dfield[rows_of(step), :]
        dfield[rows_of(step), :] = dnormed
        return (
            pair[0] + jnp.sum(dnormed, axis=0, keepdims=True),
            pair[1] + jnp.sum(dnormed * normed, axis=0, keepdims=True),
        )

    copy = totals(3, lax.fori_loop(0, row_tiles, back_one, zero_pair))
    level_grad(3, copy, level_one, scale_one, dlevel_one, turned_one)
    edge = send_edge(4, dlevel_one)
    conv(dlevel_one, flipped_one, nt_dot, dfield, edge.wait_recv)

    unweave = unweave_matrix()
    for piece in range(2):
        tokens = slice(piece * CH, (piece + 1) * CH)
        for a in range(2):
            parts = []
            for depth in range(2):
                at = 2 * (2 * piece + depth) + a
                rows = slice(at * CH, (at + 1) * CH)
                parts.append(dfield[rows, :] * twice(mask[rows, :]))
            apart = dot(unweave, jnp.concatenate(parts, axis=0).astype(low)).astype(low)
            for c in range(2):
                for b in range(2):
                    column = ((a * 2 + b) * 2 + c) * CH
                    dlifted[tokens, column : column + CH] = apart[
                        c * CH : (c + 1) * CH, b * CH : (b + 1) * CH
                    ]
    dtap_mine[...] = nt_dot(dlifted[...], tconv[...]).astype(low)
    give_dtap = start(9, dtap_mine, dtap_from, cross)
    grad_tconv[...] = tn_dot(tapped[...], dlifted[...]).astype(low)
    for half in range(2):
        grad_kernels[half, 27 * CH :, :] = jnp.zeros((CH, CH), low)
    kernel_grad(field_two, turned_two, 1, grad_kernels, tensor)
    kernel_grad(field_one, turned_one, 0, grad_kernels, tensor)
    give_tapped.wait_recv()
    block_all[tensor] = tapped[...]
    block_all[1 - tensor] = tapped_from[...]
    give_dtap.wait_recv()
    dtap_all[tensor] = dtap_mine[...]
    dtap_all[1 - tensor] = dtap_from[...]
    for copy in copies:
        copy.wait_send()


def decoder_section(tapped, tconv_weight, kernels, grad_decoded, mask, inverse):
    low = jnp.bfloat16
    vmem = pl.BlockSpec(memory_space=pltpu.VMEM)
    field = pltpu.VMEM((3, DEPTH + 2, SIDE + 2, WIDE, PAIR), low)
    plane = pltpu.VMEM((ROWS, PAIR), jnp.float32)
    return pl.pallas_call(
        decoder_kernel,
        out_shape=[
            jax.ShapeDtypeStruct((DEPTH, SIDE, 2, WIDE, CH), low),
            jax.ShapeDtypeStruct((2,) + tapped.shape, low),
            jax.ShapeDtypeStruct((2,) + tapped.shape, low),
            jax.ShapeDtypeStruct(tconv_weight.shape, low),
            jax.ShapeDtypeStruct((2, PADDED_TAPS * CH, CH), low),
        ],
        in_specs=[vmem] * 6,
        out_specs=[vmem] * 5,
        scratch_shapes=[field] * 4
        + [pltpu.VMEM((9, 4 * CH, PAIR), low)] * 2
        + [pltpu.VMEM((9, PAIR, 4 * CH), low)] * 2
        + [plane] * 3
        + [pltpu.VMEM((PAIR, ROWS), low)] * 2
        + [
            pltpu.VMEM((tapped.shape[0], tconv_weight.shape[1]), low),
            pltpu.VMEM(tapped.shape, low),
            pltpu.VMEM(tapped.shape, low),
            pltpu.VMEM(tapped.shape, low),
            pltpu.VMEM((4, 8, CH), jnp.float32),
            pltpu.VMEM((4, 8, CH), jnp.float32),
            pltpu.SemaphoreType.DMA((10,)),
            pltpu.SemaphoreType.DMA((10,)),
        ],
        name="decoder_section",
        compiler_params=pltpu.CompilerParams(
            collective_id=1, has_side_effects=True, vmem_limit_bytes=60 * 2**20
        ),
    )(tapped, tconv_weight, kernels, grad_decoded, mask, inverse)


GELU_RATE = 0.7978845608028654
GELU_CUBE = 0.044715


def rows_sum(value):
    return jnp.sum(value, axis=0, keepdims=True)


def lane_mean(value):
    return jnp.mean(value, axis=-1, keepdims=True)


def centred(value):
    centre = value - lane_mean(value)
    return centre, lax.rsqrt(lane_mean(centre * centre) + 1e-06)


def head_only(pair, head):
    lane = lax.broadcasted_iota(jnp.int32, pair.shape, 1)
    return jnp.where((lane // HD) == head, pair, jnp.zeros_like(pair))


def forward_kernel(
    block_in,
    gains,
    shifts,
    qkv_hbm,
    qv_bias,
    out_hbm,
    up_hbm,
    up_bias,
    down_hbm,
    key_mask,
    normed_one_hbm,
    query_hbm,
    key_value_hbm,
    probs_hbm,
    mixed_hbm,
    middle_hbm,
    normed_two_hbm,
    active_hbm,
    slope_hbm,
    tapped,
    qkv,
    out_weight,
    up,
    down,
    normed_one,
    query,
    key_value,
    probs,
    mixed,
    middle,
    normed_two,
    active,
    slope,
    values_turned,
    part_mine,
    part_from,
    feed_mine,
    feed_from,
    load_sem,
    store_sem,
    send,
    recv,
):
    dp, blk, tensor, near, far, first = place()
    core, cross, beside, along = peers()
    low = jnp.bfloat16
    items, slab, width = block_in.shape
    local = query.shape[1]
    units = active.shape[1]

    loads = []
    for index, (src, dst) in enumerate(
        [(qkv_hbm, qkv), (out_hbm, out_weight), (up_hbm, up), (down_hbm, down)]
    ):
        copy = pltpu.make_async_copy(src, dst, load_sem.at[index])
        copy.start()
        loads.append(copy)
    greet([core, cross])
    copies = []
    stores = []

    def start(index, src, dst, device):
        copy = remote(src, dst, send.at[index], recv.at[index], device)
        copy.start()
        copies.append(copy)
        return copy

    def store(src, dst):
        copy = pltpu.make_async_copy(src, dst, store_sem.at[len(stores)])
        copy.start()
        stores.append(copy)

    tile = 64

    for item in range(items):

        @pl.loop(0, slab // tile)
        def _(step):
            value = block_in[item, rows_at(step * tile, tile), :].astype(jnp.float32)
            centre, scale = centred(value)
            normed = centre * scale * gains[0:1, :] + shifts[0:1, :]
            normed_one[rows_at(item * slab + step * tile, tile), :] = normed.astype(low)

    store(normed_one, normed_one_hbm)
    loads[0].wait()
    kv_copies = []
    for item in range(items):
        rows = slice(item * slab, (item + 1) * slab)
        for c in range(2):
            project = dot(normed_one[rows, :], qkv[1 + c])
            if c == 1:
                project = project + qv_bias[1:2, :]
            key_value[item, c, :slab, :] = project.astype(low)
        kv_copies.append(
            start(
                item,
                key_value.at[item, :, pl.ds(0, slab), :],
                key_value.at[item, :, pl.ds(slab, slab), :],
                core,
            )
        )
    for item in range(items):
        rows = slice(item * slab, (item + 1) * slab)
        query[rows, :] = (dot(normed_one[rows, :], qkv[0]) + qv_bias[0:1, :]).astype(low)
    store(query, query_hbm)

    part_copies = []
    for item in range(items):
        rows = slice(item * slab, (item + 1) * slab)
        kv_copies[item].wait_recv()
        values_turned[...] = key_value[item, 1].astype(jnp.float32).T.astype(low)
        keep = key_mask[item] > 0.5
        keep = jnp.concatenate([keep] * (slab // 128), axis=1)
        for pair in range(local // 128):
            lanes = slice(pair * 128, (pair + 1) * 128)
            keys = key_value[item, 0, :, lanes]
            asked = query[rows, lanes] * jnp.asarray(HD ** (-0.5), low)
            turned = []
            for head in range(2):
                scores = nt_dot(keys, head_only(asked, head))
                scores = jnp.where(keep, scores, -1000000000.0)
                weights = jnp.exp(scores - jnp.max(scores, axis=0, keepdims=True))
                prob = (weights * (1.0 / rows_sum(weights))).astype(low)
                probs[item, 2 * pair + head] = prob
                at = pair * 128 + head * HD
                turned.append(dot(values_turned[at : at + HD, :], prob))
            mixed[rows, lanes] = jnp.concatenate(turned, axis=0).T.astype(low)
        store(probs.at[item], probs_hbm.at[item])
        if item == 0:
            loads[1].wait()
        part_mine[item] = dot(mixed[rows, :], out_weight[...]).astype(low)
        part_copies.append(start(2 + item, part_mine.at[item], part_from.at[item], cross))
    store(key_value, key_value_hbm)
    store(mixed, mixed_hbm)

    for item in range(items):
        if item == 0:
            loads[2].wait()
        part_copies[item].wait_recv()

        @pl.loop(0, slab // tile)
        def _(step):
            at = rows_at(step * tile, tile)
            attended = part_mine[item, at, :].astype(jnp.float32) + part_from[item, at, :].astype(
                jnp.float32
            )
            value = block_in[item, at, :].astype(jnp.float32) + (attended + shifts[2:3, :])
            middle[item, at, :] = value
            centre, scale = centred(value)
            normed = centre * scale * gains[1:2, :] + shifts[1:2, :]
            normed_two[rows_at(item * slab + step * tile, tile), :] = normed.astype(low)

        rows = slice(item * slab, (item + 1) * slab)

        @pl.loop(0, units // 256)
        def _(step):
            lanes = pl.ds(pl.multiple_of(step * 256, 256), 256)
            value = dot(normed_two[rows, :], up[:, lanes]) + up_bias[:, lanes]
            square = value * value
            bent = jnp.tanh(GELU_RATE * value * (1.0 + GELU_CUBE * square))
            half = 0.5 * (1.0 + bent)
            active[rows, lanes] = (value * half).astype(low)
            inner = GELU_RATE * (1.0 + 3.0 * GELU_CUBE * square)
            slope[rows, lanes] = (half + 0.5 * value * (1.0 - bent * bent) * inner).astype(low)

        if item == 0:
            loads[3].wait()

        @pl.loop(0, width // 256)
        def _(step):
            lanes = pl.ds(pl.multiple_of(step * 256, 256), 256)
            feed_mine[item, :, lanes] = dot(active[rows, :], down[:, lanes]).astype(low)

    store(middle, middle_hbm)
    store(normed_two, normed_two_hbm)
    store(active, active_hbm)
    store(slope, slope_hbm)
    feed = start(4, feed_mine.at[1 - tensor], feed_from, cross)
    feed.wait_recv()

    @pl.loop(0, slab // tile)
    def _(step):
        at = rows_at(step * tile, tile)
        fed = feed_mine[tensor, at, :].astype(jnp.float32) + feed_from[at, :].astype(jnp.float32)
        tapped[at, :] = (middle[tensor, at, :] + (fed + shifts[3:4, :])).astype(low)

    for copy in copies:
        copy.wait_send()
    for copy in stores:
        copy.wait()


def forward_section(
    block_in, gains, shifts, qkv, qv_bias, out_weight, up, up_bias, down, key_mask
):
    low = jnp.bfloat16
    items, slab, width = block_in.shape
    tokens = items * slab
    local = qkv.shape[2]
    units = up.shape[1]
    heads = local // HD
    patches = key_mask.shape[1]
    vmem = pl.BlockSpec(memory_space=pltpu.VMEM)
    hbm = pl.BlockSpec(memory_space=pl.ANY)
    kept = [
        ((tokens, width), low),
        ((tokens, local), low),
        ((items, 2, patches, local), low),
        ((items, heads, patches, slab), low),
        ((tokens, local), low),
        ((items, slab, width), jnp.float32),
        ((tokens, width), low),
        ((tokens, units), low),
        ((tokens, units), low),
    ]
    return pl.pallas_call(
        forward_kernel,
        out_shape=[jax.ShapeDtypeStruct(*one) for one in kept]
        + [jax.ShapeDtypeStruct((slab, width), low)],
        in_specs=[vmem, vmem, vmem, hbm, vmem, hbm, hbm, vmem, hbm, vmem],
        out_specs=[hbm] * 9 + [vmem],
        scratch_shapes=[pltpu.VMEM(one.shape, low) for one in (qkv, out_weight, up, down)]
        + [pltpu.VMEM(*one) for one in kept]
        + [
            pltpu.VMEM((local, patches), low),
            pltpu.VMEM(block_in.shape, low),
            pltpu.VMEM(block_in.shape, low),
            pltpu.VMEM(block_in.shape, low),
            pltpu.VMEM((slab, width), low),
            pltpu.SemaphoreType.DMA((4,)),
            pltpu.SemaphoreType.DMA((16,)),
            pltpu.SemaphoreType.DMA((5,)),
            pltpu.SemaphoreType.DMA((5,)),
        ],
        name="forward_section",
        compiler_params=pltpu.CompilerParams(
            collective_id=2, has_side_effects=True, vmem_limit_bytes=60 * 2**20
        ),
    )(block_in, gains, shifts, qkv, qv_bias, out_weight, up, up_bias, down, key_mask)


def fold(value):
    rows, width = value.shape
    return jnp.sum(value.reshape(rows // 8, 8, width), axis=0)


def add_into(target, target_at, parts, rows, tile):
    @pl.loop(0, rows // tile)
    def _(step):
        at = step * tile
        total = None
        for ref, offset in parts:
            piece = ref[rows_at(offset + at, tile), :].astype(jnp.float32)
            total = piece if total is None else total + piece
        target[rows_at(target_at + at, tile), :] = total.astype(jnp.bfloat16)


COPIES = 2 * FAR + 2


class Sum:
    def __init__(self, own, from_core, from_near, from_far, piece, total, send, recv, local):
        self.own, self.from_core, self.from_near = own, from_core, from_near
        self.from_far, self.part, self.total = from_far, piece, total
        self.send, self.recv, self.local = send, recv, local
        self.rows = own.shape[0]
        self.half, self.quarter, self.piece = self.rows // 2, self.rows // 4, self.rows // 16
        dp, self.blk, tensor, self.near, self.far, first = place()
        self.core, cross, self.beside, self.along = peers()
        self.waiting = []

    def start(self, index, src, dst, device):
        copy = remote(src, dst, self.send.at[index], self.recv.at[index], device)
        copy.start()
        self.waiting.append(copy)
        return copy

    def step0(self):
        self.c0 = self.start(
            0, self.own.at[rows_at((1 - self.blk) * self.half, self.half)], self.from_core,
            self.core,
        )

    def step1(self):
        self.c0.wait_recv()
        add_into(
            self.from_core, 0, [(self.from_core, 0), (self.own, self.blk * self.half)],
            self.half, self.piece,
        )
        self.c1 = self.start(
            1, self.from_core.at[rows_at((1 - self.near) * self.quarter, self.quarter)],
            self.from_near, self.beside,
        )

    def step2(self):
        self.c1.wait_recv()
        add_into(
            self.from_near, 0,
            [(self.from_near, 0), (self.from_core, self.near * self.quarter)],
            self.quarter, self.piece,
        )
        self.c2 = []
        for step in range(1, FAR):
            whose = lax.rem(self.far + step, FAR)
            self.c2.append(
                self.start(
                    1 + step, self.from_near.at[rows_at(whose * self.piece, self.piece)],
                    self.from_far.at[step - 1], self.along[step - 1],
                )
            )

    def step3(self):
        for copy in self.c2:
            copy.wait_recv()
        self.base = self.blk * self.half + self.near * self.quarter
        at = self.base + self.far * self.piece
        add_into(
            self.part, 0,
            [(self.from_near, self.far * self.piece)]
            + [(self.from_far.at[step], 0) for step in range(FAR - 1)],
            self.piece, self.piece,
        )
        where = self.total.at[rows_at(at, self.piece)]
        self.keep = pltpu.make_async_copy(self.part, where, self.local)
        self.keep.start()
        self.c3 = [
            self.start(FAR + step, self.part, where, self.along[step - 1])
            for step in range(1, FAR)
        ]

    def step4(self):
        self.keep.wait()
        for copy in self.c3:
            copy.wait_recv()
        where = self.total.at[rows_at(self.base, self.quarter)]
        self.c4 = self.start(2 * FAR, where, where, self.beside)

    def step5(self):
        self.c4.wait_recv()
        where = self.total.at[rows_at(self.blk * self.half, self.half)]
        self.c5 = self.start(2 * FAR + 1, where, where, self.core)

    def step6(self):
        self.c5.wait_recv()
        for copy in self.waiting:
            copy.wait_send()


def sum_scratch(rows, columns):
    low = jnp.bfloat16
    return [
        pltpu.VMEM((rows // 2, columns), low),
        pltpu.VMEM((rows // 4, columns), low),
        pltpu.VMEM((FAR - 1, rows // 16, columns), low),
        pltpu.VMEM((rows // 16, columns), low),
    ]


def norm_back(value, grad, gain):
    centre, scale = centred(value)
    normed = centre * scale
    scaled = grad * gain
    inner = lane_mean(scaled * normed)
    return scale * (scaled - lane_mean(scaled) - normed * inner), normed


def backward_kernel(layout, *refs):
    r = types.SimpleNamespace(**dict(zip(layout, refs)))
    dp, blk, tensor, near, far, first = place()
    core, cross, beside, along = peers()
    low = jnp.bfloat16
    items, slab, width = r.grad_out.shape
    local = r.query.shape[1]
    units = r.active.shape[1]
    pairs = local // 128
    tile = 64
    half_width = width // 2

    loads = {}
    for index, name in enumerate(LOADED):
        copy = pltpu.make_async_copy(getattr(r, name + "_hbm"), getattr(r, name), r.load_sem.at[index])
        copy.start()
        loads[name] = copy
    keep_kernels = pltpu.make_async_copy(
        r.grad_kernels_hbm.at[tensor], r.own_kernels, r.load_sem.at[len(LOADED)]
    )
    keep_tconv = pltpu.make_async_copy(
        r.grad_tconv_hbm.at[:, pl.ds(pl.multiple_of(tensor * 512, 512), 512)],
        r.own_tconv,
        r.load_sem.at[len(LOADED) + 1],
    )
    keep_kernels.start()
    keep_tconv.start()
    greet([core, cross, beside] + along)
    copies = []

    def start(index, src, dst, device):
        copy = remote(src, dst, r.send.at[index], r.recv.at[index], device)
        copy.start()
        copies.append(copy)
        return copy

    def unit(name, index, own, total):
        scratch = [getattr(r, name + end) for end in ("_core", "_near", "_far", "_piece")]
        return Sum(
            own, *scratch, total, r.sum_send.at[index], r.sum_recv.at[index], r.sum_local.at[index]
        )

    sum_d = [
        unit("down%d" % h, h, r.own_down.at[h], r.total_down.at[h]) for h in range(2)
    ]
    sum_u = [unit("up%d" % h, 2 + h, r.own_up.at[h], r.total_up.at[h]) for h in range(2)]
    sum_o = unit("out", 4, r.own_out, r.total_out)
    sum_q = [unit("qkv%d" % c, 5 + c, r.own_qkv.at[c], r.total_qkv.at[c]) for c in range(3)]
    sum_k = unit("kernels", 8, r.own_kernels, r.total_kernels)
    sum_t = unit("tconv", 9, r.own_tconv, r.total_tconv)

    def rows_of(item):
        return slice(item * slab, (item + 1) * slab)

    def lanes_of(step, size=256):
        return pl.ds(pl.multiple_of(step * size, size), size)

    r.small[...] = jnp.zeros_like(r.small)

    def dout_rows(item, at):
        return r.grad_out[item, at, :].astype(jnp.float32) + r.dtap[item, at, :].astype(
            jnp.float32
        )

    zero = jnp.zeros((8, width), jnp.float32)

    sent_two = []
    for item in range(items):
        rows = rows_of(item)

        def shade(step, total):
            value = dout_rows(item, rows_at(step * tile, tile)).astype(low)
            r.ddown[rows_at(item * slab + step * tile, tile), :] = value
            return total + fold(value.astype(jnp.float32))

        total = lax.fori_loop(0, slab // tile, shade, zero)
        r.small[5:6, :] += rows_sum(total)
        if item == 0:
            loads["down"].wait()
            loads["slope"].wait()

        @pl.loop(0, units // 256)
        def _(step):
            lanes = lanes_of(step)
            dactive = nt_dot(r.ddown[rows, :], r.down[lanes, :])
            value = (dactive * r.slope[rows, lanes].astype(jnp.float32)).astype(low)
            r.dhidden[rows, lanes] = value
            summed = rows_sum(fold(value.astype(jnp.float32)))
            if item == 0:
                r.bias_sum[0:1, lanes] = summed
            else:
                r.bias_sum[0:1, lanes] += summed

        if item == 0:
            loads["up"].wait()

        @pl.loop(0, width // 256)
        def _(step):
            value = nt_dot(r.dhidden[rows, :], r.up[lanes_of(step), :])
            r.two_mine[item, :, lanes_of(step)] = value.astype(low)

        sent_two.append(start(item, r.two_mine.at[item], r.two_from.at[item], cross))

    r.small[7:8, :] = r.bias_sum[0:1, :width]
    r.small[8:9, :] = r.bias_sum[0:1, width:]

    def grad_down(h):
        @pl.loop(0, units // 2 // 256)
        def _(step):
            lanes = pl.ds(pl.multiple_of(h * (units // 2) + step * 256, 256), 256)
            r.own_down[h, lanes_of(step), :] = tn_dot(r.active[:, lanes], r.ddown[...]).astype(low)

    def grad_up(h):
        @pl.loop(0, width // 256)
        def _(step):
            right = r.dhidden[:, h * (units // 2) : (h + 1) * (units // 2)]
            r.own_up[h, lanes_of(step), :] = tn_dot(r.normed_two[:, lanes_of(step)], right).astype(
                low
            )

    loads["active"].wait()
    grad_down(0)
    sum_d[0].step0()
    grad_down(1)
    sum_d[1].step0()
    sum_d[0].step1()
    loads["normed_two"].wait()
    grad_up(0)
    sum_u[0].step0()
    sum_d[1].step1()
    grad_up(1)
    sum_u[1].step0()
    sum_u[0].step1()

    def middle_back(item):
        sent_two[item].wait_recv()

        def back(step, totals):
            at = rows_at(step * tile, tile)
            grad = r.two_mine[item, at, :].astype(jnp.float32) + r.two_from[item, at, :].astype(
                jnp.float32
            )
            dvalue, normed = norm_back(r.middle[item, at, :], grad, r.gains[1:2, :])
            dmiddle = dout_rows(item, at) + dvalue
            r.dmiddle[item, at, :] = dmiddle
            dattn = dmiddle.astype(low)
            r.dattn[rows_at(item * slab + step * tile, tile), :] = dattn
            return (
                totals[0] + fold(grad * normed),
                totals[1] + fold(grad),
                totals[2] + fold(dattn.astype(jnp.float32)),
            )

        totals = lax.fori_loop(0, slab // tile, back, (zero, zero, zero))
        for row, total in zip((2, 3, 4), totals):
            r.small[row : row + 1, :] += rows_sum(total)

    def attention_back(item, between):
        rows = rows_of(item)
        r.keys_turned[...] = r.key_value[item, 0].astype(jnp.float32).T.astype(low)
        r.dmixed[...] = nt_dot(r.dattn[rows, :], r.out_weight[...]).astype(low)
        scale = HD ** (-0.5)
        for pair in range(pairs):
            lanes = slice(pair * 128, (pair + 1) * 128)
            values = r.key_value[item, 1, :, lanes]
            asked = r.query[rows, lanes]
            dmixed = r.dmixed[:, lanes]
            dkeys = dvalues = None
            turned = []
            for head in range(2):
                prob = r.probs[item, 2 * pair + head]
                dmixed_head = head_only(dmixed, head)
                dprob = nt_dot(values, dmixed_head)
                wide = prob.astype(jnp.float32)
                inner = rows_sum(wide * dprob)
                dscores = (wide * (dprob - inner)).astype(low)
                key_part = dot(dscores, head_only(asked, head))
                value_part = dot(prob, dmixed_head)
                dkeys = key_part if dkeys is None else dkeys + key_part
                dvalues = value_part if dvalues is None else dvalues + value_part
                at = pair * 128 + head * HD
                turned.append(dot(r.keys_turned[at : at + HD, :], dscores))
            r.dproject[0, rows, lanes] = (jnp.concatenate(turned, axis=0).T * scale).astype(low)
            dkeys = (dkeys * scale).astype(low)
            dvalues = dvalues.astype(low)
            r.dproject[1, rows, lanes] = dkeys[:slab]
            r.dproject[2, rows, lanes] = dvalues[:slab]
            r.give_kv[item, 0, :, lanes] = dkeys[slab:]
            r.give_kv[item, 1, :, lanes] = dvalues[slab:]
            between(pair)
        return start(2 + item, r.give_kv.at[item], r.got_kv.at[item], core)

    for name in ("out_weight", "middle", "key_value", "query", "probs"):
        loads[name].wait()
    middle_back(0)
    sum_u[1].step1()

    def first_between(pair):
        if pair == 1:
            sum_d[0].step2()

    sent_kv = [attention_back(0, first_between)]
    middle_back(1)
    sum_d[1].step2()

    def second_between(pair):
        if pair == 1:
            sum_d[0].step3()

    sent_kv.append(attention_back(1, second_between))
    sum_u[0].step2()
    loads["mixed"].wait()
    for h in range(2):
        value = tn_dot(r.mixed[...], r.dattn[:, h * half_width : (h + 1) * half_width])
        r.own_out[h * local : (h + 1) * local, :] = value.astype(low)
    sum_o.step0()
    for item in range(items):
        sent_kv[item].wait_recv()
        rows = rows_of(item)
        for c in range(2):
            value = r.dproject[1 + c, rows, :].astype(jnp.float32) + r.got_kv[item, c].astype(
                jnp.float32
            )
            r.dproject[1 + c, rows, :] = value.astype(low)
    loads["qkv"].wait()
    sent_one = []
    for item in range(items):
        rows = rows_of(item)

        @pl.loop(0, width // 256)
        def _(step):
            lanes = lanes_of(step)
            value = None
            for c in range(3):
                part = nt_dot(r.dproject[c, rows, :], r.qkv[c, lanes, :])
                value = part if value is None else value + part
            r.one_mine[item, :, lanes] = value.astype(low)

        sent_one.append(start(4 + item, r.one_mine.at[item], r.one_from.at[item], cross))
    give_kernels = start(6, r.grad_kernels_hbm.at[1 - tensor], r.cross_kernels, cross)
    give_tconv = start(
        7,
        r.grad_tconv_hbm.at[:, pl.ds(pl.multiple_of((1 - tensor) * 512, 512), 512)],
        r.cross_tconv,
        cross,
    )
    sum_o.step1()
    loads["normed_one"].wait()
    for c in (2, 1, 0):
        r.own_qkv[c] = tn_dot(r.normed_one[...], r.dproject[c]).astype(low)
        sum_q[c].step0()
        if c == 2:
            sum_d[1].step3()
        if c == 1:
            sum_q[2].step1()
    for c in (0, 2):
        value = rows_sum(fold(r.dproject[c].astype(jnp.float32)))
        r.small[6:7, (c // 2) * local : (c // 2 + 1) * local] = value
    sum_q[1].step1()
    sum_q[0].step1()
    sum_d[0].step4()
    sum_u[1].step2()
    sum_u[0].step3()
    sum_o.step2()
    sum_d[1].step4()
    sum_q[2].step2()

    for item in range(items):
        sent_one[item].wait_recv()

        def back(step, totals):
            at = rows_at(step * tile, tile)
            grad = r.one_mine[item, at, :].astype(jnp.float32) + r.one_from[item, at, :].astype(
                jnp.float32
            )
            value = r.block_in[item, at, :].astype(jnp.float32)
            dvalue, normed = norm_back(value, grad, r.gains[0:1, :])
            r.grad_input[item, at, :] = (r.dmiddle[item, at, :] + dvalue).astype(low)
            return totals[0] + fold(grad * normed), totals[1] + fold(grad)

        totals = lax.fori_loop(0, slab // tile, back, (zero, zero))
        for row, total in zip((0, 1), totals):
            r.small[row : row + 1, :] += rows_sum(total)
        if item == 0:
            sum_u[1].step3()
            sum_q[1].step2()

    small_copy = start(8, r.small, r.small_from.at[0], core)
    sum_o.step3()
    sum_q[0].step2()
    sum_u[0].step4()
    small_copy.wait_recv()
    r.small_two[0] = r.small[...] + r.small_from[0]
    small_copy = start(9, r.small_two.at[0], r.small_from.at[1], beside)
    keep_kernels.wait()
    give_kernels.wait_recv()
    add_into(
        r.own_kernels, 0, [(r.own_kernels, 0), (r.cross_kernels, 0)], r.own_kernels.shape[0],
        r.own_kernels.shape[0] // 16,
    )
    sum_k.step0()
    sum_q[2].step3()
    keep_tconv.wait()
    give_tconv.wait_recv()
    add_into(
        r.own_tconv, 0, [(r.own_tconv, 0), (r.cross_tconv, 0)], r.own_tconv.shape[0],
        r.own_tconv.shape[0] // 16,
    )
    sum_t.step0()
    sum_k.step1()
    sum_t.step1()
    small_copy.wait_recv()
    r.small_two[1] = r.small_two[0] + r.small_from[1]
    r.small_far[far] = r.small_two[1]
    small_far = [
        start(9 + step, r.small_two.at[1], r.small_far.at[far], along[step - 1])
        for step in range(1, FAR)
    ]
    sum_u[1].step4()
    sum_q[1].step3()
    sum_q[0].step3()
    sum_o.step4()
    sum_d[0].step5()
    sum_k.step2()
    sum_t.step2()
    for step in range(FAR - 1):
        small_far[step].wait_recv()
    total = r.small_far[0]
    for at in range(1, FAR):
        total = total + r.small_far[at]
    r.small_total[...] = total
    for one in (sum_q[2], sum_q[1], sum_q[0]):
        one.step4()
    sum_d[1].step5()
    sum_u[0].step5()
    sum_k.step3()
    sum_t.step3()
    sum_u[1].step5()
    sum_o.step5()
    sum_k.step4()
    sum_t.step4()
    for one in (sum_q[2], sum_q[1], sum_q[0], sum_k, sum_t):
        one.step5()
    for one in sum_d + sum_u + [sum_o] + sum_q + [sum_k, sum_t]:
        one.step6()
    for copy in copies:
        copy.wait_send()


LOADED = (
    "down",
    "slope",
    "up",
    "active",
    "normed_two",
    "middle",
    "out_weight",
    "key_value",
    "query",
    "probs",
    "mixed",
    "qkv",
    "normed_one",
)


def backward_section(arrays):
    low = jnp.bfloat16
    wide = jnp.float32
    items, slab, width = arrays["grad_out"].shape
    tokens = items * slab
    local = arrays["qkv"].shape[2]
    units = arrays["down"].shape[0]
    patches = arrays["key_value"].shape[2]
    kernel_rows = arrays["grad_kernels"].shape[1]
    near = ["grad_out", "dtap", "block_in", "gains"]
    distant = list(LOADED) + ["grad_kernels", "grad_tconv"]
    totals = {
        "down": (2, units // 2, width),
        "up": (2, width, units // 2),
        "out": (2 * local, width // 2),
        "qkv": (3, width, local),
        "kernels": (kernel_rows, CH),
        "tconv": (width, arrays["grad_tconv"].shape[1] // 2),
    }
    scratch = {name: pltpu.VMEM(arrays[name].shape, arrays[name].dtype) for name in LOADED}
    for name, shape in totals.items():
        scratch["own_" + name] = pltpu.VMEM(shape, low)
    for name, parts in (("down", 2), ("up", 2), ("out", 0), ("qkv", 3), ("kernels", 0), ("tconv", 0)):
        for part in range(max(parts, 1)):
            label = name + (str(part) if parts else "")
            for end, one in zip(
                ("_core", "_near", "_far", "_piece"), sum_scratch(*totals[name][-2:])
            ):
                scratch[label + end] = one
    block = (items, slab, width)
    for name, shape, dtype in (
        ("ddown", (tokens, width), low),
        ("dhidden", (tokens, units), low),
        ("bias_sum", (8, units), wide),
        ("two_mine", block, low),
        ("two_from", block, low),
        ("dmiddle", block, wide),
        ("dattn", (tokens, width), low),
        ("dmixed", (slab, local), low),
        ("keys_turned", (local, patches), low),
        ("give_kv", (items, 2, slab, local), low),
        ("got_kv", (items, 2, slab, local), low),
        ("dproject", (3, tokens, local), low),
        ("one_mine", block, low),
        ("one_from", block, low),
        ("cross_kernels", totals["kernels"], low),
        ("cross_tconv", totals["tconv"], low),
        ("small", (16, width), wide),
        ("small_two", (2, 16, width), wide),
        ("small_from", (2, 16, width), wide),
        ("small_far", (FAR, 16, width), wide),
    ):
        scratch[name] = pltpu.VMEM(shape, dtype)
    dma = pltpu.SemaphoreType.DMA
    scratch["load_sem"] = dma((len(LOADED) + 2,))
    scratch["send"] = dma((13,))
    scratch["recv"] = dma((13,))
    scratch["sum_send"] = dma((10, COPIES))
    scratch["sum_recv"] = dma((10, COPIES))
    scratch["sum_local"] = dma((10,))
    outputs = ["grad_input", "small_total"] + ["total_" + name for name in totals]
    layout = near + [name + "_hbm" for name in distant] + outputs + list(scratch)
    vmem = pl.BlockSpec(memory_space=pltpu.VMEM)
    hbm = pl.BlockSpec(memory_space=pl.ANY)
    results = pl.pallas_call(
        functools.partial(backward_kernel, tuple(layout)),
        out_shape=[
            jax.ShapeDtypeStruct(block, low),
            jax.ShapeDtypeStruct((16, width), wide),
        ]
        + [jax.ShapeDtypeStruct(shape, low) for shape in totals.values()],
        in_specs=[vmem] * len(near) + [hbm] * len(distant),
        out_specs=[vmem] * 2 + [hbm] * len(totals),
        scratch_shapes=list(scratch.values()),
        name="backward_section",
        compiler_params=pltpu.CompilerParams(
            collective_id=3, has_side_effects=True, vmem_limit_bytes=62 * 2**20
        ),
    )(*[arrays[name] for name in near + distant])
    return dict(zip(outputs, results))


def patch_valid(crop_ids):
    extent_depth = jnp.where(
        crop_ids == 0, GRID * 3 // 4, jnp.where(crop_ids == 1, GRID // 2, GRID)
    )
    extent_side = jnp.where(crop_ids == 0, GRID * 3 // 4, GRID)
    places = jnp.arange(GRID * GRID * GRID, dtype=jnp.int32)
    depth = places // (GRID * GRID)
    across = places // GRID % GRID
    along = places % GRID
    inside = (
        (depth[None, :] < extent_depth[:, None])
        & (across[None, :] < extent_side[:, None])
        & (along[None, :] < extent_side[:, None])
    )
    return inside.astype(jnp.float32)


def voxel_mask(valid):
    grid = valid.reshape(valid.shape[0], -1, GRID, GRID)
    for axis_at in (1, 2, 3):
        grid = jnp.repeat(grid, 2, axis=axis_at)
    return grid[..., None]


def body(
    block_in,
    crop_shape,
    norm_gains,
    shifts,
    qkv_weight,
    qv_bias,
    out_weight,
    up_weight,
    up_bias,
    down_weight,
    tconv_weight,
    kernels,
    grad_out,
    grad_decoded,
):
    item_count, slab_rows, width_all = block_in.shape
    local_width = qkv_weight.shape[2]
    local_heads = local_width // HD
    scale_factor = HD ** (-0.5)
    valid_full = patch_valid(crop_shape)
    patch_total = valid_full.shape[1]
    valid_local = lax.dynamic_slice_in_dim(
        valid_full, lax.axis_index("blk") * slab_rows, slab_rows, 1
    )
    valid_other = lax.dynamic_slice_in_dim(
        valid_full, (1 - lax.axis_index("blk")) * slab_rows, slab_rows, 1
    )
    key_order = jnp.concatenate([valid_local, valid_other], axis=1)
    key_mask = jnp.broadcast_to(key_order[:, :, None], key_order.shape + (128,))
    (
        normed_one,
        query,
        key_value,
        probs_turned,
        mixed_low,
        middle,
        normed_two,
        active_low,
        slope,
        tapped,
    ) = forward_section(
        block_in,
        norm_gains,
        shifts,
        qkv_weight,
        qv_bias,
        out_weight,
        up_weight,
        up_bias[None, :],
        down_weight,
        key_mask,
    )
    per_device = item_count // lax.axis_size("tensor")
    first_item = lax.axis_index("tensor") * per_device
    my_valid = lax.dynamic_slice_in_dim(valid_local, first_item, per_device, 0)
    voxel_count = 8.0 * jnp.sum(
        lax.dynamic_slice_in_dim(valid_full, first_item, per_device, 0), axis=1, keepdims=True
    )
    voxel_valid = voxel_mask(my_valid)
    mask = jnp.broadcast_to(
        voxel_valid[0, :, ::2].reshape(ROWS, 1), (ROWS, CH)
    )
    inverse = jnp.broadcast_to(1.0 / voxel_count, (8, CH))
    decoded, block_all, dtap_all, grad_tconv, kernel_halves = decoder_section(
        tapped,
        tconv_weight,
        kernels,
        grad_decoded.reshape(DEPTH, SIDE, 2, WIDE, CH),
        mask,
        inverse,
    )
    decoded = decoded.reshape(grad_decoded.shape)
    result = backward_section(
        {
            "grad_out": grad_out,
            "dtap": dtap_all,
            "block_in": block_in,
            "gains": norm_gains,
            "down": down_weight,
            "slope": slope,
            "up": up_weight,
            "active": active_low,
            "normed_two": normed_two,
            "middle": middle,
            "out_weight": out_weight,
            "key_value": key_value,
            "query": query,
            "probs": probs_turned,
            "mixed": mixed_low,
            "qkv": qkv_weight,
            "normed_one": normed_one,
            "grad_kernels": kernel_halves,
            "grad_tconv": grad_tconv,
        }
    )
    names = ("small_total", "total_kernels", "total_tconv", "total_down", "total_up", "total_out",
             "total_qkv")
    big = [result[name].astype(jnp.float32) for name in names]
    groups = lax.axis_size("dp") // GROUP
    if groups > 1:
        same = [[part * GROUP + i for part in range(groups)] for i in range(GROUP)]
        big = [lax.psum(array, "dp", axis_index_groups=same) for array in big]
    small, sum_kernel, sum_tconv, sum_down, sum_up, sum_out, sum_qkv = big
    sum_kernel = sum_kernel[:3456].reshape(3456, 2, 64).transpose(1, 0, 2)
    return (
        block_all,
        decoded,
        result["grad_input"],
        small[0:3:2],
        jnp.stack([small[1], small[3], small[4], small[5]]),
        sum_qkv,
        small[6].reshape(2, -1),
        jnp.concatenate([sum_out[:384], sum_out[384:]], axis=1),
        jnp.concatenate([sum_up[0], sum_up[1]], axis=1),
        small[7:9].reshape(-1),
        sum_down.reshape(down_weight.shape),
        sum_tconv,
        sum_kernel,
    )


def solution(mesh):
    return jax.shard_map(
        body,
        mesh=mesh,
        in_specs=(
            P("dp", "blk", None),
            P("dp"),
            P(),
            P(),
            P(None, None, "tensor"),
            P(None, "tensor"),
            P("tensor", None),
            P(None, "tensor"),
            P("tensor"),
            P("tensor", None),
            P(),
            P(),
            P("dp", "blk", None),
            P(("dp", "tensor"), "blk", None, None, None),
        ),
        out_specs=(
            P("dp", "blk", None),
            P(("dp", "tensor"), "blk", None, None, None),
            P("dp", "blk", None),
            P(),
            P(),
            P(None, None, "tensor"),
            P(None, "tensor"),
            P("tensor", None),
            P(None, "tensor"),
            P("tensor"),
            P("tensor", None),
            P(None, "tensor"),
            P(None, None, "tensor"),
        ),
        check_vma=False,
    )
```

```python
import functools
import types

import jax
import jax.numpy as jnp
from jax import lax
from jax.experimental import pallas as pl
from jax.experimental.pallas import tpu as pltpu
from jax.sharding import PartitionSpec as P

HD = 64

MESH = pl.DeviceIdType.MESH
GROUP = 8
FAR = 4


def place():
    dp = lax.axis_index("dp")
    blk = lax.axis_index("blk")
    tensor = lax.axis_index("tensor")
    near = lax.rem(dp, 2)
    far = lax.rem(dp // 2, FAR)
    first = dp // GROUP * GROUP
    return (dp, blk, tensor, near, far, first)


def peers():
    dp, blk, tensor, near, far, first = place()
    core = (dp, 1 - blk, tensor)
    cross = (dp, blk, 1 - tensor)
    beside = (first + 2 * far + 1 - near, blk, tensor)
    side = (first + 2 * (far + 1 - 2 * lax.rem(far, 2)) + near, blk, tensor)
    over = (first + 2 * lax.rem(far + 2, FAR) + near, blk, tensor)
    return (core, cross, beside, side, over)


def greet(devices):
    barrier = pltpu.get_barrier_semaphore()
    for device in devices:
        pl.semaphore_signal(barrier, inc=1, device_id=device, device_id_type=MESH)
    pl.semaphore_wait(barrier, len(devices))


def remote(src, dst, send, recv, device):
    return pltpu.make_async_remote_copy(
        src_ref=src, dst_ref=dst, send_sem=send, recv_sem=recv, device_id=device,
        device_id_type=MESH,
    )


def rows_at(start, size):
    return pl.ds(pl.multiple_of(start, 16), size)


DEPTH = 8
SIDE = 8
WIDE = 16
CH = 128
PAIR = 2 * CH
ROWS = DEPTH * SIDE * WIDE
TAPS = [(deep, wide) for deep in range(3) for wide in range(3)]
PADDED_TAPS = 28


def nt_dot(left, right):
    return lax.dot_general(
        left, right, (((1,), (1,)), ((), ())), preferred_element_type=jnp.float32
    )


def tn_dot(left, right):
    return lax.dot_general(
        left, right, (((0,), (0,)), ((), ())), preferred_element_type=jnp.float32
    )


def dot(left, right):
    return jnp.dot(left, right, preferred_element_type=jnp.float32)


def half_sums(row):
    return row[:, :CH] + row[:, CH:]


def twice(row):
    return jnp.concatenate([row, row], axis=1)


def row_and_column(size):
    return (
        lax.broadcasted_iota(jnp.int32, (size, size), 0),
        lax.broadcasted_iota(jnp.int32, (size, size), 1),
    )


def shift_matrix(step):
    row, column = row_and_column(PAIR)
    same = (row // WIDE) == (column // WIDE)
    return jnp.where(same & (row + step == column), 1.0, 0.0).astype(jnp.bfloat16)


def weave_matrix():
    row, column = row_and_column(PAIR)
    source = lax.rem(row, 2) * CH + row // WIDE * SIDE + lax.rem(row, WIDE) // 2
    return jnp.where(source == column, 1.0, 0.0).astype(jnp.bfloat16)


def unweave_matrix():
    row, column = row_and_column(PAIR)
    source = lax.rem(column, 2) * CH + column // WIDE * SIDE + lax.rem(column, WIDE) // 2
    return jnp.where(source == row, 1.0, 0.0).astype(jnp.bfloat16)


def lay_kernel(kernels_ref, index, weights):
    zero = jnp.zeros((CH, CH), jnp.bfloat16)
    for at, (deep, wide) in enumerate(TAPS):
        weights[at, 3 * CH :, :CH] = zero
        weights[at, :CH, CH:] = zero
        for high in range(3):
            offset = ((deep * 3 + high) * 3 + wide) * CH
            block = kernels_ref[index, offset : offset + CH, :]
            weights[at, high * CH : (high + 1) * CH, :CH] = block
            weights[at, (high + 1) * CH : (high + 2) * CH, CH:] = block


def lay_flipped(kernels_ref, index, weights):
    zero = jnp.zeros((CH, CH), jnp.bfloat16)
    for at, (deep, wide) in enumerate(TAPS):
        weights[at, :CH, 3 * CH :] = zero
        weights[at, CH:, :CH] = zero
        for high in range(3):
            offset = (((2 - deep) * 3 + 2 - high) * 3 + 2 - wide) * CH
            block = kernels_ref[index, offset : offset + CH, :]
            weights[at, :CH, high * CH : (high + 1) * CH] = block
            weights[at, CH:, (high + 1) * CH : (high + 2) * CH] = block


def four_heights(field, wide, start, count):
    depths = pl.ds(start, count)
    low = field[wide, depths, 0:SIDE, :, CH:]
    middle = field[wide, depths, 1 : SIDE + 1, :, :]
    high = field[wide, depths, 2 : SIDE + 2, :, :CH]
    joined = jnp.concatenate([low, middle, high], axis=-1)
    return joined.reshape(count * SIDE * WIDE, 4 * CH)


def conv_tile(field, weights, multiply, level, start):
    total = None
    for at, (deep, wide) in enumerate(TAPS):
        product = multiply(four_heights(field, wide, start + deep, 2), weights[at])
        total = product if total is None else total + product
    level[pl.ds(pl.multiple_of(start * CH, 2 * CH), 2 * CH), :] = total


def conv(field, weights, multiply, level, arrive):
    @pl.loop(0, 2)
    def _(step):
        conv_tile(field, weights, multiply, level, 2 + 2 * step)

    arrive()

    @pl.loop(0, 2)
    def _(step):
        conv_tile(field, weights, multiply, level, 6 * step)


def clear_rims(field, blk):
    for wide in range(3):
        field[wide, :, 0] = jnp.zeros((DEPTH + 2, WIDE, PAIR), jnp.bfloat16)
        field[wide, :, SIDE + 1] = jnp.zeros((DEPTH + 2, WIDE, PAIR), jnp.bfloat16)
        field[wide, 9 * blk] = jnp.zeros((SIDE + 2, WIDE, PAIR), jnp.bfloat16)


def place_rows(field, before, after, step, value):
    shape = (2, SIDE, WIDE, PAIR)
    depths = pl.ds(1 + 2 * step, 2)
    field[1, depths, 1 : SIDE + 1] = value.reshape(shape)
    field[0, depths, 1 : SIDE + 1] = dot(before, value).astype(jnp.bfloat16).reshape(shape)
    field[2, depths, 1 : SIDE + 1] = dot(after, value).astype(jnp.bfloat16).reshape(shape)


def kernel_grad(field, dlevel_turned, index, out, tensor_half):
    for at, (deep, wide) in enumerate(TAPS):
        joined = four_heights(field, wide, deep, DEPTH)
        block = dot(dlevel_turned[...], joined)
        for high in range(3):
            part = (
                block[:CH, high * CH : (high + 1) * CH]
                + block[CH:, (high + 1) * CH : (high + 2) * CH]
            )
            offset = ((deep * 3 + high) * 3 + wide) * CH
            part = part.astype(jnp.bfloat16)
            at = index * PADDED_TAPS * 64 + offset // 2
            for half in range(2):
                out[half, at : at + 64, :] = part[half * 64 : (half + 1) * 64, :]


def decoder_kernel(
    tapped,
    tconv,
    kernels,
    grad_decoded,
    crop_shape,
    decoded,
    block_all,
    dtap_all,
    grad_tconv,
    grad_kernels,
    mask,
    inverse,
    field_one,
    field_two,
    dlevel_two,
    dlevel_one,
    weights_one,
    weights_two,
    flipped_two,
    flipped_one,
    level_one,
    level_two,
    dfield,
    turned_two,
    turned_one,
    dlifted,
    tapped_from,
    dtap_mine,
    dtap_from,
    sums_mine,
    sums_from,
    send,
    recv,
):
    dp, blk, tensor, near, far, first = place()
    core, cross, beside, side, over = peers()
    greet([core, cross])
    low = jnp.bfloat16
    row_tiles = ROWS // PAIR

    copies = []

    def start(index, src, dst, device):
        copy = remote(src, dst, send.at[index], recv.at[index], device)
        copy.start()
        copies.append(copy)
        return copy

    give_tapped = start(0, tapped, tapped_from, cross)

    depth_end, side_end = extents(crop_shape[tensor])
    row = lax.broadcasted_iota(jnp.int32, mask.shape, 0)
    inside = (
        (blk * (DEPTH // 2) + row // (2 * CH) < depth_end)
        & (lax.rem(row // WIDE, SIDE) < side_end)
        & (lax.rem(row, WIDE) // 2 < side_end)
    )
    mask[...] = jnp.where(inside, 1.0, 0.0)
    voxels = (8 * depth_end * side_end * side_end).astype(jnp.float32)
    inverse[...] = 1.0 / jnp.full(inverse.shape, voxels)

    before, after = shift_matrix(-1), shift_matrix(1)

    def send_edge(index, field):
        return start(
            index,
            field.at[:, DEPTH - 7 * blk, 1 : SIDE + 1],
            field.at[:, 9 * blk, 1 : SIDE + 1],
            core,
        )

    def rows_of(step):
        return pl.ds(pl.multiple_of(step * PAIR, PAIR), PAIR)

    def mask_rows(step):
        return twice(mask[rows_of(step), :])

    def totals(slot, pair):
        sums_mine[slot, 0:1, :] = half_sums(pair[0])
        sums_mine[slot, 1:2, :] = half_sums(pair[1])
        return start(5 + slot, sums_mine.at[slot], sums_from.at[slot], core)

    def means(slot, copy):
        copy.wait_recv()
        both = (sums_mine[slot] + sums_from[slot]) * inverse[...]
        return both[0:1, :], both[1:2, :]

    zero_pair = (jnp.zeros((1, PAIR), jnp.float32), jnp.zeros((1, PAIR), jnp.float32))

    for field in (field_one, field_two, dlevel_two, dlevel_one):
        clear_rims(field, blk)
    weave = weave_matrix()
    for piece in range(2):
        tokens = slice(piece * CH, (piece + 1) * CH)
        for a in range(2):
            lifted = dot(tapped[tokens, :], tconv[:, a * 512 : (a + 1) * 512])
            side = [
                jnp.concatenate([lifted[:, c * CH : (c + 1) * CH],
                                 lifted[:, (2 + c) * CH : (3 + c) * CH]], axis=1)
                for c in range(2)
            ]
            woven = dot(weave, jnp.concatenate(side, axis=0).astype(low))
            for depth in range(2):
                at = 2 * (2 * piece + depth) + a
                rows = slice(depth * CH, (depth + 1) * CH)
                value = woven[rows, :] * twice(mask[at * CH : (at + 1) * CH, :])
                level_one[at * CH : (at + 1) * CH, :] = value

    @pl.loop(0, row_tiles)
    def _(step):
        place_rows(field_one, before, after, step, level_one[rows_of(step), :].astype(low))

    edge = send_edge(1, field_one)
    lay_kernel(kernels, 0, weights_one)
    conv(field_one, weights_one, dot, level_one, edge.wait_recv)

    def forward_sums(level):
        def add(step, pair):
            value = level[rows_of(step), :]
            kept = value * mask_rows(step)
            return (
                pair[0] + jnp.sum(kept, axis=0, keepdims=True),
                pair[1] + jnp.sum(kept * value, axis=0, keepdims=True),
            )

        return lax.fori_loop(0, row_tiles, add, zero_pair)

    def mean_and_scale(slot, copy):
        mean, second = means(slot, copy)
        return twice(mean), twice(lax.rsqrt(second - mean * mean + 1e-05))

    def sigmoid(value):
        return 0.5 * jnp.tanh(0.5 * value) + 0.5

    copy = totals(0, forward_sums(level_one))
    lay_kernel(kernels, 1, weights_two)
    mean_one, scale_one = mean_and_scale(0, copy)

    @pl.loop(0, row_tiles)
    def _(step):
        normed = (level_one[rows_of(step), :] - mean_one) * scale_one
        level_one[rows_of(step), :] = normed
        value = normed * sigmoid(normed) * mask_rows(step)
        place_rows(field_two, before, after, step, value.astype(low))

    edge = send_edge(2, field_two)
    lay_flipped(kernels, 1, flipped_two)
    conv(field_two, weights_two, dot, level_two, edge.wait_recv)
    copy = totals(1, forward_sums(level_two))
    lay_flipped(kernels, 0, flipped_one)
    mean_two, scale_two = mean_and_scale(1, copy)

    def two_depths(ref, step, b):
        return ref[pl.ds(2 * step, 2), :, b].reshape(PAIR, CH)

    def decode(step, pair):
        normed = (level_two[rows_of(step), :] - mean_two) * scale_two
        level_two[rows_of(step), :] = normed
        kept = mask_rows(step)
        gate = sigmoid(normed)
        value = (normed * gate * kept).astype(low)
        for b in range(2):
            decoded[pl.ds(2 * step, 2), :, b] = value[:, b * CH : (b + 1) * CH].reshape(
                2, SIDE, WIDE, CH
            )
        grad = jnp.concatenate(
            [two_depths(grad_decoded, step, 0), two_depths(grad_decoded, step, 1)], axis=1
        ).astype(jnp.float32)
        dnormed = gate * (1.0 + normed * (1.0 - gate)) * kept * grad
        dfield[rows_of(step), :] = dnormed
        return (
            pair[0] + jnp.sum(dnormed, axis=0, keepdims=True),
            pair[1] + jnp.sum(dnormed * normed, axis=0, keepdims=True),
        )

    copy = totals(2, lax.fori_loop(0, row_tiles, decode, zero_pair))

    def level_grad(slot, copy, level, scale, field, turned):
        mean_grad, mean_cross = means(slot, copy)
        mean_grad, mean_cross = twice(mean_grad), twice(mean_cross)

        @pl.loop(0, row_tiles)
        def _(step):
            centred = mean_grad + level[rows_of(step), :] * mean_cross
            value = scale * (dfield[rows_of(step), :] - mask_rows(step) * centred)
            place_rows(field, before, after, step, value.astype(low))
            turned[:, rows_of(step)] = value.T.astype(low)

    level_grad(2, copy, level_two, scale_two, dlevel_two, turned_two)
    edge = send_edge(3, dlevel_two)
    conv(dlevel_two, flipped_two, nt_dot, dfield, edge.wait_recv)

    def back_one(step, pair):
        normed = level_one[rows_of(step), :]
        gate = sigmoid(normed)
        dnormed = gate * (1.0 + normed * (1.0 - gate)) * mask_rows(step) * dfield[rows_of(step), :]
        dfield[rows_of(step), :] = dnormed
        return (
            pair[0] + jnp.sum(dnormed, axis=0, keepdims=True),
            pair[1] + jnp.sum(dnormed * normed, axis=0, keepdims=True),
        )

    copy = totals(3, lax.fori_loop(0, row_tiles, back_one, zero_pair))
    level_grad(3, copy, level_one, scale_one, dlevel_one, turned_one)
    edge = send_edge(4, dlevel_one)
    conv(dlevel_one, flipped_one, nt_dot, dfield, edge.wait_recv)

    unweave = unweave_matrix()
    for piece in range(2):
        tokens = slice(piece * CH, (piece + 1) * CH)
        for a in range(2):
            parts = []
            for depth in range(2):
                at = 2 * (2 * piece + depth) + a
                rows = slice(at * CH, (at + 1) * CH)
                parts.append(dfield[rows, :] * twice(mask[rows, :]))
            apart = dot(unweave, jnp.concatenate(parts, axis=0).astype(low)).astype(low)
            for c in range(2):
                for b in range(2):
                    column = ((a * 2 + b) * 2 + c) * CH
                    dlifted[tokens, column : column + CH] = apart[
                        c * CH : (c + 1) * CH, b * CH : (b + 1) * CH
                    ]
    dtap_mine[...] = nt_dot(dlifted[...], tconv[...]).astype(low)
    give_dtap = start(9, dtap_mine, dtap_from, cross)
    for half in range(2):
        lanes = slice(half * 512, (half + 1) * 512)
        grad_tconv[half] = tn_dot(tapped[...], dlifted[:, lanes]).astype(low)
        for index in range(2):
            at = ((index + 1) * PADDED_TAPS - 1) * 64
            grad_kernels[half, at : at + 64, :] = jnp.zeros((64, CH), low)
    kernel_grad(field_two, turned_two, 1, grad_kernels, tensor)
    kernel_grad(field_one, turned_one, 0, grad_kernels, tensor)
    give_tapped.wait_recv()
    block_all[tensor] = tapped[...]
    block_all[1 - tensor] = tapped_from[...]
    give_dtap.wait_recv()
    dtap_all[tensor] = dtap_mine[...]
    dtap_all[1 - tensor] = dtap_from[...]
    for copy in copies:
        copy.wait_send()


def decoder_section(tapped, tconv_weight, kernels, grad_decoded, crop_shape):
    low = jnp.bfloat16
    vmem = pl.BlockSpec(memory_space=pltpu.VMEM)
    field = pltpu.VMEM((3, DEPTH + 2, SIDE + 2, WIDE, PAIR), low)
    plane = pltpu.VMEM((ROWS, PAIR), jnp.float32)
    return pl.pallas_call(
        decoder_kernel,
        out_shape=[
            jax.ShapeDtypeStruct((DEPTH, SIDE, 2, WIDE, CH), low),
            jax.ShapeDtypeStruct((2,) + tapped.shape, low),
            jax.ShapeDtypeStruct((2,) + tapped.shape, low),
            jax.ShapeDtypeStruct((2, tapped.shape[1], tconv_weight.shape[1] // 2), low),
            jax.ShapeDtypeStruct((2, PADDED_TAPS * CH, CH), low),
        ],
        in_specs=[vmem] * 4 + [pl.BlockSpec(memory_space=pltpu.SMEM)],
        out_specs=[vmem] * 5,
        scratch_shapes=[pltpu.VMEM((ROWS, CH), jnp.float32), pltpu.VMEM((8, CH), jnp.float32)]
        + [field] * 4
        + [pltpu.VMEM((9, 4 * CH, PAIR), low)] * 2
        + [pltpu.VMEM((9, PAIR, 4 * CH), low)] * 2
        + [plane] * 3
        + [pltpu.VMEM((PAIR, ROWS), low)] * 2
        + [
            pltpu.VMEM((tapped.shape[0], tconv_weight.shape[1]), low),
            pltpu.VMEM(tapped.shape, low),
            pltpu.VMEM(tapped.shape, low),
            pltpu.VMEM(tapped.shape, low),
            pltpu.VMEM((4, 8, CH), jnp.float32),
            pltpu.VMEM((4, 8, CH), jnp.float32),
            pltpu.SemaphoreType.DMA((10,)),
            pltpu.SemaphoreType.DMA((10,)),
        ],
        name="decoder_section",
        compiler_params=pltpu.CompilerParams(
            collective_id=1, has_side_effects=True, vmem_limit_bytes=60 * 2**20
        ),
    )(tapped, tconv_weight, kernels, grad_decoded, crop_shape)


def widen_rows(src, dst, tile=64):
    @pl.loop(0, src.shape[0] // tile)
    def _(step):
        at = rows_at(step * tile, tile)
        dst[at, :] = src[at, :].astype(jnp.float32)


def finish_kernel(count, *refs):
    sources, refs = refs[:count], refs[count:]
    passed, small, refs = refs[:3], refs[3], refs[4:]
    targets, refs = refs[:count], refs[count:]
    handed, smalls, refs = refs[:3], refs[3:7], refs[7:]
    lows, wides, refs = refs[:count], refs[count : 2 * count], refs[2 * count :]
    held, refs = refs[:3], refs[3:]
    load_sem, store_sem, pass_sem = refs
    loads, stores = [], []
    for index in range(count):
        loads.append(pltpu.make_async_copy(sources[index], lows[index], load_sem.at[index]))
    passes = [
        pltpu.make_async_copy(passed[index], held[index], pass_sem.at[index])
        for index in range(3)
    ]
    for copy in passes + loads:
        copy.start()
    gains, shifts, qv_bias, up_bias = smalls
    width = small.shape[1]
    gains[0:1, :] = small[0:1, :]
    gains[1:2, :] = small[2:3, :]
    shifts[0:1, :] = small[1:2, :]
    shifts[1:4, :] = small[3:6, :]
    qv_bias[0:1, :] = small[6:7, : width // 2]
    qv_bias[1:2, :] = small[6:7, width // 2 :]
    up_bias[:width] = small[7, :]
    up_bias[width:] = small[8, :]

    def store(src, dst):
        copy = pltpu.make_async_copy(src, dst, store_sem.at[len(stores)])
        copy.start()
        stores.append(copy)

    for index in range(3):
        passes[index].wait()
        store(held[index], handed[index])
    for index in range(count):
        src, dst, wide, low = sources[index], targets[index], wides[index], lows[index]
        loads[index].wait()
        if dst.shape == src.shape and len(src.shape) == 2:
            widen_rows(low, wide)
            store(wide, dst)
        elif dst.shape == src.shape:
            for part in range(src.shape[0]):
                widen_rows(low.at[part], wide.at[part])
                store(wide.at[part], dst.at[part])
        elif len(src.shape) == 3:
            for part in range(src.shape[0]):
                widen_rows(low.at[part], wide.at[part])
                columns = src.shape[2]
                store(wide.at[part], dst.at[:, pl.ds(part * columns, columns)])
        elif len(dst.shape) == 2:
            widen_rows(low, wide)
            rows, columns = dst.shape[0], src.shape[1]
            for part in range(2):
                store(
                    wide.at[pl.ds(part * rows, rows)], dst.at[:, pl.ds(part * columns, columns)]
                )
        else:
            kinds, outs, columns = dst.shape
            ins = src.shape[1]
            for kind in range(kinds):
                for tap in range(columns // ins):
                    at = (kind * PADDED_TAPS + tap) * outs
                    wide[kind, :, tap * ins : (tap + 1) * ins] = low[at : at + outs, :].astype(
                        jnp.float32
                    )
                store(wide.at[kind], dst.at[kind])
    for copy in stores:
        copy.wait()


def finish_section(totals, passed, small):
    wide = jnp.float32
    local = totals["qkv"].shape[2]
    width = totals["qkv"].shape[1]
    units = totals["up"].shape[2] * 2
    shapes = {
        "qkv": totals["qkv"].shape,
        "out": (local, width),
        "up": (width, units),
        "down": totals["down"].shape,
        "tconv": totals["tconv"].shape,
        "kernels": (2, 64, 27 * CH),
    }
    count = len(shapes)
    sources = [totals[name] for name in shapes]
    kept = [
        shapes[name] if name == "kernels" else totals[name].shape for name in shapes
    ]
    vmem = pl.BlockSpec(memory_space=pltpu.VMEM)
    hbm = pl.BlockSpec(memory_space=pl.ANY)
    results = pl.pallas_call(
        functools.partial(finish_kernel, count),
        out_shape=[jax.ShapeDtypeStruct(shape, wide) for shape in shapes.values()]
        + [jax.ShapeDtypeStruct(array.shape, array.dtype) for array in passed]
        + [
            jax.ShapeDtypeStruct(shape, wide)
            for shape in ((2, width), (4, width), (2, local), (units,))
        ],
        in_specs=[hbm] * (count + 3) + [vmem],
        out_specs=[hbm] * (count + 3) + [vmem] * 4,
        scratch_shapes=[pltpu.VMEM(array.shape, array.dtype) for array in sources]
        + [pltpu.VMEM(shape, wide) for shape in kept]
        + [pltpu.VMEM(array.shape, array.dtype) for array in passed]
        + [
            pltpu.SemaphoreType.DMA((count,)),
            pltpu.SemaphoreType.DMA((16,)),
            pltpu.SemaphoreType.DMA((3,)),
        ],
        name="finish",
        compiler_params=pltpu.CompilerParams(vmem_limit_bytes=60 * 2**20),
    )(*sources, *passed, small)
    return dict(zip(shapes, results)), results[count : count + 3], results[count + 3 :]


def extents(crop):
    depth = jnp.where(crop == 0, SIDE * 3 // 4, jnp.where(crop == 1, SIDE // 2, SIDE))
    side = jnp.where(crop == 0, SIDE * 3 // 4, SIDE)
    return depth, side


GELU_RATE = 0.7978845608028654
GELU_CUBE = 0.044715


def rows_sum(value):
    return jnp.sum(value, axis=0, keepdims=True)


def lane_mean(value):
    return jnp.mean(value, axis=-1, keepdims=True)


def centred(value):
    centre = value - lane_mean(value)
    return centre, lax.rsqrt(lane_mean(centre * centre) + 1e-06)


def head_only(pair, head):
    lane = lax.broadcasted_iota(jnp.int32, pair.shape, 1)
    return jnp.where((lane // HD) == head, pair, jnp.zeros_like(pair))


def forward_kernel(
    block_in,
    gains,
    shifts,
    qkv_hbm,
    qv_bias,
    out_hbm,
    up_hbm,
    up_bias,
    down_hbm,
    crop_shape,
    normed_one_hbm,
    query_hbm,
    key_value_hbm,
    probs_hbm,
    mixed_hbm,
    middle_hbm,
    normed_two_hbm,
    active_hbm,
    slope_hbm,
    tapped,
    qkv,
    out_weight,
    up,
    down,
    normed_one,
    query,
    key_value,
    probs,
    mixed,
    middle,
    normed_two,
    active,
    slope,
    values_turned,
    part_mine,
    part_from,
    feed_mine,
    feed_from,
    load_sem,
    store_sem,
    send,
    recv,
):
    dp, blk, tensor, near, far, first = place()
    core, cross, beside, side, over = peers()
    low = jnp.bfloat16
    items, slab, width = block_in.shape
    local = query.shape[1]
    units = active.shape[1]

    loads = []
    for index, (src, dst) in enumerate(
        [(qkv_hbm, qkv), (out_hbm, out_weight), (up_hbm, up), (down_hbm, down)]
    ):
        copy = pltpu.make_async_copy(src, dst, load_sem.at[index])
        copy.start()
        loads.append(copy)
    greet([core, cross])
    copies = []
    stores = []

    def start(index, src, dst, device):
        copy = remote(src, dst, send.at[index], recv.at[index], device)
        copy.start()
        copies.append(copy)
        return copy

    def store(src, dst):
        copy = pltpu.make_async_copy(src, dst, store_sem.at[len(stores)])
        copy.start()
        stores.append(copy)

    tile = 64

    for item in range(items):

        @pl.loop(0, slab // tile)
        def _(step):
            value = block_in[item, rows_at(step * tile, tile), :].astype(jnp.float32)
            centre, scale = centred(value)
            normed = centre * scale * gains[0:1, :] + shifts[0:1, :]
            normed_one[rows_at(item * slab + step * tile, tile), :] = normed.astype(low)

    store(normed_one, normed_one_hbm)
    loads[0].wait()
    kv_copies = []
    for item in range(items):
        rows = slice(item * slab, (item + 1) * slab)
        for c in range(2):
            project = dot(normed_one[rows, :], qkv[1 + c])
            if c == 1:
                project = project + qv_bias[1:2, :]
            key_value[item, c, :slab, :] = project.astype(low)
        kv_copies.append(
            start(
                item,
                key_value.at[item, :, pl.ds(0, slab), :],
                key_value.at[item, :, pl.ds(slab, slab), :],
                core,
            )
        )
    for item in range(items):
        rows = slice(item * slab, (item + 1) * slab)
        query[rows, :] = (dot(normed_one[rows, :], qkv[0]) + qv_bias[0:1, :]).astype(low)
    store(query, query_hbm)

    part_copies = []
    for item in range(items):
        rows = slice(item * slab, (item + 1) * slab)
        kv_copies[item].wait_recv()
        values_turned[...] = key_value[item, 1].astype(jnp.float32).T.astype(low)
        depth_end, side_end = extents(crop_shape[item])
        key = lax.broadcasted_iota(jnp.int32, (probs.shape[2], slab), 0)
        patch = jnp.where(key < slab, blk * slab + key, (1 - blk) * slab + key - slab)
        keep = (
            (patch // (SIDE * SIDE) < depth_end)
            & (lax.rem(patch // SIDE, SIDE) < side_end)
            & (lax.rem(patch, SIDE) < side_end)
        )
        for pair in range(local // 128):
            lanes = slice(pair * 128, (pair + 1) * 128)
            keys = key_value[item, 0, :, lanes]
            asked = query[rows, lanes] * jnp.asarray(HD ** (-0.5), low)
            turned = []
            for head in range(2):
                scores = nt_dot(keys, head_only(asked, head))
                scores = jnp.where(keep, scores, -1000000000.0)
                weights = jnp.exp(scores - jnp.max(scores, axis=0, keepdims=True))
                prob = (weights * (1.0 / rows_sum(weights))).astype(low)
                probs[item, 2 * pair + head] = prob
                at = pair * 128 + head * HD
                turned.append(dot(values_turned[at : at + HD, :], prob))
            mixed[rows, lanes] = jnp.concatenate(turned, axis=0).T.astype(low)
        store(probs.at[item], probs_hbm.at[item])
        if item == 0:
            loads[1].wait()
        part_mine[item] = dot(mixed[rows, :], out_weight[...]).astype(low)
        part_copies.append(start(2 + item, part_mine.at[item], part_from.at[item], cross))
    store(key_value, key_value_hbm)
    store(mixed, mixed_hbm)

    for item in range(items):
        if item == 0:
            loads[2].wait()
        part_copies[item].wait_recv()

        @pl.loop(0, slab // tile)
        def _(step):
            at = rows_at(step * tile, tile)
            attended = part_mine[item, at, :].astype(jnp.float32) + part_from[item, at, :].astype(
                jnp.float32
            )
            value = block_in[item, at, :].astype(jnp.float32) + (attended + shifts[2:3, :])
            middle[item, at, :] = value
            centre, scale = centred(value)
            normed = centre * scale * gains[1:2, :] + shifts[1:2, :]
            normed_two[rows_at(item * slab + step * tile, tile), :] = normed.astype(low)

        rows = slice(item * slab, (item + 1) * slab)

        @pl.loop(0, units // 256)
        def _(step):
            lanes = pl.ds(pl.multiple_of(step * 256, 256), 256)
            value = dot(normed_two[rows, :], up[:, lanes]) + up_bias[lanes].reshape(1, -1)
            square = value * value
            bent = jnp.tanh(GELU_RATE * value * (1.0 + GELU_CUBE * square))
            half = 0.5 * (1.0 + bent)
            active[rows, lanes] = (value * half).astype(low)
            inner = GELU_RATE * (1.0 + 3.0 * GELU_CUBE * square)
            slope[rows, lanes] = (half + 0.5 * value * (1.0 - bent * bent) * inner).astype(low)

        if item == 0:
            loads[3].wait()

        @pl.loop(0, width // 256)
        def _(step):
            lanes = pl.ds(pl.multiple_of(step * 256, 256), 256)
            feed_mine[item, :, lanes] = dot(active[rows, :], down[:, lanes]).astype(low)

    store(middle, middle_hbm)
    store(normed_two, normed_two_hbm)
    store(active, active_hbm)
    store(slope, slope_hbm)
    feed = start(4, feed_mine.at[1 - tensor], feed_from, cross)
    feed.wait_recv()

    @pl.loop(0, slab // tile)
    def _(step):
        at = rows_at(step * tile, tile)
        fed = feed_mine[tensor, at, :].astype(jnp.float32) + feed_from[at, :].astype(jnp.float32)
        tapped[at, :] = (middle[tensor, at, :] + (fed + shifts[3:4, :])).astype(low)

    for copy in copies:
        copy.wait_send()
    for copy in stores:
        copy.wait()


def forward_section(
    block_in, gains, shifts, qkv, qv_bias, out_weight, up, up_bias, down, crop_shape
):
    low = jnp.bfloat16
    items, slab, width = block_in.shape
    tokens = items * slab
    local = qkv.shape[2]
    units = up.shape[1]
    heads = local // HD
    patches = 2 * slab
    vmem = pl.BlockSpec(memory_space=pltpu.VMEM)
    hbm = pl.BlockSpec(memory_space=pl.ANY)
    kept = [
        ((tokens, width), low),
        ((tokens, local), low),
        ((items, 2, patches, local), low),
        ((items, heads, patches, slab), low),
        ((tokens, local), low),
        ((items, slab, width), jnp.float32),
        ((tokens, width), low),
        ((tokens, units), low),
        ((tokens, units), low),
    ]
    return pl.pallas_call(
        forward_kernel,
        out_shape=[jax.ShapeDtypeStruct(*one) for one in kept]
        + [jax.ShapeDtypeStruct((slab, width), low)],
        in_specs=[vmem, vmem, vmem, hbm, vmem, hbm, hbm, vmem, hbm]
        + [pl.BlockSpec(memory_space=pltpu.SMEM)],
        out_specs=[hbm] * 9 + [vmem],
        scratch_shapes=[pltpu.VMEM(one.shape, low) for one in (qkv, out_weight, up, down)]
        + [pltpu.VMEM(*one) for one in kept]
        + [
            pltpu.VMEM((local, patches), low),
            pltpu.VMEM(block_in.shape, low),
            pltpu.VMEM(block_in.shape, low),
            pltpu.VMEM(block_in.shape, low),
            pltpu.VMEM((slab, width), low),
            pltpu.SemaphoreType.DMA((4,)),
            pltpu.SemaphoreType.DMA((16,)),
            pltpu.SemaphoreType.DMA((5,)),
            pltpu.SemaphoreType.DMA((5,)),
        ],
        name="forward_section",
        compiler_params=pltpu.CompilerParams(
            collective_id=2, has_side_effects=True, vmem_limit_bytes=60 * 2**20
        ),
    )(block_in, gains, shifts, qkv, qv_bias, out_weight, up, up_bias, down, crop_shape)


def fold(value):
    rows, width = value.shape
    return jnp.sum(value.reshape(rows // 8, 8, width), axis=0)


def add_into(target, target_at, parts, rows, tile):
    @pl.loop(0, rows // tile)
    def _(step):
        at = step * tile
        total = None
        for ref, offset in parts:
            piece = ref[rows_at(offset + at, tile), :].astype(jnp.float32)
            total = piece if total is None else total + piece
        target[rows_at(target_at + at, tile), :] = total.astype(jnp.bfloat16)


COPIES = 10


class Sum:
    def __init__(self, refs, name, index, own, total, full=None):
        self.own, self.total, self.full = own, total, full
        self.from_core = getattr(refs, name + "_core")
        self.from_near = getattr(refs, name + "_near")
        self.from_side = getattr(refs, name + "_side")
        self.from_over = getattr(refs, name + "_over")
        self.part = getattr(refs, name + "_part")
        if full is not None:
            self.both = getattr(refs, name + "_both")
            self.cross_part = getattr(refs, name + "_cross")
        self.send, self.recv = refs.sum_send.at[index], refs.sum_recv.at[index]
        self.local = refs.sum_local.at[index]
        self.rows = total.shape[0]
        self.half, self.quarter = self.rows // 2, self.rows // 4
        self.eighth, self.piece = self.rows // 8, self.rows // 16
        dp, self.blk, self.tensor, self.near, self.far, first = place()
        self.core, self.cross, self.beside, self.side, self.over = peers()
        self.low_bit, self.high_bit = lax.rem(self.far, 2), self.far // 2
        self.near_at = self.blk * self.half + self.near * self.quarter
        self.side_at = self.near_at + self.low_bit * self.eighth
        self.part_at = self.side_at + self.high_bit * self.piece
        self.waiting = []

    def start(self, index, src, dst, device):
        copy = remote(src, dst, self.send.at[index], self.recv.at[index], device)
        copy.start()
        self.waiting.append(copy)
        return copy

    def spread(self, index, at, size, device):
        where = self.total.at[rows_at(at, size)]
        return self.start(index, where, where, device)

    def sA(self):
        give = rows_at((1 - self.blk) * self.half, self.half)
        self.c0 = self.start(0, self.full.at[:, give], self.both, self.core)

    def sB(self):
        self.c0.wait_recv()
        mine = self.blk * self.half
        for which in (1 - self.tensor, self.tensor):
            add_into(
                self.both.at[which], 0, [(self.both.at[which], 0), (self.own.at[which], 0)],
                self.half, self.piece,
            )
        self.cx = self.start(1, self.both.at[1 - self.tensor], self.cross_part, self.cross)

    def s0(self):
        give = rows_at((1 - self.blk) * self.half, self.half)
        self.c0 = self.start(0, self.own.at[give], self.from_core, self.core)

    def s1(self):
        if self.full is None:
            self.c0.wait_recv()
            parts = [(self.from_core, 0), (self.own, self.blk * self.half)]
        else:
            self.cx.wait_recv()
            parts = [(self.both.at[self.tensor], 0), (self.cross_part, 0)]
        add_into(self.from_core, 0, parts, self.half, self.piece)
        give = rows_at((1 - self.near) * self.quarter, self.quarter)
        self.c1 = self.start(2, self.from_core.at[give], self.from_near, self.beside)

    def s2(self):
        self.c1.wait_recv()
        add_into(
            self.from_near, 0, [(self.from_near, 0), (self.from_core, self.near * self.quarter)],
            self.quarter, self.piece,
        )
        give = rows_at((1 - self.low_bit) * self.eighth, self.eighth)
        self.c2 = self.start(3, self.from_near.at[give], self.from_side, self.side)

    def s2b(self):
        self.c2.wait_recv()
        add_into(
            self.from_side, 0, [(self.from_side, 0), (self.from_near, self.low_bit * self.eighth)],
            self.eighth, self.piece,
        )
        give = rows_at((1 - self.high_bit) * self.piece, self.piece)
        self.c2 = self.start(4, self.from_side.at[give], self.from_over, self.over)

    def s3(self):
        self.c2.wait_recv()
        add_into(
            self.part, 0, [(self.from_over, 0), (self.from_side, self.high_bit * self.piece)],
            self.piece, self.piece,
        )
        where = self.total.at[rows_at(self.part_at, self.piece)]
        self.keep = pltpu.make_async_copy(self.part, where, self.local)
        self.keep.start()
        self.c3 = self.start(5, self.part, where, self.over)

    def s3b(self):
        self.keep.wait()
        self.c3.wait_recv()
        self.c3 = self.spread(6, self.side_at, self.eighth, self.side)

    def s4(self):
        self.c3.wait_recv()
        self.c4 = self.spread(7, self.near_at, self.quarter, self.beside)

    def s5(self):
        self.c4.wait_recv()
        self.c5 = self.spread(8, self.blk * self.half, self.half, self.core)

    def s6(self):
        self.c5.wait_recv()
        for copy in self.waiting:
            copy.wait_send()


def sum_scratch(rows, columns):
    low = jnp.bfloat16
    return {
        end: pltpu.VMEM((rows // share, columns), low)
        for end, share in (("_core", 2), ("_near", 4), ("_side", 8), ("_over", 16), ("_part", 16))
    }


def norm_back(value, grad, gain):
    centre, scale = centred(value)
    normed = centre * scale
    scaled = grad * gain
    inner = lane_mean(scaled * normed)
    return scale * (scaled - lane_mean(scaled) - normed * inner), normed


def backward_kernel(layout, *refs):
    r = types.SimpleNamespace(**dict(zip(layout, refs)))
    dp, blk, tensor, near, far, first = place()
    core, cross, beside, side, over = peers()
    low = jnp.bfloat16
    items, slab, width = r.grad_out.shape
    local = r.query.shape[1]
    units = r.active.shape[1]
    pairs = local // 128
    tile = 64
    half_width = width // 2

    loads = {}
    for index, name in enumerate(LOADED):
        copy = pltpu.make_async_copy(getattr(r, name + "_hbm"), getattr(r, name), r.load_sem.at[index])
        copy.start()
        loads[name] = copy
    keep_full = {}
    for index, name in enumerate(("kernels", "tconv")):
        full = getattr(r, "grad_" + name + "_hbm")
        rows = full.shape[1] // 2
        copy = pltpu.make_async_copy(
            full.at[:, rows_at(blk * rows, rows)],
            getattr(r, "own_" + name),
            r.load_sem.at[len(LOADED) + index],
        )
        copy.start()
        keep_full[name] = copy
    greet([core, cross, beside, side, over])
    copies = []

    def start(index, src, dst, device):
        copy = remote(src, dst, r.send.at[index], r.recv.at[index], device)
        copy.start()
        copies.append(copy)
        return copy

    sums = {}
    for h in range(2):
        sums["d%d" % h] = Sum(r, "down%d" % h, h, r.own_down.at[h], r.total_down.at[h])
        sums["u%d" % h] = Sum(r, "up%d" % h, 2 + h, r.own_up.at[h], r.total_up.at[h])
    sums["o"] = Sum(r, "out", 4, r.own_out, r.total_out)
    for c in range(3):
        sums["q%d" % c] = Sum(r, "qkv%d" % c, 5 + c, r.own_qkv.at[c], r.total_qkv.at[c])
    sums["k"] = Sum(r, "kernels", 8, r.own_kernels, r.total_kernels, r.grad_kernels_hbm)
    sums["t"] = Sum(r, "tconv", 9, r.own_tconv, r.total_tconv, r.grad_tconv_hbm)

    def rows_of(item):
        return slice(item * slab, (item + 1) * slab)

    def lanes_of(step, size=256):
        return pl.ds(pl.multiple_of(step * size, size), size)

    r.small[...] = jnp.zeros_like(r.small)

    def dout_rows(item, at):
        return r.grad_out[item, at, :].astype(jnp.float32) + r.dtap[item, at, :].astype(
            jnp.float32
        )

    zero = jnp.zeros((8, width), jnp.float32)

    sent = {}
    waited = set()

    def loaded(*names):
        for name in names:
            if name not in waited:
                loads[name].wait()
                waited.add(name)

    def feed_back(item):
        rows = rows_of(item)

        def shade(step, total):
            value = dout_rows(item, rows_at(step * tile, tile)).astype(low)
            r.ddown[rows_at(item * slab + step * tile, tile), :] = value
            return total + fold(value.astype(jnp.float32))

        total = lax.fori_loop(0, slab // tile, shade, zero)
        r.small[5:6, :] += rows_sum(total)
        loaded("down", "slope")

        @pl.loop(0, units // 256)
        def _(step):
            lanes = lanes_of(step)
            dactive = nt_dot(r.ddown[rows, :], r.down[lanes, :])
            value = (dactive * r.slope[rows, lanes].astype(jnp.float32)).astype(low)
            r.dhidden[rows, lanes] = value
            summed = rows_sum(fold(value.astype(jnp.float32)))
            if item == 0:
                r.bias_sum[0:1, lanes] = summed
            else:
                r.bias_sum[0:1, lanes] += summed

        loaded("up")

        @pl.loop(0, width // 256)
        def _(step):
            value = nt_dot(r.dhidden[rows, :], r.up[lanes_of(step), :])
            r.two_mine[item, :, lanes_of(step)] = value.astype(low)

        sent["dn%d" % item] = start(item, r.two_mine.at[item], r.two_from.at[item], cross)

    def grad_down(h):
        loaded("active")

        @pl.loop(0, units // 2 // 256)
        def _(step):
            lanes = pl.ds(pl.multiple_of(h * (units // 2) + step * 256, 256), 256)
            r.own_down[h, lanes_of(step), :] = tn_dot(r.active[:, lanes], r.ddown[...]).astype(low)

    def grad_up(h):
        loaded("normed_two")

        @pl.loop(0, width // 256)
        def _(step):
            right = r.dhidden[:, h * (units // 2) : (h + 1) * (units // 2)]
            r.own_up[h, lanes_of(step), :] = tn_dot(r.normed_two[:, lanes_of(step)], right).astype(
                low
            )

    def middle_back(item):
        loaded("middle")
        sent["dn%d" % item].wait_recv()

        def back(step, totals):
            at = rows_at(step * tile, tile)
            grad = r.two_mine[item, at, :].astype(jnp.float32) + r.two_from[item, at, :].astype(
                jnp.float32
            )
            dvalue, normed = norm_back(r.middle[item, at, :], grad, r.gains[1:2, :])
            dmiddle = dout_rows(item, at) + dvalue
            r.dmiddle[item, at, :] = dmiddle
            dattn = dmiddle.astype(low)
            r.dattn[rows_at(item * slab + step * tile, tile), :] = dattn
            return (
                totals[0] + fold(grad * normed),
                totals[1] + fold(grad),
                totals[2] + fold(dattn.astype(jnp.float32)),
            )

        totals = lax.fori_loop(0, slab // tile, back, (zero, zero, zero))
        for row, total in zip((2, 3, 4), totals):
            r.small[row : row + 1, :] += rows_sum(total)

    def attention_back(item):
        loaded("out_weight", "key_value", "query", "probs")
        rows = rows_of(item)
        r.keys_turned[...] = r.key_value[item, 0].astype(jnp.float32).T.astype(low)
        r.dmixed[...] = nt_dot(r.dattn[rows, :], r.out_weight[...]).astype(low)
        scale = HD ** (-0.5)
        for pair in range(pairs):
            lanes = slice(pair * 128, (pair + 1) * 128)
            values = r.key_value[item, 1, :, lanes]
            asked = r.query[rows, lanes]
            dmixed = r.dmixed[:, lanes]
            dkeys = dvalues = None
            turned = []
            for head in range(2):
                prob = r.probs[item, 2 * pair + head]
                dmixed_head = head_only(dmixed, head)
                dprob = nt_dot(values, dmixed_head)
                wide = prob.astype(jnp.float32)
                inner = rows_sum(wide * dprob)
                dscores = (wide * (dprob - inner)).astype(low)
                key_part = dot(dscores, head_only(asked, head))
                value_part = dot(prob, dmixed_head)
                dkeys = key_part if dkeys is None else dkeys + key_part
                dvalues = value_part if dvalues is None else dvalues + value_part
                at = pair * 128 + head * HD
                turned.append(dot(r.keys_turned[at : at + HD, :], dscores))
            r.dproject[0, rows, lanes] = (jnp.concatenate(turned, axis=0).T * scale).astype(low)
            dkeys = (dkeys * scale).astype(low)
            dvalues = dvalues.astype(low)
            r.dproject[1, rows, lanes] = dkeys[:slab]
            r.dproject[2, rows, lanes] = dvalues[:slab]
            r.give_kv[item, 0, :, lanes] = dkeys[slab:]
            r.give_kv[item, 1, :, lanes] = dvalues[slab:]
        sent["kv%d" % item] = start(2 + item, r.give_kv.at[item], r.got_kv.at[item], core)

    def grad_out_weight():
        loaded("mixed")
        for h in range(2):
            value = tn_dot(r.mixed[...], r.dattn[:, h * half_width : (h + 1) * half_width])
            r.own_out[h * local : (h + 1) * local, :] = value.astype(low)

    def join_heads():
        for item in range(items):
            sent["kv%d" % item].wait_recv()
            rows = rows_of(item)
            for c in range(2):
                value = r.dproject[1 + c, rows, :].astype(jnp.float32)
                value = value + r.got_kv[item, c].astype(jnp.float32)
                r.dproject[1 + c, rows, :] = value.astype(low)

    def project_back(item):
        loaded("qkv")
        rows = rows_of(item)

        @pl.loop(0, width // 256)
        def _(step):
            lanes = lanes_of(step)
            value = None
            for c in range(3):
                part = nt_dot(r.dproject[c, rows, :], r.qkv[c, lanes, :])
                value = part if value is None else value + part
            r.one_mine[item, :, lanes] = value.astype(low)

        sent["pn%d" % item] = start(4 + item, r.one_mine.at[item], r.one_from.at[item], cross)

    def grad_qkv(c):
        loaded("normed_one")
        r.own_qkv[c] = tn_dot(r.normed_one[...], r.dproject[c]).astype(low)

    def bias_sums():
        for c in (0, 2):
            value = rows_sum(fold(r.dproject[c].astype(jnp.float32)))
            r.small[6:7, (c // 2) * local : (c // 2 + 1) * local] = value
        r.small[7:8, :] = r.bias_sum[0:1, :width]
        r.small[8:9, :] = r.bias_sum[0:1, width:]

    def input_back(item):
        sent["pn%d" % item].wait_recv()

        def back(step, totals):
            at = rows_at(step * tile, tile)
            grad = r.one_mine[item, at, :].astype(jnp.float32) + r.one_from[item, at, :].astype(
                jnp.float32
            )
            value = r.block_in[item, at, :].astype(jnp.float32)
            dvalue, normed = norm_back(value, grad, r.gains[0:1, :])
            r.grad_input[item, at, :] = (r.dmiddle[item, at, :] + dvalue).astype(low)
            return totals[0] + fold(grad * normed), totals[1] + fold(grad)

        totals = lax.fori_loop(0, slab // tile, back, (zero, zero))
        for row, total in zip((0, 1), totals):
            r.small[row : row + 1, :] += rows_sum(total)

    def small_step(index):
        if index > 0:
            sent["small"].wait_recv()
            r.small_sum[index] = r.small_sum[index - 1] + r.small_from[index - 1]
        else:
            r.small_sum[0] = r.small[...]
        if index < 4:
            device = (core, beside, side, over)[index]
            sent["small"] = start(
                6 + index, r.small_sum.at[index], r.small_from.at[index], device
            )
        else:
            r.small_total[...] = r.small_sum[4]

    tasks = {"kv": join_heads, "og": grad_out_weight, "bias": bias_sums}
    for index in range(2):
        for name, work in (
            ("ffn", feed_back),
            ("gd", grad_down),
            ("gu", grad_up),
            ("ln", middle_back),
            ("at", attention_back),
            ("p", project_back),
            ("f", input_back),
        ):
            tasks[name + str(index)] = functools.partial(work, index)
    for c in range(3):
        tasks["gq" + str(c)] = functools.partial(grad_qkv, c)
    for index in range(5):
        tasks["sm" + str(index)] = functools.partial(small_step, index)

    def full_step(name, unit):
        keep_full[{"k": "kernels", "t": "tconv"}[name]].wait()
        unit.sB()

    for name, unit in sums.items():
        for step in ("sA", "sB", "s0", "s1", "s2", "s2b", "s3", "s3b", "s4", "s5", "s6"):
            tasks[name + "." + step] = getattr(unit, step)
        if unit.full is not None:
            tasks[name + ".sB"] = functools.partial(full_step, name, unit)
    for name in ORDER:
        tasks[name]()
    for copy in copies:
        copy.wait_send()


ORDER = (
    "k.sA", "t.sA", "ffn0", "ffn1", "gd1", "d1.s0", "gu1", "u1.s0", "d1.s1", "t.sB", "gd0", "u1.s1",
    "d0.s0", "gu0", "u0.s0", "d0.s1", "ln0", "u0.s1", "at0", "d1.s2", "k.sB", "t.s1", "ln1", "at1",
    "d0.s2", "d1.s2b", "og", "o.s0", "u1.s2", "kv", "p0", "p1", "gq2", "q2.s0", "o.s1", "gq1",
    "q1.s0", "q2.s1", "gq0", "q0.s0", "q1.s1", "d0.s2b", "d1.s3", "u0.s2", "q0.s1", "bias", "u1.s2b", "t.s2",
    "d0.s3", "d1.s3b", "u0.s2b", "u1.s3", "f0", "o.s2", "k.s1", "t.s2b", "d0.s3b", "q2.s2", "d1.s4", "u0.s3",
    "u1.s3b", "q1.s2", "f1", "t.s3", "o.s2b", "q0.s2", "d0.s4", "q2.s2b", "u0.s3b", "sm0", "o.s3", "t.s3b",
    "k.s2", "q1.s2b", "u1.s4", "d1.s5", "q2.s3", "o.s3b", "sm1", "q0.s2b", "q1.s3", "q2.s3b", "k.s2b", "sm2",
    "u0.s4", "q0.s3", "q1.s3b", "d0.s5", "t.s4", "k.s3", "sm3", "q0.s3b", "u1.s5", "o.s4", "d1.s6", "k.s3b",
    "u0.s5", "sm4", "q2.s4", "d0.s6", "t.s5", "q1.s4", "u1.s6", "q0.s4", "o.s5", "u0.s6", "k.s4", "q2.s5",
    "t.s6", "q1.s5", "o.s6", "q0.s5", "q2.s6", "k.s5", "q1.s6", "q0.s6", "k.s6",
)

LOADED = (
    "down",
    "slope",
    "up",
    "active",
    "normed_two",
    "middle",
    "out_weight",
    "key_value",
    "query",
    "probs",
    "mixed",
    "qkv",
    "normed_one",
)


def backward_section(arrays):
    low = jnp.bfloat16
    wide = jnp.float32
    items, slab, width = arrays["grad_out"].shape
    tokens = items * slab
    local = arrays["qkv"].shape[2]
    units = arrays["down"].shape[0]
    patches = arrays["key_value"].shape[2]
    kernel_rows = arrays["grad_kernels"].shape[1]
    near = ["grad_out", "dtap", "block_in", "gains"]
    distant = list(LOADED) + ["grad_kernels", "grad_tconv"]
    totals = {
        "down": (2, units // 2, width),
        "up": (2, width, units // 2),
        "out": (2 * local, width // 2),
        "qkv": (3, width, local),
        "kernels": (kernel_rows, CH),
        "tconv": arrays["grad_tconv"].shape[1:],
    }
    scratch = {name: pltpu.VMEM(arrays[name].shape, arrays[name].dtype) for name in LOADED}
    for name, shape in totals.items():
        full = name in ("kernels", "tconv")
        rows, columns = shape[-2:]
        scratch["own_" + name] = pltpu.VMEM((2, rows // 2, columns) if full else shape, low)
        labels = [name] if len(shape) == 2 else [name + str(part) for part in range(shape[0])]
        for label in labels:
            for end, one in sum_scratch(rows, columns).items():
                scratch[label + end] = one
            if full:
                scratch[label + "_both"] = pltpu.VMEM((2, rows // 2, columns), low)
                scratch[label + "_cross"] = pltpu.VMEM((rows // 2, columns), low)
    block = (items, slab, width)
    for name, shape, dtype in (
        ("ddown", (tokens, width), low),
        ("dhidden", (tokens, units), low),
        ("bias_sum", (8, units), wide),
        ("two_mine", block, low),
        ("two_from", block, low),
        ("dmiddle", block, wide),
        ("dattn", (tokens, width), low),
        ("dmixed", (slab, local), low),
        ("keys_turned", (local, patches), low),
        ("give_kv", (items, 2, slab, local), low),
        ("got_kv", (items, 2, slab, local), low),
        ("dproject", (3, tokens, local), low),
        ("one_mine", block, low),
        ("one_from", block, low),
        ("small", (16, width), wide),
        ("small_sum", (5, 16, width), wide),
        ("small_from", (4, 16, width), wide),
    ):
        scratch[name] = pltpu.VMEM(shape, dtype)
    dma = pltpu.SemaphoreType.DMA
    scratch["load_sem"] = dma((len(LOADED) + 2,))
    scratch["send"] = dma((10,))
    scratch["recv"] = dma((10,))
    scratch["sum_send"] = dma((10, COPIES))
    scratch["sum_recv"] = dma((10, COPIES))
    scratch["sum_local"] = dma((10,))
    outputs = ["grad_input", "small_total"] + ["total_" + name for name in totals]
    layout = near + [name + "_hbm" for name in distant] + outputs + list(scratch)
    vmem = pl.BlockSpec(memory_space=pltpu.VMEM)
    hbm = pl.BlockSpec(memory_space=pl.ANY)
    results = pl.pallas_call(
        functools.partial(backward_kernel, tuple(layout)),
        out_shape=[
            jax.ShapeDtypeStruct(block, low),
            jax.ShapeDtypeStruct((16, width), wide),
        ]
        + [jax.ShapeDtypeStruct(shape, low) for shape in totals.values()],
        in_specs=[vmem] * len(near) + [hbm] * len(distant),
        out_specs=[vmem] * 2 + [hbm] * len(totals),
        scratch_shapes=list(scratch.values()),
        name="backward_section",
        compiler_params=pltpu.CompilerParams(
            collective_id=3, has_side_effects=True, vmem_limit_bytes=62 * 2**20
        ),
    )(*[arrays[name] for name in near + distant])
    return dict(zip(outputs, results))


def body(
    block_in,
    crop_shape,
    norm_gains,
    shifts,
    qkv_weight,
    qv_bias,
    out_weight,
    up_weight,
    up_bias,
    down_weight,
    tconv_weight,
    kernels,
    grad_out,
    grad_decoded,
):
    (
        normed_one,
        query,
        key_value,
        probs,
        mixed,
        middle,
        normed_two,
        active,
        slope,
        tapped,
    ) = forward_section(
        block_in,
        norm_gains,
        shifts,
        qkv_weight,
        qv_bias,
        out_weight,
        up_weight,
        up_bias,
        down_weight,
        crop_shape,
    )
    decoded, block_all, dtap, grad_tconv, grad_kernels = decoder_section(
        tapped,
        tconv_weight,
        kernels,
        grad_decoded.reshape(DEPTH, SIDE, 2, WIDE, CH),
        crop_shape,
    )
    result = backward_section(
        {
            "grad_out": grad_out,
            "dtap": dtap,
            "block_in": block_in,
            "gains": norm_gains,
            "down": down_weight,
            "slope": slope,
            "up": up_weight,
            "active": active,
            "normed_two": normed_two,
            "middle": middle,
            "out_weight": out_weight,
            "key_value": key_value,
            "query": query,
            "probs": probs,
            "mixed": mixed,
            "qkv": qkv_weight,
            "normed_one": normed_one,
            "grad_kernels": grad_kernels,
            "grad_tconv": grad_tconv,
        }
    )
    small = result["small_total"]
    totals = {name[6:]: array for name, array in result.items() if name.startswith("total_")}
    groups = lax.axis_size("dp") // GROUP
    if groups > 1:
        same = [[part * GROUP + i for part in range(groups)] for i in range(GROUP)]
        small = lax.psum(small, "dp", axis_index_groups=same)
        totals = {
            name: lax.psum(array, "dp", axis_index_groups=same) for name, array in totals.items()
        }
    sums, passed, smalls = finish_section(
        totals, (block_all, decoded, result["grad_input"]), small
    )
    return (
        passed[0],
        passed[1].reshape(grad_decoded.shape),
        passed[2],
        smalls[0],
        smalls[1],
        sums["qkv"],
        smalls[2],
        sums["out"],
        sums["up"],
        smalls[3],
        sums["down"].reshape(down_weight.shape),
        sums["tconv"],
        sums["kernels"].transpose(0, 2, 1),
    )


def solution(mesh):
    return jax.shard_map(
        body,
        mesh=mesh,
        in_specs=(
            P("dp", "blk", None),
            P("dp"),
            P(),
            P(),
            P(None, None, "tensor"),
            P(None, "tensor"),
            P("tensor", None),
            P(None, "tensor"),
            P("tensor"),
            P("tensor", None),
            P(),
            P(),
            P("dp", "blk", None),
            P(("dp", "tensor"), "blk", None, None, None),
        ),
        out_specs=(
            P("dp", "blk", None),
            P(("dp", "tensor"), "blk", None, None, None),
            P("dp", "blk", None),
            P(),
            P(),
            P(None, None, "tensor"),
            P(None, "tensor"),
            P("tensor", None),
            P(None, "tensor"),
            P("tensor"),
            P("tensor", None),
            P(None, "tensor"),
            P(None, None, "tensor"),
        ),
        check_vma=False,
    )
```

```python
import functools
import types

import jax
import jax.numpy as jnp
from jax import lax
from jax.experimental import pallas as pl
from jax.experimental.pallas import tpu as pltpu
from jax.sharding import PartitionSpec as P

HD = 64

MESH = pl.DeviceIdType.MESH
GROUP = 8
FAR = 4


def place():
    dp = lax.axis_index("dp")
    blk = lax.axis_index("blk")
    tensor = lax.axis_index("tensor")
    near = lax.rem(dp, 2)
    far = lax.rem(dp // 2, FAR)
    first = dp // GROUP * GROUP
    return (dp, blk, tensor, near, far, first)


def peers():
    dp, blk, tensor, near, far, first = place()
    core = (dp, 1 - blk, tensor)
    cross = (dp, blk, 1 - tensor)
    beside = (first + 2 * far + 1 - near, blk, tensor)
    side = (first + 2 * (far + 1 - 2 * lax.rem(far, 2)) + near, blk, tensor)
    over = (first + 2 * lax.rem(far + 2, FAR) + near, blk, tensor)
    return (core, cross, beside, side, over)


def greet(devices):
    barrier = pltpu.get_barrier_semaphore()
    for device in devices:
        pl.semaphore_signal(barrier, inc=1, device_id=device, device_id_type=MESH)
    pl.semaphore_wait(barrier, len(devices))


def remote(src, dst, send, recv, device):
    return pltpu.make_async_remote_copy(
        src_ref=src, dst_ref=dst, send_sem=send, recv_sem=recv, device_id=device,
        device_id_type=MESH,
    )


def rows_at(start, size):
    return pl.ds(pl.multiple_of(start, 16), size)


DEPTH = 8
SIDE = 8
WIDE = 16
CH = 128
PAIR = 2 * CH
ROWS = DEPTH * SIDE * WIDE
TAPS = [(deep, wide) for deep in range(3) for wide in range(3)]
PADDED_TAPS = 28


def nt_dot(left, right):
    return lax.dot_general(
        left, right, (((1,), (1,)), ((), ())), preferred_element_type=jnp.float32
    )


def tn_dot(left, right):
    return lax.dot_general(
        left, right, (((0,), (0,)), ((), ())), preferred_element_type=jnp.float32
    )


def dot(left, right):
    return jnp.dot(left, right, preferred_element_type=jnp.float32)


def half_sums(row):
    return row[:, :CH] + row[:, CH:]


def twice(row):
    return jnp.concatenate([row, row], axis=1)


def row_and_column(size):
    return (
        lax.broadcasted_iota(jnp.int32, (size, size), 0),
        lax.broadcasted_iota(jnp.int32, (size, size), 1),
    )


def shift_matrix(step):
    row, column = row_and_column(PAIR)
    same = (row // WIDE) == (column // WIDE)
    return jnp.where(same & (row + step == column), 1.0, 0.0).astype(jnp.bfloat16)


def weave_matrix():
    row, column = row_and_column(PAIR)
    source = lax.rem(row, 2) * CH + row // WIDE * SIDE + lax.rem(row, WIDE) // 2
    return jnp.where(source == column, 1.0, 0.0).astype(jnp.bfloat16)


def unweave_matrix():
    row, column = row_and_column(PAIR)
    source = lax.rem(column, 2) * CH + column // WIDE * SIDE + lax.rem(column, WIDE) // 2
    return jnp.where(source == row, 1.0, 0.0).astype(jnp.bfloat16)


def lay_kernel(kernels_ref, index, weights):
    zero = jnp.zeros((CH, CH), jnp.bfloat16)
    for at, (deep, wide) in enumerate(TAPS):
        weights[at, 3 * CH :, :CH] = zero
        weights[at, :CH, CH:] = zero
        for high in range(3):
            offset = ((deep * 3 + high) * 3 + wide) * CH
            block = kernels_ref[index, offset : offset + CH, :]
            weights[at, high * CH : (high + 1) * CH, :CH] = block
            weights[at, (high + 1) * CH : (high + 2) * CH, CH:] = block


def lay_flipped(kernels_ref, index, weights):
    zero = jnp.zeros((CH, CH), jnp.bfloat16)
    for at, (deep, wide) in enumerate(TAPS):
        weights[at, :CH, 3 * CH :] = zero
        weights[at, CH:, :CH] = zero
        for high in range(3):
            offset = (((2 - deep) * 3 + 2 - high) * 3 + 2 - wide) * CH
            block = kernels_ref[index, offset : offset + CH, :]
            weights[at, :CH, high * CH : (high + 1) * CH] = block
            weights[at, CH:, (high + 1) * CH : (high + 2) * CH] = block


def four_heights(field, wide, start, count):
    depths = pl.ds(start, count)
    low = field[wide, depths, 0:SIDE, :, CH:]
    middle = field[wide, depths, 1 : SIDE + 1, :, :]
    high = field[wide, depths, 2 : SIDE + 2, :, :CH]
    joined = jnp.concatenate([low, middle, high], axis=-1)
    return joined.reshape(count * SIDE * WIDE, 4 * CH)


def conv_tile(field, weights, multiply, level, start):
    total = None
    for at, (deep, wide) in enumerate(TAPS):
        product = multiply(four_heights(field, wide, start + deep, 2), weights[at])
        total = product if total is None else total + product
    level[pl.ds(pl.multiple_of(start * CH, 2 * CH), 2 * CH), :] = total


def conv(field, weights, multiply, level, arrive):
    @pl.loop(0, 2)
    def _(step):
        conv_tile(field, weights, multiply, level, 2 + 2 * step)

    arrive()

    @pl.loop(0, 2)
    def _(step):
        conv_tile(field, weights, multiply, level, 6 * step)


def clear_rims(field, blk):
    for wide in range(3):
        field[wide, :, 0] = jnp.zeros((DEPTH + 2, WIDE, PAIR), jnp.bfloat16)
        field[wide, :, SIDE + 1] = jnp.zeros((DEPTH + 2, WIDE, PAIR), jnp.bfloat16)
        field[wide, 9 * blk] = jnp.zeros((SIDE + 2, WIDE, PAIR), jnp.bfloat16)


def place_rows(field, before, after, step, value):
    shape = (2, SIDE, WIDE, PAIR)
    depths = pl.ds(1 + 2 * step, 2)
    field[1, depths, 1 : SIDE + 1] = value.reshape(shape)
    field[0, depths, 1 : SIDE + 1] = dot(before, value).astype(jnp.bfloat16).reshape(shape)
    field[2, depths, 1 : SIDE + 1] = dot(after, value).astype(jnp.bfloat16).reshape(shape)


def kernel_grad(field, dlevel_turned, index, out, tensor_half):
    for at, (deep, wide) in enumerate(TAPS):
        joined = four_heights(field, wide, deep, DEPTH)
        block = dot(dlevel_turned[...], joined)
        for high in range(3):
            part = (
                block[:CH, high * CH : (high + 1) * CH]
                + block[CH:, (high + 1) * CH : (high + 2) * CH]
            )
            offset = ((deep * 3 + high) * 3 + wide) * CH
            part = part.astype(jnp.bfloat16)
            at = index * PADDED_TAPS * 64 + offset // 2
            for half in range(2):
                out[half, at : at + 64, :] = part[half * 64 : (half + 1) * 64, :]


def decoder_kernel(
    tapped,
    tconv,
    kernels,
    grad_decoded,
    crop_shape,
    decoded,
    block_all,
    dtap_all,
    grad_tconv,
    grad_kernels,
    mask,
    inverse,
    field_one,
    field_two,
    dlevel_two,
    dlevel_one,
    weights_one,
    weights_two,
    flipped_two,
    flipped_one,
    level_one,
    level_two,
    dfield,
    turned_two,
    turned_one,
    dlifted,
    tapped_from,
    dtap_mine,
    dtap_from,
    sums_mine,
    sums_from,
    send,
    recv,
):
    dp, blk, tensor, near, far, first = place()
    core, cross, beside, side, over = peers()
    greet([core, cross])
    low = jnp.bfloat16
    row_tiles = ROWS // PAIR

    copies = []

    def start(index, src, dst, device):
        copy = remote(src, dst, send.at[index], recv.at[index], device)
        copy.start()
        copies.append(copy)
        return copy

    give_tapped = start(0, tapped, tapped_from, cross)

    depth_end, side_end = extents(crop_shape[tensor])
    row = lax.broadcasted_iota(jnp.int32, mask.shape, 0)
    inside = (
        (blk * (DEPTH // 2) + row // (2 * CH) < depth_end)
        & (lax.rem(row // WIDE, SIDE) < side_end)
        & (lax.rem(row, WIDE) // 2 < side_end)
    )
    mask[...] = jnp.where(inside, 1.0, 0.0)
    voxels = (8 * depth_end * side_end * side_end).astype(jnp.float32)
    inverse[...] = 1.0 / jnp.full(inverse.shape, voxels)

    before, after = shift_matrix(-1), shift_matrix(1)

    def send_edge(index, field):
        return start(
            index,
            field.at[:, DEPTH - 7 * blk, 1 : SIDE + 1],
            field.at[:, 9 * blk, 1 : SIDE + 1],
            core,
        )

    def rows_of(step):
        return pl.ds(pl.multiple_of(step * PAIR, PAIR), PAIR)

    def mask_rows(step):
        return twice(mask[rows_of(step), :])

    def totals(slot, pair):
        sums_mine[slot, 0:1, :] = half_sums(pair[0])
        sums_mine[slot, 1:2, :] = half_sums(pair[1])
        return start(5 + slot, sums_mine.at[slot], sums_from.at[slot], core)

    def means(slot, copy):
        copy.wait_recv()
        both = (sums_mine[slot] + sums_from[slot]) * inverse[...]
        return both[0:1, :], both[1:2, :]

    zero_pair = (jnp.zeros((1, PAIR), jnp.float32), jnp.zeros((1, PAIR), jnp.float32))

    for field in (field_one, field_two, dlevel_two, dlevel_one):
        clear_rims(field, blk)
    weave = weave_matrix()
    for piece in range(2):
        tokens = slice(piece * CH, (piece + 1) * CH)
        for a in range(2):
            lifted = dot(tapped[tokens, :], tconv[:, a * 512 : (a + 1) * 512])
            side = [
                jnp.concatenate([lifted[:, c * CH : (c + 1) * CH],
                                 lifted[:, (2 + c) * CH : (3 + c) * CH]], axis=1)
                for c in range(2)
            ]
            woven = dot(weave, jnp.concatenate(side, axis=0).astype(low))
            for depth in range(2):
                at = 2 * (2 * piece + depth) + a
                rows = slice(depth * CH, (depth + 1) * CH)
                value = woven[rows, :] * twice(mask[at * CH : (at + 1) * CH, :])
                level_one[at * CH : (at + 1) * CH, :] = value

    @pl.loop(0, row_tiles)
    def _(step):
        place_rows(field_one, before, after, step, level_one[rows_of(step), :].astype(low))

    edge = send_edge(1, field_one)
    lay_kernel(kernels, 0, weights_one)
    conv(field_one, weights_one, dot, level_one, edge.wait_recv)

    def forward_sums(level):
        def add(step, pair):
            value = level[rows_of(step), :]
            kept = value * mask_rows(step)
            return (
                pair[0] + jnp.sum(kept, axis=0, keepdims=True),
                pair[1] + jnp.sum(kept * value, axis=0, keepdims=True),
            )

        return lax.fori_loop(0, row_tiles, add, zero_pair)

    def mean_and_scale(slot, copy):
        mean, second = means(slot, copy)
        return twice(mean), twice(lax.rsqrt(second - mean * mean + 1e-05))

    def sigmoid(value):
        return 0.5 * jnp.tanh(0.5 * value) + 0.5

    copy = totals(0, forward_sums(level_one))
    lay_kernel(kernels, 1, weights_two)
    mean_one, scale_one = mean_and_scale(0, copy)

    @pl.loop(0, row_tiles)
    def _(step):
        normed = (level_one[rows_of(step), :] - mean_one) * scale_one
        level_one[rows_of(step), :] = normed
        value = normed * sigmoid(normed) * mask_rows(step)
        place_rows(field_two, before, after, step, value.astype(low))

    edge = send_edge(2, field_two)
    lay_flipped(kernels, 1, flipped_two)
    conv(field_two, weights_two, dot, level_two, edge.wait_recv)
    copy = totals(1, forward_sums(level_two))
    lay_flipped(kernels, 0, flipped_one)
    mean_two, scale_two = mean_and_scale(1, copy)

    def two_depths(ref, step, b):
        return ref[pl.ds(2 * step, 2), :, b].reshape(PAIR, CH)

    def decode(step, pair):
        normed = (level_two[rows_of(step), :] - mean_two) * scale_two
        level_two[rows_of(step), :] = normed
        kept = mask_rows(step)
        gate = sigmoid(normed)
        value = (normed * gate * kept).astype(low)
        for b in range(2):
            decoded[pl.ds(2 * step, 2), :, b] = value[:, b * CH : (b + 1) * CH].reshape(
                2, SIDE, WIDE, CH
            )
        grad = jnp.concatenate(
            [two_depths(grad_decoded, step, 0), two_depths(grad_decoded, step, 1)], axis=1
        ).astype(jnp.float32)
        dnormed = gate * (1.0 + normed * (1.0 - gate)) * kept * grad
        dfield[rows_of(step), :] = dnormed
        return (
            pair[0] + jnp.sum(dnormed, axis=0, keepdims=True),
            pair[1] + jnp.sum(dnormed * normed, axis=0, keepdims=True),
        )

    copy = totals(2, lax.fori_loop(0, row_tiles, decode, zero_pair))

    def level_grad(slot, copy, level, scale, field, turned):
        mean_grad, mean_cross = means(slot, copy)
        mean_grad, mean_cross = twice(mean_grad), twice(mean_cross)

        @pl.loop(0, row_tiles)
        def _(step):
            centred = mean_grad + level[rows_of(step), :] * mean_cross
            value = scale * (dfield[rows_of(step), :] - mask_rows(step) * centred)
            place_rows(field, before, after, step, value.astype(low))
            turned[:, rows_of(step)] = value.T.astype(low)

    level_grad(2, copy, level_two, scale_two, dlevel_two, turned_two)
    edge = send_edge(3, dlevel_two)
    conv(dlevel_two, flipped_two, nt_dot, dfield, edge.wait_recv)

    def back_one(step, pair):
        normed = level_one[rows_of(step), :]
        gate = sigmoid(normed)
        dnormed = gate * (1.0 + normed * (1.0 - gate)) * mask_rows(step) * dfield[rows_of(step), :]
        dfield[rows_of(step), :] = dnormed
        return (
            pair[0] + jnp.sum(dnormed, axis=0, keepdims=True),
            pair[1] + jnp.sum(dnormed * normed, axis=0, keepdims=True),
        )

    copy = totals(3, lax.fori_loop(0, row_tiles, back_one, zero_pair))
    level_grad(3, copy, level_one, scale_one, dlevel_one, turned_one)
    edge = send_edge(4, dlevel_one)
    conv(dlevel_one, flipped_one, nt_dot, dfield, edge.wait_recv)

    unweave = unweave_matrix()
    for piece in range(2):
        tokens = slice(piece * CH, (piece + 1) * CH)
        for a in range(2):
            parts = []
            for depth in range(2):
                at = 2 * (2 * piece + depth) + a
                rows = slice(at * CH, (at + 1) * CH)
                parts.append(dfield[rows, :] * twice(mask[rows, :]))
            apart = dot(unweave, jnp.concatenate(parts, axis=0).astype(low)).astype(low)
            for c in range(2):
                for b in range(2):
                    column = ((a * 2 + b) * 2 + c) * CH
                    dlifted[tokens, column : column + CH] = apart[
                        c * CH : (c + 1) * CH, b * CH : (b + 1) * CH
                    ]
    dtap_mine[...] = nt_dot(dlifted[...], tconv[...]).astype(low)
    give_dtap = start(9, dtap_mine, dtap_from, cross)
    for half in range(2):
        lanes = slice(half * 512, (half + 1) * 512)
        grad_tconv[half] = tn_dot(tapped[...], dlifted[:, lanes]).astype(low)
        for index in range(2):
            at = ((index + 1) * PADDED_TAPS - 1) * 64
            grad_kernels[half, at : at + 64, :] = jnp.zeros((64, CH), low)
    kernel_grad(field_two, turned_two, 1, grad_kernels, tensor)
    kernel_grad(field_one, turned_one, 0, grad_kernels, tensor)
    give_tapped.wait_recv()
    block_all[tensor] = tapped[...]
    block_all[1 - tensor] = tapped_from[...]
    give_dtap.wait_recv()
    dtap_all[tensor] = dtap_mine[...]
    dtap_all[1 - tensor] = dtap_from[...]
    for copy in copies:
        copy.wait_send()


def decoder_section(tapped, tconv_weight, kernels, grad_decoded, crop_shape):
    low = jnp.bfloat16
    vmem = pl.BlockSpec(memory_space=pltpu.VMEM)
    field = pltpu.VMEM((3, DEPTH + 2, SIDE + 2, WIDE, PAIR), low)
    plane = pltpu.VMEM((ROWS, PAIR), jnp.float32)
    return pl.pallas_call(
        decoder_kernel,
        out_shape=[
            jax.ShapeDtypeStruct((DEPTH, SIDE, 2, WIDE, CH), low),
            jax.ShapeDtypeStruct((2,) + tapped.shape, low),
            jax.ShapeDtypeStruct((2,) + tapped.shape, low),
            jax.ShapeDtypeStruct((2, tapped.shape[1], tconv_weight.shape[1] // 2), low),
            jax.ShapeDtypeStruct((2, PADDED_TAPS * CH, CH), low),
        ],
        in_specs=[vmem] * 4 + [pl.BlockSpec(memory_space=pltpu.SMEM)],
        out_specs=[vmem] * 5,
        scratch_shapes=[pltpu.VMEM((ROWS, CH), jnp.float32), pltpu.VMEM((8, CH), jnp.float32)]
        + [field] * 4
        + [pltpu.VMEM((9, 4 * CH, PAIR), low)] * 2
        + [pltpu.VMEM((9, PAIR, 4 * CH), low)] * 2
        + [plane] * 3
        + [pltpu.VMEM((PAIR, ROWS), low)] * 2
        + [
            pltpu.VMEM((tapped.shape[0], tconv_weight.shape[1]), low),
            pltpu.VMEM(tapped.shape, low),
            pltpu.VMEM(tapped.shape, low),
            pltpu.VMEM(tapped.shape, low),
            pltpu.VMEM((4, 8, CH), jnp.float32),
            pltpu.VMEM((4, 8, CH), jnp.float32),
            pltpu.SemaphoreType.DMA((10,)),
            pltpu.SemaphoreType.DMA((10,)),
        ],
        name="decoder_section",
        compiler_params=pltpu.CompilerParams(
            collective_id=1, has_side_effects=True, vmem_limit_bytes=60 * 2**20
        ),
    )(tapped, tconv_weight, kernels, grad_decoded, crop_shape)


def widen_rows(src, dst, tile=64):
    @pl.loop(0, src.shape[0] // tile)
    def _(step):
        at = rows_at(step * tile, tile)
        dst[at, :] = src[at, :].astype(jnp.float32)


def finish_kernel(count, *refs):
    sources, refs = refs[:count], refs[count:]
    passed, small, refs = refs[:3], refs[3], refs[4:]
    targets, refs = refs[:count], refs[count:]
    handed, smalls, refs = refs[:3], refs[3:7], refs[7:]
    lows, wides, refs = refs[:count], refs[count : 2 * count], refs[2 * count :]
    held, refs = refs[:3], refs[3:]
    load_sem, store_sem, pass_sem = refs
    loads, stores = [], []
    for index in range(count):
        loads.append(pltpu.make_async_copy(sources[index], lows[index], load_sem.at[index]))
    passes = [
        pltpu.make_async_copy(passed[index], held[index], pass_sem.at[index])
        for index in range(3)
    ]
    for copy in passes + loads:
        copy.start()
    gains, shifts, qv_bias, up_bias = smalls
    width = small.shape[1]
    gains[0:1, :] = small[0:1, :]
    gains[1:2, :] = small[2:3, :]
    shifts[0:1, :] = small[1:2, :]
    shifts[1:4, :] = small[3:6, :]
    qv_bias[0:1, :] = small[6:7, : width // 2]
    qv_bias[1:2, :] = small[6:7, width // 2 :]
    up_bias[:width] = small[7, :]
    up_bias[width:] = small[8, :]

    def store(src, dst):
        copy = pltpu.make_async_copy(src, dst, store_sem.at[len(stores)])
        copy.start()
        stores.append(copy)

    for index in range(3):
        passes[index].wait()
        store(held[index], handed[index])
    for index in range(count):
        src, dst, wide, low = sources[index], targets[index], wides[index], lows[index]
        loads[index].wait()
        if dst.shape == src.shape and len(src.shape) == 2:
            widen_rows(low, wide)
            store(wide, dst)
        elif dst.shape == src.shape:
            for part in range(src.shape[0]):
                widen_rows(low.at[part], wide.at[part])
                store(wide.at[part], dst.at[part])
        elif len(src.shape) == 3:
            for part in range(src.shape[0]):
                widen_rows(low.at[part], wide.at[part])
                columns = src.shape[2]
                store(wide.at[part], dst.at[:, pl.ds(part * columns, columns)])
        elif len(dst.shape) == 2:
            widen_rows(low, wide)
            rows, columns = dst.shape[0], src.shape[1]
            for part in range(2):
                store(
                    wide.at[pl.ds(part * rows, rows)], dst.at[:, pl.ds(part * columns, columns)]
                )
        else:
            kinds, outs, columns = dst.shape
            ins = src.shape[1]
            for kind in range(kinds):
                for tap in range(columns // ins):
                    at = (kind * PADDED_TAPS + tap) * outs
                    wide[kind, :, tap * ins : (tap + 1) * ins] = low[at : at + outs, :].astype(
                        jnp.float32
                    )
                store(wide.at[kind], dst.at[kind])
    for copy in stores:
        copy.wait()


def finish_section(totals, passed, small):
    wide = jnp.float32
    local = totals["qkv"].shape[2]
    width = totals["qkv"].shape[1]
    units = totals["up"].shape[2] * 2
    shapes = {
        "qkv": totals["qkv"].shape,
        "out": (local, width),
        "up": (width, units),
        "down": totals["down"].shape,
        "tconv": totals["tconv"].shape,
        "kernels": (2, 64, 27 * CH),
    }
    count = len(shapes)
    sources = [totals[name] for name in shapes]
    kept = [
        shapes[name] if name == "kernels" else totals[name].shape for name in shapes
    ]
    vmem = pl.BlockSpec(memory_space=pltpu.VMEM)
    hbm = pl.BlockSpec(memory_space=pl.ANY)
    results = pl.pallas_call(
        functools.partial(finish_kernel, count),
        out_shape=[jax.ShapeDtypeStruct(shape, wide) for shape in shapes.values()]
        + [jax.ShapeDtypeStruct(array.shape, array.dtype) for array in passed]
        + [
            jax.ShapeDtypeStruct(shape, wide)
            for shape in ((2, width), (4, width), (2, local), (units,))
        ],
        in_specs=[hbm] * (count + 3) + [vmem],
        out_specs=[hbm] * (count + 3) + [vmem] * 4,
        scratch_shapes=[pltpu.VMEM(array.shape, array.dtype) for array in sources]
        + [pltpu.VMEM(shape, wide) for shape in kept]
        + [pltpu.VMEM(array.shape, array.dtype) for array in passed]
        + [
            pltpu.SemaphoreType.DMA((count,)),
            pltpu.SemaphoreType.DMA((16,)),
            pltpu.SemaphoreType.DMA((3,)),
        ],
        name="finish",
        compiler_params=pltpu.CompilerParams(vmem_limit_bytes=60 * 2**20),
    )(*sources, *passed, small)
    return dict(zip(shapes, results)), results[count : count + 3], results[count + 3 :]


def extents(crop):
    depth = jnp.where(crop == 0, SIDE * 3 // 4, jnp.where(crop == 1, SIDE // 2, SIDE))
    side = jnp.where(crop == 0, SIDE * 3 // 4, SIDE)
    return depth, side


GELU_RATE = 0.7978845608028654
GELU_CUBE = 0.044715


def rows_sum(value):
    return jnp.sum(value, axis=0, keepdims=True)


def lane_mean(value):
    return jnp.mean(value, axis=-1, keepdims=True)


def centred(value):
    centre = value - lane_mean(value)
    return centre, lax.rsqrt(lane_mean(centre * centre) + 1e-06)


def head_only(pair, head):
    lane = lax.broadcasted_iota(jnp.int32, pair.shape, 1)
    return jnp.where((lane // HD) == head, pair, jnp.zeros_like(pair))


def forward_kernel(
    block_in,
    gains,
    shifts,
    qkv_hbm,
    qv_bias,
    out_hbm,
    up_hbm,
    up_bias,
    down_hbm,
    crop_shape,
    normed_one_hbm,
    query_hbm,
    key_value_hbm,
    probs_hbm,
    mixed_hbm,
    middle_hbm,
    normed_two_hbm,
    active_hbm,
    slope_hbm,
    tapped,
    qkv,
    out_weight,
    up,
    down,
    normed_one,
    query,
    key_value,
    probs,
    mixed,
    middle,
    normed_two,
    active,
    slope,
    values_turned,
    part_mine,
    part_from,
    feed_mine,
    feed_from,
    load_sem,
    store_sem,
    send,
    recv,
):
    dp, blk, tensor, near, far, first = place()
    core, cross, beside, side, over = peers()
    low = jnp.bfloat16
    items, slab, width = block_in.shape
    local = query.shape[1]
    units = active.shape[1]

    loads = []
    for index, (src, dst) in enumerate(
        [(qkv_hbm, qkv), (out_hbm, out_weight), (up_hbm, up), (down_hbm, down)]
    ):
        copy = pltpu.make_async_copy(src, dst, load_sem.at[index])
        copy.start()
        loads.append(copy)
    greet([core, cross])
    copies = []
    stores = []

    def start(index, src, dst, device):
        copy = remote(src, dst, send.at[index], recv.at[index], device)
        copy.start()
        copies.append(copy)
        return copy

    def store(src, dst):
        copy = pltpu.make_async_copy(src, dst, store_sem.at[len(stores)])
        copy.start()
        stores.append(copy)

    tile = 64

    for item in range(items):

        @pl.loop(0, slab // tile)
        def _(step):
            value = block_in[item, rows_at(step * tile, tile), :].astype(jnp.float32)
            centre, scale = centred(value)
            normed = centre * scale * gains[0:1, :] + shifts[0:1, :]
            normed_one[rows_at(item * slab + step * tile, tile), :] = normed.astype(low)

    store(normed_one, normed_one_hbm)
    loads[0].wait()
    others = [lax.rem(tensor + step, items) for step in range(items)]
    kv_copies = []
    for place_at, item in enumerate(others):
        rows = rows_at(item * slab, slab)
        for c in range(2):
            project = dot(normed_one[rows, :], qkv[1 + c])
            if c == 1:
                project = project + qv_bias[1:2, :]
            key_value[item, c, :slab, :] = project.astype(low)
        kv_copies.append(
            start(
                place_at,
                key_value.at[item, :, pl.ds(0, slab), :],
                key_value.at[item, :, pl.ds(slab, slab), :],
                core,
            )
        )
    for item in others:
        rows = rows_at(item * slab, slab)
        query[rows, :] = (dot(normed_one[rows, :], qkv[0]) + qv_bias[0:1, :]).astype(low)
    store(query, query_hbm)

    part_copies = []
    for place_at, item in enumerate(others):
        rows = rows_at(item * slab, slab)
        kv_copies[place_at].wait_recv()
        values_turned[...] = key_value[item, 1].astype(jnp.float32).T.astype(low)
        depth_end, side_end = extents(crop_shape[item])
        key = lax.broadcasted_iota(jnp.int32, (probs.shape[2], slab), 0)
        patch = jnp.where(key < slab, blk * slab + key, (1 - blk) * slab + key - slab)
        keep = (
            (patch // (SIDE * SIDE) < depth_end)
            & (lax.rem(patch // SIDE, SIDE) < side_end)
            & (lax.rem(patch, SIDE) < side_end)
        )
        for pair in range(local // 128):
            lanes = slice(pair * 128, (pair + 1) * 128)
            keys = key_value[item, 0, :, lanes]
            asked = query[rows, lanes] * jnp.asarray(HD ** (-0.5), low)
            turned = []
            for head in range(2):
                scores = nt_dot(keys, head_only(asked, head))
                scores = jnp.where(keep, scores, -1000000000.0)
                weights = jnp.exp(scores - jnp.max(scores, axis=0, keepdims=True))
                prob = (weights * (1.0 / rows_sum(weights))).astype(low)
                probs[item, 2 * pair + head] = prob
                at = pair * 128 + head * HD
                turned.append(dot(values_turned[at : at + HD, :], prob))
            mixed[rows, lanes] = jnp.concatenate(turned, axis=0).T.astype(low)
        store(probs.at[item], probs_hbm.at[item])
        if place_at == 0:
            loads[1].wait()
        part_mine[item] = dot(mixed[rows, :], out_weight[...]).astype(low)
        part_copies.append(start(2 + place_at, part_mine.at[item], part_from.at[item], cross))
    store(key_value, key_value_hbm)
    store(mixed, mixed_hbm)

    for place_at, item in enumerate(others[1:] + others[:1]):
        if place_at == 0:
            loads[2].wait()
        part_copies[place_at].wait_recv()

        @pl.loop(0, slab // tile)
        def _(step):
            at = rows_at(step * tile, tile)
            attended = part_mine[item, at, :].astype(jnp.float32) + part_from[item, at, :].astype(
                jnp.float32
            )
            value = block_in[item, at, :].astype(jnp.float32) + (attended + shifts[2:3, :])
            middle[item, at, :] = value
            centre, scale = centred(value)
            normed = centre * scale * gains[1:2, :] + shifts[1:2, :]
            normed_two[rows_at(item * slab + step * tile, tile), :] = normed.astype(low)

        rows = rows_at(item * slab, slab)

        @pl.loop(0, units // 256)
        def _(step):
            lanes = pl.ds(pl.multiple_of(step * 256, 256), 256)
            value = dot(normed_two[rows, :], up[:, lanes]) + up_bias[lanes].reshape(1, -1)
            square = value * value
            bent = jnp.tanh(GELU_RATE * value * (1.0 + GELU_CUBE * square))
            half = 0.5 * (1.0 + bent)
            active[rows, lanes] = (value * half).astype(low)
            inner = GELU_RATE * (1.0 + 3.0 * GELU_CUBE * square)
            slope[rows, lanes] = (half + 0.5 * value * (1.0 - bent * bent) * inner).astype(low)

        if place_at == 0:
            loads[3].wait()

        @pl.loop(0, width // 256)
        def _(step):
            lanes = pl.ds(pl.multiple_of(step * 256, 256), 256)
            feed_mine[item, :, lanes] = dot(active[rows, :], down[:, lanes]).astype(low)

        if place_at == 0:
            feed = start(4, feed_mine.at[item], feed_from, cross)

    store(middle, middle_hbm)
    store(normed_two, normed_two_hbm)
    store(active, active_hbm)
    store(slope, slope_hbm)
    feed.wait_recv()

    @pl.loop(0, slab // tile)
    def _(step):
        at = rows_at(step * tile, tile)
        fed = feed_mine[tensor, at, :].astype(jnp.float32) + feed_from[at, :].astype(jnp.float32)
        tapped[at, :] = (middle[tensor, at, :] + (fed + shifts[3:4, :])).astype(low)

    for copy in copies:
        copy.wait_send()
    for copy in stores:
        copy.wait()


def forward_section(
    block_in, gains, shifts, qkv, qv_bias, out_weight, up, up_bias, down, crop_shape
):
    low = jnp.bfloat16
    items, slab, width = block_in.shape
    tokens = items * slab
    local = qkv.shape[2]
    units = up.shape[1]
    heads = local // HD
    patches = 2 * slab
    vmem = pl.BlockSpec(memory_space=pltpu.VMEM)
    hbm = pl.BlockSpec(memory_space=pl.ANY)
    kept = [
        ((tokens, width), low),
        ((tokens, local), low),
        ((items, 2, patches, local), low),
        ((items, heads, patches, slab), low),
        ((tokens, local), low),
        ((items, slab, width), jnp.float32),
        ((tokens, width), low),
        ((tokens, units), low),
        ((tokens, units), low),
    ]
    return pl.pallas_call(
        forward_kernel,
        out_shape=[jax.ShapeDtypeStruct(*one) for one in kept]
        + [jax.ShapeDtypeStruct((slab, width), low)],
        in_specs=[vmem, vmem, vmem, hbm, vmem, hbm, hbm, vmem, hbm]
        + [pl.BlockSpec(memory_space=pltpu.SMEM)],
        out_specs=[hbm] * 9 + [vmem],
        scratch_shapes=[pltpu.VMEM(one.shape, low) for one in (qkv, out_weight, up, down)]
        + [pltpu.VMEM(*one) for one in kept]
        + [
            pltpu.VMEM((local, patches), low),
            pltpu.VMEM(block_in.shape, low),
            pltpu.VMEM(block_in.shape, low),
            pltpu.VMEM(block_in.shape, low),
            pltpu.VMEM((slab, width), low),
            pltpu.SemaphoreType.DMA((4,)),
            pltpu.SemaphoreType.DMA((16,)),
            pltpu.SemaphoreType.DMA((5,)),
            pltpu.SemaphoreType.DMA((5,)),
        ],
        name="forward_section",
        compiler_params=pltpu.CompilerParams(
            collective_id=2, has_side_effects=True, vmem_limit_bytes=60 * 2**20
        ),
    )(block_in, gains, shifts, qkv, qv_bias, out_weight, up, up_bias, down, crop_shape)


def fold(value):
    rows, width = value.shape
    return jnp.sum(value.reshape(rows // 8, 8, width), axis=0)


def add_into(target, target_at, parts, rows, tile):
    @pl.loop(0, rows // tile)
    def _(step):
        at = step * tile
        total = None
        for ref, offset in parts:
            piece = ref[rows_at(offset + at, tile), :].astype(jnp.float32)
            total = piece if total is None else total + piece
        target[rows_at(target_at + at, tile), :] = total.astype(jnp.bfloat16)


COPIES = 10


class Sum:
    def __init__(self, refs, name, index, path, own, total, full=None):
        self.own, self.total, self.full = own, total, full
        self.held = [getattr(refs, name + end) for end in ("_core", "_first", "_second", "_third")]
        self.part = getattr(refs, name + "_part")
        if full is not None:
            self.both = getattr(refs, name + "_both")
            self.cross_part = getattr(refs, name + "_cross")
        self.send, self.recv = refs.sum_send.at[index], refs.sum_recv.at[index]
        self.local = refs.sum_local.at[index]
        rows = total.shape[0]
        self.half, self.piece = rows // 2, rows // 16
        dp, self.blk, self.tensor, near, far, first = place()
        self.core, self.cross, beside, side, over = peers()
        self.stages = [
            {"y": (beside, near), "s": (side, lax.rem(far, 2)), "o": (over, far // 2)}[one]
            for one in path
        ]
        self.at = [self.blk * self.half]
        for stage, (device, bit) in enumerate(self.stages):
            self.at.append(self.at[-1] + bit * (rows >> (stage + 2)))
        self.sizes = [rows >> (stage + 1) for stage in range(4)]
        self.waiting = []

    def start(self, index, src, dst, device):
        copy = remote(src, dst, self.send.at[index], self.recv.at[index], device)
        copy.start()
        self.waiting.append(copy)
        self.last = copy

    def sA(self):
        give = rows_at((1 - self.blk) * self.half, self.half)
        self.start(0, self.full.at[:, give], self.both, self.core)

    def sB(self):
        self.last.wait_recv()
        for which in (1 - self.tensor, self.tensor):
            add_into(
                self.both.at[which], 0, [(self.both.at[which], 0), (self.own.at[which], 0)],
                self.half, self.piece,
            )
        self.start(1, self.both.at[1 - self.tensor], self.cross_part, self.cross)

    def s0(self):
        give = rows_at((1 - self.blk) * self.half, self.half)
        self.start(0, self.own.at[give], self.held[0], self.core)

    def narrow(self, stage):
        device, bit = self.stages[stage]
        give = rows_at((1 - bit) * self.sizes[stage + 1], self.sizes[stage + 1])
        self.start(2 + stage, self.held[stage].at[give], self.held[stage + 1], device)

    def gather(self, stage, target):
        self.last.wait_recv()
        size = self.sizes[stage]
        kept = (self.held[stage - 1], self.stages[stage - 1][1] * size)
        add_into(target, 0, [(self.held[stage], 0), kept], size, self.piece)

    def s1(self):
        self.last.wait_recv()
        parts = [(self.held[0], 0), (self.own, self.blk * self.half)]
        if self.full is not None:
            parts = [(self.both.at[self.tensor], 0), (self.cross_part, 0)]
        add_into(self.held[0], 0, parts, self.half, self.piece)
        self.narrow(0)

    def s2(self):
        self.gather(1, self.held[1])
        self.narrow(1)

    def s2b(self):
        self.gather(2, self.held[2])
        self.narrow(2)

    def s3(self):
        self.gather(3, self.part)
        where = self.total.at[rows_at(self.at[3], self.piece)]
        self.keep = pltpu.make_async_copy(self.part, where, self.local)
        self.keep.start()
        self.start(5, self.part, where, self.stages[2][0])

    def spread(self, index, at, size, device):
        self.last.wait_recv()
        where = self.total.at[rows_at(at, size)]
        self.start(index, where, where, device)

    def s3b(self):
        self.keep.wait()
        self.spread(6, self.at[2], self.sizes[2], self.stages[1][0])

    def s4(self):
        self.spread(7, self.at[1], self.sizes[1], self.stages[0][0])

    def s5(self):
        self.spread(8, self.at[0], self.sizes[0], self.core)

    def s6(self):
        self.last.wait_recv()
        for copy in self.waiting:
            copy.wait_send()


def sum_scratch(rows, columns):
    low = jnp.bfloat16
    shares = {"_core": 2, "_first": 4, "_second": 8, "_third": 16, "_part": 16}
    return {end: pltpu.VMEM((rows // share, columns), low) for end, share in shares.items()}


def norm_back(value, grad, gain):
    centre, scale = centred(value)
    normed = centre * scale
    scaled = grad * gain
    inner = lane_mean(scaled * normed)
    return scale * (scaled - lane_mean(scaled) - normed * inner), normed


def backward_kernel(layout, *refs):
    r = types.SimpleNamespace(**dict(zip(layout, refs)))
    dp, blk, tensor, near, far, first = place()
    core, cross, beside, side, over = peers()
    low = jnp.bfloat16
    items, slab, width = r.grad_out.shape
    local = r.query.shape[1]
    units = r.active.shape[1]
    pairs = local // 128
    tile = 64
    half_width = width // 2

    loads = {}
    for index, name in enumerate(LOADED):
        copy = pltpu.make_async_copy(getattr(r, name + "_hbm"), getattr(r, name), r.load_sem.at[index])
        copy.start()
        loads[name] = copy
    keep_full = {}
    for index, name in enumerate(("kernels", "tconv")):
        full = getattr(r, "grad_" + name + "_hbm")
        rows = full.shape[1] // 2
        copy = pltpu.make_async_copy(
            full.at[:, rows_at(blk * rows, rows)],
            getattr(r, "own_" + name),
            r.load_sem.at[len(LOADED) + index],
        )
        copy.start()
        keep_full[name] = copy
    greet([core, cross, beside, side, over])
    copies = []

    def start(index, src, dst, device):
        copy = remote(src, dst, r.send.at[index], r.recv.at[index], device)
        copy.start()
        copies.append(copy)
        return copy

    sums = {}
    for h in range(2):
        sums["d%d" % h] = ("down%d" % h, r.own_down.at[h], r.total_down.at[h])
        sums["u%d" % h] = ("up%d" % h, r.own_up.at[h], r.total_up.at[h])
    sums["o"] = ("out", r.own_out, r.total_out)
    for c in range(3):
        sums["q%d" % c] = ("qkv%d" % c, r.own_qkv.at[c], r.total_qkv.at[c])
    sums["k"] = ("kernels", r.own_kernels, r.total_kernels, r.grad_kernels_hbm)
    sums["t"] = ("tconv", r.own_tconv, r.total_tconv, r.grad_tconv_hbm)
    sums = {
        name: Sum(r, one[0], index, PATHS[name], *one[1:])
        for index, (name, one) in enumerate(sums.items())
    }

    def rows_of(item):
        return slice(item * slab, (item + 1) * slab)

    def lanes_of(step, size=256):
        return pl.ds(pl.multiple_of(step * size, size), size)

    r.small[...] = jnp.zeros_like(r.small)

    def dout_rows(item, at):
        return r.grad_out[item, at, :].astype(jnp.float32) + r.dtap[item, at, :].astype(
            jnp.float32
        )

    zero = jnp.zeros((8, width), jnp.float32)

    sent = {}
    waited = set()

    def loaded(*names):
        for name in names:
            if name not in waited:
                loads[name].wait()
                waited.add(name)

    def shade_rows(item):
        def shade(step, total):
            value = dout_rows(item, rows_at(step * tile, tile)).astype(low)
            r.ddown[rows_at(item * slab + step * tile, tile), :] = value
            return total + fold(value.astype(jnp.float32))

        total = lax.fori_loop(0, slab // tile, shade, zero)
        r.small[5:6, :] += rows_sum(total)

    def feed_back(item):
        rows = rows_of(item)
        loaded("down", "slope")

        @pl.loop(0, units // 256)
        def _(step):
            lanes = lanes_of(step)
            dactive = nt_dot(r.ddown[rows, :], r.down[lanes, :])
            value = (dactive * r.slope[rows, lanes].astype(jnp.float32)).astype(low)
            r.dhidden[rows, lanes] = value
            summed = rows_sum(fold(value.astype(jnp.float32)))
            r.bias_sum[item : item + 1, lanes] = summed

        loaded("up")

        @pl.loop(0, width // 256)
        def _(step):
            value = nt_dot(r.dhidden[rows, :], r.up[lanes_of(step), :])
            r.two_mine[item, :, lanes_of(step)] = value.astype(low)

        sent["dn%d" % item] = start(item, r.two_mine.at[item], r.two_from.at[item], cross)

    def grad_down(h):
        loaded("active")

        @pl.loop(0, units // 2 // 256)
        def _(step):
            lanes = pl.ds(pl.multiple_of(h * (units // 2) + step * 256, 256), 256)
            r.own_down[h, lanes_of(step), :] = tn_dot(r.active[:, lanes], r.ddown[...]).astype(low)

    def grad_up(h):
        loaded("normed_two")

        @pl.loop(0, width // 256)
        def _(step):
            right = r.dhidden[:, h * (units // 2) : (h + 1) * (units // 2)]
            r.own_up[h, lanes_of(step), :] = tn_dot(r.normed_two[:, lanes_of(step)], right).astype(
                low
            )

    def middle_back(item):
        loaded("middle")
        sent["dn%d" % item].wait_recv()

        def back(step, totals):
            at = rows_at(step * tile, tile)
            grad = r.two_mine[item, at, :].astype(jnp.float32) + r.two_from[item, at, :].astype(
                jnp.float32
            )
            dvalue, normed = norm_back(r.middle[item, at, :], grad, r.gains[1:2, :])
            dmiddle = dout_rows(item, at) + dvalue
            r.dmiddle[item, at, :] = dmiddle
            dattn = dmiddle.astype(low)
            r.dattn[rows_at(item * slab + step * tile, tile), :] = dattn
            return (
                totals[0] + fold(grad * normed),
                totals[1] + fold(grad),
                totals[2] + fold(dattn.astype(jnp.float32)),
            )

        totals = lax.fori_loop(0, slab // tile, back, (zero, zero, zero))
        for row, total in zip((2, 3, 4), totals):
            r.small[row : row + 1, :] += rows_sum(total)

    def attention_back(item):
        loaded("out_weight", "key_value", "query", "probs")
        rows = rows_of(item)
        r.keys_turned[...] = r.key_value[item, 0].astype(jnp.float32).T.astype(low)
        r.dmixed[...] = nt_dot(r.dattn[rows, :], r.out_weight[...]).astype(low)
        scale = HD ** (-0.5)
        for pair in range(pairs):
            lanes = slice(pair * 128, (pair + 1) * 128)
            values = r.key_value[item, 1, :, lanes]
            asked = r.query[rows, lanes]
            dmixed = r.dmixed[:, lanes]
            dkeys = dvalues = None
            turned = []
            for head in range(2):
                prob = r.probs[item, 2 * pair + head]
                dmixed_head = head_only(dmixed, head)
                dprob = nt_dot(values, dmixed_head)
                wide = prob.astype(jnp.float32)
                inner = rows_sum(wide * dprob)
                dscores = (wide * (dprob - inner)).astype(low)
                key_part = dot(dscores, head_only(asked, head))
                value_part = dot(prob, dmixed_head)
                dkeys = key_part if dkeys is None else dkeys + key_part
                dvalues = value_part if dvalues is None else dvalues + value_part
                at = pair * 128 + head * HD
                turned.append(dot(r.keys_turned[at : at + HD, :], dscores))
            r.dproject[0, rows, lanes] = (jnp.concatenate(turned, axis=0).T * scale).astype(low)
            dkeys = (dkeys * scale).astype(low)
            dvalues = dvalues.astype(low)
            r.dproject[1, rows, lanes] = dkeys[:slab]
            r.dproject[2, rows, lanes] = dvalues[:slab]
            r.give_kv[item, 0, :, lanes] = dkeys[slab:]
            r.give_kv[item, 1, :, lanes] = dvalues[slab:]
        sent["kv%d" % item] = start(2 + item, r.give_kv.at[item], r.got_kv.at[item], core)

    def grad_out_weight():
        loaded("mixed")
        for h in range(2):
            value = tn_dot(r.mixed[...], r.dattn[:, h * half_width : (h + 1) * half_width])
            r.own_out[h * local : (h + 1) * local, :] = value.astype(low)

    def join_heads():
        for item in range(items):
            sent["kv%d" % item].wait_recv()
            rows = rows_of(item)
            for c in range(2):
                value = r.dproject[1 + c, rows, :].astype(jnp.float32)
                value = value + r.got_kv[item, c].astype(jnp.float32)
                r.dproject[1 + c, rows, :] = value.astype(low)

    def project_back(item):
        loaded("qkv")
        rows = rows_of(item)

        @pl.loop(0, width // 256)
        def _(step):
            lanes = lanes_of(step)
            value = None
            for c in range(3):
                part = nt_dot(r.dproject[c, rows, :], r.qkv[c, lanes, :])
                value = part if value is None else value + part
            r.one_mine[item, :, lanes] = value.astype(low)

        sent["pn%d" % item] = start(4 + item, r.one_mine.at[item], r.one_from.at[item], cross)

    def grad_qkv(c):
        loaded("normed_one")
        r.own_qkv[c] = tn_dot(r.normed_one[...], r.dproject[c]).astype(low)

    def bias_sums():
        for c in (0, 2):
            value = rows_sum(fold(r.dproject[c].astype(jnp.float32)))
            r.small[6:7, (c // 2) * local : (c // 2 + 1) * local] = value
        total = rows_sum(r.bias_sum[0:items, :])
        r.small[7:8, :] = total[:, :width]
        r.small[8:9, :] = total[:, width:]

    def input_back(item):
        sent["pn%d" % item].wait_recv()

        def back(step, totals):
            at = rows_at(step * tile, tile)
            grad = r.one_mine[item, at, :].astype(jnp.float32) + r.one_from[item, at, :].astype(
                jnp.float32
            )
            value = r.block_in[item, at, :].astype(jnp.float32)
            dvalue, normed = norm_back(value, grad, r.gains[0:1, :])
            r.grad_input[item, at, :] = (r.dmiddle[item, at, :] + dvalue).astype(low)
            return totals[0] + fold(grad * normed), totals[1] + fold(grad)

        totals = lax.fori_loop(0, slab // tile, back, (zero, zero))
        for row, total in zip((0, 1), totals):
            r.small[row : row + 1, :] += rows_sum(total)

    def small_step(index):
        if index > 0:
            sent["small"].wait_recv()
            r.small_sum[index] = r.small_sum[index - 1] + r.small_from[index - 1]
        else:
            r.small_sum[0] = r.small[...]
        if index < 4:
            device = (core, beside, side, over)[index]
            sent["small"] = start(
                6 + index, r.small_sum.at[index], r.small_from.at[index], device
            )
        else:
            r.small_total[...] = r.small_sum[4]

    tasks = {"kv": join_heads, "og": grad_out_weight, "bias": bias_sums}
    for index in range(2):
        for name, work in (
            ("sh", shade_rows),
            ("ffn", feed_back),
            ("gd", grad_down),
            ("gu", grad_up),
            ("ln", middle_back),
            ("at", attention_back),
            ("p", project_back),
            ("f", input_back),
        ):
            tasks[name + str(index)] = functools.partial(work, index)
    for c in range(3):
        tasks["gq" + str(c)] = functools.partial(grad_qkv, c)
    for index in range(5):
        tasks["sm" + str(index)] = functools.partial(small_step, index)

    def full_step(name, unit):
        keep_full[{"k": "kernels", "t": "tconv"}[name]].wait()
        unit.sB()

    for name, unit in sums.items():
        for step in ("sA", "sB", "s0", "s1", "s2", "s2b", "s3", "s3b", "s4", "s5", "s6"):
            tasks[name + "." + step] = getattr(unit, step)
        if unit.full is not None:
            tasks[name + ".sB"] = functools.partial(full_step, name, unit)
    for name in ORDER:
        tasks[name]()
    for copy in copies:
        copy.wait_send()


PATHS = {
    "t": "yso",
    "k": "yso",
    "d0": "yso",
    "d1": "yso",
    "u0": "yso",
    "u1": "yso",
    "o": "yso",
    "q2": "yso",
    "q1": "yso",
    "q0": "yso",
}

ORDER = (
    "sh1", "sh0", "gd1", "d1.s0", "ffn0", "d1.s1", "k.sA", "gd0", "d0.s0", "ffn1", "gu0", "u0.s0",
    "k.sB", "d0.s1", "gu1", "d1.s2", "u0.s1", "u1.s0", "t.sA", "ln0", "at0", "d1.s2b", "u1.s1", "t.sB",
    "d0.s2", "ln1", "at1", "d1.s3", "og", "o.s0", "u0.s2", "d0.s2b", "kv", "bias", "o.s1", "gq0",
    "p0", "k.s1", "d1.s3b", "p1", "u1.s2", "gq2", "u0.s2b", "gq1", "o.s2", "d0.s3", "q2.s0", "q0.s0",
    "q1.s0", "d1.s4", "q2.s1", "q0.s1", "q1.s1", "t.s1", "k.s2", "u1.s2b", "u0.s3", "o.s2b", "d0.s3b", "d1.s5",
    "f0", "d1.s6", "k.s2b", "u1.s3", "q2.s2", "u0.s3b", "o.s3", "q0.s2", "d0.s4", "q1.s2", "f1", "k.s3",
    "sm0", "u1.s3b", "q2.s2b", "t.s2", "sm1", "u0.s4", "o.s3b", "q0.s2b", "d0.s5", "q1.s2b", "sm2", "k.s3b",
    "d0.s6", "u1.s4", "q2.s3", "u0.s5", "t.s2b", "o.s4", "u0.s6", "q0.s3", "q1.s3", "sm3", "u1.s5", "k.s4",
    "q2.s3b", "t.s3", "u1.s6", "sm4", "o.s5", "q0.s3b", "q1.s3b", "o.s6", "q2.s4", "t.s3b", "k.s5", "q0.s4",
    "q1.s4", "k.s6", "q2.s5", "t.s4", "q2.s6", "q0.s5", "q0.s6", "q1.s5", "q1.s6", "t.s5", "t.s6",
)

LOADED = (
    "down",
    "slope",
    "up",
    "active",
    "normed_two",
    "middle",
    "out_weight",
    "key_value",
    "query",
    "probs",
    "mixed",
    "qkv",
    "normed_one",
)


def backward_section(arrays):
    low = jnp.bfloat16
    wide = jnp.float32
    items, slab, width = arrays["grad_out"].shape
    tokens = items * slab
    local = arrays["qkv"].shape[2]
    units = arrays["down"].shape[0]
    patches = arrays["key_value"].shape[2]
    kernel_rows = arrays["grad_kernels"].shape[1]
    near = ["grad_out", "dtap", "block_in", "gains"]
    distant = list(LOADED) + ["grad_kernels", "grad_tconv"]
    totals = {
        "down": (2, units // 2, width),
        "up": (2, width, units // 2),
        "out": (2 * local, width // 2),
        "qkv": (3, width, local),
        "kernels": (kernel_rows, CH),
        "tconv": arrays["grad_tconv"].shape[1:],
    }
    scratch = {name: pltpu.VMEM(arrays[name].shape, arrays[name].dtype) for name in LOADED}
    for name, shape in totals.items():
        full = name in ("kernels", "tconv")
        rows, columns = shape[-2:]
        scratch["own_" + name] = pltpu.VMEM((2, rows // 2, columns) if full else shape, low)
        labels = [name] if len(shape) == 2 else [name + str(part) for part in range(shape[0])]
        for label in labels:
            for end, one in sum_scratch(rows, columns).items():
                scratch[label + end] = one
            if full:
                scratch[label + "_both"] = pltpu.VMEM((2, rows // 2, columns), low)
                scratch[label + "_cross"] = pltpu.VMEM((rows // 2, columns), low)
    block = (items, slab, width)
    for name, shape, dtype in (
        ("ddown", (tokens, width), low),
        ("dhidden", (tokens, units), low),
        ("bias_sum", (8, units), wide),
        ("two_mine", block, low),
        ("two_from", block, low),
        ("dmiddle", block, wide),
        ("dattn", (tokens, width), low),
        ("dmixed", (slab, local), low),
        ("keys_turned", (local, patches), low),
        ("give_kv", (items, 2, slab, local), low),
        ("got_kv", (items, 2, slab, local), low),
        ("dproject", (3, tokens, local), low),
        ("one_mine", block, low),
        ("one_from", block, low),
        ("small", (16, width), wide),
        ("small_sum", (5, 16, width), wide),
        ("small_from", (4, 16, width), wide),
    ):
        scratch[name] = pltpu.VMEM(shape, dtype)
    dma = pltpu.SemaphoreType.DMA
    scratch["load_sem"] = dma((len(LOADED) + 2,))
    scratch["send"] = dma((10,))
    scratch["recv"] = dma((10,))
    scratch["sum_send"] = dma((10, COPIES))
    scratch["sum_recv"] = dma((10, COPIES))
    scratch["sum_local"] = dma((10,))
    outputs = ["grad_input", "small_total"] + ["total_" + name for name in totals]
    layout = near + [name + "_hbm" for name in distant] + outputs + list(scratch)
    vmem = pl.BlockSpec(memory_space=pltpu.VMEM)
    hbm = pl.BlockSpec(memory_space=pl.ANY)
    results = pl.pallas_call(
        functools.partial(backward_kernel, tuple(layout)),
        out_shape=[
            jax.ShapeDtypeStruct(block, low),
            jax.ShapeDtypeStruct((16, width), wide),
        ]
        + [jax.ShapeDtypeStruct(shape, low) for shape in totals.values()],
        in_specs=[vmem] * len(near) + [hbm] * len(distant),
        out_specs=[vmem] * 2 + [hbm] * len(totals),
        scratch_shapes=list(scratch.values()),
        name="backward_section",
        compiler_params=pltpu.CompilerParams(
            collective_id=3, has_side_effects=True, vmem_limit_bytes=62 * 2**20
        ),
    )(*[arrays[name] for name in near + distant])
    return dict(zip(outputs, results))


def body(
    block_in,
    crop_shape,
    norm_gains,
    shifts,
    qkv_weight,
    qv_bias,
    out_weight,
    up_weight,
    up_bias,
    down_weight,
    tconv_weight,
    kernels,
    grad_out,
    grad_decoded,
):
    (
        normed_one,
        query,
        key_value,
        probs,
        mixed,
        middle,
        normed_two,
        active,
        slope,
        tapped,
    ) = forward_section(
        block_in,
        norm_gains,
        shifts,
        qkv_weight,
        qv_bias,
        out_weight,
        up_weight,
        up_bias,
        down_weight,
        crop_shape,
    )
    decoded, block_all, dtap, grad_tconv, grad_kernels = decoder_section(
        tapped,
        tconv_weight,
        kernels,
        grad_decoded.reshape(DEPTH, SIDE, 2, WIDE, CH),
        crop_shape,
    )
    result = backward_section(
        {
            "grad_out": grad_out,
            "dtap": dtap,
            "block_in": block_in,
            "gains": norm_gains,
            "down": down_weight,
            "slope": slope,
            "up": up_weight,
            "active": active,
            "normed_two": normed_two,
            "middle": middle,
            "out_weight": out_weight,
            "key_value": key_value,
            "query": query,
            "probs": probs,
            "mixed": mixed,
            "qkv": qkv_weight,
            "normed_one": normed_one,
            "grad_kernels": grad_kernels,
            "grad_tconv": grad_tconv,
        }
    )
    small = result["small_total"]
    totals = {name[6:]: array for name, array in result.items() if name.startswith("total_")}
    groups = lax.axis_size("dp") // GROUP
    if groups > 1:
        same = [[part * GROUP + i for part in range(groups)] for i in range(GROUP)]
        small = lax.psum(small, "dp", axis_index_groups=same)
        totals = {
            name: lax.psum(array, "dp", axis_index_groups=same) for name, array in totals.items()
        }
    sums, passed, smalls = finish_section(
        totals, (block_all, decoded, result["grad_input"]), small
    )
    return (
        passed[0],
        passed[1].reshape(grad_decoded.shape),
        passed[2],
        smalls[0],
        smalls[1],
        sums["qkv"],
        smalls[2],
        sums["out"],
        sums["up"],
        smalls[3],
        sums["down"].reshape(down_weight.shape),
        sums["tconv"],
        sums["kernels"].transpose(0, 2, 1),
    )


def solution(mesh):
    return jax.shard_map(
        body,
        mesh=mesh,
        in_specs=(
            P("dp", "blk", None),
            P("dp"),
            P(),
            P(),
            P(None, None, "tensor"),
            P(None, "tensor"),
            P("tensor", None),
            P(None, "tensor"),
            P("tensor"),
            P("tensor", None),
            P(),
            P(),
            P("dp", "blk", None),
            P(("dp", "tensor"), "blk", None, None, None),
        ),
        out_specs=(
            P("dp", "blk", None),
            P(("dp", "tensor"), "blk", None, None, None),
            P("dp", "blk", None),
            P(),
            P(),
            P(None, None, "tensor"),
            P(None, "tensor"),
            P("tensor", None),
            P(None, "tensor"),
            P("tensor"),
            P("tensor", None),
            P(None, "tensor"),
            P(None, None, "tensor"),
        ),
        check_vma=False,
    )
```

```python
import functools
import types

import jax
import jax.numpy as jnp
from jax import lax
from jax.experimental import pallas as pl
from jax.experimental.pallas import tpu as pltpu
from jax.sharding import PartitionSpec as P

HD = 64

MESH = pl.DeviceIdType.MESH
GROUP = 8
FAR = 4


def place():
    dp = lax.axis_index("dp")
    blk = lax.axis_index("blk")
    tensor = lax.axis_index("tensor")
    near = lax.rem(dp, 2)
    far = lax.rem(dp // 2, FAR)
    first = dp // GROUP * GROUP
    return (dp, blk, tensor, near, far, first)


def peers():
    dp, blk, tensor, near, far, first = place()
    core = (dp, 1 - blk, tensor)
    cross = (dp, blk, 1 - tensor)
    beside = (first + 2 * far + 1 - near, blk, tensor)
    side = (first + 2 * (far + 1 - 2 * lax.rem(far, 2)) + near, blk, tensor)
    over = (first + 2 * lax.rem(far + 2, FAR) + near, blk, tensor)
    return (core, cross, beside, side, over)


def greet(devices):
    barrier = pltpu.get_barrier_semaphore()
    for device in devices:
        pl.semaphore_signal(barrier, inc=1, device_id=device, device_id_type=MESH)
    pl.semaphore_wait(barrier, len(devices))


def remote(src, dst, send, recv, device):
    return pltpu.make_async_remote_copy(
        src_ref=src, dst_ref=dst, send_sem=send, recv_sem=recv, device_id=device,
        device_id_type=MESH,
    )


def rows_at(start, size):
    return pl.ds(pl.multiple_of(start, 16), size)


DEPTH = 8
SIDE = 8
WIDE = 16
CH = 128
PAIR = 2 * CH
ROWS = DEPTH * SIDE * WIDE
TAPS = [(deep, wide) for deep in range(3) for wide in range(3)]
PADDED_TAPS = 28


def nt_dot(left, right):
    return lax.dot_general(
        left, right, (((1,), (1,)), ((), ())), preferred_element_type=jnp.float32
    )


def tn_dot(left, right):
    return lax.dot_general(
        left, right, (((0,), (0,)), ((), ())), preferred_element_type=jnp.float32
    )


def dot(left, right):
    return jnp.dot(left, right, preferred_element_type=jnp.float32)


def half_sums(row):
    return row[:, :CH] + row[:, CH:]


def twice(row):
    return jnp.concatenate([row, row], axis=1)


def row_and_column(size):
    return (
        lax.broadcasted_iota(jnp.int32, (size, size), 0),
        lax.broadcasted_iota(jnp.int32, (size, size), 1),
    )


def shift_matrix(step):
    row, column = row_and_column(PAIR)
    same = (row // WIDE) == (column // WIDE)
    return jnp.where(same & (row + step == column), 1.0, 0.0).astype(jnp.bfloat16)


def weave_matrix():
    row, column = row_and_column(PAIR)
    source = lax.rem(row, 2) * CH + row // WIDE * SIDE + lax.rem(row, WIDE) // 2
    return jnp.where(source == column, 1.0, 0.0).astype(jnp.bfloat16)


def unweave_matrix():
    row, column = row_and_column(PAIR)
    source = lax.rem(column, 2) * CH + column // WIDE * SIDE + lax.rem(column, WIDE) // 2
    return jnp.where(source == row, 1.0, 0.0).astype(jnp.bfloat16)


def lay_kernel(kernels_ref, index, weights):
    zero = jnp.zeros((CH, CH), jnp.bfloat16)
    for at, (deep, wide) in enumerate(TAPS):
        weights[at, 3 * CH :, :CH] = zero
        weights[at, :CH, CH:] = zero
        for high in range(3):
            offset = ((deep * 3 + high) * 3 + wide) * CH
            block = kernels_ref[index, offset : offset + CH, :]
            weights[at, high * CH : (high + 1) * CH, :CH] = block
            weights[at, (high + 1) * CH : (high + 2) * CH, CH:] = block


def lay_flipped(kernels_ref, index, weights):
    zero = jnp.zeros((CH, CH), jnp.bfloat16)
    for at, (deep, wide) in enumerate(TAPS):
        weights[at, :CH, 3 * CH :] = zero
        weights[at, CH:, :CH] = zero
        for high in range(3):
            offset = (((2 - deep) * 3 + 2 - high) * 3 + 2 - wide) * CH
            block = kernels_ref[index, offset : offset + CH, :]
            weights[at, :CH, high * CH : (high + 1) * CH] = block
            weights[at, CH:, (high + 1) * CH : (high + 2) * CH] = block


def four_heights(field, wide, start, count):
    depths = pl.ds(start, count)
    low = field[wide, depths, 0:SIDE, :, CH:]
    middle = field[wide, depths, 1 : SIDE + 1, :, :]
    high = field[wide, depths, 2 : SIDE + 2, :, :CH]
    joined = jnp.concatenate([low, middle, high], axis=-1)
    return joined.reshape(count * SIDE * WIDE, 4 * CH)


def conv_tile(field, weights, multiply, level, start):
    total = None
    for at, (deep, wide) in enumerate(TAPS):
        product = multiply(four_heights(field, wide, start + deep, 2), weights[at])
        total = product if total is None else total + product
    level[pl.ds(pl.multiple_of(start * CH, 2 * CH), 2 * CH), :] = total


def conv(field, weights, multiply, level, arrive):
    @pl.loop(0, 2)
    def _(step):
        conv_tile(field, weights, multiply, level, 2 + 2 * step)

    arrive()

    @pl.loop(0, 2)
    def _(step):
        conv_tile(field, weights, multiply, level, 6 * step)


def clear_rims(field, blk):
    for wide in range(3):
        field[wide, :, 0] = jnp.zeros((DEPTH + 2, WIDE, PAIR), jnp.bfloat16)
        field[wide, :, SIDE + 1] = jnp.zeros((DEPTH + 2, WIDE, PAIR), jnp.bfloat16)
        field[wide, 9 * blk] = jnp.zeros((SIDE + 2, WIDE, PAIR), jnp.bfloat16)


def place_rows(field, before, after, step, value):
    shape = (2, SIDE, WIDE, PAIR)
    depths = pl.ds(1 + 2 * step, 2)
    field[1, depths, 1 : SIDE + 1] = value.reshape(shape)
    field[0, depths, 1 : SIDE + 1] = dot(before, value).astype(jnp.bfloat16).reshape(shape)
    field[2, depths, 1 : SIDE + 1] = dot(after, value).astype(jnp.bfloat16).reshape(shape)


def kernel_grad(field, dlevel_turned, index, out, tensor_half):
    for at, (deep, wide) in enumerate(TAPS):
        joined = four_heights(field, wide, deep, DEPTH)
        block = dot(dlevel_turned[...], joined)
        for high in range(3):
            part = (
                block[:CH, high * CH : (high + 1) * CH]
                + block[CH:, (high + 1) * CH : (high + 2) * CH]
            )
            offset = ((deep * 3 + high) * 3 + wide) * CH
            part = part.astype(jnp.bfloat16)
            at = index * PADDED_TAPS * 64 + offset // 2
            for half in range(2):
                out[half, at : at + 64, :] = part[half * 64 : (half + 1) * 64, :]


def decoder_kernel(
    tapped,
    tconv_hbm,
    kernels_hbm,
    grad_decoded_hbm,
    crop_shape,
    grad_out_hbm,
    down_hbm,
    slope_hbm,
    up_hbm,
    decoded_hbm,
    block_all_hbm,
    dtap_all_hbm,
    grad_tconv_hbm,
    grad_kernels_hbm,
    ddown_hbm,
    dhidden_hbm,
    two_hbm,
    bias_sum,
    shift_sum,
    tconv,
    kernels,
    grad_decoded,
    grad_out,
    down,
    slope,
    up,
    decoded,
    grad_tconv,
    grad_kernels,
    ddown,
    dhidden,
    two,
    mask,
    inverse,
    field_one,
    field_two,
    dlevel_two,
    dlevel_one,
    weights_one,
    weights_two,
    flipped_two,
    flipped_one,
    level_one,
    level_two,
    dfield,
    turned_two,
    turned_one,
    dlifted,
    tapped_from,
    dtap_mine,
    dtap_from,
    sums_mine,
    sums_from,
    load_sem,
    store_sem,
    send,
    recv,
):
    dp, blk, tensor, near, far, first = place()
    core, cross, beside, side, over = peers()
    low = jnp.bfloat16
    row_tiles = ROWS // PAIR
    slab, width = tapped.shape
    units = dhidden.shape[1]
    own_rows = rows_at(tensor * slab, slab)
    loads = {}
    for index, (name, src, dst) in enumerate(
        (
            ("tconv", tconv_hbm, tconv),
            ("kernels", kernels_hbm, kernels),
            ("grad_decoded", grad_decoded_hbm, grad_decoded),
            ("grad_out", grad_out_hbm.at[tensor], grad_out),
            ("down", down_hbm, down),
            ("slope", slope_hbm.at[own_rows], slope),
            ("up", up_hbm, up),
        )
    ):
        copy = pltpu.make_async_copy(src, dst, load_sem.at[index])
        copy.start()
        loads[name] = copy

    stores = []

    def store(src, dst):
        copy = pltpu.make_async_copy(src, dst, store_sem.at[len(stores)])
        copy.start()
        stores.append(copy)

    store(tapped, block_all_hbm.at[tensor])
    copies = []

    def start(index, src, dst, device):
        copy = remote(src, dst, send.at[index], recv.at[index], device)
        copy.start()
        copies.append(copy)
        return copy

    depth_end, side_end = extents(crop_shape[tensor])
    row = lax.broadcasted_iota(jnp.int32, mask.shape, 0)
    inside = (
        (blk * (DEPTH // 2) + row // (2 * CH) < depth_end)
        & (lax.rem(row // WIDE, SIDE) < side_end)
        & (lax.rem(row, WIDE) // 2 < side_end)
    )
    mask[...] = jnp.where(inside, 1.0, 0.0)
    voxels = (8 * depth_end * side_end * side_end).astype(jnp.float32)
    inverse[...] = 1.0 / jnp.full(inverse.shape, voxels)

    for field in (field_one, field_two, dlevel_two, dlevel_one):
        clear_rims(field, blk)
    greet([core, cross])
    give_tapped = start(0, tapped, tapped_from, cross)

    before, after = shift_matrix(-1), shift_matrix(1)

    def send_edge(index, field):
        return start(
            index,
            field.at[:, DEPTH - 7 * blk, 1 : SIDE + 1],
            field.at[:, 9 * blk, 1 : SIDE + 1],
            core,
        )

    def rows_of(step):
        return pl.ds(pl.multiple_of(step * PAIR, PAIR), PAIR)

    def mask_rows(step):
        return twice(mask[rows_of(step), :])

    def totals(slot, pair):
        sums_mine[slot, 0:1, :] = half_sums(pair[0])
        sums_mine[slot, 1:2, :] = half_sums(pair[1])
        return start(5 + slot, sums_mine.at[slot], sums_from.at[slot], core)

    def means(slot, copy):
        copy.wait_recv()
        both = (sums_mine[slot] + sums_from[slot]) * inverse[...]
        return both[0:1, :], both[1:2, :]

    zero_pair = (jnp.zeros((1, PAIR), jnp.float32), jnp.zeros((1, PAIR), jnp.float32))

    weave = weave_matrix()
    loads["tconv"].wait()
    for piece in range(2):
        tokens = slice(piece * CH, (piece + 1) * CH)
        for a in range(2):
            lifted = dot(tapped[tokens, :], tconv[:, a * 512 : (a + 1) * 512])
            side = [
                jnp.concatenate([lifted[:, c * CH : (c + 1) * CH],
                                 lifted[:, (2 + c) * CH : (3 + c) * CH]], axis=1)
                for c in range(2)
            ]
            woven = dot(weave, jnp.concatenate(side, axis=0).astype(low))
            for depth in range(2):
                at = 2 * (2 * piece + depth) + a
                rows = slice(depth * CH, (depth + 1) * CH)
                value = woven[rows, :] * twice(mask[at * CH : (at + 1) * CH, :])
                level_one[at * CH : (at + 1) * CH, :] = value

    @pl.loop(0, row_tiles)
    def _(step):
        place_rows(field_one, before, after, step, level_one[rows_of(step), :].astype(low))

    edge = send_edge(1, field_one)
    loads["kernels"].wait()
    lay_kernel(kernels, 0, weights_one)
    conv(field_one, weights_one, dot, level_one, edge.wait_recv)

    def forward_sums(level):
        def add(step, pair):
            value = level[rows_of(step), :]
            kept = value * mask_rows(step)
            return (
                pair[0] + jnp.sum(kept, axis=0, keepdims=True),
                pair[1] + jnp.sum(kept * value, axis=0, keepdims=True),
            )

        return lax.fori_loop(0, row_tiles, add, zero_pair)

    def mean_and_scale(slot, copy):
        mean, second = means(slot, copy)
        return twice(mean), twice(lax.rsqrt(second - mean * mean + 1e-05))

    def sigmoid(value):
        return 0.5 * jnp.tanh(0.5 * value) + 0.5

    copy = totals(0, forward_sums(level_one))
    lay_kernel(kernels, 1, weights_two)
    mean_one, scale_one = mean_and_scale(0, copy)

    @pl.loop(0, row_tiles)
    def _(step):
        normed = (level_one[rows_of(step), :] - mean_one) * scale_one
        level_one[rows_of(step), :] = normed
        value = normed * sigmoid(normed) * mask_rows(step)
        place_rows(field_two, before, after, step, value.astype(low))

    edge = send_edge(2, field_two)
    lay_flipped(kernels, 1, flipped_two)
    conv(field_two, weights_two, dot, level_two, edge.wait_recv)
    copy = totals(1, forward_sums(level_two))
    lay_flipped(kernels, 0, flipped_one)
    mean_two, scale_two = mean_and_scale(1, copy)

    loads["grad_decoded"].wait()

    def two_depths(ref, step, b):
        return ref[pl.ds(2 * step, 2), :, b].reshape(PAIR, CH)

    def decode(step, pair):
        normed = (level_two[rows_of(step), :] - mean_two) * scale_two
        level_two[rows_of(step), :] = normed
        kept = mask_rows(step)
        gate = sigmoid(normed)
        value = (normed * gate * kept).astype(low)
        for b in range(2):
            decoded[pl.ds(2 * step, 2), :, b] = value[:, b * CH : (b + 1) * CH].reshape(
                2, SIDE, WIDE, CH
            )
        grad = jnp.concatenate(
            [two_depths(grad_decoded, step, 0), two_depths(grad_decoded, step, 1)], axis=1
        ).astype(jnp.float32)
        dnormed = gate * (1.0 + normed * (1.0 - gate)) * kept * grad
        dfield[rows_of(step), :] = dnormed
        return (
            pair[0] + jnp.sum(dnormed, axis=0, keepdims=True),
            pair[1] + jnp.sum(dnormed * normed, axis=0, keepdims=True),
        )

    copy = totals(2, lax.fori_loop(0, row_tiles, decode, zero_pair))

    store(decoded, decoded_hbm)

    def level_grad(slot, copy, level, scale, field, turned):
        mean_grad, mean_cross = means(slot, copy)
        mean_grad, mean_cross = twice(mean_grad), twice(mean_cross)

        @pl.loop(0, row_tiles)
        def _(step):
            centred = mean_grad + level[rows_of(step), :] * mean_cross
            value = scale * (dfield[rows_of(step), :] - mask_rows(step) * centred)
            place_rows(field, before, after, step, value.astype(low))
            turned[:, rows_of(step)] = value.T.astype(low)

    level_grad(2, copy, level_two, scale_two, dlevel_two, turned_two)
    edge = send_edge(3, dlevel_two)
    conv(dlevel_two, flipped_two, nt_dot, dfield, edge.wait_recv)

    def back_one(step, pair):
        normed = level_one[rows_of(step), :]
        gate = sigmoid(normed)
        dnormed = gate * (1.0 + normed * (1.0 - gate)) * mask_rows(step) * dfield[rows_of(step), :]
        dfield[rows_of(step), :] = dnormed
        return (
            pair[0] + jnp.sum(dnormed, axis=0, keepdims=True),
            pair[1] + jnp.sum(dnormed * normed, axis=0, keepdims=True),
        )

    copy = totals(3, lax.fori_loop(0, row_tiles, back_one, zero_pair))
    level_grad(3, copy, level_one, scale_one, dlevel_one, turned_one)
    edge = send_edge(4, dlevel_one)
    conv(dlevel_one, flipped_one, nt_dot, dfield, edge.wait_recv)

    unweave = unweave_matrix()
    for piece in range(2):
        tokens = slice(piece * CH, (piece + 1) * CH)
        for a in range(2):
            parts = []
            for depth in range(2):
                at = 2 * (2 * piece + depth) + a
                rows = slice(at * CH, (at + 1) * CH)
                parts.append(dfield[rows, :] * twice(mask[rows, :]))
            apart = dot(unweave, jnp.concatenate(parts, axis=0).astype(low)).astype(low)
            for c in range(2):
                for b in range(2):
                    column = ((a * 2 + b) * 2 + c) * CH
                    dlifted[tokens, column : column + CH] = apart[
                        c * CH : (c + 1) * CH, b * CH : (b + 1) * CH
                    ]
    dtap_mine[...] = nt_dot(dlifted[...], tconv[...]).astype(low)
    give_dtap = start(9, dtap_mine, dtap_from, cross)
    for half in range(2):
        lanes = slice(half * 512, (half + 1) * 512)
        grad_tconv[half] = tn_dot(tapped[...], dlifted[:, lanes]).astype(low)
        for index in range(2):
            at = ((index + 1) * PADDED_TAPS - 1) * 64
            grad_kernels[half, at : at + 64, :] = jnp.zeros((64, CH), low)
    store(grad_tconv, grad_tconv_hbm)

    loads["grad_out"].wait()
    tile = 64

    def shade(step, total):
        at = rows_at(step * tile, tile)
        value = grad_out[at, :].astype(jnp.float32) + dtap_mine[at, :].astype(jnp.float32)
        value = value.astype(low)
        ddown[at, :] = value
        return total + fold(value.astype(jnp.float32))

    shift_sum[...] = lax.fori_loop(0, slab // tile, shade, jnp.zeros((8, width), jnp.float32))
    store(ddown, ddown_hbm)
    loads["down"].wait()
    loads["slope"].wait()

    @pl.loop(0, units // 256)
    def _(step):
        lanes = pl.ds(pl.multiple_of(step * 256, 256), 256)
        dactive = nt_dot(ddown[...], down[lanes, :])
        value = (dactive * slope[:, lanes].astype(jnp.float32)).astype(low)
        dhidden[:, lanes] = value
        bias_sum[:, lanes] = fold(value.astype(jnp.float32))

    store(dhidden, dhidden_hbm)
    loads["up"].wait()

    @pl.loop(0, width // 256)
    def _(step):
        lanes = pl.ds(pl.multiple_of(step * 256, 256), 256)
        two[:, lanes] = nt_dot(dhidden[...], up[lanes, :]).astype(low)

    store(two, two_hbm)
    kernel_grad(field_two, turned_two, 1, grad_kernels, tensor)
    kernel_grad(field_one, turned_one, 0, grad_kernels, tensor)
    store(grad_kernels, grad_kernels_hbm)
    store(dtap_mine, dtap_all_hbm.at[tensor])
    give_tapped.wait_recv()
    store(tapped_from, block_all_hbm.at[1 - tensor])
    give_dtap.wait_recv()
    store(dtap_from, dtap_all_hbm.at[1 - tensor])
    for copy in copies:
        copy.wait_send()
    for copy in stores:
        copy.wait()


def decoder_section(
    tapped, tconv_weight, kernels, grad_decoded, crop_shape, grad_out, down, slope, up
):
    low = jnp.bfloat16
    wide = jnp.float32
    slab, width = tapped.shape
    units = down.shape[0]
    vmem = pl.BlockSpec(memory_space=pltpu.VMEM)
    hbm = pl.BlockSpec(memory_space=pl.ANY)
    field = pltpu.VMEM((3, DEPTH + 2, SIDE + 2, WIDE, PAIR), low)
    plane = pltpu.VMEM((ROWS, PAIR), wide)
    kept = {
        "decoded": (DEPTH, SIDE, 2, WIDE, CH),
        "grad_tconv": (2, width, tconv_weight.shape[1] // 2),
        "grad_kernels": (2, 2 * PADDED_TAPS * 64, CH),
        "ddown": (slab, width),
        "dhidden": (slab, units),
        "two": (slab, width),
    }
    block = (2, slab, width)
    shapes = [kept["decoded"], block, block] + list(kept.values())[1:]
    names = ["decoded", "block_all", "dtap"] + list(kept)[1:] + ["bias_own", "shift_own"]
    dma = pltpu.SemaphoreType.DMA
    results = pl.pallas_call(
        decoder_kernel,
        out_shape=[jax.ShapeDtypeStruct(shape, low) for shape in shapes]
        + [
            jax.ShapeDtypeStruct((8, units), wide),
            jax.ShapeDtypeStruct((8, width), wide),
        ],
        in_specs=[vmem] + [hbm] * 3 + [pl.BlockSpec(memory_space=pltpu.SMEM)] + [hbm] * 4,
        out_specs=[hbm] * 8 + [vmem] * 2,
        scratch_shapes=[
            pltpu.VMEM(array.shape, array.dtype) for array in (tconv_weight, kernels, grad_decoded)
        ]
        + [
            pltpu.VMEM((slab, width), low),
            pltpu.VMEM(down.shape, low),
            pltpu.VMEM((slab, units), low),
            pltpu.VMEM(up.shape, low),
        ]
        + [pltpu.VMEM(shape, low) for shape in kept.values()]
        + [pltpu.VMEM((ROWS, CH), wide), pltpu.VMEM((8, CH), wide)]
        + [field] * 4
        + [pltpu.VMEM((9, 4 * CH, PAIR), low)] * 2
        + [pltpu.VMEM((9, PAIR, 4 * CH), low)] * 2
        + [plane] * 3
        + [pltpu.VMEM((PAIR, ROWS), low)] * 2
        + [
            pltpu.VMEM((slab, tconv_weight.shape[1]), low),
            pltpu.VMEM(tapped.shape, low),
            pltpu.VMEM(tapped.shape, low),
            pltpu.VMEM(tapped.shape, low),
            pltpu.VMEM((4, 8, CH), wide),
            pltpu.VMEM((4, 8, CH), wide),
            dma((7,)),
            dma((10,)),
            dma((10,)),
            dma((10,)),
        ],
        name="decoder_section",
        compiler_params=pltpu.CompilerParams(
            collective_id=1, has_side_effects=True, vmem_limit_bytes=60 * 2**20
        ),
    )(tapped, tconv_weight, kernels, grad_decoded, crop_shape, grad_out, down, slope, up)
    return dict(zip(names, results))


def widen_rows(src, dst, tile=64):
    @pl.loop(0, src.shape[0] // tile)
    def _(step):
        at = rows_at(step * tile, tile)
        dst[at, :] = src[at, :].astype(jnp.float32)


def finish_kernel(count, *refs):
    sources, refs = refs[:count], refs[count:]
    passed, small, refs = refs[:3], refs[3], refs[4:]
    targets, refs = refs[:count], refs[count:]
    handed, smalls, refs = refs[:3], refs[3:7], refs[7:]
    lows, wides, refs = refs[:count], refs[count : 2 * count], refs[2 * count :]
    held, refs = refs[:3], refs[3:]
    load_sem, store_sem, pass_sem = refs
    loads, stores = [], []
    for index in range(count):
        loads.append(pltpu.make_async_copy(sources[index], lows[index], load_sem.at[index]))
    passes = [
        pltpu.make_async_copy(passed[index], held[index], pass_sem.at[index])
        for index in range(3)
    ]
    for copy in passes + loads:
        copy.start()
    gains, shifts, qv_bias, up_bias = smalls
    width = small.shape[1]
    gains[0:1, :] = small[0:1, :]
    gains[1:2, :] = small[2:3, :]
    shifts[0:1, :] = small[1:2, :]
    shifts[1:4, :] = small[3:6, :]
    qv_bias[0:1, :] = small[6:7, : width // 2]
    qv_bias[1:2, :] = small[6:7, width // 2 :]
    up_bias[:width] = small[7, :]
    up_bias[width:] = small[8, :]

    def store(src, dst):
        copy = pltpu.make_async_copy(src, dst, store_sem.at[len(stores)])
        copy.start()
        stores.append(copy)

    for index in range(3):
        passes[index].wait()
        store(held[index], handed[index])
    for index in range(count):
        src, dst, wide, low = sources[index], targets[index], wides[index], lows[index]
        loads[index].wait()
        if dst.shape == src.shape and len(src.shape) == 2:
            widen_rows(low, wide)
            store(wide, dst)
        elif dst.shape == src.shape:
            for part in range(src.shape[0]):
                widen_rows(low.at[part], wide.at[part])
                store(wide.at[part], dst.at[part])
        elif len(src.shape) == 3:
            for part in range(src.shape[0]):
                widen_rows(low.at[part], wide.at[part])
                rows, columns = src.shape[1:]
                across = dst.shape[1] // columns
                store(
                    wide.at[part],
                    dst.at[
                        pl.ds(part // across * rows, rows),
                        pl.ds(part % across * columns, columns),
                    ],
                )
        elif len(dst.shape) == 2:
            widen_rows(low, wide)
            rows, columns = dst.shape[0], src.shape[1]
            for part in range(2):
                store(
                    wide.at[pl.ds(part * rows, rows)], dst.at[:, pl.ds(part * columns, columns)]
                )
        else:
            kinds, outs, columns = dst.shape
            ins = src.shape[1]
            for kind in range(kinds):
                for tap in range(columns // ins):
                    at = (kind * PADDED_TAPS + tap) * outs
                    wide[kind, :, tap * ins : (tap + 1) * ins] = low[at : at + outs, :].astype(
                        jnp.float32
                    )
                store(wide.at[kind], dst.at[kind])
    for copy in stores:
        copy.wait()


def finish_section(totals, passed, small):
    wide = jnp.float32
    local = totals["qkv"].shape[2]
    width = totals["qkv"].shape[1]
    units = totals["up"].shape[2] * 4
    shapes = {
        "qkv": totals["qkv"].shape,
        "out": (local, width),
        "up": (width, units),
        "down": (units, width),
        "tconv": totals["tconv"].shape,
        "kernels": (2, 64, 27 * CH),
    }
    count = len(shapes)
    sources = [totals[name] for name in shapes]
    kept = [
        shapes[name] if name == "kernels" else totals[name].shape for name in shapes
    ]
    vmem = pl.BlockSpec(memory_space=pltpu.VMEM)
    hbm = pl.BlockSpec(memory_space=pl.ANY)
    results = pl.pallas_call(
        functools.partial(finish_kernel, count),
        out_shape=[jax.ShapeDtypeStruct(shape, wide) for shape in shapes.values()]
        + [jax.ShapeDtypeStruct(array.shape, array.dtype) for array in passed]
        + [
            jax.ShapeDtypeStruct(shape, wide)
            for shape in ((2, width), (4, width), (2, local), (units,))
        ],
        in_specs=[hbm] * (count + 3) + [vmem],
        out_specs=[hbm] * (count + 3) + [vmem] * 4,
        scratch_shapes=[pltpu.VMEM(array.shape, array.dtype) for array in sources]
        + [pltpu.VMEM(shape, wide) for shape in kept]
        + [pltpu.VMEM(array.shape, array.dtype) for array in passed]
        + [
            pltpu.SemaphoreType.DMA((count,)),
            pltpu.SemaphoreType.DMA((24,)),
            pltpu.SemaphoreType.DMA((3,)),
        ],
        name="finish",
        compiler_params=pltpu.CompilerParams(vmem_limit_bytes=60 * 2**20),
    )(*sources, *passed, small)
    return dict(zip(shapes, results)), results[count : count + 3], results[count + 3 :]


def extents(crop):
    depth = jnp.where(crop == 0, SIDE * 3 // 4, jnp.where(crop == 1, SIDE // 2, SIDE))
    side = jnp.where(crop == 0, SIDE * 3 // 4, SIDE)
    return depth, side


GELU_RATE = 0.7978845608028654
GELU_CUBE = 0.044715


def rows_sum(value):
    return jnp.sum(value, axis=0, keepdims=True)


def lane_mean(value):
    return jnp.mean(value, axis=-1, keepdims=True)


def centred(value):
    centre = value - lane_mean(value)
    return centre, lax.rsqrt(lane_mean(centre * centre) + 1e-06)


def head_only(pair, head):
    lane = lax.broadcasted_iota(jnp.int32, pair.shape, 1)
    return jnp.where((lane // HD) == head, pair, jnp.zeros_like(pair))


def forward_kernel(
    block_in,
    gains,
    shifts,
    qkv_hbm,
    qv_bias,
    out_hbm,
    up_hbm,
    up_bias,
    down_hbm,
    crop_shape,
    normed_one_hbm,
    query_hbm,
    key_value_hbm,
    probs_hbm,
    mixed_hbm,
    middle_hbm,
    normed_two_hbm,
    active_hbm,
    slope_hbm,
    tapped,
    qkv,
    out_weight,
    up,
    down,
    normed_one,
    query,
    key_value,
    probs,
    mixed,
    middle,
    normed_two,
    active,
    slope,
    values_turned,
    part_mine,
    part_from,
    feed_mine,
    feed_from,
    load_sem,
    store_sem,
    send,
    recv,
):
    dp, blk, tensor, near, far, first = place()
    core, cross, beside, side, over = peers()
    low = jnp.bfloat16
    items, slab, width = block_in.shape
    local = query.shape[1]
    units = active.shape[1]

    loads = []
    for index, (src, dst) in enumerate(
        [(qkv_hbm, qkv), (out_hbm, out_weight), (up_hbm, up), (down_hbm, down)]
    ):
        copy = pltpu.make_async_copy(src, dst, load_sem.at[index])
        copy.start()
        loads.append(copy)
    greet([core, cross])
    copies = []
    stores = []

    def start(index, src, dst, device):
        copy = remote(src, dst, send.at[index], recv.at[index], device)
        copy.start()
        copies.append(copy)
        return copy

    def store(src, dst):
        copy = pltpu.make_async_copy(src, dst, store_sem.at[len(stores)])
        copy.start()
        stores.append(copy)

    tile = 64

    for item in range(items):

        @pl.loop(0, slab // tile)
        def _(step):
            value = block_in[item, rows_at(step * tile, tile), :].astype(jnp.float32)
            centre, scale = centred(value)
            normed = centre * scale * gains[0:1, :] + shifts[0:1, :]
            normed_one[rows_at(item * slab + step * tile, tile), :] = normed.astype(low)

    store(normed_one, normed_one_hbm)
    loads[0].wait()
    others = [lax.rem(tensor + step, items) for step in range(items)]
    kv_copies = []
    for place_at, item in enumerate(others):
        rows = rows_at(item * slab, slab)
        for c in range(2):
            project = dot(normed_one[rows, :], qkv[1 + c])
            if c == 1:
                project = project + qv_bias[1:2, :]
            key_value[item, c, :slab, :] = project.astype(low)
        kv_copies.append(
            start(
                place_at,
                key_value.at[item, :, pl.ds(0, slab), :],
                key_value.at[item, :, pl.ds(slab, slab), :],
                core,
            )
        )
    for item in others:
        rows = rows_at(item * slab, slab)
        query[rows, :] = (dot(normed_one[rows, :], qkv[0]) + qv_bias[0:1, :]).astype(low)
    store(query, query_hbm)

    part_copies = []
    for place_at, item in enumerate(others):
        rows = rows_at(item * slab, slab)
        kv_copies[place_at].wait_recv()
        values_turned[...] = key_value[item, 1].astype(jnp.float32).T.astype(low)
        depth_end, side_end = extents(crop_shape[item])
        key = lax.broadcasted_iota(jnp.int32, (probs.shape[2], slab), 0)
        patch = jnp.where(key < slab, blk * slab + key, (1 - blk) * slab + key - slab)
        keep = (
            (patch // (SIDE * SIDE) < depth_end)
            & (lax.rem(patch // SIDE, SIDE) < side_end)
            & (lax.rem(patch, SIDE) < side_end)
        )
        for pair in range(local // 128):
            lanes = slice(pair * 128, (pair + 1) * 128)
            keys = key_value[item, 0, :, lanes]
            asked = query[rows, lanes] * jnp.asarray(HD ** (-0.5), low)
            turned = []
            for head in range(2):
                scores = nt_dot(keys, head_only(asked, head))
                scores = jnp.where(keep, scores, -1000000000.0)
                weights = jnp.exp(scores - jnp.max(scores, axis=0, keepdims=True))
                prob = (weights * (1.0 / rows_sum(weights))).astype(low)
                probs[item, 2 * pair + head] = prob
                at = pair * 128 + head * HD
                turned.append(dot(values_turned[at : at + HD, :], prob))
            mixed[rows, lanes] = jnp.concatenate(turned, axis=0).T.astype(low)
        store(probs.at[item], probs_hbm.at[item])
        if place_at == 0:
            loads[1].wait()
        part_mine[item] = dot(mixed[rows, :], out_weight[...]).astype(low)
        part_copies.append(start(2 + place_at, part_mine.at[item], part_from.at[item], cross))
    store(key_value, key_value_hbm)
    store(mixed, mixed_hbm)

    for place_at, item in enumerate(others[1:] + others[:1]):
        if place_at == 0:
            loads[2].wait()
        part_copies[place_at].wait_recv()

        @pl.loop(0, slab // tile)
        def _(step):
            at = rows_at(step * tile, tile)
            attended = part_mine[item, at, :].astype(jnp.float32) + part_from[item, at, :].astype(
                jnp.float32
            )
            value = block_in[item, at, :].astype(jnp.float32) + (attended + shifts[2:3, :])
            middle[item, at, :] = value
            centre, scale = centred(value)
            normed = centre * scale * gains[1:2, :] + shifts[1:2, :]
            normed_two[rows_at(item * slab + step * tile, tile), :] = normed.astype(low)

        rows = rows_at(item * slab, slab)

        @pl.loop(0, units // 256)
        def _(step):
            lanes = pl.ds(pl.multiple_of(step * 256, 256), 256)
            value = dot(normed_two[rows, :], up[:, lanes]) + up_bias[lanes].reshape(1, -1)
            square = value * value
            bent = jnp.tanh(GELU_RATE * value * (1.0 + GELU_CUBE * square))
            half = 0.5 * (1.0 + bent)
            active[rows, lanes] = (value * half).astype(low)
            inner = GELU_RATE * (1.0 + 3.0 * GELU_CUBE * square)
            slope[rows, lanes] = (half + 0.5 * value * (1.0 - bent * bent) * inner).astype(low)

        if place_at == 0:
            loads[3].wait()

        @pl.loop(0, width // 256)
        def _(step):
            lanes = pl.ds(pl.multiple_of(step * 256, 256), 256)
            feed_mine[item, :, lanes] = dot(active[rows, :], down[:, lanes]).astype(low)

        if place_at == 0:
            feed = start(4, feed_mine.at[item], feed_from, cross)

    store(middle, middle_hbm)
    store(normed_two, normed_two_hbm)
    store(active, active_hbm)
    store(slope, slope_hbm)
    feed.wait_recv()

    @pl.loop(0, slab // tile)
    def _(step):
        at = rows_at(step * tile, tile)
        fed = feed_mine[tensor, at, :].astype(jnp.float32) + feed_from[at, :].astype(jnp.float32)
        tapped[at, :] = (middle[tensor, at, :] + (fed + shifts[3:4, :])).astype(low)

    for copy in copies:
        copy.wait_send()
    for copy in stores:
        copy.wait()


def forward_section(
    block_in, gains, shifts, qkv, qv_bias, out_weight, up, up_bias, down, crop_shape
):
    low = jnp.bfloat16
    items, slab, width = block_in.shape
    tokens = items * slab
    local = qkv.shape[2]
    units = up.shape[1]
    heads = local // HD
    patches = 2 * slab
    vmem = pl.BlockSpec(memory_space=pltpu.VMEM)
    hbm = pl.BlockSpec(memory_space=pl.ANY)
    kept = [
        ((tokens, width), low),
        ((tokens, local), low),
        ((items, 2, patches, local), low),
        ((items, heads, patches, slab), low),
        ((tokens, local), low),
        ((items, slab, width), jnp.float32),
        ((tokens, width), low),
        ((tokens, units), low),
        ((tokens, units), low),
    ]
    return pl.pallas_call(
        forward_kernel,
        out_shape=[jax.ShapeDtypeStruct(*one) for one in kept]
        + [jax.ShapeDtypeStruct((slab, width), low)],
        in_specs=[vmem, vmem, vmem, hbm, vmem, hbm, hbm, vmem, hbm]
        + [pl.BlockSpec(memory_space=pltpu.SMEM)],
        out_specs=[hbm] * 9 + [vmem],
        scratch_shapes=[pltpu.VMEM(one.shape, low) for one in (qkv, out_weight, up, down)]
        + [pltpu.VMEM(*one) for one in kept]
        + [
            pltpu.VMEM((local, patches), low),
            pltpu.VMEM(block_in.shape, low),
            pltpu.VMEM(block_in.shape, low),
            pltpu.VMEM(block_in.shape, low),
            pltpu.VMEM((slab, width), low),
            pltpu.SemaphoreType.DMA((4,)),
            pltpu.SemaphoreType.DMA((16,)),
            pltpu.SemaphoreType.DMA((5,)),
            pltpu.SemaphoreType.DMA((5,)),
        ],
        name="forward_section",
        compiler_params=pltpu.CompilerParams(
            collective_id=2, has_side_effects=True, vmem_limit_bytes=60 * 2**20
        ),
    )(block_in, gains, shifts, qkv, qv_bias, out_weight, up, up_bias, down, crop_shape)


def fold(value):
    rows, width = value.shape
    return jnp.sum(value.reshape(rows // 8, 8, width), axis=0)


def add_into(target, target_at, parts, rows, tile):
    @pl.loop(0, rows // tile)
    def _(step):
        at = step * tile
        total = None
        for ref, offset in parts:
            piece = ref[rows_at(offset + at, tile), :].astype(jnp.float32)
            total = piece if total is None else total + piece
        target[rows_at(target_at + at, tile), :] = total.astype(jnp.bfloat16)


COPIES = 10


class Sum:
    def __init__(self, refs, name, index, path, own, total, full=None):
        self.own, self.total, self.full = own, total, full
        self.held = [getattr(refs, name + end) for end in ("_core", "_first", "_second", "_third")]
        self.part = getattr(refs, name + "_part")
        if full is not None:
            self.both = getattr(refs, name + "_both")
            self.cross_part = getattr(refs, name + "_cross")
        self.send, self.recv = refs.sum_send.at[index], refs.sum_recv.at[index]
        self.local = refs.sum_local.at[index]
        rows = total.shape[0]
        self.half, self.piece = rows // 2, rows // 16
        dp, self.blk, self.tensor, near, far, first = place()
        self.core, self.cross, beside, side, over = peers()
        self.stages = [
            {"y": (beside, near), "s": (side, lax.rem(far, 2)), "o": (over, far // 2)}[one]
            for one in path
        ]
        self.at = [self.blk * self.half]
        for stage, (device, bit) in enumerate(self.stages):
            self.at.append(self.at[-1] + bit * (rows >> (stage + 2)))
        self.sizes = [rows >> (stage + 1) for stage in range(4)]
        self.waiting = []

    def start(self, index, src, dst, device):
        copy = remote(src, dst, self.send.at[index], self.recv.at[index], device)
        copy.start()
        self.waiting.append(copy)
        self.last = copy

    def sA(self):
        give = rows_at((1 - self.blk) * self.half, self.half)
        self.start(0, self.full.at[:, give], self.both, self.core)

    def sB(self):
        self.last.wait_recv()
        for which in (1 - self.tensor, self.tensor):
            add_into(
                self.both.at[which], 0, [(self.both.at[which], 0), (self.own.at[which], 0)],
                self.half, self.piece,
            )
        self.start(1, self.both.at[1 - self.tensor], self.cross_part, self.cross)

    def s0(self):
        give = rows_at((1 - self.blk) * self.half, self.half)
        self.start(0, self.own.at[give], self.held[0], self.core)

    def narrow(self, stage):
        device, bit = self.stages[stage]
        give = rows_at((1 - bit) * self.sizes[stage + 1], self.sizes[stage + 1])
        self.start(2 + stage, self.held[stage].at[give], self.held[stage + 1], device)

    def gather(self, stage, target):
        self.last.wait_recv()
        size = self.sizes[stage]
        kept = (self.held[stage - 1], self.stages[stage - 1][1] * size)
        add_into(target, 0, [(self.held[stage], 0), kept], size, self.piece)

    def s1(self):
        self.last.wait_recv()
        parts = [(self.held[0], 0), (self.own, self.blk * self.half)]
        if self.full is not None:
            parts = [(self.both.at[self.tensor], 0), (self.cross_part, 0)]
        add_into(self.held[0], 0, parts, self.half, self.piece)
        self.narrow(0)

    def s2(self):
        self.gather(1, self.held[1])
        self.narrow(1)

    def s2b(self):
        self.gather(2, self.held[2])
        self.narrow(2)

    def s3(self):
        self.gather(3, self.part)
        where = self.total.at[rows_at(self.at[3], self.piece)]
        self.keep = pltpu.make_async_copy(self.part, where, self.local)
        self.keep.start()
        self.start(5, self.part, where, self.stages[2][0])

    def spread(self, index, at, size, device):
        self.last.wait_recv()
        where = self.total.at[rows_at(at, size)]
        self.start(index, where, where, device)

    def s3b(self):
        self.keep.wait()
        self.spread(6, self.at[2], self.sizes[2], self.stages[1][0])

    def s4(self):
        self.spread(7, self.at[1], self.sizes[1], self.stages[0][0])

    def s5(self):
        self.spread(8, self.at[0], self.sizes[0], self.core)

    def s6(self):
        self.last.wait_recv()
        for copy in self.waiting:
            copy.wait_send()


def sum_scratch(rows, columns):
    low = jnp.bfloat16
    shares = {"_core": 2, "_first": 4, "_second": 8, "_third": 16, "_part": 16}
    return {end: pltpu.VMEM((rows // share, columns), low) for end, share in shares.items()}


def norm_back(value, grad, gain):
    centre, scale = centred(value)
    normed = centre * scale
    scaled = grad * gain
    inner = lane_mean(scaled * normed)
    return scale * (scaled - lane_mean(scaled) - normed * inner), normed


def backward_kernel(layout, *refs):
    r = types.SimpleNamespace(**dict(zip(layout, refs)))
    dp, blk, tensor, near, far, first = place()
    core, cross, beside, side, over = peers()
    low = jnp.bfloat16
    items, slab, width = r.grad_out.shape
    local = r.query.shape[1]
    units = r.active.shape[1]
    pairs = local // 128
    tile = 64
    half_width = width // 2

    loads = {}
    own_rows = rows_at(tensor * slab, slab)
    landing = {
        "two_own": r.two_mine.at[tensor],
        "ddown_own": r.ddown.at[own_rows],
        "dhidden_own": r.dhidden.at[own_rows],
    }
    for index, name in enumerate(LOADED):
        target = landing[name] if name in landing else getattr(r, name)
        copy = pltpu.make_async_copy(getattr(r, name + "_hbm"), target, r.load_sem.at[index])
        copy.start()
        loads[name] = copy
    keep_full = {}
    for index, name in enumerate(("kernels", "tconv")):
        full = getattr(r, "grad_" + name + "_hbm")
        rows = full.shape[1] // 2
        copy = pltpu.make_async_copy(
            full.at[:, rows_at(blk * rows, rows)],
            getattr(r, "own_" + name),
            r.load_sem.at[len(LOADED) + index],
        )
        copy.start()
        keep_full[name] = copy
    greet([core, cross, beside, side, over])
    copies = []

    def start(index, src, dst, device):
        copy = remote(src, dst, r.send.at[index], r.recv.at[index], device)
        copy.start()
        copies.append(copy)
        return copy

    sums = {}
    for h in range(4):
        sums["d%d" % h] = ("down%d" % h, r.own_down.at[h], r.total_down.at[h])
        sums["u%d" % h] = ("up%d" % h, r.own_up.at[h], r.total_up.at[h])
    sums["o"] = ("out", r.own_out, r.total_out)
    for c in range(3):
        sums["q%d" % c] = ("qkv%d" % c, r.own_qkv.at[c], r.total_qkv.at[c])
    sums["k"] = ("kernels", r.own_kernels, r.total_kernels, r.grad_kernels_hbm)
    sums["t"] = ("tconv", r.own_tconv, r.total_tconv, r.grad_tconv_hbm)
    sums = {
        name: Sum(r, one[0], index, PATHS[name], *one[1:])
        for index, (name, one) in enumerate(sums.items())
    }

    def rows_of(item):
        return rows_at(item * slab, slab)

    def lanes_of(step, size=256):
        return pl.ds(pl.multiple_of(step * size, size), size)

    r.small[...] = jnp.zeros_like(r.small)

    def dout_rows(item, at):
        return r.grad_out[item, at, :].astype(jnp.float32) + r.dtap[item, at, :].astype(
            jnp.float32
        )

    zero = jnp.zeros((8, width), jnp.float32)

    sent = {}
    waited = set()

    def loaded(*names):
        for name in names:
            if name not in waited:
                loads[name].wait()
                waited.add(name)

    own, other = tensor, 1 - tensor

    def take_own():
        loaded("two_own", "shift_own")
        r.small[5:6, :] += rows_sum(r.shift_own[...])
        sent["dn0"] = start(0, r.two_mine.at[own], r.two_from.at[own], cross)

    def shade_other():
        def shade(step, total):
            value = dout_rows(other, rows_at(step * tile, tile)).astype(low)
            r.ddown[rows_at(other * slab + step * tile, tile), :] = value
            return total + fold(value.astype(jnp.float32))

        total = lax.fori_loop(0, slab // tile, shade, zero)
        r.small[5:6, :] += rows_sum(total)

    def feed_back():
        item = other
        rows = rows_of(item)
        loaded("down", "slope")

        @pl.loop(0, units // 256)
        def _(step):
            lanes = lanes_of(step)
            dactive = nt_dot(r.ddown[rows, :], r.down[lanes, :])
            value = (dactive * r.slope[rows, lanes].astype(jnp.float32)).astype(low)
            r.dhidden[rows, lanes] = value
            summed = rows_sum(fold(value.astype(jnp.float32)))
            r.bias_sum[0:1, lanes] = summed

        loaded("up")

        @pl.loop(0, width // 256)
        def _(step):
            value = nt_dot(r.dhidden[rows, :], r.up[lanes_of(step), :])
            r.two_mine[item, :, lanes_of(step)] = value.astype(low)

        sent["dn1"] = start(1, r.two_mine.at[item], r.two_from.at[item], cross)

    def grad_down(h):
        loaded("active", "ddown_own")

        @pl.loop(0, units // 2 // 256)
        def _(step):
            lanes = pl.ds(pl.multiple_of(h * (units // 2) + step * 256, 256), 256)
            value = tn_dot(r.active[:, lanes], r.ddown[...]).astype(low)
            for part in range(2):
                columns = slice(part * half_width, (part + 1) * half_width)
                r.own_down[2 * h + part, lanes_of(step), :] = value[:, columns]

    def grad_up(h):
        loaded("normed_two", "dhidden_own")

        @pl.loop(0, width // 256)
        def _(step):
            right = r.dhidden[:, h * (units // 2) : (h + 1) * (units // 2)]
            value = tn_dot(r.normed_two[:, lanes_of(step)], right).astype(low)
            for part in range(2):
                columns = slice(part * (units // 4), (part + 1) * (units // 4))
                r.own_up[2 * h + part, lanes_of(step), :] = value[:, columns]

    def middle_back(index):
        item = (other, own)[index]
        loaded("middle")
        sent["dn%d" % index].wait_recv()

        def back(step, totals):
            at = rows_at(step * tile, tile)
            grad = r.two_mine[item, at, :].astype(jnp.float32) + r.two_from[item, at, :].astype(
                jnp.float32
            )
            dvalue, normed = norm_back(r.middle[item, at, :], grad, r.gains[1:2, :])
            dmiddle = dout_rows(item, at) + dvalue
            r.dmiddle[item, at, :] = dmiddle
            dattn = dmiddle.astype(low)
            r.dattn[rows_at(item * slab + step * tile, tile), :] = dattn
            return (
                totals[0] + fold(grad * normed),
                totals[1] + fold(grad),
                totals[2] + fold(dattn.astype(jnp.float32)),
            )

        totals = lax.fori_loop(0, slab // tile, back, (zero, zero, zero))
        for row, total in zip((2, 3, 4), totals):
            r.small[row : row + 1, :] += rows_sum(total)

    def attention_back(index):
        item = (other, own)[index]
        loaded("out_weight", "key_value", "query", "probs")
        rows = rows_of(item)
        r.keys_turned[...] = r.key_value[item, 0].astype(jnp.float32).T.astype(low)
        r.dmixed[...] = nt_dot(r.dattn[rows, :], r.out_weight[...]).astype(low)
        scale = HD ** (-0.5)
        for pair in range(pairs):
            lanes = slice(pair * 128, (pair + 1) * 128)
            values = r.key_value[item, 1, :, lanes]
            asked = r.query[rows, lanes]
            dmixed = r.dmixed[:, lanes]
            dkeys = dvalues = None
            turned = []
            for head in range(2):
                prob = r.probs[item, 2 * pair + head]
                dmixed_head = head_only(dmixed, head)
                dprob = nt_dot(values, dmixed_head)
                wide = prob.astype(jnp.float32)
                inner = rows_sum(wide * dprob)
                dscores = (wide * (dprob - inner)).astype(low)
                key_part = dot(dscores, head_only(asked, head))
                value_part = dot(prob, dmixed_head)
                dkeys = key_part if dkeys is None else dkeys + key_part
                dvalues = value_part if dvalues is None else dvalues + value_part
                at = pair * 128 + head * HD
                turned.append(dot(r.keys_turned[at : at + HD, :], dscores))
            r.dproject[0, rows, lanes] = (jnp.concatenate(turned, axis=0).T * scale).astype(low)
            dkeys = (dkeys * scale).astype(low)
            dvalues = dvalues.astype(low)
            r.dproject[1, rows, lanes] = dkeys[:slab]
            r.dproject[2, rows, lanes] = dvalues[:slab]
            r.give_kv[item, 0, :, lanes] = dkeys[slab:]
            r.give_kv[item, 1, :, lanes] = dvalues[slab:]
        sent["kv%d" % index] = start(2 + index, r.give_kv.at[item], r.got_kv.at[item], core)

    def grad_out_weight():
        loaded("mixed")
        for h in range(2):
            value = tn_dot(r.mixed[...], r.dattn[:, h * half_width : (h + 1) * half_width])
            r.own_out[h * local : (h + 1) * local, :] = value.astype(low)

    def join_heads():
        for index, item in enumerate((other, own)):
            sent["kv%d" % index].wait_recv()
            rows = rows_of(item)
            for c in range(2):
                value = r.dproject[1 + c, rows, :].astype(jnp.float32)
                value = value + r.got_kv[item, c].astype(jnp.float32)
                r.dproject[1 + c, rows, :] = value.astype(low)

    def project_back(index):
        item = (other, own)[index]
        loaded("qkv")
        rows = rows_of(item)

        @pl.loop(0, width // 256)
        def _(step):
            lanes = lanes_of(step)
            value = None
            for c in range(3):
                part = nt_dot(r.dproject[c, rows, :], r.qkv[c, lanes, :])
                value = part if value is None else value + part
            r.one_mine[item, :, lanes] = value.astype(low)

        sent["pn%d" % index] = start(4 + index, r.one_mine.at[item], r.one_from.at[item], cross)

    def grad_qkv(c):
        loaded("normed_one")
        r.own_qkv[c] = tn_dot(r.normed_one[...], r.dproject[c]).astype(low)

    def bias_sums():
        for c in (0, 2):
            value = rows_sum(fold(r.dproject[c].astype(jnp.float32)))
            r.small[6:7, (c // 2) * local : (c // 2 + 1) * local] = value
        loaded("bias_own")
        total = r.bias_sum[0:1, :] + rows_sum(r.bias_own[...])
        r.small[7:8, :] = total[:, :width]
        r.small[8:9, :] = total[:, width:]

    def input_back(index):
        item = (own, other)[index]
        loaded("block_in")
        sent["pn%d" % index].wait_recv()

        def back(step, totals):
            at = rows_at(step * tile, tile)
            grad = r.one_mine[item, at, :].astype(jnp.float32) + r.one_from[item, at, :].astype(
                jnp.float32
            )
            value = r.block_in[item, at, :].astype(jnp.float32)
            dvalue, normed = norm_back(value, grad, r.gains[0:1, :])
            r.grad_input[item, at, :] = (r.dmiddle[item, at, :] + dvalue).astype(low)
            return totals[0] + fold(grad * normed), totals[1] + fold(grad)

        totals = lax.fori_loop(0, slab // tile, back, (zero, zero))
        for row, total in zip((0, 1), totals):
            r.small[row : row + 1, :] += rows_sum(total)

    def small_step(index):
        if index > 0:
            sent["small"].wait_recv()
            r.small_sum[index] = r.small_sum[index - 1] + r.small_from[index - 1]
        else:
            r.small_sum[0] = r.small[...]
        if index < 4:
            device = (core, beside, side, over)[index]
            sent["small"] = start(
                6 + index, r.small_sum.at[index], r.small_from.at[index], device
            )
        else:
            r.small_total[...] = r.small_sum[4]

    tasks = {
        "sh0": take_own,
        "sh1": shade_other,
        "ffn0": lambda: None,
        "ffn1": feed_back,
        "kv": join_heads,
        "og": grad_out_weight,
        "bias": bias_sums,
    }
    for index in range(2):
        for name, work in (
            ("gd", grad_down),
            ("gu", grad_up),
            ("ln", middle_back),
            ("at", attention_back),
            ("p", project_back),
            ("f", input_back),
        ):
            tasks[name + str(index)] = functools.partial(work, index)
    for c in range(3):
        tasks["gq" + str(c)] = functools.partial(grad_qkv, c)
    for index in range(5):
        tasks["sm" + str(index)] = functools.partial(small_step, index)

    def full_step(name, unit):
        keep_full[{"k": "kernels", "t": "tconv"}[name]].wait()
        unit.sB()

    for name, unit in sums.items():
        for step in ("sA", "sB", "s0", "s1", "s2", "s2b", "s3", "s3b", "s4", "s5", "s6"):
            tasks[name + "." + step] = getattr(unit, step)
        if unit.full is not None:
            tasks[name + ".sB"] = functools.partial(full_step, name, unit)
    for name in ORDER:
        tasks[name]()
    for copy in copies:
        copy.wait_send()


PATHS = {
    "d2": "yso",
    "d3": "yso",
    "u2": "yso",
    "u3": "yso",
    "t": "yso",
    "k": "yso",
    "d0": "yso",
    "d1": "yso",
    "u0": "syo",
    "u1": "yso",
    "o": "yso",
    "q2": "syo",
    "q1": "yso",
    "q0": "yso",
}

ORDER = (
    "k.sA", "sh0", "sh1", "gd0", "d1.s0", "gd1", "d2.s0", "k.sB", "d1.s1", "d3.s0", "d0.s0", "ffn0",
    "ffn1", "d3.s1", "gu0", "u0.s0", "u1.s0", "d2.s1", "d0.s1", "d1.s2", "gu1", "u0.s1", "u2.s0", "ln0",
    "u1.s1", "d3.s2", "d1.s2b", "u3.s0", "at0", "d2.s2", "u2.s1", "u3.s1", "u0.s2", "t.sA", "d3.s2b", "d0.s2",
    "d1.s3", "k.s1", "d2.s2b", "t.sB", "u1.s2", "d3.s3", "d0.s2b", "d1.s3b", "u2.s2", "d2.s3", "u1.s2b", "d3.s3b",
    "u3.s2", "ln1", "d0.s3", "d1.s4", "u0.s2b", "at1", "u1.s3", "og", "o.s0", "d3.s4", "d2.s3b", "u2.s2b",
    "k.s2", "u3.s2b", "kv", "bias", "gq2", "t.s1", "d1.s5", "u0.s3", "gq0", "u1.s3b", "p0", "d2.s4",
    "gq1", "d3.s5", "p1", "u2.s3", "q1.s0", "q0.s0", "d0.s3b", "k.s2b", "q2.s0", "d1.s6", "o.s1", "d3.s6",
    "u3.s3", "q1.s1", "u0.s3b", "t.s2", "q0.s1", "q2.s1", "u1.s4", "u2.s3b", "d2.s5", "d0.s4", "k.s3", "d2.s6",
    "f0", "o.s2", "t.s2b", "u3.s3b", "q1.s2", "q2.s2", "u0.s4", "u2.s4", "k.s3b", "f1", "sm0", "t.s3",
    "o.s2b", "q0.s2", "u1.s5", "u3.s4", "sm1", "q1.s2b", "u1.s6", "d0.s5", "q2.s2b", "u0.s5", "d0.s6", "u0.s6",
    "k.s4", "u2.s5", "t.s3b", "o.s3", "u2.s6", "q0.s2b", "u3.s5", "q1.s3", "sm2", "q2.s3", "u3.s6", "t.s4",
    "o.s3b", "q0.s3", "k.s5", "q1.s3b", "sm3", "q2.s3b", "k.s6", "o.s4", "t.s5", "sm4", "q0.s3b", "q1.s4",
    "q2.s4", "t.s6", "q0.s4", "o.s5", "o.s6", "q2.s5", "q1.s5", "q2.s6", "q1.s6", "q0.s5", "q0.s6",
)

LANDED = ("two_own", "ddown_own", "dhidden_own")
LOADED = (
    "two_own",
    "shift_own",
    "ddown_own",
    "active",
    "down",
    "slope",
    "up",
    "dhidden_own",
    "normed_two",
    "middle",
    "out_weight",
    "key_value",
    "query",
    "probs",
    "mixed",
    "qkv",
    "normed_one",
    "block_in",
    "bias_own",
)


def backward_section(arrays):
    low = jnp.bfloat16
    wide = jnp.float32
    items, slab, width = arrays["grad_out"].shape
    tokens = items * slab
    local = arrays["qkv"].shape[2]
    units = arrays["down"].shape[0]
    patches = arrays["key_value"].shape[2]
    kernel_rows = arrays["grad_kernels"].shape[1]
    near = ["grad_out", "dtap", "gains"]
    distant = list(LOADED) + ["grad_kernels", "grad_tconv"]
    totals = {
        "down": (4, units // 2, width // 2),
        "up": (4, width, units // 4),
        "out": (2 * local, width // 2),
        "qkv": (3, width, local),
        "kernels": (kernel_rows, CH),
        "tconv": arrays["grad_tconv"].shape[1:],
    }
    scratch = {
        name: pltpu.VMEM(arrays[name].shape, arrays[name].dtype)
        for name in LOADED
        if name not in LANDED
    }
    for name, shape in totals.items():
        full = name in ("kernels", "tconv")
        rows, columns = shape[-2:]
        scratch["own_" + name] = pltpu.VMEM((2, rows // 2, columns) if full else shape, low)
        labels = [name] if len(shape) == 2 else [name + str(part) for part in range(shape[0])]
        for label in labels:
            for end, one in sum_scratch(rows, columns).items():
                scratch[label + end] = one
            if full:
                scratch[label + "_both"] = pltpu.VMEM((2, rows // 2, columns), low)
                scratch[label + "_cross"] = pltpu.VMEM((rows // 2, columns), low)
    block = (items, slab, width)
    for name, shape, dtype in (
        ("ddown", (tokens, width), low),
        ("dhidden", (tokens, units), low),
        ("bias_sum", (8, units), wide),
        ("two_mine", block, low),
        ("two_from", block, low),
        ("dmiddle", block, wide),
        ("dattn", (tokens, width), low),
        ("dmixed", (slab, local), low),
        ("keys_turned", (local, patches), low),
        ("give_kv", (items, 2, slab, local), low),
        ("got_kv", (items, 2, slab, local), low),
        ("dproject", (3, tokens, local), low),
        ("one_mine", block, low),
        ("one_from", block, low),
        ("small", (16, width), wide),
        ("small_sum", (5, 16, width), wide),
        ("small_from", (4, 16, width), wide),
    ):
        scratch[name] = pltpu.VMEM(shape, dtype)
    dma = pltpu.SemaphoreType.DMA
    scratch["load_sem"] = dma((len(LOADED) + 2,))
    scratch["send"] = dma((10,))
    scratch["recv"] = dma((10,))
    scratch["sum_send"] = dma((14, COPIES))
    scratch["sum_recv"] = dma((14, COPIES))
    scratch["sum_local"] = dma((14,))
    outputs = ["grad_input", "small_total"] + ["total_" + name for name in totals]
    layout = near + [name + "_hbm" for name in distant] + outputs + list(scratch)
    vmem = pl.BlockSpec(memory_space=pltpu.VMEM)
    hbm = pl.BlockSpec(memory_space=pl.ANY)
    results = pl.pallas_call(
        functools.partial(backward_kernel, tuple(layout)),
        out_shape=[
            jax.ShapeDtypeStruct(block, low),
            jax.ShapeDtypeStruct((16, width), wide),
        ]
        + [jax.ShapeDtypeStruct(shape, low) for shape in totals.values()],
        in_specs=[vmem] * len(near) + [hbm] * len(distant),
        out_specs=[vmem] * 2 + [hbm] * len(totals),
        scratch_shapes=list(scratch.values()),
        name="backward_section",
        compiler_params=pltpu.CompilerParams(
            collective_id=3, has_side_effects=True, vmem_limit_bytes=62 * 2**20
        ),
    )(*[arrays[name] for name in near + distant])
    return dict(zip(outputs, results))


def body(
    block_in,
    crop_shape,
    norm_gains,
    shifts,
    qkv_weight,
    qv_bias,
    out_weight,
    up_weight,
    up_bias,
    down_weight,
    tconv_weight,
    kernels,
    grad_out,
    grad_decoded,
):
    (
        normed_one,
        query,
        key_value,
        probs,
        mixed,
        middle,
        normed_two,
        active,
        slope,
        tapped,
    ) = forward_section(
        block_in,
        norm_gains,
        shifts,
        qkv_weight,
        qv_bias,
        out_weight,
        up_weight,
        up_bias,
        down_weight,
        crop_shape,
    )
    tap = decoder_section(
        tapped,
        tconv_weight,
        kernels,
        grad_decoded.reshape(DEPTH, SIDE, 2, WIDE, CH),
        crop_shape,
        grad_out,
        down_weight,
        slope,
        up_weight,
    )
    result = backward_section(
        {
            "grad_out": grad_out,
            "dtap": tap["dtap"],
            "two_own": tap["two"],
            "shift_own": tap["shift_own"],
            "ddown_own": tap["ddown"],
            "dhidden_own": tap["dhidden"],
            "bias_own": tap["bias_own"],
            "block_in": block_in,
            "gains": norm_gains,
            "down": down_weight,
            "slope": slope,
            "up": up_weight,
            "active": active,
            "normed_two": normed_two,
            "middle": middle,
            "out_weight": out_weight,
            "key_value": key_value,
            "query": query,
            "probs": probs,
            "mixed": mixed,
            "qkv": qkv_weight,
            "normed_one": normed_one,
            "grad_kernels": tap["grad_kernels"],
            "grad_tconv": tap["grad_tconv"],
        }
    )
    small = result["small_total"]
    totals = {name[6:]: array for name, array in result.items() if name.startswith("total_")}
    groups = lax.axis_size("dp") // GROUP
    if groups > 1:
        same = [[part * GROUP + i for part in range(groups)] for i in range(GROUP)]
        small = lax.psum(small, "dp", axis_index_groups=same)
        totals = {
            name: lax.psum(array, "dp", axis_index_groups=same) for name, array in totals.items()
        }
    sums, passed, smalls = finish_section(
        totals, (tap["block_all"], tap["decoded"], result["grad_input"]), small
    )
    return (
        passed[0],
        passed[1].reshape(grad_decoded.shape),
        passed[2],
        smalls[0],
        smalls[1],
        sums["qkv"],
        smalls[2],
        sums["out"],
        sums["up"],
        smalls[3],
        sums["down"],
        sums["tconv"],
        sums["kernels"].transpose(0, 2, 1),
    )


def solution(mesh):
    return jax.shard_map(
        body,
        mesh=mesh,
        in_specs=(
            P("dp", "blk", None),
            P("dp"),
            P(),
            P(),
            P(None, None, "tensor"),
            P(None, "tensor"),
            P("tensor", None),
            P(None, "tensor"),
            P("tensor"),
            P("tensor", None),
            P(),
            P(),
            P("dp", "blk", None),
            P(("dp", "tensor"), "blk", None, None, None),
        ),
        out_specs=(
            P("dp", "blk", None),
            P(("dp", "tensor"), "blk", None, None, None),
            P("dp", "blk", None),
            P(),
            P(),
            P(None, None, "tensor"),
            P(None, "tensor"),
            P("tensor", None),
            P(None, "tensor"),
            P("tensor"),
            P("tensor", None),
            P(None, "tensor"),
            P(None, None, "tensor"),
        ),
        check_vma=False,
    )
```

```python
import functools
import types

import jax
import jax.numpy as jnp
from jax import lax
from jax.experimental import pallas as pl
from jax.experimental.pallas import tpu as pltpu
from jax.sharding import PartitionSpec as P

HD = 64

MESH = pl.DeviceIdType.MESH
GROUP = 8
FAR = 4


def place():
    dp = lax.axis_index("dp")
    blk = lax.axis_index("blk")
    tensor = lax.axis_index("tensor")
    near = lax.rem(dp, 2)
    far = lax.rem(dp // 2, FAR)
    first = dp // GROUP * GROUP
    return (dp, blk, tensor, near, far, first)


def peers():
    dp, blk, tensor, near, far, first = place()
    core = (dp, 1 - blk, tensor)
    cross = (dp, blk, 1 - tensor)
    beside = (first + 2 * far + 1 - near, blk, tensor)
    side = (first + 2 * (far + 1 - 2 * lax.rem(far, 2)) + near, blk, tensor)
    over = (first + 2 * lax.rem(far + 2, FAR) + near, blk, tensor)
    return (core, cross, beside, side, over)


def greet(devices):
    barrier = pltpu.get_barrier_semaphore()
    for device in devices:
        pl.semaphore_signal(barrier, inc=1, device_id=device, device_id_type=MESH)
    pl.semaphore_wait(barrier, len(devices))


def remote(src, dst, send, recv, device):
    return pltpu.make_async_remote_copy(
        src_ref=src, dst_ref=dst, send_sem=send, recv_sem=recv, device_id=device,
        device_id_type=MESH,
    )


def rows_at(start, size):
    return pl.ds(pl.multiple_of(start, 16), size)


DEPTH = 8
SIDE = 8
WIDE = 16
CH = 128
PAIR = 2 * CH
ROWS = DEPTH * SIDE * WIDE
TAPS = [(deep, wide) for deep in range(3) for wide in range(3)]
PADDED_TAPS = 28


def nt_dot(left, right):
    return lax.dot_general(
        left, right, (((1,), (1,)), ((), ())), preferred_element_type=jnp.float32
    )


def tn_dot(left, right):
    return lax.dot_general(
        left, right, (((0,), (0,)), ((), ())), preferred_element_type=jnp.float32
    )


def dot(left, right):
    return jnp.dot(left, right, preferred_element_type=jnp.float32)


def half_sums(row):
    return row[:, :CH] + row[:, CH:]


def twice(row):
    return jnp.concatenate([row, row], axis=1)


def row_and_column(size):
    return (
        lax.broadcasted_iota(jnp.int32, (size, size), 0),
        lax.broadcasted_iota(jnp.int32, (size, size), 1),
    )


def shift_matrix(step):
    row, column = row_and_column(PAIR)
    same = (row // WIDE) == (column // WIDE)
    return jnp.where(same & (row + step == column), 1.0, 0.0).astype(jnp.bfloat16)


def weave_matrix():
    row, column = row_and_column(PAIR)
    source = lax.rem(row, 2) * CH + row // WIDE * SIDE + lax.rem(row, WIDE) // 2
    return jnp.where(source == column, 1.0, 0.0).astype(jnp.bfloat16)


def unweave_matrix():
    row, column = row_and_column(PAIR)
    source = lax.rem(column, 2) * CH + column // WIDE * SIDE + lax.rem(column, WIDE) // 2
    return jnp.where(source == row, 1.0, 0.0).astype(jnp.bfloat16)


def lay_kernel(kernels_ref, index, weights):
    zero = jnp.zeros((CH, CH), jnp.bfloat16)
    for at, (deep, wide) in enumerate(TAPS):
        weights[at, 3 * CH :, :CH] = zero
        weights[at, :CH, CH:] = zero
        for high in range(3):
            offset = ((deep * 3 + high) * 3 + wide) * CH
            block = kernels_ref[index, offset : offset + CH, :]
            weights[at, high * CH : (high + 1) * CH, :CH] = block
            weights[at, (high + 1) * CH : (high + 2) * CH, CH:] = block


def lay_flipped(kernels_ref, index, weights):
    zero = jnp.zeros((CH, CH), jnp.bfloat16)
    for at, (deep, wide) in enumerate(TAPS):
        weights[at, :CH, 3 * CH :] = zero
        weights[at, CH:, :CH] = zero
        for high in range(3):
            offset = (((2 - deep) * 3 + 2 - high) * 3 + 2 - wide) * CH
            block = kernels_ref[index, offset : offset + CH, :]
            weights[at, :CH, high * CH : (high + 1) * CH] = block
            weights[at, CH:, (high + 1) * CH : (high + 2) * CH] = block


def four_heights(field, wide, start, count):
    depths = pl.ds(start, count)
    low = field[wide, depths, 0:SIDE, :, CH:]
    middle = field[wide, depths, 1 : SIDE + 1, :, :]
    high = field[wide, depths, 2 : SIDE + 2, :, :CH]
    joined = jnp.concatenate([low, middle, high], axis=-1)
    return joined.reshape(count * SIDE * WIDE, 4 * CH)


def conv_tile(field, weights, multiply, level, start):
    total = None
    for at, (deep, wide) in enumerate(TAPS):
        product = multiply(four_heights(field, wide, start + deep, 2), weights[at])
        total = product if total is None else total + product
    level[pl.ds(pl.multiple_of(start * CH, 2 * CH), 2 * CH), :] = total


def conv(field, weights, multiply, level, arrive):
    @pl.loop(0, 2)
    def _(step):
        conv_tile(field, weights, multiply, level, 2 + 2 * step)

    arrive()

    @pl.loop(0, 2)
    def _(step):
        conv_tile(field, weights, multiply, level, 6 * step)


def clear_rims(field, blk):
    for wide in range(3):
        field[wide, :, 0] = jnp.zeros((DEPTH + 2, WIDE, PAIR), jnp.bfloat16)
        field[wide, :, SIDE + 1] = jnp.zeros((DEPTH + 2, WIDE, PAIR), jnp.bfloat16)
        field[wide, 9 * blk] = jnp.zeros((SIDE + 2, WIDE, PAIR), jnp.bfloat16)


def place_rows(field, before, after, step, value):
    shape = (2, SIDE, WIDE, PAIR)
    depths = pl.ds(1 + 2 * step, 2)
    field[1, depths, 1 : SIDE + 1] = value.reshape(shape)
    field[0, depths, 1 : SIDE + 1] = dot(before, value).astype(jnp.bfloat16).reshape(shape)
    field[2, depths, 1 : SIDE + 1] = dot(after, value).astype(jnp.bfloat16).reshape(shape)


def kernel_grad(field, dlevel_turned, index, out, tensor_half):
    for at, (deep, wide) in enumerate(TAPS):
        joined = four_heights(field, wide, deep, DEPTH)
        block = dot(dlevel_turned[...], joined)
        for high in range(3):
            part = (
                block[:CH, high * CH : (high + 1) * CH]
                + block[CH:, (high + 1) * CH : (high + 2) * CH]
            )
            offset = ((deep * 3 + high) * 3 + wide) * CH
            part = part.astype(jnp.bfloat16)
            at = index * PADDED_TAPS * 64 + offset // 2
            for half in range(2):
                out[half, at : at + 64, :] = part[half * 64 : (half + 1) * 64, :]


def decoder_kernel(
    tapped,
    tconv_hbm,
    kernels_hbm,
    grad_decoded_hbm,
    crop_shape,
    grad_out_hbm,
    down_hbm,
    slope_hbm,
    up_hbm,
    decoded_hbm,
    block_all_hbm,
    dtap_all_hbm,
    grad_tconv_hbm,
    grad_kernels_hbm,
    ddown_hbm,
    dhidden_hbm,
    two_hbm,
    bias_sum,
    shift_sum,
    tconv,
    kernels,
    grad_decoded,
    grad_out,
    down,
    slope,
    up,
    decoded,
    grad_tconv,
    grad_kernels,
    ddown,
    dhidden,
    two,
    mask,
    inverse,
    field_one,
    field_two,
    dlevel_two,
    dlevel_one,
    weights_one,
    weights_two,
    flipped_two,
    flipped_one,
    level_one,
    level_two,
    dfield,
    turned_two,
    turned_one,
    dlifted,
    tapped_from,
    dtap_mine,
    dtap_from,
    sums_mine,
    sums_from,
    load_sem,
    store_sem,
    send,
    recv,
):
    dp, blk, tensor, near, far, first = place()
    core, cross, beside, side, over = peers()
    low = jnp.bfloat16
    row_tiles = ROWS // PAIR
    slab, width = tapped.shape
    units = dhidden.shape[1]
    own_rows = rows_at(tensor * slab, slab)
    loads = {}
    for index, (name, src, dst) in enumerate(
        (
            ("tconv", tconv_hbm, tconv),
            ("kernels", kernels_hbm, kernels),
            ("grad_decoded", grad_decoded_hbm, grad_decoded),
            ("grad_out", grad_out_hbm.at[tensor], grad_out),
            ("down", down_hbm, down),
            ("slope", slope_hbm.at[own_rows], slope),
            ("up", up_hbm, up),
        )
    ):
        copy = pltpu.make_async_copy(src, dst, load_sem.at[index])
        copy.start()
        loads[name] = copy

    stores = []

    def store(src, dst):
        copy = pltpu.make_async_copy(src, dst, store_sem.at[len(stores)])
        copy.start()
        stores.append(copy)

    store(tapped, block_all_hbm.at[tensor])
    copies = []

    def start(index, src, dst, device):
        copy = remote(src, dst, send.at[index], recv.at[index], device)
        copy.start()
        copies.append(copy)
        return copy

    depth_end, side_end = extents(crop_shape[tensor])
    row = lax.broadcasted_iota(jnp.int32, mask.shape, 0)
    inside = (
        (blk * (DEPTH // 2) + row // (2 * CH) < depth_end)
        & (lax.rem(row // WIDE, SIDE) < side_end)
        & (lax.rem(row, WIDE) // 2 < side_end)
    )
    mask[...] = jnp.where(inside, 1.0, 0.0)
    voxels = (8 * depth_end * side_end * side_end).astype(jnp.float32)
    inverse[...] = 1.0 / jnp.full(inverse.shape, voxels)

    for field in (field_one, field_two, dlevel_two, dlevel_one):
        clear_rims(field, blk)
    greet([core, cross])
    give_tapped = start(0, tapped, tapped_from, cross)

    before, after = shift_matrix(-1), shift_matrix(1)

    def send_edge(index, field):
        return start(
            index,
            field.at[:, DEPTH - 7 * blk, 1 : SIDE + 1],
            field.at[:, 9 * blk, 1 : SIDE + 1],
            core,
        )

    def rows_of(step):
        return pl.ds(pl.multiple_of(step * PAIR, PAIR), PAIR)

    def mask_rows(step):
        return twice(mask[rows_of(step), :])

    def totals(slot, pair):
        sums_mine[slot, 0:1, :] = half_sums(pair[0])
        sums_mine[slot, 1:2, :] = half_sums(pair[1])
        return start(5 + slot, sums_mine.at[slot], sums_from.at[slot], core)

    def means(slot, copy):
        copy.wait_recv()
        both = (sums_mine[slot] + sums_from[slot]) * inverse[...]
        return both[0:1, :], both[1:2, :]

    zero_pair = (jnp.zeros((1, PAIR), jnp.float32), jnp.zeros((1, PAIR), jnp.float32))

    weave = weave_matrix()
    loads["tconv"].wait()
    for piece in range(2):
        tokens = slice(piece * CH, (piece + 1) * CH)
        for a in range(2):
            lifted = dot(tapped[tokens, :], tconv[:, a * 512 : (a + 1) * 512])
            side = [
                jnp.concatenate([lifted[:, c * CH : (c + 1) * CH],
                                 lifted[:, (2 + c) * CH : (3 + c) * CH]], axis=1)
                for c in range(2)
            ]
            woven = dot(weave, jnp.concatenate(side, axis=0).astype(low))
            for depth in range(2):
                at = 2 * (2 * piece + depth) + a
                rows = slice(depth * CH, (depth + 1) * CH)
                value = woven[rows, :] * twice(mask[at * CH : (at + 1) * CH, :])
                level_one[at * CH : (at + 1) * CH, :] = value

    @pl.loop(0, row_tiles)
    def _(step):
        place_rows(field_one, before, after, step, level_one[rows_of(step), :].astype(low))

    edge = send_edge(1, field_one)
    loads["kernels"].wait()
    lay_kernel(kernels, 0, weights_one)
    conv(field_one, weights_one, dot, level_one, edge.wait_recv)

    def forward_sums(level):
        def add(step, pair):
            value = level[rows_of(step), :]
            kept = value * mask_rows(step)
            return (
                pair[0] + jnp.sum(kept, axis=0, keepdims=True),
                pair[1] + jnp.sum(kept * value, axis=0, keepdims=True),
            )

        return lax.fori_loop(0, row_tiles, add, zero_pair)

    def mean_and_scale(slot, copy):
        mean, second = means(slot, copy)
        return twice(mean), twice(lax.rsqrt(second - mean * mean + 1e-05))

    def sigmoid(value):
        return 0.5 * jnp.tanh(0.5 * value) + 0.5

    copy = totals(0, forward_sums(level_one))
    lay_kernel(kernels, 1, weights_two)
    mean_one, scale_one = mean_and_scale(0, copy)

    @pl.loop(0, row_tiles)
    def _(step):
        normed = (level_one[rows_of(step), :] - mean_one) * scale_one
        level_one[rows_of(step), :] = normed
        value = normed * sigmoid(normed) * mask_rows(step)
        place_rows(field_two, before, after, step, value.astype(low))

    edge = send_edge(2, field_two)
    lay_flipped(kernels, 1, flipped_two)
    conv(field_two, weights_two, dot, level_two, edge.wait_recv)
    copy = totals(1, forward_sums(level_two))
    lay_flipped(kernels, 0, flipped_one)
    mean_two, scale_two = mean_and_scale(1, copy)

    loads["grad_decoded"].wait()

    def two_depths(ref, step, b):
        return ref[pl.ds(2 * step, 2), :, b].reshape(PAIR, CH)

    def decode(step, pair):
        normed = (level_two[rows_of(step), :] - mean_two) * scale_two
        level_two[rows_of(step), :] = normed
        kept = mask_rows(step)
        gate = sigmoid(normed)
        value = (normed * gate * kept).astype(low)
        for b in range(2):
            decoded[pl.ds(2 * step, 2), :, b] = value[:, b * CH : (b + 1) * CH].reshape(
                2, SIDE, WIDE, CH
            )
        grad = jnp.concatenate(
            [two_depths(grad_decoded, step, 0), two_depths(grad_decoded, step, 1)], axis=1
        ).astype(jnp.float32)
        dnormed = gate * (1.0 + normed * (1.0 - gate)) * kept * grad
        dfield[rows_of(step), :] = dnormed
        return (
            pair[0] + jnp.sum(dnormed, axis=0, keepdims=True),
            pair[1] + jnp.sum(dnormed * normed, axis=0, keepdims=True),
        )

    copy = totals(2, lax.fori_loop(0, row_tiles, decode, zero_pair))

    store(decoded, decoded_hbm)

    def level_grad(slot, copy, level, scale, field, turned):
        mean_grad, mean_cross = means(slot, copy)
        mean_grad, mean_cross = twice(mean_grad), twice(mean_cross)

        @pl.loop(0, row_tiles)
        def _(step):
            centred = mean_grad + level[rows_of(step), :] * mean_cross
            value = scale * (dfield[rows_of(step), :] - mask_rows(step) * centred)
            place_rows(field, before, after, step, value.astype(low))
            turned[:, rows_of(step)] = value.T.astype(low)

    level_grad(2, copy, level_two, scale_two, dlevel_two, turned_two)
    edge = send_edge(3, dlevel_two)
    conv(dlevel_two, flipped_two, nt_dot, dfield, edge.wait_recv)

    def back_one(step, pair):
        normed = level_one[rows_of(step), :]
        gate = sigmoid(normed)
        dnormed = gate * (1.0 + normed * (1.0 - gate)) * mask_rows(step) * dfield[rows_of(step), :]
        dfield[rows_of(step), :] = dnormed
        return (
            pair[0] + jnp.sum(dnormed, axis=0, keepdims=True),
            pair[1] + jnp.sum(dnormed * normed, axis=0, keepdims=True),
        )

    copy = totals(3, lax.fori_loop(0, row_tiles, back_one, zero_pair))
    level_grad(3, copy, level_one, scale_one, dlevel_one, turned_one)
    edge = send_edge(4, dlevel_one)
    conv(dlevel_one, flipped_one, nt_dot, dfield, edge.wait_recv)

    unweave = unweave_matrix()
    for piece in range(2):
        tokens = slice(piece * CH, (piece + 1) * CH)
        for a in range(2):
            parts = []
            for depth in range(2):
                at = 2 * (2 * piece + depth) + a
                rows = slice(at * CH, (at + 1) * CH)
                parts.append(dfield[rows, :] * twice(mask[rows, :]))
            apart = dot(unweave, jnp.concatenate(parts, axis=0).astype(low)).astype(low)
            for c in range(2):
                for b in range(2):
                    column = ((a * 2 + b) * 2 + c) * CH
                    dlifted[tokens, column : column + CH] = apart[
                        c * CH : (c + 1) * CH, b * CH : (b + 1) * CH
                    ]
    dtap_mine[...] = nt_dot(dlifted[...], tconv[...]).astype(low)
    give_dtap = start(9, dtap_mine, dtap_from, cross)
    for half in range(2):
        lanes = slice(half * 512, (half + 1) * 512)
        grad_tconv[half] = tn_dot(tapped[...], dlifted[:, lanes]).astype(low)
        for index in range(2):
            at = ((index + 1) * PADDED_TAPS - 1) * 64
            grad_kernels[half, at : at + 64, :] = jnp.zeros((64, CH), low)
    store(grad_tconv, grad_tconv_hbm)

    loads["grad_out"].wait()
    tile = 64

    def shade(step, total):
        at = rows_at(step * tile, tile)
        value = grad_out[at, :].astype(jnp.float32) + dtap_mine[at, :].astype(jnp.float32)
        value = value.astype(low)
        ddown[at, :] = value
        return total + fold(value.astype(jnp.float32))

    shift_sum[...] = lax.fori_loop(0, slab // tile, shade, jnp.zeros((8, width), jnp.float32))
    store(ddown, ddown_hbm)
    loads["down"].wait()
    loads["slope"].wait()

    @pl.loop(0, units // 256)
    def _(step):
        lanes = pl.ds(pl.multiple_of(step * 256, 256), 256)
        dactive = nt_dot(ddown[...], down[lanes, :])
        value = (dactive * slope[:, lanes].astype(jnp.float32)).astype(low)
        dhidden[:, lanes] = value
        bias_sum[:, lanes] = fold(value.astype(jnp.float32))

    store(dhidden, dhidden_hbm)
    loads["up"].wait()

    @pl.loop(0, width // 256)
    def _(step):
        lanes = pl.ds(pl.multiple_of(step * 256, 256), 256)
        two[:, lanes] = nt_dot(dhidden[...], up[lanes, :]).astype(low)

    store(two, two_hbm)
    kernel_grad(field_two, turned_two, 1, grad_kernels, tensor)
    kernel_grad(field_one, turned_one, 0, grad_kernels, tensor)
    store(grad_kernels, grad_kernels_hbm)
    store(dtap_mine, dtap_all_hbm.at[tensor])
    give_tapped.wait_recv()
    store(tapped_from, block_all_hbm.at[1 - tensor])
    give_dtap.wait_recv()
    store(dtap_from, dtap_all_hbm.at[1 - tensor])
    for copy in copies:
        copy.wait_send()
    for copy in stores:
        copy.wait()


def decoder_section(
    tapped, tconv_weight, kernels, grad_decoded, crop_shape, grad_out, down, slope, up
):
    low = jnp.bfloat16
    wide = jnp.float32
    slab, width = tapped.shape
    units = down.shape[0]
    vmem = pl.BlockSpec(memory_space=pltpu.VMEM)
    hbm = pl.BlockSpec(memory_space=pl.ANY)
    field = pltpu.VMEM((3, DEPTH + 2, SIDE + 2, WIDE, PAIR), low)
    plane = pltpu.VMEM((ROWS, PAIR), wide)
    kept = {
        "decoded": (DEPTH, SIDE, 2, WIDE, CH),
        "grad_tconv": (2, width, tconv_weight.shape[1] // 2),
        "grad_kernels": (2, 2 * PADDED_TAPS * 64, CH),
        "ddown": (slab, width),
        "dhidden": (slab, units),
        "two": (slab, width),
    }
    block = (2, slab, width)
    shapes = [kept["decoded"], block, block] + list(kept.values())[1:]
    names = ["decoded", "block_all", "dtap"] + list(kept)[1:] + ["bias_own", "shift_own"]
    dma = pltpu.SemaphoreType.DMA
    results = pl.pallas_call(
        decoder_kernel,
        out_shape=[jax.ShapeDtypeStruct(shape, low) for shape in shapes]
        + [
            jax.ShapeDtypeStruct((8, units), wide),
            jax.ShapeDtypeStruct((8, width), wide),
        ],
        in_specs=[vmem] + [hbm] * 3 + [pl.BlockSpec(memory_space=pltpu.SMEM)] + [hbm] * 4,
        out_specs=[hbm] * 8 + [vmem] * 2,
        scratch_shapes=[
            pltpu.VMEM(array.shape, array.dtype) for array in (tconv_weight, kernels, grad_decoded)
        ]
        + [
            pltpu.VMEM((slab, width), low),
            pltpu.VMEM(down.shape, low),
            pltpu.VMEM((slab, units), low),
            pltpu.VMEM(up.shape, low),
        ]
        + [pltpu.VMEM(shape, low) for shape in kept.values()]
        + [pltpu.VMEM((ROWS, CH), wide), pltpu.VMEM((8, CH), wide)]
        + [field] * 4
        + [pltpu.VMEM((9, 4 * CH, PAIR), low)] * 2
        + [pltpu.VMEM((9, PAIR, 4 * CH), low)] * 2
        + [plane] * 3
        + [pltpu.VMEM((PAIR, ROWS), low)] * 2
        + [
            pltpu.VMEM((slab, tconv_weight.shape[1]), low),
            pltpu.VMEM(tapped.shape, low),
            pltpu.VMEM(tapped.shape, low),
            pltpu.VMEM(tapped.shape, low),
            pltpu.VMEM((4, 8, CH), wide),
            pltpu.VMEM((4, 8, CH), wide),
            dma((7,)),
            dma((10,)),
            dma((10,)),
            dma((10,)),
        ],
        name="decoder_section",
        compiler_params=pltpu.CompilerParams(
            collective_id=1, has_side_effects=True, vmem_limit_bytes=60 * 2**20
        ),
    )(tapped, tconv_weight, kernels, grad_decoded, crop_shape, grad_out, down, slope, up)
    return dict(zip(names, results))


def widen_rows(src, dst, tile=64):
    @pl.loop(0, src.shape[0] // tile)
    def _(step):
        at = rows_at(step * tile, tile)
        dst[at, :] = src[at, :].astype(jnp.float32)


def finish_kernel(count, *refs):
    sources, refs = refs[:count], refs[count:]
    passed, small, refs = refs[:3], refs[3], refs[4:]
    targets, refs = refs[:count], refs[count:]
    handed, smalls, refs = refs[:3], refs[3:7], refs[7:]
    lows, wides, refs = refs[:count], refs[count : 2 * count], refs[2 * count :]
    held, refs = refs[:3], refs[3:]
    load_sem, store_sem, pass_sem = refs
    loads, stores = [], []
    for index in range(count):
        loads.append(pltpu.make_async_copy(sources[index], lows[index], load_sem.at[index]))
    passes = [
        pltpu.make_async_copy(passed[index], held[index], pass_sem.at[index])
        for index in range(3)
    ]
    for copy in passes + loads:
        copy.start()
    gains, shifts, qv_bias, up_bias = smalls
    width = small.shape[1]
    gains[0:1, :] = small[0:1, :]
    gains[1:2, :] = small[2:3, :]
    shifts[0:1, :] = small[1:2, :]
    shifts[1:4, :] = small[3:6, :]
    qv_bias[0:1, :] = small[6:7, : width // 2]
    qv_bias[1:2, :] = small[6:7, width // 2 :]
    up_bias[:width] = small[7, :]
    up_bias[width:] = small[8, :]

    def store(src, dst):
        copy = pltpu.make_async_copy(src, dst, store_sem.at[len(stores)])
        copy.start()
        stores.append(copy)

    for index in range(3):
        passes[index].wait()
        store(held[index], handed[index])
    for index in range(count):
        src, dst, wide, low = sources[index], targets[index], wides[index], lows[index]
        loads[index].wait()
        if dst.shape == src.shape and len(src.shape) == 2:
            widen_rows(low, wide)
            store(wide, dst)
        elif dst.shape == src.shape:
            for part in range(src.shape[0]):
                widen_rows(low.at[part], wide.at[part])
                store(wide.at[part], dst.at[part])
        elif len(src.shape) == 3:
            for part in range(src.shape[0]):
                widen_rows(low.at[part], wide.at[part])
                rows, columns = src.shape[1:]
                across = dst.shape[1] // columns
                store(
                    wide.at[part],
                    dst.at[
                        pl.ds(part // across * rows, rows),
                        pl.ds(part % across * columns, columns),
                    ],
                )
        elif len(dst.shape) == 2:
            widen_rows(low, wide)
            rows, columns = dst.shape[0], src.shape[1]
            for part in range(2):
                store(
                    wide.at[pl.ds(part * rows, rows)], dst.at[:, pl.ds(part * columns, columns)]
                )
        else:
            kinds, outs, columns = dst.shape
            ins = src.shape[1]
            for kind in range(kinds):
                for tap in range(columns // ins):
                    at = (kind * PADDED_TAPS + tap) * outs
                    wide[kind, :, tap * ins : (tap + 1) * ins] = low[at : at + outs, :].astype(
                        jnp.float32
                    )
                store(wide.at[kind], dst.at[kind])
    for copy in stores:
        copy.wait()


def finish_section(totals, passed, small):
    wide = jnp.float32
    local = totals["qkv"].shape[2]
    width = totals["qkv"].shape[1]
    units = totals["up"].shape[2] * 4
    shapes = {
        "qkv": totals["qkv"].shape,
        "out": (local, width),
        "up": (width, units),
        "down": (units, width),
        "tconv": totals["tconv"].shape,
        "kernels": (2, 64, 27 * CH),
    }
    count = len(shapes)
    sources = [totals[name] for name in shapes]
    kept = [
        shapes[name] if name == "kernels" else totals[name].shape for name in shapes
    ]
    vmem = pl.BlockSpec(memory_space=pltpu.VMEM)
    hbm = pl.BlockSpec(memory_space=pl.ANY)
    results = pl.pallas_call(
        functools.partial(finish_kernel, count),
        out_shape=[jax.ShapeDtypeStruct(shape, wide) for shape in shapes.values()]
        + [jax.ShapeDtypeStruct(array.shape, array.dtype) for array in passed]
        + [
            jax.ShapeDtypeStruct(shape, wide)
            for shape in ((2, width), (4, width), (2, local), (units,))
        ],
        in_specs=[hbm] * (count + 3) + [vmem],
        out_specs=[hbm] * (count + 3) + [vmem] * 4,
        scratch_shapes=[pltpu.VMEM(array.shape, array.dtype) for array in sources]
        + [pltpu.VMEM(shape, wide) for shape in kept]
        + [pltpu.VMEM(array.shape, array.dtype) for array in passed]
        + [
            pltpu.SemaphoreType.DMA((count,)),
            pltpu.SemaphoreType.DMA((24,)),
            pltpu.SemaphoreType.DMA((3,)),
        ],
        name="finish",
        compiler_params=pltpu.CompilerParams(vmem_limit_bytes=60 * 2**20),
    )(*sources, *passed, small)
    return dict(zip(shapes, results)), results[count : count + 3], results[count + 3 :]


def extents(crop):
    depth = jnp.where(crop == 0, SIDE * 3 // 4, jnp.where(crop == 1, SIDE // 2, SIDE))
    side = jnp.where(crop == 0, SIDE * 3 // 4, SIDE)
    return depth, side


GELU_RATE = 0.7978845608028654
GELU_CUBE = 0.044715


def rows_sum(value):
    return jnp.sum(value, axis=0, keepdims=True)


def lane_mean(value):
    return jnp.mean(value, axis=-1, keepdims=True)


def centred(value):
    centre = value - lane_mean(value)
    return centre, lax.rsqrt(lane_mean(centre * centre) + 1e-06)


def head_only(pair, head):
    lane = lax.broadcasted_iota(jnp.int32, pair.shape, 1)
    return jnp.where((lane // HD) == head, pair, jnp.zeros_like(pair))


def forward_kernel(
    block_in,
    gains,
    shifts,
    qkv_hbm,
    qv_bias,
    out_hbm,
    up_hbm,
    up_bias,
    down_hbm,
    crop_shape,
    normed_one_hbm,
    query_hbm,
    key_value_hbm,
    probs_hbm,
    mixed_hbm,
    middle_hbm,
    normed_two_hbm,
    active_hbm,
    slope_hbm,
    tapped,
    qkv,
    out_weight,
    up,
    down,
    normed_one,
    query,
    key_value,
    probs,
    mixed,
    middle,
    normed_two,
    active,
    slope,
    values_turned,
    part_mine,
    part_from,
    feed_mine,
    feed_from,
    load_sem,
    store_sem,
    send,
    recv,
):
    dp, blk, tensor, near, far, first = place()
    core, cross, beside, side, over = peers()
    low = jnp.bfloat16
    items, slab, width = block_in.shape
    local = query.shape[1]
    units = active.shape[1]

    loads = []
    for index, (src, dst) in enumerate(
        [(qkv_hbm, qkv), (out_hbm, out_weight), (up_hbm, up), (down_hbm, down)]
    ):
        copy = pltpu.make_async_copy(src, dst, load_sem.at[index])
        copy.start()
        loads.append(copy)
    greet([core, cross])
    copies = []
    stores = []

    def start(index, src, dst, device):
        copy = remote(src, dst, send.at[index], recv.at[index], device)
        copy.start()
        copies.append(copy)
        return copy

    def store(src, dst):
        copy = pltpu.make_async_copy(src, dst, store_sem.at[len(stores)])
        copy.start()
        stores.append(copy)

    tile = 64

    for item in range(items):

        @pl.loop(0, slab // tile)
        def _(step):
            value = block_in[item, rows_at(step * tile, tile), :].astype(jnp.float32)
            centre, scale = centred(value)
            normed = centre * scale * gains[0:1, :] + shifts[0:1, :]
            normed_one[rows_at(item * slab + step * tile, tile), :] = normed.astype(low)

    store(normed_one, normed_one_hbm)
    loads[0].wait()
    others = [lax.rem(tensor + step, items) for step in range(items)]
    kv_copies = []
    for place_at, item in enumerate(others):
        rows = rows_at(item * slab, slab)
        for c in range(2):
            project = dot(normed_one[rows, :], qkv[1 + c])
            if c == 1:
                project = project + qv_bias[1:2, :]
            key_value[item, c, :slab, :] = project.astype(low)
        kv_copies.append(
            start(
                place_at,
                key_value.at[item, :, pl.ds(0, slab), :],
                key_value.at[item, :, pl.ds(slab, slab), :],
                core,
            )
        )
    for item in others:
        rows = rows_at(item * slab, slab)
        query[rows, :] = (dot(normed_one[rows, :], qkv[0]) + qv_bias[0:1, :]).astype(low)
    store(query, query_hbm)

    part_copies = []
    for place_at, item in enumerate(others):
        rows = rows_at(item * slab, slab)
        kv_copies[place_at].wait_recv()
        values_turned[...] = key_value[item, 1].astype(jnp.float32).T.astype(low)
        depth_end, side_end = extents(crop_shape[item])
        key = lax.broadcasted_iota(jnp.int32, (probs.shape[2], slab), 0)
        patch = jnp.where(key < slab, blk * slab + key, (1 - blk) * slab + key - slab)
        keep = (
            (patch // (SIDE * SIDE) < depth_end)
            & (lax.rem(patch // SIDE, SIDE) < side_end)
            & (lax.rem(patch, SIDE) < side_end)
        )
        for pair in range(local // 128):
            lanes = slice(pair * 128, (pair + 1) * 128)
            keys = key_value[item, 0, :, lanes]
            asked = query[rows, lanes] * jnp.asarray(HD ** (-0.5), low)
            turned = []
            for head in range(2):
                scores = nt_dot(keys, head_only(asked, head))
                scores = jnp.where(keep, scores, -1000000000.0)
                weights = jnp.exp(scores - jnp.max(scores, axis=0, keepdims=True))
                prob = (weights * (1.0 / rows_sum(weights))).astype(low)
                probs[item, 2 * pair + head] = prob
                at = pair * 128 + head * HD
                turned.append(dot(values_turned[at : at + HD, :], prob))
            mixed[rows, lanes] = jnp.concatenate(turned, axis=0).T.astype(low)
        store(probs.at[item], probs_hbm.at[item])
        if place_at == 0:
            loads[1].wait()
        part_mine[item] = dot(mixed[rows, :], out_weight[...]).astype(low)
        part_copies.append(start(2 + place_at, part_mine.at[item], part_from.at[item], cross))
    store(key_value, key_value_hbm)
    store(mixed, mixed_hbm)

    for place_at, item in enumerate(others[1:] + others[:1]):
        if place_at == 0:
            loads[2].wait()
        part_copies[place_at].wait_recv()

        @pl.loop(0, slab // tile)
        def _(step):
            at = rows_at(step * tile, tile)
            attended = part_mine[item, at, :].astype(jnp.float32) + part_from[item, at, :].astype(
                jnp.float32
            )
            value = block_in[item, at, :].astype(jnp.float32) + (attended + shifts[2:3, :])
            middle[item, at, :] = value
            centre, scale = centred(value)
            normed = centre * scale * gains[1:2, :] + shifts[1:2, :]
            normed_two[rows_at(item * slab + step * tile, tile), :] = normed.astype(low)

        rows = rows_at(item * slab, slab)

        @pl.loop(0, units // 256)
        def _(step):
            lanes = pl.ds(pl.multiple_of(step * 256, 256), 256)
            value = dot(normed_two[rows, :], up[:, lanes]) + up_bias[lanes].reshape(1, -1)
            square = value * value
            bent = jnp.tanh(GELU_RATE * value * (1.0 + GELU_CUBE * square))
            half = 0.5 * (1.0 + bent)
            active[rows, lanes] = (value * half).astype(low)
            inner = GELU_RATE * (1.0 + 3.0 * GELU_CUBE * square)
            slope[rows, lanes] = (half + 0.5 * value * (1.0 - bent * bent) * inner).astype(low)

        if place_at == 0:
            loads[3].wait()

        @pl.loop(0, width // 256)
        def _(step):
            lanes = pl.ds(pl.multiple_of(step * 256, 256), 256)
            feed_mine[item, :, lanes] = dot(active[rows, :], down[:, lanes]).astype(low)

        if place_at == 0:
            feed = start(4, feed_mine.at[item], feed_from, cross)

    store(middle, middle_hbm)
    store(normed_two, normed_two_hbm)
    store(active, active_hbm)
    store(slope, slope_hbm)
    feed.wait_recv()

    @pl.loop(0, slab // tile)
    def _(step):
        at = rows_at(step * tile, tile)
        fed = feed_mine[tensor, at, :].astype(jnp.float32) + feed_from[at, :].astype(jnp.float32)
        tapped[at, :] = (middle[tensor, at, :] + (fed + shifts[3:4, :])).astype(low)

    for copy in copies:
        copy.wait_send()
    for copy in stores:
        copy.wait()


def forward_section(
    block_in, gains, shifts, qkv, qv_bias, out_weight, up, up_bias, down, crop_shape
):
    low = jnp.bfloat16
    items, slab, width = block_in.shape
    tokens = items * slab
    local = qkv.shape[2]
    units = up.shape[1]
    heads = local // HD
    patches = 2 * slab
    vmem = pl.BlockSpec(memory_space=pltpu.VMEM)
    hbm = pl.BlockSpec(memory_space=pl.ANY)
    kept = [
        ((tokens, width), low),
        ((tokens, local), low),
        ((items, 2, patches, local), low),
        ((items, heads, patches, slab), low),
        ((tokens, local), low),
        ((items, slab, width), jnp.float32),
        ((tokens, width), low),
        ((tokens, units), low),
        ((tokens, units), low),
    ]
    return pl.pallas_call(
        forward_kernel,
        out_shape=[jax.ShapeDtypeStruct(*one) for one in kept]
        + [jax.ShapeDtypeStruct((slab, width), low)],
        in_specs=[vmem, vmem, vmem, hbm, vmem, hbm, hbm, vmem, hbm]
        + [pl.BlockSpec(memory_space=pltpu.SMEM)],
        out_specs=[hbm] * 9 + [vmem],
        scratch_shapes=[pltpu.VMEM(one.shape, low) for one in (qkv, out_weight, up, down)]
        + [pltpu.VMEM(*one) for one in kept]
        + [
            pltpu.VMEM((local, patches), low),
            pltpu.VMEM(block_in.shape, low),
            pltpu.VMEM(block_in.shape, low),
            pltpu.VMEM(block_in.shape, low),
            pltpu.VMEM((slab, width), low),
            pltpu.SemaphoreType.DMA((4,)),
            pltpu.SemaphoreType.DMA((16,)),
            pltpu.SemaphoreType.DMA((5,)),
            pltpu.SemaphoreType.DMA((5,)),
        ],
        name="forward_section",
        compiler_params=pltpu.CompilerParams(
            collective_id=2, has_side_effects=True, vmem_limit_bytes=60 * 2**20
        ),
    )(block_in, gains, shifts, qkv, qv_bias, out_weight, up, up_bias, down, crop_shape)


def fold(value):
    rows, width = value.shape
    return jnp.sum(value.reshape(rows // 8, 8, width), axis=0)


def add_into(target, target_at, parts, rows, tile):
    @pl.loop(0, rows // tile)
    def _(step):
        at = step * tile
        total = None
        for ref, offset in parts:
            piece = ref[rows_at(offset + at, tile), :].astype(jnp.float32)
            total = piece if total is None else total + piece
        target[rows_at(target_at + at, tile), :] = total.astype(jnp.bfloat16)


COPIES = 10


class Sum:
    def __init__(self, refs, name, index, path, own, out, total=None, full=None):
        self.own, self.out, self.full = own, out, full
        self.total = own if total is None else total
        self.held = [getattr(refs, name + end) for end in ("_core", "_first", "_second", "_third")]
        if full is not None:
            self.both = getattr(refs, name + "_both")
            self.cross_part = getattr(refs, name + "_cross")
        self.send, self.recv = refs.sum_send.at[index], refs.sum_recv.at[index]
        self.local = refs.sum_local.at[index]
        rows = out.shape[0]
        self.half, self.piece = rows // 2, rows // 16
        dp, self.blk, self.tensor, near, far, first = place()
        self.core, self.cross, beside, side, over = peers()
        self.stages = [
            {"y": (beside, near), "s": (side, lax.rem(far, 2)), "o": (over, far // 2)}[one]
            for one in path
        ]
        self.at = [self.blk * self.half]
        for stage, (device, bit) in enumerate(self.stages):
            self.at.append(self.at[-1] + bit * (rows >> (stage + 2)))
        self.sizes = [rows >> (stage + 1) for stage in range(4)]
        self.waiting = []

    def start(self, index, src, dst, device):
        copy = remote(src, dst, self.send.at[index], self.recv.at[index], device)
        copy.start()
        self.waiting.append(copy)
        self.last = copy

    def sA(self):
        give = rows_at((1 - self.blk) * self.half, self.half)
        self.start(0, self.full.at[:, give], self.both, self.core)

    def sB(self):
        self.last.wait_recv()
        for which in (1 - self.tensor, self.tensor):
            add_into(
                self.both.at[which], 0, [(self.both.at[which], 0), (self.own.at[which], 0)],
                self.half, self.piece,
            )
        self.start(1, self.both.at[1 - self.tensor], self.cross_part, self.cross)

    def s0(self):
        give = rows_at((1 - self.blk) * self.half, self.half)
        self.start(0, self.own.at[give], self.held[0], self.core)

    def narrow(self, stage):
        device, bit = self.stages[stage]
        give = rows_at((1 - bit) * self.sizes[stage + 1], self.sizes[stage + 1])
        self.start(2 + stage, self.held[stage].at[give], self.held[stage + 1], device)

    def gather(self, stage, target, at=0):
        self.last.wait_recv()
        size = self.sizes[stage]
        kept = (self.held[stage - 1], self.stages[stage - 1][1] * size)
        add_into(target, at, [(self.held[stage], 0), kept], size, self.piece)

    def s1(self):
        self.last.wait()
        self.waiting.pop()
        parts = [(self.held[0], 0), (self.own, self.blk * self.half)]
        if self.full is not None:
            parts = [(self.both.at[self.tensor], 0), (self.cross_part, 0)]
        add_into(self.held[0], 0, parts, self.half, self.piece)
        self.narrow(0)

    def s2(self):
        self.gather(1, self.held[1])
        self.narrow(1)

    def s2b(self):
        self.gather(2, self.held[2])
        self.narrow(2)

    def s3(self):
        self.gather(3, self.total, self.at[3])
        self.spread(5, self.at[3], self.sizes[3], self.stages[2][0])

    def spread(self, index, at, size, device):
        where = self.total.at[rows_at(at, size)]
        self.start(index, where, where, device)

    def s3b(self):
        self.last.wait_recv()
        self.spread(6, self.at[2], self.sizes[2], self.stages[1][0])

    def s4(self):
        self.last.wait_recv()
        self.spread(7, self.at[1], self.sizes[1], self.stages[0][0])

    def s5(self):
        self.last.wait_recv()
        self.spread(8, self.at[0], self.sizes[0], self.core)

    def s6(self):
        self.last.wait_recv()
        for copy in self.waiting:
            copy.wait_send()
        self.keep = pltpu.make_async_copy(self.total, self.out, self.local)
        self.keep.start()


def sum_scratch(rows, columns):
    low = jnp.bfloat16
    shares = {"_core": 2, "_first": 4, "_second": 8, "_third": 16}
    return {end: pltpu.VMEM((rows // share, columns), low) for end, share in shares.items()}


def norm_back(value, grad, gain):
    centre, scale = centred(value)
    normed = centre * scale
    scaled = grad * gain
    inner = lane_mean(scaled * normed)
    return scale * (scaled - lane_mean(scaled) - normed * inner), normed


def backward_kernel(layout, *refs):
    r = types.SimpleNamespace(**dict(zip(layout, refs)))
    dp, blk, tensor, near, far, first = place()
    core, cross, beside, side, over = peers()
    low = jnp.bfloat16
    items, slab, width = r.grad_out.shape
    local = r.query.shape[1]
    units = r.active.shape[1]
    pairs = local // 128
    tile = 64
    half_width = width // 2

    loads = {}
    own_rows = rows_at(tensor * slab, slab)
    landing = {
        "two_own": r.two_mine.at[tensor],
        "ddown_own": r.ddown.at[own_rows],
        "dhidden_own": r.dhidden.at[own_rows],
    }
    for index, name in enumerate(LOADED):
        target = landing[name] if name in landing else getattr(r, name)
        copy = pltpu.make_async_copy(getattr(r, name + "_hbm"), target, r.load_sem.at[index])
        copy.start()
        loads[name] = copy
    keep_full = {}
    for index, name in enumerate(("kernels", "tconv")):
        full = getattr(r, "grad_" + name + "_hbm")
        rows = full.shape[1] // 2
        copy = pltpu.make_async_copy(
            full.at[:, rows_at(blk * rows, rows)],
            getattr(r, "own_" + name),
            r.load_sem.at[len(LOADED) + index],
        )
        copy.start()
        keep_full[name] = copy
    greet([core, cross, beside, side, over])
    copies = []

    def start(index, src, dst, device):
        copy = remote(src, dst, r.send.at[index], r.recv.at[index], device)
        copy.start()
        copies.append(copy)
        return copy

    sums = {}
    for h in range(4):
        sums["d%d" % h] = ("down%d" % h, r.own_down.at[h], r.total_down.at[h])
        sums["u%d" % h] = ("up%d" % h, r.own_up.at[h], r.total_up.at[h])
    sums["o"] = ("out", r.own_out, r.total_out)
    for c in range(3):
        sums["q%d" % c] = ("qkv%d" % c, r.own_qkv.at[c], r.total_qkv.at[c])
    sums["k"] = ("kernels", r.own_kernels, r.total_kernels, r.sum_kernels, r.grad_kernels_hbm)
    sums["t"] = ("tconv", r.own_tconv, r.total_tconv, r.sum_tconv, r.grad_tconv_hbm)
    sums = {
        name: Sum(r, one[0], index, PATHS[name], *one[1:])
        for index, (name, one) in enumerate(sums.items())
    }

    def rows_of(item):
        return rows_at(item * slab, slab)

    def lanes_of(step, size=256):
        return pl.ds(pl.multiple_of(step * size, size), size)

    r.small[...] = jnp.zeros_like(r.small)

    def dout_rows(item, at):
        return r.grad_out[item, at, :].astype(jnp.float32) + r.dtap[item, at, :].astype(
            jnp.float32
        )

    zero = jnp.zeros((8, width), jnp.float32)

    sent = {}
    waited = set()

    def loaded(*names):
        for name in names:
            if name not in waited:
                loads[name].wait()
                waited.add(name)

    own, other = tensor, 1 - tensor

    def take_own():
        loaded("two_own", "shift_own")
        r.small[5:6, :] += rows_sum(r.shift_own[...])
        sent["dn0"] = start(0, r.two_mine.at[own], r.two_from.at[own], cross)

    def shade_other():
        def shade(step, total):
            value = dout_rows(other, rows_at(step * tile, tile)).astype(low)
            r.ddown[rows_at(other * slab + step * tile, tile), :] = value
            return total + fold(value.astype(jnp.float32))

        total = lax.fori_loop(0, slab // tile, shade, zero)
        r.small[5:6, :] += rows_sum(total)

    def feed_back():
        item = other
        rows = rows_of(item)
        loaded("down", "slope")

        @pl.loop(0, units // 256)
        def _(step):
            lanes = lanes_of(step)
            dactive = nt_dot(r.ddown[rows, :], r.down[lanes, :])
            value = (dactive * r.slope[rows, lanes].astype(jnp.float32)).astype(low)
            r.dhidden[rows, lanes] = value
            summed = rows_sum(fold(value.astype(jnp.float32)))
            r.bias_sum[0:1, lanes] = summed

        loaded("up")

        @pl.loop(0, width // 256)
        def _(step):
            value = nt_dot(r.dhidden[rows, :], r.up[lanes_of(step), :])
            r.two_mine[item, :, lanes_of(step)] = value.astype(low)

        sent["dn1"] = start(1, r.two_mine.at[item], r.two_from.at[item], cross)

    def grad_down(h):
        loaded("active", "ddown_own")

        @pl.loop(0, units // 2 // 256)
        def _(step):
            lanes = pl.ds(pl.multiple_of(h * (units // 2) + step * 256, 256), 256)
            value = tn_dot(r.active[:, lanes], r.ddown[...]).astype(low)
            for part in range(2):
                columns = slice(part * half_width, (part + 1) * half_width)
                r.own_down[2 * h + part, lanes_of(step), :] = value[:, columns]

    def grad_up(h):
        loaded("normed_two", "dhidden_own")

        @pl.loop(0, width // 256)
        def _(step):
            right = r.dhidden[:, h * (units // 2) : (h + 1) * (units // 2)]
            value = tn_dot(r.normed_two[:, lanes_of(step)], right).astype(low)
            for part in range(2):
                columns = slice(part * (units // 4), (part + 1) * (units // 4))
                r.own_up[2 * h + part, lanes_of(step), :] = value[:, columns]

    def middle_back(index):
        item = (other, own)[index]
        loaded("middle")
        sent["dn%d" % index].wait_recv()

        def back(step, totals):
            at = rows_at(step * tile, tile)
            grad = r.two_mine[item, at, :].astype(jnp.float32) + r.two_from[item, at, :].astype(
                jnp.float32
            )
            dvalue, normed = norm_back(r.middle[item, at, :], grad, r.gains[1:2, :])
            dmiddle = dout_rows(item, at) + dvalue
            r.dmiddle[item, at, :] = dmiddle
            dattn = dmiddle.astype(low)
            r.dattn[rows_at(item * slab + step * tile, tile), :] = dattn
            return (
                totals[0] + fold(grad * normed),
                totals[1] + fold(grad),
                totals[2] + fold(dattn.astype(jnp.float32)),
            )

        totals = lax.fori_loop(0, slab // tile, back, (zero, zero, zero))
        for row, total in zip((2, 3, 4), totals):
            r.small[row : row + 1, :] += rows_sum(total)

    def attention_back(index):
        item = (other, own)[index]
        loaded("out_weight", "key_value", "query", "probs")
        rows = rows_of(item)
        r.keys_turned[...] = r.key_value[item, 0].astype(jnp.float32).T.astype(low)
        r.dmixed[...] = nt_dot(r.dattn[rows, :], r.out_weight[...]).astype(low)
        scale = HD ** (-0.5)
        for pair in range(pairs):
            lanes = slice(pair * 128, (pair + 1) * 128)
            values = r.key_value[item, 1, :, lanes]
            asked = r.query[rows, lanes]
            dmixed = r.dmixed[:, lanes]
            dkeys = dvalues = None
            turned = []
            for head in range(2):
                prob = r.probs[item, 2 * pair + head]
                dmixed_head = head_only(dmixed, head)
                dprob = nt_dot(values, dmixed_head)
                wide = prob.astype(jnp.float32)
                inner = rows_sum(wide * dprob)
                dscores = (wide * (dprob - inner)).astype(low)
                key_part = dot(dscores, head_only(asked, head))
                value_part = dot(prob, dmixed_head)
                dkeys = key_part if dkeys is None else dkeys + key_part
                dvalues = value_part if dvalues is None else dvalues + value_part
                at = pair * 128 + head * HD
                turned.append(dot(r.keys_turned[at : at + HD, :], dscores))
            r.dproject[0, rows, lanes] = (jnp.concatenate(turned, axis=0).T * scale).astype(low)
            dkeys = (dkeys * scale).astype(low)
            dvalues = dvalues.astype(low)
            r.dproject[1, rows, lanes] = dkeys[:slab]
            r.dproject[2, rows, lanes] = dvalues[:slab]
            r.give_kv[item, 0, :, lanes] = dkeys[slab:]
            r.give_kv[item, 1, :, lanes] = dvalues[slab:]
        sent["kv%d" % index] = start(2 + index, r.give_kv.at[item], r.got_kv.at[item], core)

    def grad_out_weight():
        loaded("mixed")
        for h in range(2):
            value = tn_dot(r.mixed[...], r.dattn[:, h * half_width : (h + 1) * half_width])
            r.own_out[h * local : (h + 1) * local, :] = value.astype(low)

    def join_heads():
        for index, item in enumerate((other, own)):
            sent["kv%d" % index].wait_recv()
            rows = rows_of(item)
            for c in range(2):
                value = r.dproject[1 + c, rows, :].astype(jnp.float32)
                value = value + r.got_kv[item, c].astype(jnp.float32)
                r.dproject[1 + c, rows, :] = value.astype(low)

    def project_back(index):
        item = (other, own)[index]
        loaded("qkv")
        rows = rows_of(item)

        @pl.loop(0, width // 256)
        def _(step):
            lanes = lanes_of(step)
            value = None
            for c in range(3):
                part = nt_dot(r.dproject[c, rows, :], r.qkv[c, lanes, :])
                value = part if value is None else value + part
            r.one_mine[item, :, lanes] = value.astype(low)

        sent["pn%d" % index] = start(4 + index, r.one_mine.at[item], r.one_from.at[item], cross)

    def grad_qkv(c):
        loaded("normed_one")
        r.own_qkv[c] = tn_dot(r.normed_one[...], r.dproject[c]).astype(low)

    def bias_sums():
        for c in (0, 2):
            value = rows_sum(fold(r.dproject[c].astype(jnp.float32)))
            r.small[6:7, (c // 2) * local : (c // 2 + 1) * local] = value
        loaded("bias_own")
        total = r.bias_sum[0:1, :] + rows_sum(r.bias_own[...])
        r.small[7:8, :] = total[:, :width]
        r.small[8:9, :] = total[:, width:]

    def input_back(index):
        item = (own, other)[index]
        loaded("block_in")
        sent["pn%d" % index].wait_recv()

        def back(step, totals):
            at = rows_at(step * tile, tile)
            grad = r.one_mine[item, at, :].astype(jnp.float32) + r.one_from[item, at, :].astype(
                jnp.float32
            )
            value = r.block_in[item, at, :].astype(jnp.float32)
            dvalue, normed = norm_back(value, grad, r.gains[0:1, :])
            r.grad_input[item, at, :] = (r.dmiddle[item, at, :] + dvalue).astype(low)
            return totals[0] + fold(grad * normed), totals[1] + fold(grad)

        totals = lax.fori_loop(0, slab // tile, back, (zero, zero))
        for row, total in zip((0, 1), totals):
            r.small[row : row + 1, :] += rows_sum(total)

    def small_step(index):
        if index > 0:
            sent["small"].wait_recv()
            r.small_sum[index] = r.small_sum[index - 1] + r.small_from[index - 1]
        else:
            r.small_sum[0] = r.small[...]
        if index < 4:
            device = (core, beside, side, over)[index]
            sent["small"] = start(
                6 + index, r.small_sum.at[index], r.small_from.at[index], device
            )
        else:
            r.small_total[...] = r.small_sum[4]

    tasks = {
        "sh0": take_own,
        "sh1": shade_other,
        "ffn0": lambda: None,
        "ffn1": feed_back,
        "kv": join_heads,
        "og": grad_out_weight,
        "bias": bias_sums,
    }
    for index in range(2):
        for name, work in (
            ("gd", grad_down),
            ("gu", grad_up),
            ("ln", middle_back),
            ("at", attention_back),
            ("p", project_back),
            ("f", input_back),
        ):
            tasks[name + str(index)] = functools.partial(work, index)
    for c in range(3):
        tasks["gq" + str(c)] = functools.partial(grad_qkv, c)
    for index in range(5):
        tasks["sm" + str(index)] = functools.partial(small_step, index)

    def full_step(name, unit):
        keep_full[{"k": "kernels", "t": "tconv"}[name]].wait()
        unit.sB()

    for name, unit in sums.items():
        for step in ("sA", "sB", "s0", "s1", "s2", "s2b", "s3", "s3b", "s4", "s5", "s6"):
            tasks[name + "." + step] = getattr(unit, step)
        if unit.full is not None:
            tasks[name + ".sB"] = functools.partial(full_step, name, unit)
    for name in ORDER:
        tasks[name]()
    for copy in copies:
        copy.wait_send()
    for unit in sums.values():
        unit.keep.wait()


PATHS = {
    "d2": "yso",
    "d3": "yso",
    "u2": "yso",
    "u3": "yso",
    "t": "yso",
    "k": "yso",
    "d0": "yso",
    "d1": "yso",
    "u0": "syo",
    "u1": "yso",
    "o": "yso",
    "q2": "syo",
    "q1": "yso",
    "q0": "yso",
}

ORDER = (
    "k.sA", "sh0", "sh1", "gd0", "d1.s0", "gd1", "d2.s0", "k.sB", "d1.s1", "d3.s0", "d0.s0", "ffn0",
    "ffn1", "d3.s1", "gu0", "u0.s0", "u1.s0", "d2.s1", "d0.s1", "d1.s2", "gu1", "u0.s1", "u2.s0", "ln0",
    "u1.s1", "d3.s2", "d1.s2b", "u3.s0", "at0", "d2.s2", "u2.s1", "u3.s1", "u0.s2", "t.sA", "d3.s2b", "d0.s2",
    "d1.s3", "k.s1", "d2.s2b", "t.sB", "u1.s2", "d3.s3", "d0.s2b", "d1.s3b", "u2.s2", "d2.s3", "u1.s2b", "d3.s3b",
    "u3.s2", "ln1", "d0.s3", "d1.s4", "u0.s2b", "at1", "u1.s3", "og", "o.s0", "d3.s4", "d2.s3b", "u2.s2b",
    "k.s2", "u3.s2b", "kv", "bias", "gq2", "t.s1", "d1.s5", "u0.s3", "gq0", "u1.s3b", "p0", "d2.s4",
    "gq1", "d3.s5", "p1", "u2.s3", "q1.s0", "q0.s0", "d0.s3b", "k.s2b", "q2.s0", "d1.s6", "o.s1", "d3.s6",
    "u3.s3", "q1.s1", "u0.s3b", "t.s2", "q0.s1", "q2.s1", "u1.s4", "u2.s3b", "d2.s5", "d0.s4", "k.s3", "d2.s6",
    "f0", "o.s2", "t.s2b", "u3.s3b", "q1.s2", "q2.s2", "u0.s4", "u2.s4", "k.s3b", "f1", "sm0", "t.s3",
    "o.s2b", "q0.s2", "u1.s5", "u3.s4", "sm1", "q1.s2b", "u1.s6", "d0.s5", "q2.s2b", "u0.s5", "d0.s6", "u0.s6",
    "k.s4", "u2.s5", "t.s3b", "o.s3", "u2.s6", "q0.s2b", "u3.s5", "q1.s3", "sm2", "q2.s3", "u3.s6", "t.s4",
    "o.s3b", "q0.s3", "k.s5", "q1.s3b", "sm3", "q2.s3b", "k.s6", "o.s4", "t.s5", "sm4", "q0.s3b", "q1.s4",
    "q2.s4", "t.s6", "q0.s4", "o.s5", "o.s6", "q2.s5", "q1.s5", "q2.s6", "q1.s6", "q0.s5", "q0.s6",
)

LANDED = ("two_own", "ddown_own", "dhidden_own")
LOADED = (
    "two_own",
    "shift_own",
    "ddown_own",
    "active",
    "down",
    "slope",
    "up",
    "dhidden_own",
    "normed_two",
    "middle",
    "out_weight",
    "key_value",
    "query",
    "probs",
    "mixed",
    "qkv",
    "normed_one",
    "block_in",
    "bias_own",
)


def backward_section(arrays):
    low = jnp.bfloat16
    wide = jnp.float32
    items, slab, width = arrays["grad_out"].shape
    tokens = items * slab
    local = arrays["qkv"].shape[2]
    units = arrays["down"].shape[0]
    patches = arrays["key_value"].shape[2]
    kernel_rows = arrays["grad_kernels"].shape[1]
    near = ["grad_out", "dtap", "gains"]
    distant = list(LOADED) + ["grad_kernels", "grad_tconv"]
    totals = {
        "down": (4, units // 2, width // 2),
        "up": (4, width, units // 4),
        "out": (2 * local, width // 2),
        "qkv": (3, width, local),
        "kernels": (kernel_rows, CH),
        "tconv": arrays["grad_tconv"].shape[1:],
    }
    scratch = {
        name: pltpu.VMEM(arrays[name].shape, arrays[name].dtype)
        for name in LOADED
        if name not in LANDED
    }
    for name, shape in totals.items():
        full = name in ("kernels", "tconv")
        rows, columns = shape[-2:]
        scratch["own_" + name] = pltpu.VMEM((2, rows // 2, columns) if full else shape, low)
        labels = [name] if len(shape) == 2 else [name + str(part) for part in range(shape[0])]
        for label in labels:
            for end, one in sum_scratch(rows, columns).items():
                scratch[label + end] = one
            if full:
                scratch["sum_" + name] = pltpu.VMEM(shape, low)
                scratch[label + "_both"] = pltpu.VMEM((2, rows // 2, columns), low)
                scratch[label + "_cross"] = pltpu.VMEM((rows // 2, columns), low)
    block = (items, slab, width)
    for name, shape, dtype in (
        ("ddown", (tokens, width), low),
        ("dhidden", (tokens, units), low),
        ("bias_sum", (8, units), wide),
        ("two_mine", block, low),
        ("two_from", block, low),
        ("dmiddle", block, wide),
        ("dattn", (tokens, width), low),
        ("dmixed", (slab, local), low),
        ("keys_turned", (local, patches), low),
        ("give_kv", (items, 2, slab, local), low),
        ("got_kv", (items, 2, slab, local), low),
        ("dproject", (3, tokens, local), low),
        ("one_mine", block, low),
        ("one_from", block, low),
        ("small", (16, width), wide),
        ("small_sum", (5, 16, width), wide),
        ("small_from", (4, 16, width), wide),
    ):
        scratch[name] = pltpu.VMEM(shape, dtype)
    dma = pltpu.SemaphoreType.DMA
    scratch["load_sem"] = dma((len(LOADED) + 2,))
    scratch["send"] = dma((10,))
    scratch["recv"] = dma((10,))
    scratch["sum_send"] = dma((14, COPIES))
    scratch["sum_recv"] = dma((14, COPIES))
    scratch["sum_local"] = dma((14,))
    outputs = ["grad_input", "small_total"] + ["total_" + name for name in totals]
    layout = near + [name + "_hbm" for name in distant] + outputs + list(scratch)
    vmem = pl.BlockSpec(memory_space=pltpu.VMEM)
    hbm = pl.BlockSpec(memory_space=pl.ANY)
    results = pl.pallas_call(
        functools.partial(backward_kernel, tuple(layout)),
        out_shape=[
            jax.ShapeDtypeStruct(block, low),
            jax.ShapeDtypeStruct((16, width), wide),
        ]
        + [jax.ShapeDtypeStruct(shape, low) for shape in totals.values()],
        in_specs=[vmem] * len(near) + [hbm] * len(distant),
        out_specs=[vmem] * 2 + [hbm] * len(totals),
        scratch_shapes=list(scratch.values()),
        name="backward_section",
        compiler_params=pltpu.CompilerParams(
            collective_id=3, has_side_effects=True, vmem_limit_bytes=62 * 2**20
        ),
    )(*[arrays[name] for name in near + distant])
    return dict(zip(outputs, results))


def body(
    block_in,
    crop_shape,
    norm_gains,
    shifts,
    qkv_weight,
    qv_bias,
    out_weight,
    up_weight,
    up_bias,
    down_weight,
    tconv_weight,
    kernels,
    grad_out,
    grad_decoded,
):
    (
        normed_one,
        query,
        key_value,
        probs,
        mixed,
        middle,
        normed_two,
        active,
        slope,
        tapped,
    ) = forward_section(
        block_in,
        norm_gains,
        shifts,
        qkv_weight,
        qv_bias,
        out_weight,
        up_weight,
        up_bias,
        down_weight,
        crop_shape,
    )
    tap = decoder_section(
        tapped,
        tconv_weight,
        kernels,
        grad_decoded.reshape(DEPTH, SIDE, 2, WIDE, CH),
        crop_shape,
        grad_out,
        down_weight,
        slope,
        up_weight,
    )
    result = backward_section(
        {
            "grad_out": grad_out,
            "dtap": tap["dtap"],
            "two_own": tap["two"],
            "shift_own": tap["shift_own"],
            "ddown_own": tap["ddown"],
            "dhidden_own": tap["dhidden"],
            "bias_own": tap["bias_own"],
            "block_in": block_in,
            "gains": norm_gains,
            "down": down_weight,
            "slope": slope,
            "up": up_weight,
            "active": active,
            "normed_two": normed_two,
            "middle": middle,
            "out_weight": out_weight,
            "key_value": key_value,
            "query": query,
            "probs": probs,
            "mixed": mixed,
            "qkv": qkv_weight,
            "normed_one": normed_one,
            "grad_kernels": tap["grad_kernels"],
            "grad_tconv": tap["grad_tconv"],
        }
    )
    small = result["small_total"]
    totals = {name[6:]: array for name, array in result.items() if name.startswith("total_")}
    groups = lax.axis_size("dp") // GROUP
    if groups > 1:
        same = [[part * GROUP + i for part in range(groups)] for i in range(GROUP)]
        small = lax.psum(small, "dp", axis_index_groups=same)
        totals = {
            name: lax.psum(array, "dp", axis_index_groups=same) for name, array in totals.items()
        }
    sums, passed, smalls = finish_section(
        totals, (tap["block_all"], tap["decoded"], result["grad_input"]), small
    )
    return (
        passed[0],
        passed[1].reshape(grad_decoded.shape),
        passed[2],
        smalls[0],
        smalls[1],
        sums["qkv"],
        smalls[2],
        sums["out"],
        sums["up"],
        smalls[3],
        sums["down"],
        sums["tconv"],
        sums["kernels"].transpose(0, 2, 1),
    )


def solution(mesh):
    return jax.shard_map(
        body,
        mesh=mesh,
        in_specs=(
            P("dp", "blk", None),
            P("dp"),
            P(),
            P(),
            P(None, None, "tensor"),
            P(None, "tensor"),
            P("tensor", None),
            P(None, "tensor"),
            P("tensor"),
            P("tensor", None),
            P(),
            P(),
            P("dp", "blk", None),
            P(("dp", "tensor"), "blk", None, None, None),
        ),
        out_specs=(
            P("dp", "blk", None),
            P(("dp", "tensor"), "blk", None, None, None),
            P("dp", "blk", None),
            P(),
            P(),
            P(None, None, "tensor"),
            P(None, "tensor"),
            P("tensor", None),
            P(None, "tensor"),
            P("tensor"),
            P("tensor", None),
            P(None, "tensor"),
            P(None, None, "tensor"),
        ),
        check_vma=False,
    )
```
